32 devices in a mesh: blk: 8 (over y, x, core), dom: 4 (over z).
Axes of the slice: x: 2, y: 2, z: 4, core: 2. Of those that a mesh axis runs over, the one named last changes fastest.
Arguments:
- pno_basis: float32 [256, 64, 256], P(('blk', 'dom')), may hold values from -0.375 to 0.375
- amplitudes: float32 [256, 4096], P(('blk', 'dom')), may hold values from -6 to 6
- send_list: int32 [8, 4, 8, 1], P('blk', 'dom'), may hold values from 0 to 7
- couple: int32 [256, 8], P(('blk', 'dom')), may hold values from 0 to 7, as said below
- couple_weight: float32 [256, 8], P(('blk', 'dom')), may hold values from 0.25 to 1
- fit_weight: float32 [256, 16], P(('blk', 'dom')), may hold values from 0.25 to 1
- fit_blocks: float32 [16, 2, 256, 256], P('blk', None, 'dom'), may hold values from -0.375 to 0.375
Outputs:
- updated: float32 [256, 4096], P(('blk', 'dom'))
The draws below stay inside these ranges and needn't reach their ends.
Inputs may be any that keep to these rules, and one draw needn't show every extreme that they name: `couple`: slot j of a device holds what peer j // 1 of blk sent it in its place j % 1; on every device each slot is named by at least one coupling.
All inputs are finite; a program needn't handle non-finite values.
Results may differ from the reference program's by a relative error of at most 0.0003.
Values sent between devices are 32-bit elements; how exact they have to be, the bound alone decides.
No kernel may reach another device: no remote copies, remote signals or barrier semaphores. Data moves between devices by JAX's collectives and lax.ppermute only.
A program may use at most 64 MiB of HBM per device.

```python
import math
import jax
import jax.numpy as jnp
from jax import lax

NORB = 256
NPNO = 64
PAIR_DEV = 8
NCPL = 8
CAP = 1
STOPS = 8
FB_DEV = 2
PAIRS = 256
FBLOCKS = 16
N_BLK = 8
N_DOM = 4


def draw_couple(key, part):
    read_count = PAIR_DEV * NCPL
    slot_count = N_BLK * CAP
    owner_count = PAIRS // PAIR_DEV
    random_scores = jax.random.randint(key, (owner_count, read_count), 0, 1 << 20) * read_count + jnp.arange(read_count, dtype=jnp.int32)[None, :]
    ordering = jnp.argsort(random_scores, axis=1, stable=True).astype(jnp.int32)
    return (ordering % slot_count).reshape(PAIRS, NCPL)


def place_ends(drawn, key, least, top_value):
    extent = drawn.shape
    place = [jax.random.randint(jax.random.fold_in(key, axis), (), 0, extent[axis]) for axis in range(len(extent))]
    drawn = drawn.at[tuple(place)].set(least)
    longest = extent.index(max(extent))
    place[longest] = (place[longest] + 1) % extent[longest]
    return drawn.at[tuple(place)].set(top_value)


def steps_of(stream_key, extent, split, smallest, largest):
    factor_of, own = 1.0, jax.random.fold_in(stream_key, 6)
    for dim, parts in split:
        draws = jnp.exp(jax.random.uniform(jax.random.fold_in(own, dim), (parts,), jnp.float32, smallest / len(split), largest / len(split)))
        factor_of = factor_of * jnp.repeat(draws, extent[dim] // parts).reshape([-1 if axis == dim else 1 for axis in range(len(extent))])
    return factor_of


def scatter_about(key, shape, deviation, bound, pieces=(), kind=jnp.bfloat16):
    values = deviation * jax.random.normal(key, shape, jnp.float32)
    if pieces:
        values = values * steps_of(key, shape, pieces, -0.22, 0.18)
    return jnp.clip(values, -bound, bound).astype(kind)


def setup_inputs(seed: int = 0) -> dict:
    streams_of = jax.random.split(jax.random.key(seed), 8)
    pno_basis = scatter_about(streams_of[0], (PAIRS, NPNO, NORB), NORB ** -0.5, 0.375, ((0, 32),), jnp.float32)
    amplitudes = scatter_about(streams_of[1], (PAIRS, NPNO * NPNO), 1.0, 6.0, ((0, 32),), jnp.float32)
    send_list = place_ends(jax.random.randint(streams_of[2], (N_BLK, N_DOM, N_BLK, CAP), 0, PAIR_DEV), jax.random.fold_in(streams_of[2], 1), 0, PAIR_DEV - 1).astype(jnp.int32)
    couple = draw_couple(jax.random.fold_in(streams_of[7], 71), 0)
    couple_weight = jnp.clip(jnp.exp(math.log(1.0) - 1.3862944 * jax.random.uniform(streams_of[4], (PAIRS, NCPL), jnp.float32) ** steps_of(streams_of[4], (PAIRS, NCPL), ((0, 32),), -0.2, 0.2)), 0.25, 1.0)
    fit_weight = jnp.clip(jnp.exp(math.log(1.0) - 1.3862944 * jax.random.uniform(streams_of[5], (PAIRS, STOPS * FB_DEV), jnp.float32) ** steps_of(streams_of[5], (PAIRS, STOPS * FB_DEV), ((0, 32),), -0.2, 0.2)), 0.25, 1.0)
    fit_blocks = scatter_about(streams_of[6], (FBLOCKS, 2, NORB, NORB), NORB ** -0.5, 0.375, ((0, 8), (2, 4)), jnp.float32)
    return dict(pno_basis=pno_basis, amplitudes=amplitudes, send_list=send_list, couple=couple, couple_weight=couple_weight, fit_weight=fit_weight, fit_blocks=fit_blocks)


HIGHEST = lax.Precision.HIGHEST


def couple_term(pair_basis, pair_amps, partner_basis, partner_amps, weights):
    intersection = jnp.einsum('par,pcbr->pcab', pair_basis, partner_basis, precision=HIGHEST)
    half_product = jnp.einsum('pcab,pcbe->pcae', intersection, partner_amps, precision=HIGHEST)
    sandwich = jnp.einsum('pcae,pcfe->pcaf', half_product, intersection, precision=HIGHEST)
    return pair_amps + jnp.einsum('pc,pcaf->paf', weights, sandwich, precision=HIGHEST)


def fit_term(pair_basis, dressed, blocks, weights):
    pair_count, pno_count, orbital_count = pair_basis.shape
    flat_basis = pair_basis.reshape(pair_count * pno_count, orbital_count)
    stacked = blocks.reshape(2 * orbital_count, orbital_count)
    projected = jnp.dot(flat_basis, stacked.T, precision=HIGHEST, preferred_element_type=jnp.float32)
    projected = projected.reshape(pair_count, pno_count, 2, orbital_count)
    inner_blocks = jnp.einsum('par,pbmr->mpab', pair_basis, projected, precision=HIGHEST)
    left_product = jnp.einsum('pai,pij->paj', inner_blocks[0], dressed, precision=HIGHEST)
    fit_contrib = jnp.einsum('paj,pbj->pab', left_product, inner_blocks[1], precision=HIGHEST)
    return weights[:, None, None] * fit_contrib


def reference(pno_basis, amplitudes, send_list, couple, couple_weight, fit_weight, fit_blocks):
    pno_count = pno_basis.shape[1]
    group_size = PAIR_DEV * N_DOM
    all_amps = amplitudes.reshape(-1, pno_count, pno_count)

    def per_group(group_index):
        start = group_index * group_size
        pair_basis = lax.dynamic_slice_in_dim(pno_basis, start, group_size, 0)
        own_amps = lax.dynamic_slice_in_dim(all_amps, start, group_size, 0)
        coupled = lax.dynamic_slice_in_dim(couple, start, group_size, 0)
        coupling_weights = lax.dynamic_slice_in_dim(couple_weight, start, group_size, 0)
        fitting_weights = lax.dynamic_slice_in_dim(fit_weight, start, group_size, 0)
        domain_index = (jnp.arange(group_size, dtype=jnp.int32) // PAIR_DEV)[:, None]
        peer_index = coupled // CAP
        slot_index = coupled % CAP
        local_index = send_list[peer_index, domain_index, group_index, slot_index]
        partner = (peer_index * N_DOM + domain_index) * PAIR_DEV + local_index
        dressed = couple_term(pair_basis, own_amps, pno_basis[partner], all_amps[partner], coupling_weights)
        updated_amps = dressed
        for stop_index in range(STOPS):
            source = (group_index - stop_index) % N_BLK
            for block_index in range(FB_DEV):
                blocks = lax.dynamic_index_in_dim(fit_blocks, source * FB_DEV + block_index, 0, keepdims=False)
                updated_amps = updated_amps + fit_term(pair_basis, dressed, blocks, fitting_weights[:, stop_index * FB_DEV + block_index])
        return updated_amps.reshape(group_size, pno_count * pno_count)

    result = lax.map(per_group, jnp.arange(N_BLK, dtype=jnp.int32))
    return result.reshape(-1, pno_count * pno_count)
```

```python
import functools

import jax
import jax.numpy as jnp
from jax import lax
from jax.experimental import pallas as pl
from jax.experimental.pallas import tpu as pltpu
from jax.sharding import PartitionSpec as P

HIGHEST = lax.Precision.HIGHEST
VMEM_BYTES = 48 * 2**20
NN = (((1,), (0,)), ((), ()))
NT = (((1,), (1,)), ((), ()))
TN = (((0,), (0,)), ((), ()))


def halves(x):
    high = x.astype(jnp.bfloat16)
    return high, (x - high.astype(jnp.float32)).astype(jnp.bfloat16)


def dot(a, b, dims):
    return lax.dot_general(a, b, dims, preferred_element_type=jnp.float32)


def dot3(a, b, dims):
    (a_high, a_low), (b_high, b_low) = a, b
    return dot(a_high, b_high, dims) + (dot(a_high, b_low, dims) + dot(a_low, b_high, dims))


def middle_of(basis_halves, dressed, middle_high, middle_low, pair):
    right = dot3(halves(dressed), basis_halves, NN)
    middle_high[pair], middle_low[pair] = halves(dot3(basis_halves, halves(right), TN))


def dress_kernel(slot_weight, basis, basis_in, amps, amps_in, dressed, basis_high, basis_low, middle_high, middle_low):
    pair_count, pno_count, orbital_count = basis.shape
    slot_count = basis_in.shape[0]
    own = halves(basis[...].reshape(pair_count * pno_count, orbital_count))
    basis_high[...], basis_low[...] = own
    others = halves(basis_in[...].reshape(slot_count * pno_count, orbital_count))
    overlap = dot3(own, others, NT)
    overlap_high, overlap_low = halves(overlap)
    left = []
    for slot in range(slot_count):
        cols = slice(slot * pno_count, (slot + 1) * pno_count)
        left.append(dot3((overlap_high[:, cols], overlap_low[:, cols]), halves(amps_in[slot]), NN))
    for pair in range(pair_count):
        rows = slice(pair * pno_count, (pair + 1) * pno_count)
        scaled = jnp.concatenate([left[slot][rows] * slot_weight[pair, slot] for slot in range(slot_count)], axis=1)
        total = amps[pair] + dot3(halves(scaled), (overlap_high[rows], overlap_low[rows]), NT)
        dressed[pair] = total
        middle_of((own[0][rows], own[1][rows]), total, middle_high, middle_low, pair)


def middle_kernel(basis, dressed, basis_high, basis_low, middle_high, middle_low):
    pair_count, pno_count, orbital_count = basis.shape
    own = halves(basis[...].reshape(pair_count * pno_count, orbital_count))
    basis_high[...], basis_low[...] = own
    for pair in range(pair_count):
        rows = slice(pair * pno_count, (pair + 1) * pno_count)
        middle_of((own[0][rows], own[1][rows]), dressed[pair], middle_high, middle_low, pair)


def fit_kernel(weight, blocks, basis_high, basis_low, middle_high, middle_low, before, after, left_high, left_low, right):
    pair_count, pno_count, _ = before.shape
    flat_count, orbital_count = basis_high.shape
    group_count = left_high.shape[0]
    group = pl.program_id(0)
    own = basis_high[...], basis_low[...]

    def projected(part):
        return dot3(own, halves(blocks[0, :, part].reshape(orbital_count, orbital_count)), NN)

    left_high[group], left_low[group] = halves(projected(0))
    right_high, right_low = halves(projected(1))
    right[group, :, :pno_count] = right_high.reshape(pair_count, pno_count, orbital_count)
    right[group, :, pno_count:] = right_low.reshape(pair_count, pno_count, orbital_count)

    @pl.when(group == group_count - 1)
    def _():
        for pair in range(pair_count):
            rows = slice(pair * pno_count, (pair + 1) * pno_count)
            left = tuple(x[:, rows].reshape(group_count * pno_count, orbital_count) for x in (left_high, left_low))
            moved = dot3(left, (middle_high[pair], middle_low[pair]), NN)
            quarters = jnp.zeros((2 * pno_count, 2 * pno_count), jnp.float32)
            for g in range(group_count):
                scaled = halves(moved[g * pno_count:(g + 1) * pno_count] * weight[pair, g])
                quarters += dot(jnp.concatenate(scaled, axis=0), right[g, pair], NT)
            tops = quarters[:pno_count] + quarters[pno_count:]
            after[pair] = before[pair] + (tops[:, :pno_count] + tops[:, pno_count:])


def whole(shape):
    return pl.BlockSpec(shape, lambda *_: (0,) * len(shape))


def prepared_shapes(pair_count, pno_count, orbital_count):
    flat = jax.ShapeDtypeStruct((pair_count * pno_count, orbital_count), jnp.bfloat16)
    middle = jax.ShapeDtypeStruct((pair_count, orbital_count, orbital_count), jnp.bfloat16)
    return flat, flat, middle, middle


def add_groups(updated, prepared, blocks, weight):
    pair_count, pno_count, _ = updated.shape
    group_count, dom_count, part_count, row_count, orbital_count = blocks.shape
    flat_count = pair_count * pno_count
    rows = group_count * flat_count
    return pl.pallas_call(
        fit_kernel,
        grid=(group_count,),
        out_shape=jax.ShapeDtypeStruct(updated.shape, jnp.float32),
        in_specs=[
            pl.BlockSpec(memory_space=pltpu.SMEM),
            pl.BlockSpec((1, dom_count, part_count, row_count, orbital_count), lambda g: (g, 0, 0, 0, 0)),
            *[whole(x.shape) for x in prepared],
            whole(updated.shape),
        ],
        out_specs=whole(updated.shape),
        scratch_shapes=[
            pltpu.VMEM((group_count, flat_count, orbital_count), jnp.bfloat16),
            pltpu.VMEM((group_count, flat_count, orbital_count), jnp.bfloat16),
            pltpu.VMEM((group_count, pair_count, 2 * pno_count, orbital_count), jnp.bfloat16),
        ],
        compiler_params=pltpu.CompilerParams(vmem_limit_bytes=VMEM_BYTES),
        cost_estimate=pl.CostEstimate(
            flops=3 * 2 * rows * orbital_count * (3 * orbital_count + 2 * pno_count),
            bytes_accessed=4 * blocks.size,
            transcendentals=0,
        ),
    )(weight, blocks, *prepared, updated)


def from_behind(x, axis, by):
    count = lax.axis_size(axis)
    return lax.ppermute(x, axis, [(i, (i + by) % count) for i in range(count)])


def dress_with(pair_amps, intersection, partner_amps, weights):
    half_product = jnp.einsum("pcab,pcbe->pcae", intersection, partner_amps, precision=HIGHEST)
    sandwich = jnp.einsum("pcae,pcfe->pcaf", half_product, intersection, precision=HIGHEST)
    return pair_amps + jnp.einsum("pc,pcaf->paf", weights, sandwich, precision=HIGHEST)


def dress(pno_basis, pair_amps, basis_in, amps_in, couple, couple_weight):
    pair_count, pno_count, orbital_count = pno_basis.shape
    slot_count, couple_count = basis_in.shape[0], couple.shape[1]
    prepared = prepared_shapes(pair_count, pno_count, orbital_count)
    params = pltpu.CompilerParams(vmem_limit_bytes=VMEM_BYTES)
    if slot_count <= couple_count:
        named = couple[:, :, None] == jnp.arange(slot_count, dtype=couple.dtype)
        slot_weight = jnp.sum(jnp.where(named, couple_weight[:, :, None], 0.0), axis=1)
        operands = pno_basis, basis_in, pair_amps, amps_in
        dressed, *prepared = pl.pallas_call(
            dress_kernel,
            out_shape=(jax.ShapeDtypeStruct(pair_amps.shape, jnp.float32), *prepared),
            in_specs=[pl.BlockSpec(memory_space=pltpu.SMEM), *[whole(x.shape) for x in operands]],
            compiler_params=params,
        )(slot_weight, *operands)
        return dressed, prepared
    partner_basis = jnp.take(basis_in, couple, axis=0)
    intersection = jnp.einsum("par,pcbr->pcab", pno_basis, partner_basis, precision=HIGHEST)
    dressed = dress_with(pair_amps, intersection, jnp.take(amps_in, couple, axis=0), couple_weight)
    prepared = pl.pallas_call(middle_kernel, out_shape=prepared, compiler_params=params)(pno_basis, dressed)
    return dressed, prepared


def on_device(pno_basis, amplitudes, send_list, couple, couple_weight, fit_weight, fit_blocks):
    pair_count, pno_count, orbital_count = pno_basis.shape
    block_count, part_count, row_count, _ = fit_blocks.shape
    group_total, dom_count = lax.axis_size("blk"), lax.axis_size("dom")
    stops = fit_weight.shape[1] // block_count
    pair_amps = amplitudes.reshape(pair_count, pno_count, pno_count)
    send_order = send_list.reshape(-1)
    basis_in = lax.all_to_all(jnp.take(pno_basis, send_order, axis=0), "blk", split_axis=0, concat_axis=0, tiled=True)
    amps_in = lax.all_to_all(jnp.take(pair_amps, send_order, axis=0), "blk", split_axis=0, concat_axis=0, tiled=True)
    stop_weight = fit_weight.reshape(pair_count, stops, block_count)
    if stops == group_total:
        gathered = [
            lax.all_gather(fit_blocks[b], ("blk", "dom"), axis=0).reshape(
                group_total, dom_count, part_count, row_count, orbital_count
            )
            for b in range(block_count)
        ]
        order = jnp.mod(lax.axis_index("blk") - jnp.arange(group_total), group_total)
        weights = jnp.take(stop_weight, order, axis=1)
    updated, prepared = dress(pno_basis, pair_amps, basis_in, amps_in, couple, couple_weight)
    if stops == group_total:
        for b in range(block_count):
            updated = add_groups(updated, prepared, gathered[b], weights[:, :, b])
    else:
        current = jnp.moveaxis(lax.all_gather(fit_blocks, "dom", axis=0), 1, 0)
        for stop in range(stops):
            if stop > 0:
                current = from_behind(current, "blk", 1)
            updated = add_groups(updated, prepared, current, stop_weight[:, stop])
    return updated.reshape(pair_count, pno_count * pno_count)


def solution(mesh):
    placed = (
        P(("blk", "dom"), None, None),
        P(("blk", "dom"), None),
        P("blk", "dom", None, None),
        P(("blk", "dom"), None),
        P(("blk", "dom"), None),
        P(("blk", "dom"), None),
        P("blk", None, "dom", None),
    )
    return jax.shard_map(
        on_device, mesh=mesh, in_specs=placed, out_specs=P(("blk", "dom"), None), check_vma=False
    )
```

```python
import jax
import jax.numpy as jnp
from jax import lax
from jax.experimental import pallas as pl
from jax.experimental.pallas import tpu as pltpu
from jax.sharding import PartitionSpec as P

HIGHEST = lax.Precision.HIGHEST
VMEM_BYTES = 48 * 2**20
SET = 4
NN = (((1,), (0,)), ((), ()))
NT = (((1,), (1,)), ((), ()))


def halves(x):
    high = x.astype(jnp.bfloat16)
    return high, (x - high.astype(jnp.float32)).astype(jnp.bfloat16)


def dot(a, b, dims):
    return lax.dot_general(a, b, dims, preferred_element_type=jnp.float32)


def dot3(a, b, dims):
    (a_high, a_low), (b_high, b_low) = a, b
    return dot(a_high, b_high, dims) + (dot(a_high, b_low, dims) + dot(a_low, b_high, dims))


def fold_rows(x):
    return x[: x.shape[0] // 2] + x[x.shape[0] // 2:]


def fold_lanes(x):
    return x[:, : x.shape[1] // 2] + x[:, x.shape[1] // 2:]


def stack(parts, axis=0):
    return jnp.concatenate(parts, axis=axis)


def from_partner(x, axis, flip):
    return lax.ppermute(x, axis, [(i, i ^ flip) for i in range(lax.axis_size(axis))])


def from_behind(x, axis, by):
    count = lax.axis_size(axis)
    return lax.ppermute(x, axis, [(i, (i + by) % count) for i in range(count)])


def vmem(count):
    return [pl.BlockSpec(memory_space=pltpu.VMEM)] * count


def pack_kernel(send, basis, amps, *sent):
    me = lax.axis_index("blk")
    pno_count = amps.shape[1]
    lanes = basis.shape[2] // pno_count
    step = pno_count // lanes
    for flip, out in enumerate(sent):
        pair = send[me ^ flip]
        out[:pno_count] = basis[pair]
        listed = amps[pair]
        out[pno_count:] = stack([listed[i * step:(i + 1) * step] for i in range(lanes)], 1)


def pack_pairs(send_order, basis, amps):
    _, pno_count, orbital_count = basis.shape
    rows = pno_count + pno_count * pno_count // orbital_count
    shape = jax.ShapeDtypeStruct((rows, orbital_count), jnp.float32)
    return pl.pallas_call(
        pack_kernel,
        out_shape=[shape] * send_order.shape[0],
        in_specs=[pl.BlockSpec(memory_space=pltpu.SMEM), *vmem(2)],
        out_specs=vmem(send_order.shape[0]),
        compiler_params=pltpu.CompilerParams(vmem_limit_bytes=VMEM_BYTES),
        cost_estimate=pl.CostEstimate(flops=0, bytes_accessed=4 * basis.size, transcendentals=0),
    )(send_order, basis, amps)


def dress_kernel(couple, couple_weight, fit_weight, basis, amps, *refs):
    *coupled, dressed, turned = refs
    pair_count, pno_count, orbital_count = basis.shape
    half = pno_count // 2
    me = lax.axis_index("blk")
    own = halves(basis[...].reshape(pair_count * pno_count, orbital_count))
    others = halves(stack([x[:pno_count] for x in coupled]))
    overlap = halves(dot3(own, others, NT))
    left, slot_weight = [], []
    for flip, x in enumerate(coupled):
        cols = slice(flip * pno_count, (flip + 1) * pno_count)
        packed = x[pno_count:]
        partner = stack([packed[:, i:i + pno_count] for i in range(0, orbital_count, pno_count)])
        left.append(dot3([x[:, cols] for x in overlap], halves(partner), NN))
        named = jnp.where(couple[...] == (me ^ flip), couple_weight[...], 0.0)
        slot_weight.append(jnp.sum(named, axis=1, keepdims=True))
    dressed[:, half:, :] = jnp.zeros((pair_count, dressed.shape[1] - half, 2 * pno_count), jnp.float32)
    for pair in range(pair_count):
        rows = slice(pair * pno_count, (pair + 1) * pno_count)
        scaled = stack([x[rows] * w[pair:pair + 1] for x, w in zip(left, slot_weight)], 1)
        turned[pair] = amps[pair] + dot3(halves(scaled), [x[rows] for x in overlap], NT)
        dressed[pair, :half] = two_to_one(turned, pair, half)
        dressed[pair, half:half + 1, : fit_weight.shape[1]] = fit_weight[pair:pair + 1, :]


def two_to_one(ref, pair, half):
    return stack([ref[pair, pl.ds(i, half, stride=2), :] for i in range(2)], 1)


def dress(couple, couple_weight, fit_weight, basis, amps, coupled):
    pair_count, pno_count, _ = basis.shape
    return pl.pallas_call(
        dress_kernel,
        out_shape=jax.ShapeDtypeStruct((pair_count, pno_count // 2 + 8, 2 * pno_count), jnp.float32),
        in_specs=vmem(5 + len(coupled)),
        out_specs=vmem(1)[0],
        scratch_shapes=[pltpu.VMEM((pair_count, pno_count, pno_count), jnp.float32)],
        compiler_params=pltpu.CompilerParams(vmem_limit_bytes=VMEM_BYTES),
        cost_estimate=pl.CostEstimate(flops=4 * 10**9, bytes_accessed=8 * basis.size, transcendentals=0),
    )(couple, couple_weight, fit_weight, basis, amps, *coupled)


def fit_kernel(behind, first, *refs):
    per_set = [refs[i * SET:(i + 1) * SET] for i in range(2 if first else 3)]
    refs = refs[SET * len(per_set):]
    bases, dressed = per_set[:2]
    dom_count = len(refs) - SET - 7
    pieces, refs = refs[:dom_count], refs[dom_count:]
    after, (block_high, block_low, basis_cat, dressed_cat, weight_rows, projected, turned) = refs[:SET], refs[SET:]
    pair_count, pno_count, orbital_count = bases[0].shape
    half = pno_count // 2
    block_count, part_count, row_count, _ = pieces[0].shape
    group_total = lax.axis_size("blk")
    me, place = lax.axis_index("blk"), lax.axis_index("dom")
    source = lax.rem(me + group_total - behind, group_total)

    for shift, piece in enumerate(pieces):
        start = pl.multiple_of(lax.rem(place + dom_count - shift, dom_count) * row_count, row_count)
        for b in range(block_count):
            for m in range(part_count):
                high, low = halves(piece[b, m])
                block_high[m, b, pl.ds(start, row_count), :] = high
                block_low[m, b, pl.ds(start, row_count), :] = low
    for member in range(SET):
        span = slice(member * pair_count, (member + 1) * pair_count)
        high, low = halves(bases[member][...])
        basis_cat[span, :pno_count] = high
        basis_cat[span, pno_count:] = low
        stop = lax.rem((me ^ member) + group_total - source, group_total)
        row = dressed[member][:, half:half + 1, :]
        lane = lax.broadcasted_iota(jnp.int32, row.shape, 2)
        for b in range(block_count):
            weight = jnp.sum(jnp.where(lane == stop * block_count + b, row, 0.0), axis=2, keepdims=True)
            weight_rows[b, span] = jnp.broadcast_to(weight, (pair_count, 1, pno_count))
        for pair in range(pair_count):
            packed = dressed[member][pair, :half]
            at = member * pair_count + pair
            turned[at, pl.ds(0, half, stride=2), :] = packed[:, :pno_count]
            turned[at, pl.ds(1, half, stride=2), :] = packed[:, pno_count:]
            dressed_cat[at] = stack(halves(turned[at]), 1)

    def project(member, _):
        span = pl.ds(pl.multiple_of(member * pair_count, pair_count), pair_count)
        both = basis_cat[span].reshape(2 * pair_count * pno_count, orbital_count)
        high = basis_cat[span, :pno_count].reshape(pair_count * pno_count, orbital_count)
        for m in range(part_count):
            for b in range(block_count):
                by_high = dot(both, block_high[m, b], NN).reshape(pair_count, 2 * pno_count, orbital_count)
                by_low = dot(high, block_low[m, b], NN).reshape(pair_count, pno_count, orbital_count)
                product = halves(by_high[:, :pno_count] + (by_high[:, pno_count:] + by_low))
                for i in range(2):
                    at = ((i * part_count + m) * block_count + b) * pno_count
                    projected[span, at:at + pno_count] = product[i]
        return 0

    lax.fori_loop(0, SET, project, 0)

    def update(at, _):
        inner = fold_lanes(fold_rows(dot(projected[at], basis_cat[at], NT)))
        size = block_count * pno_count
        weight = stack([jnp.broadcast_to(weight_rows[b, at], (pno_count, pno_count)) for b in range(block_count)])
        moved = fold_lanes(fold_rows(dot(stack(halves(inner[:size] * weight)), dressed_cat[at], NN)))
        moved, inner = halves(moved), halves(inner[size:])
        total = jnp.zeros((2 * pno_count, 2 * pno_count), jnp.float32)
        for b in range(block_count):
            rows = slice(b * pno_count, (b + 1) * pno_count)
            total += dot(stack([x[rows] for x in moved]), stack([x[rows] for x in inner]), NT)
        turned[at] = fold_lanes(fold_rows(total))
        return 0

    lax.fori_loop(0, SET * pair_count, update, 0, unroll=4)

    for member in range(SET):
        for pair in range(pair_count):
            total = two_to_one(turned, member * pair_count + pair, half)
            if not first:
                total += per_set[2][member][pair]
            elif member == 0:
                total += dressed[0][pair, :half]
            after[member][pair] = total


def fit(behind, bases, dressed, pieces, before):
    pair_count, pno_count, orbital_count = bases[0].shape
    block_count, part_count, row_count, _ = pieces[0].shape
    pairs = SET * pair_count
    first = before is None
    operands = [*bases, *dressed, *([] if first else before), *pieces]
    products = block_count * part_count * pairs * pno_count * orbital_count * (orbital_count + pno_count)
    return pl.pallas_call(
        lambda *refs: fit_kernel(behind, first, *refs),
        out_shape=[jax.ShapeDtypeStruct((pair_count, pno_count // 2, 2 * pno_count), jnp.float32)] * SET,
        in_specs=vmem(len(operands)),
        out_specs=vmem(SET),
        scratch_shapes=[
            pltpu.VMEM((part_count, block_count, orbital_count, orbital_count), jnp.bfloat16),
            pltpu.VMEM((part_count, block_count, orbital_count, orbital_count), jnp.bfloat16),
            pltpu.VMEM((pairs, 2 * pno_count, orbital_count), jnp.bfloat16),
            pltpu.VMEM((pairs, pno_count, 2 * pno_count), jnp.bfloat16),
            pltpu.VMEM((block_count, pairs, 1, pno_count), jnp.float32),
            pltpu.VMEM((pairs, 2 * part_count * block_count * pno_count, orbital_count), jnp.bfloat16),
            pltpu.VMEM((pairs, pno_count, pno_count), jnp.float32),
        ],
        compiler_params=pltpu.CompilerParams(vmem_limit_bytes=VMEM_BYTES),
        cost_estimate=pl.CostEstimate(flops=8 * products, bytes_accessed=4 * 2**20, transcendentals=0),
    )(*operands)


def on_device_shared(pno_basis, amplitudes, send_list, couple, couple_weight, fit_weight, fit_blocks):
    pair_count, pno_count, _ = pno_basis.shape
    group_total, dom_count = lax.axis_size("blk"), lax.axis_size("dom")
    pair_amps = amplitudes.reshape(pair_count, pno_count, pno_count)
    sent = pack_pairs(send_list.reshape(-1), pno_basis, pair_amps)
    coupled = [sent[0], *[from_partner(sent[flip], "blk", flip) for flip in range(1, group_total)]]
    pieces = [fit_blocks, *[from_behind(fit_blocks, "dom", shift) for shift in range(1, dom_count)]]
    across = from_partner(pno_basis, "blk", 2)
    bases = [pno_basis, from_partner(pno_basis, "blk", 1), across, from_partner(across, "blk", 1)]
    groups = [pieces]
    for behind in range(SET, group_total, SET):
        groups.append([from_behind(x, "blk", behind) for x in pieces])
    own = dress(couple, couple_weight, fit_weight, pno_basis, pair_amps, coupled)
    dressed = [own, *[from_partner(own, "blk", flip) for flip in range(1, SET)]]
    partial = None
    for index, group in enumerate(groups):
        partial = fit(index * SET, bases, dressed, group, partial)
    updated = partial[0]
    for flip in range(1, SET):
        updated = updated + from_partner(partial[flip], "blk", flip)
    return updated.reshape(pair_count, pno_count * pno_count)


def dress_with(pair_amps, intersection, partner_amps, weights):
    half_product = jnp.einsum("pcab,pcbe->pcae", intersection, partner_amps, precision=HIGHEST)
    sandwich = jnp.einsum("pcae,pcfe->pcaf", half_product, intersection, precision=HIGHEST)
    return pair_amps + jnp.einsum("pc,pcaf->paf", weights, sandwich, precision=HIGHEST)


def fit_term(pair_basis, dressed, blocks, weights):
    pair_count, pno_count, orbital_count = pair_basis.shape
    flat_basis = pair_basis.reshape(pair_count * pno_count, orbital_count)
    stacked = blocks.reshape(2 * orbital_count, orbital_count)
    projected = jnp.dot(
        flat_basis, stacked.T, precision=HIGHEST, preferred_element_type=jnp.float32
    )
    projected = projected.reshape(pair_count, pno_count, 2, orbital_count)
    inner_blocks = jnp.einsum("par,pbmr->mpab", pair_basis, projected, precision=HIGHEST)
    left_product = jnp.einsum("pai,pij->paj", inner_blocks[0], dressed, precision=HIGHEST)
    fit_contrib = jnp.einsum("paj,pbj->pab", left_product, inner_blocks[1], precision=HIGHEST)
    return weights[:, None, None] * fit_contrib


def on_device_ring(pno_basis, amplitudes, send_list, couple, couple_weight, fit_weight, fit_blocks):
    pair_count, pno_count, _ = pno_basis.shape
    block_count = fit_blocks.shape[0]
    pair_amps = amplitudes.reshape(pair_count, pno_count, pno_count)
    send_order = send_list.reshape(-1)
    basis_in = lax.all_to_all(jnp.take(pno_basis, send_order, axis=0), "blk", split_axis=0, concat_axis=0, tiled=True)
    amps_in = lax.all_to_all(jnp.take(pair_amps, send_order, axis=0), "blk", split_axis=0, concat_axis=0, tiled=True)
    partner_basis = jnp.take(basis_in, couple, axis=0)
    intersection = jnp.einsum("par,pcbr->pcab", pno_basis, partner_basis, precision=HIGHEST)
    dressed = dress_with(pair_amps, intersection, jnp.take(amps_in, couple, axis=0), couple_weight)
    updated = dressed
    current = lax.all_gather(fit_blocks, "dom", axis=2, tiled=True)
    for stop in range(fit_weight.shape[1] // block_count):
        if stop > 0:
            current = from_behind(current, "blk", 1)
        for b in range(block_count):
            updated = updated + fit_term(pno_basis, dressed, current[b], fit_weight[:, stop * block_count + b])
    return updated.reshape(pair_count, pno_count * pno_count)


def solution(mesh):
    placed = (
        P(("blk", "dom"), None, None),
        P(("blk", "dom"), None),
        P("blk", "dom", None, None),
        P(("blk", "dom"), None),
        P(("blk", "dom"), None),
        P(("blk", "dom"), None),
        P("blk", None, "dom", None),
    )

    def on_device(*args):
        send_list, fit_weight, fit_blocks = args[2], args[5], args[6]
        group_total = mesh.shape["blk"]
        meets_all = fit_weight.shape[1] == group_total * fit_blocks.shape[0]
        if meets_all and group_total % SET == 0 and group_total & (group_total - 1) == 0 and send_list.shape[3] == 1:
            return on_device_shared(*args)
        return on_device_ring(*args)

    return jax.shard_map(
        on_device, mesh=mesh, in_specs=placed, out_specs=P(("blk", "dom"), None), check_vma=False
    )
```

```python
import jax
import jax.numpy as jnp
from jax import lax
from jax.experimental import pallas as pl
from jax.experimental.pallas import tpu as pltpu
from jax.sharding import PartitionSpec as P

HIGHEST = lax.Precision.HIGHEST
VMEM_BYTES = 48 * 2**20
SET = 4
NN = (((1,), (0,)), ((), ()))
NT = (((1,), (1,)), ((), ()))


def halves(x):
    high = x.astype(jnp.bfloat16)
    return high, (x - high.astype(jnp.float32)).astype(jnp.bfloat16)


def dot(a, b, dims):
    return lax.dot_general(a, b, dims, preferred_element_type=jnp.float32)


def dot3(a, b, dims):
    (a_high, a_low), (b_high, b_low) = a, b
    return dot(a_high, b_high, dims) + (dot(a_high, b_low, dims) + dot(a_low, b_high, dims))


def fold_rows(x):
    return x[: x.shape[0] // 2] + x[x.shape[0] // 2:]


def fold_lanes(x):
    return x[:, : x.shape[1] // 2] + x[:, x.shape[1] // 2:]


def stack(parts, axis=0):
    return jnp.concatenate(parts, axis=axis)


def from_partner(x, axis, flip):
    return lax.ppermute(x, axis, [(i, i ^ flip) for i in range(lax.axis_size(axis))])


def from_behind(x, axis, by):
    count = lax.axis_size(axis)
    return lax.ppermute(x, axis, [(i, (i + by) % count) for i in range(count)])


def vmem(count):
    return [pl.BlockSpec(memory_space=pltpu.VMEM)] * count


def pack_kernel(send, basis, amps, out):
    pno_count = amps.shape[1]
    lanes = basis.shape[2] // pno_count
    step = pno_count // lanes
    for peer in range(out.shape[0]):
        pair = send[peer]
        out[peer, :pno_count] = basis[pair]
        listed = amps[pair]
        out[peer, pno_count:] = stack([listed[i * step:(i + 1) * step] for i in range(lanes)], 1)


def pack_pairs(send_order, basis, amps):
    _, pno_count, orbital_count = basis.shape
    rows = pno_count + pno_count * pno_count // orbital_count
    return pl.pallas_call(
        pack_kernel,
        out_shape=jax.ShapeDtypeStruct((send_order.shape[0], rows, orbital_count), jnp.float32),
        in_specs=[pl.BlockSpec(memory_space=pltpu.SMEM), *vmem(2)],
        out_specs=vmem(1)[0],
        compiler_params=pltpu.CompilerParams(vmem_limit_bytes=VMEM_BYTES),
        cost_estimate=pl.CostEstimate(flops=0, bytes_accessed=4 * basis.size, transcendentals=0),
    )(send_order, basis, amps)


def dress_kernel(couple, couple_weight, fit_weight, basis, amps, coupled, dressed, turned):
    pair_count, pno_count, orbital_count = basis.shape
    half = pno_count // 2
    slot_count = coupled.shape[0]
    own = halves(basis[...].reshape(pair_count * pno_count, orbital_count))
    others = halves(coupled[:, :pno_count].reshape(slot_count * pno_count, orbital_count))
    overlap = halves(dot3(own, others, NT))
    left, slot_weight = [], []
    for slot in range(slot_count):
        cols = slice(slot * pno_count, (slot + 1) * pno_count)
        packed = coupled[slot, pno_count:]
        partner = stack([packed[:, i:i + pno_count] for i in range(0, orbital_count, pno_count)])
        left.append(dot3([x[:, cols] for x in overlap], halves(partner), NN))
        named = jnp.where(couple[...] == slot, couple_weight[...], 0.0)
        slot_weight.append(jnp.sum(named, axis=1, keepdims=True))
    dressed[:, half:, :] = jnp.zeros((pair_count, dressed.shape[1] - half, 2 * pno_count), jnp.float32)
    for pair in range(pair_count):
        rows = slice(pair * pno_count, (pair + 1) * pno_count)
        scaled = stack([x[rows] * w[pair:pair + 1] for x, w in zip(left, slot_weight)], 1)
        turned[pair] = amps[pair] + dot3(halves(scaled), [x[rows] for x in overlap], NT)
        dressed[pair, :half] = two_to_one(turned, pair, half)
        dressed[pair, half:half + 1, : fit_weight.shape[1]] = fit_weight[pair:pair + 1, :]


def two_to_one(ref, pair, half):
    return stack([ref[pair, pl.ds(i, half, stride=2), :] for i in range(2)], 1)


def dress(couple, couple_weight, fit_weight, basis, amps, coupled):
    pair_count, pno_count, _ = basis.shape
    return pl.pallas_call(
        dress_kernel,
        out_shape=jax.ShapeDtypeStruct((pair_count, pno_count // 2 + 8, 2 * pno_count), jnp.float32),
        in_specs=vmem(6),
        out_specs=vmem(1)[0],
        scratch_shapes=[pltpu.VMEM((pair_count, pno_count, pno_count), jnp.float32)],
        compiler_params=pltpu.CompilerParams(vmem_limit_bytes=VMEM_BYTES),
        cost_estimate=pl.CostEstimate(flops=4 * 10**9, bytes_accessed=8 * basis.size, transcendentals=0),
    )(couple, couple_weight, fit_weight, basis, amps, coupled)


def fit_kernel(behind, first, *refs):
    per_set = [refs[i * SET:(i + 1) * SET] for i in range(2 if first else 3)]
    refs = refs[SET * len(per_set):]
    bases, dressed = per_set[:2]
    dom_count = len(refs) - SET - 10
    pieces, refs = refs[:dom_count], refs[dom_count:]
    after, scratch = refs[:SET], refs[SET:]
    block_cat, basis_wide, basis_cat, dressed_cat, weight_rows, projected, left_cat, right_cat, moved_cat, turned = scratch
    pair_count, pno_count, orbital_count = bases[0].shape
    half = pno_count // 2
    block_count, part_count, row_count, _ = pieces[0].shape
    group_total = lax.axis_size("blk")
    me, place = lax.axis_index("blk"), lax.axis_index("dom")
    source = lax.rem(me + group_total - behind, group_total)

    for shift, piece in enumerate(pieces):
        start = lax.rem(place + dom_count - shift, dom_count) * row_count
        for b in range(block_count):
            for m in range(part_count):
                high, low = halves(piece[b, m])
                for i, x in enumerate((high, high, low)):
                    at = pl.multiple_of(start + i * orbital_count, row_count)
                    block_cat[m, b, pl.ds(at, row_count), :] = x
    for member in range(SET):
        span = slice(member * pair_count, (member + 1) * pair_count)
        high, low = halves(bases[member][...])
        basis_cat[span, :pno_count] = high
        basis_cat[span, pno_count:] = low
        for i, x in enumerate((high, low, high)):
            basis_wide[span, :, i * orbital_count:(i + 1) * orbital_count] = x
        stop = lax.rem((me ^ member) + group_total - source, group_total)
        row = dressed[member][:, half:half + 1, :]
        lane = lax.broadcasted_iota(jnp.int32, row.shape, 2)
        for b in range(block_count):
            weight = jnp.sum(jnp.where(lane == stop * block_count + b, row, 0.0), axis=2, keepdims=True)
            weight_rows[b, span] = jnp.broadcast_to(weight, (pair_count, 1, pno_count))
        for pair in range(pair_count):
            packed = dressed[member][pair, :half]
            at = member * pair_count + pair
            turned[at, pl.ds(0, half, stride=2), :] = packed[:, :pno_count]
            turned[at, pl.ds(1, half, stride=2), :] = packed[:, pno_count:]
            dressed_cat[at] = stack(halves(turned[at]), 1)

    size = block_count * pno_count

    def update(member, _):
        first_pair = pl.multiple_of(member * pair_count, pair_count)
        wide = basis_wide[pl.ds(first_pair, pair_count)].reshape(pair_count * pno_count, 3 * orbital_count)
        for m in range(part_count):
            for b in range(block_count):
                product = halves(dot(wide, block_cat[m, b], NN).reshape(pair_count, pno_count, orbital_count))
                for i in range(2):
                    at = ((i * part_count + m) * block_count + b) * pno_count
                    projected[:, at:at + pno_count] = product[i]
        for pair in range(pair_count):
            inner = fold_lanes(fold_rows(dot(projected[pair], basis_cat[first_pair + pair], NT)))
            weight = [jnp.broadcast_to(weight_rows[b, first_pair + pair], (pno_count, pno_count)) for b in range(block_count)]
            left_cat[pair] = stack(halves(inner[:size] * stack(weight)))
            high, low = halves(inner[size:])
            for b in range(block_count):
                rows = slice(b * pno_count, (b + 1) * pno_count)
                right_cat[pair, b] = stack([high[rows], low[rows]])
        for pair in range(pair_count):
            high, low = halves(fold_lanes(fold_rows(dot(left_cat[pair], dressed_cat[first_pair + pair], NN))))
            for b in range(block_count):
                rows = slice(b * pno_count, (b + 1) * pno_count)
                moved_cat[pair, b] = stack([high[rows], low[rows]])
        for pair in range(pair_count):
            total = dot(moved_cat[pair, 0], right_cat[pair, 0], NT)
            for b in range(1, block_count):
                total += dot(moved_cat[pair, b], right_cat[pair, b], NT)
            turned[first_pair + pair] = fold_lanes(fold_rows(total))
        return 0

    lax.fori_loop(0, SET, update, 0)

    for member in range(SET):
        for pair in range(pair_count):
            total = two_to_one(turned, member * pair_count + pair, half)
            if not first:
                total += per_set[2][member][pair]
            elif member == 0:
                total += dressed[0][pair, :half]
            after[member][pair] = total


def fit(behind, bases, dressed, pieces, before):
    pair_count, pno_count, orbital_count = bases[0].shape
    block_count, part_count, row_count, _ = pieces[0].shape
    pairs = SET * pair_count
    first = before is None
    operands = [*bases, *dressed, *([] if first else before), *pieces]
    products = block_count * part_count * pairs * pno_count * orbital_count * (orbital_count + pno_count)
    return pl.pallas_call(
        lambda *refs: fit_kernel(behind, first, *refs),
        out_shape=[jax.ShapeDtypeStruct((pair_count, pno_count // 2, 2 * pno_count), jnp.float32)] * SET,
        in_specs=vmem(len(operands)),
        out_specs=vmem(SET),
        scratch_shapes=[
            pltpu.VMEM((part_count, block_count, 3 * orbital_count, orbital_count), jnp.bfloat16),
            pltpu.VMEM((pairs, pno_count, 3 * orbital_count), jnp.bfloat16),
            pltpu.VMEM((pairs, 2 * pno_count, orbital_count), jnp.bfloat16),
            pltpu.VMEM((pairs, pno_count, 2 * pno_count), jnp.bfloat16),
            pltpu.VMEM((block_count, pairs, 1, pno_count), jnp.float32),
            pltpu.VMEM((pair_count, 2 * part_count * block_count * pno_count, orbital_count), jnp.bfloat16),
            pltpu.VMEM((pair_count, 2 * block_count * pno_count, pno_count), jnp.bfloat16),
            pltpu.VMEM((pair_count, block_count, 2 * pno_count, pno_count), jnp.bfloat16),
            pltpu.VMEM((pair_count, block_count, 2 * pno_count, pno_count), jnp.bfloat16),
            pltpu.VMEM((pairs, pno_count, pno_count), jnp.float32),
        ],
        compiler_params=pltpu.CompilerParams(vmem_limit_bytes=VMEM_BYTES),
        cost_estimate=pl.CostEstimate(flops=8 * products, bytes_accessed=4 * 2**20, transcendentals=0),
    )(*operands)


def on_device_shared(pno_basis, amplitudes, send_list, couple, couple_weight, fit_weight, fit_blocks):
    pair_count, pno_count, _ = pno_basis.shape
    group_total, dom_count = lax.axis_size("blk"), lax.axis_size("dom")
    pair_amps = amplitudes.reshape(pair_count, pno_count, pno_count)
    sent = pack_pairs(send_list.reshape(-1), pno_basis, pair_amps)
    coupled = lax.all_to_all(sent, "blk", split_axis=0, concat_axis=0, tiled=True)
    pieces = [fit_blocks, *[from_behind(fit_blocks, "dom", shift) for shift in range(1, dom_count)]]
    across = from_partner(pno_basis, "blk", 2)
    bases = [pno_basis, from_partner(pno_basis, "blk", 1), across, from_partner(across, "blk", 1)]
    groups = [pieces]
    for behind in range(SET, group_total, SET):
        groups.append([from_behind(x, "blk", behind) for x in pieces])
    own = dress(couple, couple_weight, fit_weight, pno_basis, pair_amps, coupled)
    dressed = [own, *[from_partner(own, "blk", flip) for flip in range(1, SET)]]
    partial = None
    for index, group in enumerate(groups):
        partial = fit(index * SET, bases, dressed, group, partial)
    updated = partial[0]
    for flip in range(1, SET):
        updated = updated + from_partner(partial[flip], "blk", flip)
    return updated.reshape(pair_count, pno_count * pno_count)


def dress_with(pair_amps, intersection, partner_amps, weights):
    half_product = jnp.einsum("pcab,pcbe->pcae", intersection, partner_amps, precision=HIGHEST)
    sandwich = jnp.einsum("pcae,pcfe->pcaf", half_product, intersection, precision=HIGHEST)
    return pair_amps + jnp.einsum("pc,pcaf->paf", weights, sandwich, precision=HIGHEST)


def fit_term(pair_basis, dressed, blocks, weights):
    pair_count, pno_count, orbital_count = pair_basis.shape
    flat_basis = pair_basis.reshape(pair_count * pno_count, orbital_count)
    stacked = blocks.reshape(2 * orbital_count, orbital_count)
    projected = jnp.dot(
        flat_basis, stacked.T, precision=HIGHEST, preferred_element_type=jnp.float32
    )
    projected = projected.reshape(pair_count, pno_count, 2, orbital_count)
    inner_blocks = jnp.einsum("par,pbmr->mpab", pair_basis, projected, precision=HIGHEST)
    left_product = jnp.einsum("pai,pij->paj", inner_blocks[0], dressed, precision=HIGHEST)
    fit_contrib = jnp.einsum("paj,pbj->pab", left_product, inner_blocks[1], precision=HIGHEST)
    return weights[:, None, None] * fit_contrib


def on_device_ring(pno_basis, amplitudes, send_list, couple, couple_weight, fit_weight, fit_blocks):
    pair_count, pno_count, _ = pno_basis.shape
    block_count = fit_blocks.shape[0]
    pair_amps = amplitudes.reshape(pair_count, pno_count, pno_count)
    send_order = send_list.reshape(-1)
    basis_in = lax.all_to_all(jnp.take(pno_basis, send_order, axis=0), "blk", split_axis=0, concat_axis=0, tiled=True)
    amps_in = lax.all_to_all(jnp.take(pair_amps, send_order, axis=0), "blk", split_axis=0, concat_axis=0, tiled=True)
    partner_basis = jnp.take(basis_in, couple, axis=0)
    intersection = jnp.einsum("par,pcbr->pcab", pno_basis, partner_basis, precision=HIGHEST)
    dressed = dress_with(pair_amps, intersection, jnp.take(amps_in, couple, axis=0), couple_weight)
    updated = dressed
    current = lax.all_gather(fit_blocks, "dom", axis=2, tiled=True)
    for stop in range(fit_weight.shape[1] // block_count):
        if stop > 0:
            current = from_behind(current, "blk", 1)
        for b in range(block_count):
            updated = updated + fit_term(pno_basis, dressed, current[b], fit_weight[:, stop * block_count + b])
    return updated.reshape(pair_count, pno_count * pno_count)


def solution(mesh):
    placed = (
        P(("blk", "dom"), None, None),
        P(("blk", "dom"), None),
        P("blk", "dom", None, None),
        P(("blk", "dom"), None),
        P(("blk", "dom"), None),
        P(("blk", "dom"), None),
        P("blk", None, "dom", None),
    )

    def on_device(*args):
        send_list, fit_weight, fit_blocks = args[2], args[5], args[6]
        group_total = mesh.shape["blk"]
        meets_all = fit_weight.shape[1] == group_total * fit_blocks.shape[0]
        if meets_all and group_total % SET == 0 and group_total & (group_total - 1) == 0 and send_list.shape[3] == 1:
            return on_device_shared(*args)
        return on_device_ring(*args)

    return jax.shard_map(
        on_device, mesh=mesh, in_specs=placed, out_specs=P(("blk", "dom"), None), check_vma=False
    )
```

```python
import jax
import jax.numpy as jnp
from jax import lax
from jax.experimental import pallas as pl
from jax.experimental.pallas import tpu as pltpu
from jax.sharding import PartitionSpec as P

HIGHEST = lax.Precision.HIGHEST
VMEM_BYTES = 24 * 2**20
SET = 4
NN = (((1,), (0,)), ((), ()))
NT = (((1,), (1,)), ((), ()))


def halves(x):
    high = x.astype(jnp.bfloat16)
    return high, (x - high.astype(jnp.float32)).astype(jnp.bfloat16)


def dot(a, b, dims):
    return lax.dot_general(a, b, dims, preferred_element_type=jnp.float32)


def dot3(a, b, dims):
    (a_high, a_low), (b_high, b_low) = a, b
    return dot(a_high, b_high, dims) + (dot(a_high, b_low, dims) + dot(a_low, b_high, dims))


def stack(parts, axis=0):
    return jnp.concatenate(parts, axis=axis)


def from_partner(x, axis, flip):
    return lax.ppermute(x, axis, [(i, i ^ flip) for i in range(lax.axis_size(axis))])


def from_behind(x, axis, by):
    count = lax.axis_size(axis)
    return lax.ppermute(x, axis, [(i, (i + by) % count) for i in range(count)])


def vmem(count):
    return [pl.BlockSpec(memory_space=pltpu.VMEM)] * count


def pack_kernel(send, basis, amps, out):
    pno_count = amps.shape[1]
    lanes = basis.shape[2] // pno_count
    step = pno_count // lanes
    for peer in range(out.shape[0]):
        pair = send[peer]
        out[peer, :pno_count] = basis[pair]
        listed = amps[pair]
        out[peer, pno_count:] = stack([listed[i * step:(i + 1) * step] for i in range(lanes)], 1)


def pack_pairs(send_order, basis, amps):
    _, pno_count, orbital_count = basis.shape
    rows = pno_count + pno_count * pno_count // orbital_count
    return pl.pallas_call(
        pack_kernel,
        out_shape=jax.ShapeDtypeStruct((send_order.shape[0], rows, orbital_count), jnp.float32),
        in_specs=[pl.BlockSpec(memory_space=pltpu.SMEM), *vmem(2)],
        out_specs=vmem(1)[0],
        compiler_params=pltpu.CompilerParams(vmem_limit_bytes=VMEM_BYTES),
        cost_estimate=pl.CostEstimate(flops=0, bytes_accessed=4 * basis.size, transcendentals=0),
    )(send_order, basis, amps)


def dress_kernel(couple, couple_weight, fit_weight, basis, amps, coupled, dressed, turned):
    pair_count, pno_count, orbital_count = basis.shape
    half = pno_count // 2
    slot_count = coupled.shape[0]
    own = halves(basis[...].reshape(pair_count * pno_count, orbital_count))
    others = halves(coupled[:, :pno_count].reshape(slot_count * pno_count, orbital_count))
    overlap = halves(dot3(own, others, NT))
    left, slot_weight = [], []
    for slot in range(slot_count):
        cols = slice(slot * pno_count, (slot + 1) * pno_count)
        packed = coupled[slot, pno_count:]
        partner = stack([packed[:, i:i + pno_count] for i in range(0, orbital_count, pno_count)])
        left.append(dot3([x[:, cols] for x in overlap], halves(partner), NN))
        named = jnp.where(couple[...] == slot, couple_weight[...], 0.0)
        slot_weight.append(jnp.sum(named, axis=1, keepdims=True))
    dressed[:, half:, :] = jnp.zeros((pair_count, dressed.shape[1] - half, 2 * pno_count), jnp.float32)
    for pair in range(pair_count):
        rows = slice(pair * pno_count, (pair + 1) * pno_count)
        scaled = stack([x[rows] * w[pair:pair + 1] for x, w in zip(left, slot_weight)], 1)
        turned[pair] = amps[pair] + dot3(halves(scaled), [x[rows] for x in overlap], NT)
        dressed[pair, :half] = two_to_one(turned, pair, half)
        dressed[pair, half:half + 1, : fit_weight.shape[1]] = fit_weight[pair:pair + 1, :]


def two_to_one(ref, pair, half):
    return stack([ref[pair, pl.ds(i, half, stride=2), :] for i in range(2)], 1)


def dress(couple, couple_weight, fit_weight, basis, amps, coupled):
    pair_count, pno_count, _ = basis.shape
    return pl.pallas_call(
        dress_kernel,
        out_shape=jax.ShapeDtypeStruct((pair_count, pno_count // 2 + 8, 2 * pno_count), jnp.float32),
        in_specs=vmem(6),
        out_specs=vmem(1)[0],
        scratch_shapes=[pltpu.VMEM((pair_count, pno_count, pno_count), jnp.float32)],
        compiler_params=pltpu.CompilerParams(vmem_limit_bytes=VMEM_BYTES),
        cost_estimate=pl.CostEstimate(flops=4 * 10**9, bytes_accessed=8 * basis.size, transcendentals=0),
    )(couple, couple_weight, fit_weight, basis, amps, coupled)


def split_kernel(*refs):
    bases, (wide, cat) = refs[:SET], refs[SET:]
    pair_count, pno_count, orbital_count = bases[0].shape
    for member, basis in enumerate(bases):
        span = slice(member * pair_count, (member + 1) * pair_count)
        high, low = halves(basis[...])
        for i, x in enumerate((high, low, high)):
            wide[span, :, i * orbital_count:(i + 1) * orbital_count] = x
        cat[span, :pno_count, :orbital_count] = high
        cat[span, :pno_count, orbital_count:] = high
        cat[span, pno_count:, :orbital_count] = low
        cat[span, pno_count:, orbital_count:] = jnp.zeros_like(low)


def split_bases(bases):
    pair_count, pno_count, orbital_count = bases[0].shape
    pairs = SET * pair_count
    return pl.pallas_call(
        split_kernel,
        out_shape=(
            jax.ShapeDtypeStruct((pairs, pno_count, 3 * orbital_count), jnp.bfloat16),
            jax.ShapeDtypeStruct((pairs, 2 * pno_count, 2 * orbital_count), jnp.bfloat16),
        ),
        in_specs=vmem(SET),
        out_specs=tuple(vmem(2)),
        compiler_params=pltpu.CompilerParams(vmem_limit_bytes=VMEM_BYTES),
        cost_estimate=pl.CostEstimate(flops=0, bytes_accessed=16 * bases[0].size, transcendentals=0),
    )(*bases)


def fold(x):
    return x + pltpu.roll(x, x.shape[1] // 2, 1)


def left_lanes(x):
    return lax.broadcasted_iota(jnp.int32, x.shape, 1) < x.shape[1] // 2


def split(x):
    high = x.astype(jnp.bfloat16)
    wide = high.astype(jnp.float32)
    return high, wide, x - wide


def high_low(x):
    _, high, low = split(x)
    return jnp.where(left_lanes(x), high, low).astype(jnp.bfloat16)


def project_kernel(wide, cat, *refs):
    *pieces, inner_left, inner_right, block_cat, projected = refs
    pairs, pno_count, _ = wide.shape
    pair_count = pairs // SET
    block_count, part_count, row_count, orbital_count = pieces[0].shape
    dom_count = len(pieces)
    place = lax.axis_index("dom")
    for shift, piece in enumerate(pieces):
        start = lax.rem(place + dom_count - shift, dom_count) * row_count
        for b in range(block_count):
            for m in range(part_count):
                high, low = halves(piece[b, m])
                for i, x in enumerate((high, high, low)):
                    at = pl.multiple_of(start + i * orbital_count, row_count)
                    block_cat[m, b, pl.ds(at, row_count), :] = x
    size = block_count * pno_count

    def one(member, _):
        first_pair = pl.multiple_of(member * pair_count, pair_count)
        basis = wide[pl.ds(first_pair, pair_count)].reshape(pair_count * pno_count, 3 * orbital_count)
        for m in range(part_count):
            for b in range(block_count):
                product = halves(dot(basis, block_cat[m, b], NN).reshape(pair_count, pno_count, orbital_count))
                at = (m * block_count + b) * pno_count
                for i in range(2):
                    projected[:, at:at + pno_count, i * orbital_count:(i + 1) * orbital_count] = product[i]
        for pair in range(pair_count):
            inner = fold(dot(projected[pair], cat[first_pair + pair], NT))
            inner_left[first_pair + pair] = high_low(inner[:size])
            high, _, low = split(inner[size:])
            low = jnp.where(left_lanes(low), low, 0.0).astype(jnp.bfloat16)
            for b in range(block_count):
                rows = slice(b * pno_count, (b + 1) * pno_count)
                lanes = slice(b * 2 * pno_count, (b + 1) * 2 * pno_count)
                inner_right[first_pair + pair, :pno_count, lanes] = high[rows]
                inner_right[first_pair + pair, pno_count:, lanes] = low[rows]
        return 0

    lax.fori_loop(0, SET, one, 0)


def project(wide, cat, pieces):
    pairs, pno_count, _ = wide.shape
    block_count, part_count, _, orbital_count = pieces[0].shape
    products = block_count * part_count * pairs * pno_count * orbital_count * (orbital_count + pno_count)
    return pl.pallas_call(
        project_kernel,
        out_shape=(
            jax.ShapeDtypeStruct((pairs, block_count * pno_count, 2 * pno_count), jnp.bfloat16),
            jax.ShapeDtypeStruct((pairs, 2 * pno_count, block_count * 2 * pno_count), jnp.bfloat16),
        ),
        in_specs=vmem(2 + len(pieces)),
        out_specs=tuple(vmem(2)),
        scratch_shapes=[
            pltpu.VMEM((part_count, block_count, 3 * orbital_count, orbital_count), jnp.bfloat16),
            pltpu.VMEM((pairs // SET, part_count * block_count * pno_count, 2 * orbital_count), jnp.bfloat16),
        ],
        compiler_params=pltpu.CompilerParams(vmem_limit_bytes=VMEM_BYTES),
        cost_estimate=pl.CostEstimate(flops=6 * products, bytes_accessed=2**20, transcendentals=0),
    )(wide, cat, *pieces)


def update_kernel(members, group_count, *refs):
    groups, refs = refs[:2 * group_count], refs[2 * group_count:]
    dressed, after, (turned, total) = refs[:len(members)], refs[len(members):2 * len(members)], refs[2 * len(members):]
    pair_count, _, lane_count = dressed[0].shape
    pno_count = lane_count // 2
    half = pno_count // 2
    block_count = groups[0].shape[1] // pno_count
    group_total = lax.axis_size("blk")
    me = lax.axis_index("blk")
    for index, member in enumerate(members):
        row = dressed[index][:, half:half + 1, :]
        lane = lax.broadcasted_iota(jnp.int32, row.shape, 2)
        weights = []
        for group in range(group_count):
            stop = lax.rem((me ^ member) + 2 * group_total + group * SET - me, group_total)
            for b in range(block_count):
                kept = jnp.where(lane == stop * block_count + b, row, 0.0)
                weights.append(jnp.sum(kept, axis=2, keepdims=True))
        for pair in range(pair_count):
            packed = dressed[index][pair, :half]
            other = pltpu.roll(packed, pno_count, 1)
            at = index * pair_count + pair
            turned[at, pl.ds(0, half, stride=2), :] = jnp.where(left_lanes(packed), packed, other)
            turned[at, pl.ds(1, half, stride=2), :] = jnp.where(left_lanes(packed), other, packed)
            twice = turned[at]
            _, high, _ = split(twice)
            square = stack([high_low(twice), jnp.where(left_lanes(twice), high, 0.0).astype(jnp.bfloat16)])
            here = member * pair_count + pair
            terms = []
            for group in range(group_count):
                moved = fold(dot(groups[2 * group][here], square, NN))
                blocks = [
                    high_low(moved[b * pno_count:(b + 1) * pno_count] * weights[group * block_count + b][pair])
                    for b in range(block_count)
                ]
                terms.append(dot(stack(blocks, 1), groups[2 * group + 1][here], NT))
            total[at] = fold(sum(terms[1:], terms[0]))
        for pair in range(pair_count):
            at = index * pair_count + pair
            rows = [total[at, pl.ds(i, half, stride=2), :] for i in range(2)]
            result = jnp.where(left_lanes(rows[0]), *rows)
            if member == 0:
                result += dressed[index][pair, :half]
            after[index][pair] = result


def update(members, groups, dressed):
    pair_count, _, lane_count = dressed[0].shape
    pno_count = lane_count // 2
    pairs = len(members) * pair_count
    operands = [x for group in groups for x in group] + dressed
    products = pairs * pno_count**3 * 2 * len(groups) * (groups[0][0].shape[1] // pno_count)
    return pl.pallas_call(
        lambda *refs: update_kernel(members, len(groups), *refs),
        out_shape=[jax.ShapeDtypeStruct((pair_count, pno_count // 2, lane_count), jnp.float32)] * len(members),
        in_specs=vmem(len(operands)),
        out_specs=vmem(len(members)),
        scratch_shapes=[pltpu.VMEM((pairs, pno_count, lane_count), jnp.float32)] * 2,
        compiler_params=pltpu.CompilerParams(vmem_limit_bytes=VMEM_BYTES),
        cost_estimate=pl.CostEstimate(flops=6 * products, bytes_accessed=2**20, transcendentals=0),
    )(*operands)


def gather_pieces(mine, axis):
    count = lax.axis_size(axis)
    up, down = [mine], []
    for shift in range(1, count):
        if shift <= count // 2:
            up.append(from_behind(up[-1], axis, 1))
        else:
            down.append(from_behind(down[-1] if down else mine, axis, count - 1))
    return up + down[::-1]


def on_device_shared(pno_basis, amplitudes, send_list, couple, couple_weight, fit_weight, fit_blocks):
    pair_count, pno_count, _ = pno_basis.shape
    group_total = lax.axis_size("blk")
    pieces = gather_pieces(fit_blocks, "dom")
    across = from_partner(pno_basis, "blk", 2)
    groups = [pieces, *[[from_behind(x, "blk", by) for x in pieces] for by in range(SET, group_total, SET)]]
    pair_amps = amplitudes.reshape(pair_count, pno_count, pno_count)
    sent = pack_pairs(send_list.reshape(-1), pno_basis, pair_amps)
    ahead = [pieces[1], pieces[-1], across, *[group[0] for group in groups[1:]]]
    sent, pieces[1], pieces[-1], across, *heads = lax.optimization_barrier((sent, *ahead))
    for group, head in zip(groups[1:], heads):
        group[0] = head
    coupled = lax.all_to_all(sent, "blk", split_axis=0, concat_axis=0, tiled=True)
    wide, cat = split_bases([pno_basis, from_partner(pno_basis, "blk", 1), across, from_partner(across, "blk", 1)])
    own = dress(couple, couple_weight, fit_weight, pno_basis, pair_amps, coupled)
    dressed = [own, *[from_partner(own, "blk", flip) for flip in range(1, SET)]]
    inner = [project(wide, cat, group) for group in groups]
    updated = None
    for members in ((3, 2), (1, 0)):
        partial = update(members, inner, [dressed[member] for member in members])
        if members[-1]:
            partial, inner = lax.optimization_barrier((partial, inner))
        for member, x in zip(members, partial):
            x = from_partner(x, "blk", member) if member else x
            updated = x if updated is None else updated + x
    return updated.reshape(pair_count, pno_count * pno_count)


def dress_with(pair_amps, intersection, partner_amps, weights):
    half_product = jnp.einsum("pcab,pcbe->pcae", intersection, partner_amps, precision=HIGHEST)
    sandwich = jnp.einsum("pcae,pcfe->pcaf", half_product, intersection, precision=HIGHEST)
    return pair_amps + jnp.einsum("pc,pcaf->paf", weights, sandwich, precision=HIGHEST)


def fit_term(pair_basis, dressed, blocks, weights):
    pair_count, pno_count, orbital_count = pair_basis.shape
    flat_basis = pair_basis.reshape(pair_count * pno_count, orbital_count)
    stacked = blocks.reshape(2 * orbital_count, orbital_count)
    projected = jnp.dot(
        flat_basis, stacked.T, precision=HIGHEST, preferred_element_type=jnp.float32
    )
    projected = projected.reshape(pair_count, pno_count, 2, orbital_count)
    inner_blocks = jnp.einsum("par,pbmr->mpab", pair_basis, projected, precision=HIGHEST)
    left_product = jnp.einsum("pai,pij->paj", inner_blocks[0], dressed, precision=HIGHEST)
    fit_contrib = jnp.einsum("paj,pbj->pab", left_product, inner_blocks[1], precision=HIGHEST)
    return weights[:, None, None] * fit_contrib


def on_device_ring(pno_basis, amplitudes, send_list, couple, couple_weight, fit_weight, fit_blocks):
    pair_count, pno_count, _ = pno_basis.shape
    block_count = fit_blocks.shape[0]
    pair_amps = amplitudes.reshape(pair_count, pno_count, pno_count)
    send_order = send_list.reshape(-1)
    basis_in = lax.all_to_all(jnp.take(pno_basis, send_order, axis=0), "blk", split_axis=0, concat_axis=0, tiled=True)
    amps_in = lax.all_to_all(jnp.take(pair_amps, send_order, axis=0), "blk", split_axis=0, concat_axis=0, tiled=True)
    partner_basis = jnp.take(basis_in, couple, axis=0)
    intersection = jnp.einsum("par,pcbr->pcab", pno_basis, partner_basis, precision=HIGHEST)
    dressed = dress_with(pair_amps, intersection, jnp.take(amps_in, couple, axis=0), couple_weight)
    updated = dressed
    current = lax.all_gather(fit_blocks, "dom", axis=2, tiled=True)
    for stop in range(fit_weight.shape[1] // block_count):
        if stop > 0:
            current = from_behind(current, "blk", 1)
        for b in range(block_count):
            updated = updated + fit_term(pno_basis, dressed, current[b], fit_weight[:, stop * block_count + b])
    return updated.reshape(pair_count, pno_count * pno_count)


def solution(mesh):
    placed = (
        P(("blk", "dom"), None, None),
        P(("blk", "dom"), None),
        P("blk", "dom", None, None),
        P(("blk", "dom"), None),
        P(("blk", "dom"), None),
        P(("blk", "dom"), None),
        P("blk", None, "dom", None),
    )

    def on_device(*args):
        send_list, fit_weight, fit_blocks = args[2], args[5], args[6]
        group_total = mesh.shape["blk"]
        meets_all = fit_weight.shape[1] == group_total * fit_blocks.shape[0]
        if meets_all and group_total % SET == 0 and group_total & (group_total - 1) == 0 and send_list.shape[3] == 1:
            return on_device_shared(*args)
        return on_device_ring(*args)

    return jax.shard_map(
        on_device, mesh=mesh, in_specs=placed, out_specs=P(("blk", "dom"), None), check_vma=False
    )
```

```python
import jax
import jax.numpy as jnp
from jax import lax
from jax.experimental import pallas as pl
from jax.experimental.pallas import tpu as pltpu
from jax.sharding import PartitionSpec as P

HIGHEST = lax.Precision.HIGHEST
SET = 4
NN = (((1,), (0,)), ((), ()))
NT = (((1,), (1,)), ((), ()))


def halves(x):
    high = x.astype(jnp.bfloat16)
    return high, (x - high.astype(jnp.float32)).astype(jnp.bfloat16)


def dot(a, b, dims):
    return lax.dot_general(a, b, dims, preferred_element_type=jnp.float32)


def dot3(a, b, dims):
    (a_high, a_low), (b_high, b_low) = a, b
    return dot(a_high, b_high, dims) + (dot(a_high, b_low, dims) + dot(a_low, b_high, dims))


def stack(parts, axis=0):
    return jnp.concatenate(parts, axis=axis)


def from_partner(x, axis, flip):
    return lax.ppermute(x, axis, [(i, i ^ flip) for i in range(lax.axis_size(axis))])


def from_behind(x, axis, by):
    count = lax.axis_size(axis)
    return lax.ppermute(x, axis, [(i, (i + by) % count) for i in range(count)])


def vmem(count):
    return [pl.BlockSpec(memory_space=pltpu.VMEM)] * count


def pack_kernel(send, basis, amps, out):
    pno_count = amps.shape[1]
    lanes = basis.shape[2] // pno_count
    step = pno_count // lanes
    for peer in range(out.shape[0]):
        pair = send[peer]
        out[peer, :pno_count] = basis[pair]
        listed = amps[pair]
        out[peer, pno_count:] = stack([listed[i * step:(i + 1) * step] for i in range(lanes)], 1)


def pack_pairs(send_order, basis, amps):
    _, pno_count, orbital_count = basis.shape
    rows = pno_count + pno_count * pno_count // orbital_count
    return pl.pallas_call(
        pack_kernel,
        out_shape=jax.ShapeDtypeStruct((send_order.shape[0], rows, orbital_count), jnp.float32),
        in_specs=[pl.BlockSpec(memory_space=pltpu.SMEM), *vmem(2)],
        out_specs=vmem(1)[0],
        compiler_params=pltpu.CompilerParams(vmem_limit_bytes=4 * 2**20),
        cost_estimate=pl.CostEstimate(flops=0, bytes_accessed=4 * basis.size, transcendentals=0),
    )(send_order, basis, amps)


def dress_kernel(couple, couple_weight, fit_weight, basis, amps, coupled, dressed, turned):
    pair_count, pno_count, orbital_count = basis.shape
    half = pno_count // 2
    slot_count = coupled.shape[0]
    own = halves(basis[...].reshape(pair_count * pno_count, orbital_count))
    others = halves(coupled[:, :pno_count].reshape(slot_count * pno_count, orbital_count))
    overlap = halves(dot3(own, others, NT))
    left, slot_weight = [], []
    for slot in range(slot_count):
        cols = slice(slot * pno_count, (slot + 1) * pno_count)
        packed = coupled[slot, pno_count:]
        partner = stack([packed[:, i:i + pno_count] for i in range(0, orbital_count, pno_count)])
        left.append(dot3([x[:, cols] for x in overlap], halves(partner), NN))
        named = jnp.where(couple[...] == slot, couple_weight[...], 0.0)
        slot_weight.append(jnp.sum(named, axis=1, keepdims=True))
    dressed[:, half:, :] = jnp.zeros((pair_count, dressed.shape[1] - half, 2 * pno_count), jnp.float32)
    for pair in range(pair_count):
        rows = slice(pair * pno_count, (pair + 1) * pno_count)
        scaled = stack([x[rows] * w[pair:pair + 1] for x, w in zip(left, slot_weight)], 1)
        turned[pair] = amps[pair] + dot3(halves(scaled), [x[rows] for x in overlap], NT)
        dressed[pair, :half] = two_to_one(turned, pair, half)
        dressed[pair, half:half + 1, : fit_weight.shape[1]] = fit_weight[pair:pair + 1, :]


def two_to_one(ref, pair, half):
    return stack([ref[pair, pl.ds(i, half, stride=2), :] for i in range(2)], 1)


def dress(couple, couple_weight, fit_weight, basis, amps, coupled):
    pair_count, pno_count, _ = basis.shape
    return pl.pallas_call(
        dress_kernel,
        out_shape=jax.ShapeDtypeStruct((pair_count, pno_count // 2 + 8, 2 * pno_count), jnp.float32),
        in_specs=vmem(6),
        out_specs=vmem(1)[0],
        scratch_shapes=[pltpu.VMEM((pair_count, pno_count, pno_count), jnp.float32)],
        compiler_params=pltpu.CompilerParams(vmem_limit_bytes=10 * 2**20),
        cost_estimate=pl.CostEstimate(flops=4 * 10**9, bytes_accessed=8 * basis.size, transcendentals=0),
    )(couple, couple_weight, fit_weight, basis, amps, coupled)


def fold(x):
    return x + pltpu.roll(x, x.shape[1] // 2, 1)


def left_lanes(x):
    return lax.broadcasted_iota(jnp.int32, x.shape, 1) < x.shape[1] // 2


def split(x):
    high = x.astype(jnp.bfloat16)
    wide = high.astype(jnp.float32)
    return high, wide, x - wide


def high_low(x):
    _, high, low = split(x)
    return jnp.where(left_lanes(x), high, low).astype(jnp.bfloat16)


def project_kernel(*refs):
    bases, refs = refs[:SET], refs[SET:]
    *pieces, inner_left, inner_right, block_cat, wide, cat, projected = refs
    pair_count, pno_count, orbital_count = bases[0].shape
    block_count, part_count, row_count, _ = pieces[0].shape
    dom_count = len(pieces)
    place = lax.axis_index("dom")
    for shift, piece in enumerate(pieces):
        start = lax.rem(place + dom_count - shift, dom_count) * row_count
        for b in range(block_count):
            for m in range(part_count):
                high, low = halves(piece[b, m])
                for i, x in enumerate((high, high, low)):
                    at = pl.multiple_of(start + i * orbital_count, row_count)
                    block_cat[m, b, pl.ds(at, row_count), :] = x
    size = block_count * pno_count
    for member in range(SET):
        slot = member % 2
        high, low = halves(bases[member][...])
        for i, x in enumerate((high, low, high)):
            wide[slot, :, :, i * orbital_count:(i + 1) * orbital_count] = x
        for i, (upper, lower) in enumerate(((high, low), (high, jnp.zeros_like(low)))):
            lanes = slice(i * orbital_count, (i + 1) * orbital_count)
            cat[slot, :, :pno_count, lanes] = upper
            cat[slot, :, pno_count:, lanes] = lower
        basis = wide[slot].reshape(pair_count * pno_count, 3 * orbital_count)
        for m in range(part_count):
            for b in range(block_count):
                product = halves(dot(basis, block_cat[m, b], NN).reshape(pair_count, pno_count, orbital_count))
                at = (m * block_count + b) * pno_count
                for i in range(2):
                    projected[slot, :, at:at + pno_count, i * orbital_count:(i + 1) * orbital_count] = product[i]
        for pair in range(pair_count):
            here = member * pair_count + pair
            inner = fold(dot(projected[slot, pair], cat[slot, pair], NT))
            inner_left[here] = high_low(inner[:size])
            high, _, low = split(inner[size:])
            low = jnp.where(left_lanes(low), low, 0.0).astype(jnp.bfloat16)
            for b in range(block_count):
                rows = slice(b * pno_count, (b + 1) * pno_count)
                lanes = slice(b * 2 * pno_count, (b + 1) * 2 * pno_count)
                inner_right[here, :pno_count, lanes] = high[rows]
                inner_right[here, pno_count:, lanes] = low[rows]


def project(bases, pieces):
    pair_count, pno_count, _ = bases[0].shape
    block_count, part_count, _, orbital_count = pieces[0].shape
    pairs = SET * pair_count
    products = block_count * part_count * pairs * pno_count * orbital_count * (orbital_count + pno_count)
    return pl.pallas_call(
        project_kernel,
        out_shape=(
            jax.ShapeDtypeStruct((pairs, block_count * pno_count, 2 * pno_count), jnp.bfloat16),
            jax.ShapeDtypeStruct((pairs, 2 * pno_count, block_count * 2 * pno_count), jnp.bfloat16),
        ),
        in_specs=vmem(SET + len(pieces)),
        out_specs=tuple(vmem(2)),
        scratch_shapes=[
            pltpu.VMEM((part_count, block_count, 3 * orbital_count, orbital_count), jnp.bfloat16),
            pltpu.VMEM((2, pair_count, pno_count, 3 * orbital_count), jnp.bfloat16),
            pltpu.VMEM((2, pair_count, 2 * pno_count, 2 * orbital_count), jnp.bfloat16),
            pltpu.VMEM((2, pair_count, part_count * block_count * pno_count, 2 * orbital_count), jnp.bfloat16),
        ],
        compiler_params=pltpu.CompilerParams(vmem_limit_bytes=20 * 2**20),
        cost_estimate=pl.CostEstimate(flops=6 * products, bytes_accessed=2**20, transcendentals=0),
    )(*bases, *pieces)


def update_kernel(members, group_count, *refs):
    groups, refs = refs[:2 * group_count], refs[2 * group_count:]
    dressed, after, (turned, total) = refs[:len(members)], refs[len(members):2 * len(members)], refs[2 * len(members):]
    pair_count, _, lane_count = dressed[0].shape
    pno_count = lane_count // 2
    half = pno_count // 2
    block_count = groups[0].shape[1] // pno_count
    group_total = lax.axis_size("blk")
    me = lax.axis_index("blk")
    for index, member in enumerate(members):
        row = dressed[index][:, half:half + 1, :]
        lane = lax.broadcasted_iota(jnp.int32, row.shape, 2)
        weights = []
        for group in range(group_count):
            stop = lax.rem((me ^ member) + 2 * group_total + group * SET - me, group_total)
            for b in range(block_count):
                kept = jnp.where(lane == stop * block_count + b, row, 0.0)
                weights.append(jnp.sum(kept, axis=2, keepdims=True))
        for pair in range(pair_count):
            packed = dressed[index][pair, :half]
            other = pltpu.roll(packed, pno_count, 1)
            at = index * pair_count + pair
            turned[at, pl.ds(0, half, stride=2), :] = jnp.where(left_lanes(packed), packed, other)
            turned[at, pl.ds(1, half, stride=2), :] = jnp.where(left_lanes(packed), other, packed)
            twice = turned[at]
            _, high, _ = split(twice)
            square = stack([high_low(twice), jnp.where(left_lanes(twice), high, 0.0).astype(jnp.bfloat16)])
            here = member * pair_count + pair
            terms = []
            for group in range(group_count):
                moved = fold(dot(groups[2 * group][here], square, NN))
                blocks = [
                    high_low(moved[b * pno_count:(b + 1) * pno_count] * weights[group * block_count + b][pair])
                    for b in range(block_count)
                ]
                terms.append(dot(stack(blocks, 1), groups[2 * group + 1][here], NT))
            total[at] = fold(sum(terms[1:], terms[0]))
        for pair in range(pair_count):
            at = index * pair_count + pair
            rows = [total[at, pl.ds(i, half, stride=2), :] for i in range(2)]
            result = jnp.where(left_lanes(rows[0]), *rows)
            if member == 0:
                result += dressed[index][pair, :half]
            after[index][pair] = result


def update(members, groups, dressed):
    pair_count, _, lane_count = dressed[0].shape
    pno_count = lane_count // 2
    pairs = len(members) * pair_count
    operands = [x for group in groups for x in group] + dressed
    products = pairs * pno_count**3 * 2 * len(groups) * (groups[0][0].shape[1] // pno_count)
    return pl.pallas_call(
        lambda *refs: update_kernel(members, len(groups), *refs),
        out_shape=[jax.ShapeDtypeStruct((pair_count, pno_count // 2, lane_count), jnp.float32)] * len(members),
        in_specs=vmem(len(operands)),
        out_specs=vmem(len(members)),
        scratch_shapes=[pltpu.VMEM((pairs, pno_count, lane_count), jnp.float32)] * 2,
        compiler_params=pltpu.CompilerParams(vmem_limit_bytes=12 * 2**20),
        cost_estimate=pl.CostEstimate(flops=6 * products, bytes_accessed=2**20, transcendentals=0),
    )(*operands)


def gather_pieces(mine, axis):
    count = lax.axis_size(axis)
    up, down = [mine], []
    for shift in range(1, count):
        if shift <= count // 2:
            up.append(from_behind(up[-1], axis, 1))
        else:
            down.append(from_behind(down[-1] if down else mine, axis, count - 1))
    return up + down[::-1]


def on_device_shared(pno_basis, amplitudes, send_list, couple, couple_weight, fit_weight, fit_blocks):
    pair_count, pno_count, _ = pno_basis.shape
    group_total = lax.axis_size("blk")
    pieces = gather_pieces(fit_blocks, "dom")
    across = from_partner(pno_basis, "blk", 2)
    groups = [pieces, *[[from_behind(x, "blk", by) for x in pieces] for by in range(SET, group_total, SET)]]
    pair_amps = amplitudes.reshape(pair_count, pno_count, pno_count)
    sent = pack_pairs(send_list.reshape(-1), pno_basis, pair_amps)
    sent, *heads = lax.optimization_barrier((sent, *[group[0] for group in groups[1:]]))
    for group, head in zip(groups[1:], heads):
        group[0] = head
    coupled = lax.all_to_all(sent, "blk", split_axis=0, concat_axis=0, tiled=True)
    bases = [pno_basis, from_partner(pno_basis, "blk", 1), across, from_partner(across, "blk", 1)]
    own = dress(couple, couple_weight, fit_weight, pno_basis, pair_amps, coupled)
    dressed = [own, *[from_partner(own, "blk", flip) for flip in range(1, SET)]]
    inner = [project(bases, group) for group in groups]
    updated = None
    for members in ((3, 2), (1, 0)):
        partial = update(members, inner, [dressed[member] for member in members])
        if members[-1]:
            partial, inner = lax.optimization_barrier((partial, inner))
        for member, x in zip(members, partial):
            x = from_partner(x, "blk", member) if member else x
            updated = x if updated is None else updated + x
    return updated.reshape(pair_count, pno_count * pno_count)


def dress_with(pair_amps, intersection, partner_amps, weights):
    half_product = jnp.einsum("pcab,pcbe->pcae", intersection, partner_amps, precision=HIGHEST)
    sandwich = jnp.einsum("pcae,pcfe->pcaf", half_product, intersection, precision=HIGHEST)
    return pair_amps + jnp.einsum("pc,pcaf->paf", weights, sandwich, precision=HIGHEST)


def fit_term(pair_basis, dressed, blocks, weights):
    pair_count, pno_count, orbital_count = pair_basis.shape
    flat_basis = pair_basis.reshape(pair_count * pno_count, orbital_count)
    stacked = blocks.reshape(2 * orbital_count, orbital_count)
    projected = jnp.dot(
        flat_basis, stacked.T, precision=HIGHEST, preferred_element_type=jnp.float32
    )
    projected = projected.reshape(pair_count, pno_count, 2, orbital_count)
    inner_blocks = jnp.einsum("par,pbmr->mpab", pair_basis, projected, precision=HIGHEST)
    left_product = jnp.einsum("pai,pij->paj", inner_blocks[0], dressed, precision=HIGHEST)
    fit_contrib = jnp.einsum("paj,pbj->pab", left_product, inner_blocks[1], precision=HIGHEST)
    return weights[:, None, None] * fit_contrib


def on_device_ring(pno_basis, amplitudes, send_list, couple, couple_weight, fit_weight, fit_blocks):
    pair_count, pno_count, _ = pno_basis.shape
    block_count = fit_blocks.shape[0]
    pair_amps = amplitudes.reshape(pair_count, pno_count, pno_count)
    send_order = send_list.reshape(-1)
    basis_in = lax.all_to_all(jnp.take(pno_basis, send_order, axis=0), "blk", split_axis=0, concat_axis=0, tiled=True)
    amps_in = lax.all_to_all(jnp.take(pair_amps, send_order, axis=0), "blk", split_axis=0, concat_axis=0, tiled=True)
    partner_basis = jnp.take(basis_in, couple, axis=0)
    intersection = jnp.einsum("par,pcbr->pcab", pno_basis, partner_basis, precision=HIGHEST)
    dressed = dress_with(pair_amps, intersection, jnp.take(amps_in, couple, axis=0), couple_weight)
    updated = dressed
    current = lax.all_gather(fit_blocks, "dom", axis=2, tiled=True)
    for stop in range(fit_weight.shape[1] // block_count):
        if stop > 0:
            current = from_behind(current, "blk", 1)
        for b in range(block_count):
            updated = updated + fit_term(pno_basis, dressed, current[b], fit_weight[:, stop * block_count + b])
    return updated.reshape(pair_count, pno_count * pno_count)


def solution(mesh):
    placed = (
        P(("blk", "dom"), None, None),
        P(("blk", "dom"), None),
        P("blk", "dom", None, None),
        P(("blk", "dom"), None),
        P(("blk", "dom"), None),
        P(("blk", "dom"), None),
        P("blk", None, "dom", None),
    )

    def on_device(*args):
        send_list, fit_weight, fit_blocks = args[2], args[5], args[6]
        group_total = mesh.shape["blk"]
        meets_all = fit_weight.shape[1] == group_total * fit_blocks.shape[0]
        if meets_all and group_total % SET == 0 and group_total & (group_total - 1) == 0 and send_list.shape[3] == 1:
            return on_device_shared(*args)
        return on_device_ring(*args)

    return jax.shard_map(
        on_device, mesh=mesh, in_specs=placed, out_specs=P(("blk", "dom"), None), check_vma=False
    )
```

```python
import jax
import jax.numpy as jnp
from jax import lax
from jax.experimental import pallas as pl
from jax.experimental.pallas import tpu as pltpu
from jax.sharding import PartitionSpec as P

HIGHEST = lax.Precision.HIGHEST
SET = 4
NN = (((1,), (0,)), ((), ()))
NT = (((1,), (1,)), ((), ()))


def halves(x):
    high = x.astype(jnp.bfloat16)
    return high, (x - high.astype(jnp.float32)).astype(jnp.bfloat16)


def dot(a, b, dims):
    return lax.dot_general(a, b, dims, preferred_element_type=jnp.float32)


def dot3(a, b, dims):
    (a_high, a_low), (b_high, b_low) = a, b
    return dot(a_high, b_high, dims) + (dot(a_high, b_low, dims) + dot(a_low, b_high, dims))


def stack(parts, axis=0):
    return jnp.concatenate(parts, axis=axis)


def from_partner(x, axis, flip):
    return lax.ppermute(x, axis, [(i, i ^ flip) for i in range(lax.axis_size(axis))])


def from_behind(x, axis, by):
    count = lax.axis_size(axis)
    return lax.ppermute(x, axis, [(i, (i + by) % count) for i in range(count)])


def vmem(count):
    return [pl.BlockSpec(memory_space=pltpu.VMEM)] * count


def pack_kernel(send, basis, amps, out):
    pno_count = amps.shape[1]
    lanes = basis.shape[2] // pno_count
    step = pno_count // lanes
    for peer in range(out.shape[0]):
        pair = send[peer]
        out[peer, :pno_count] = basis[pair]
        listed = amps[pair]
        out[peer, pno_count:] = stack([listed[i * step:(i + 1) * step] for i in range(lanes)], 1)


def pack_pairs(send_order, basis, amps):
    _, pno_count, orbital_count = basis.shape
    rows = pno_count + pno_count * pno_count // orbital_count
    return pl.pallas_call(
        pack_kernel,
        out_shape=jax.ShapeDtypeStruct((send_order.shape[0], rows, orbital_count), jnp.float32),
        in_specs=[pl.BlockSpec(memory_space=pltpu.SMEM), *vmem(2)],
        out_specs=vmem(1)[0],
        compiler_params=pltpu.CompilerParams(vmem_limit_bytes=4 * 2**20),
        cost_estimate=pl.CostEstimate(flops=0, bytes_accessed=4 * basis.size, transcendentals=0),
    )(send_order, basis, amps)


def dress_kernel(couple, couple_weight, fit_weight, basis, amps, coupled, dressed, turned):
    pair_count, pno_count, orbital_count = basis.shape
    half = pno_count // 2
    slot_count = coupled.shape[0]
    own = halves(basis[...].reshape(pair_count * pno_count, orbital_count))
    others = halves(coupled[:, :pno_count].reshape(slot_count * pno_count, orbital_count))
    overlap = halves(dot3(own, others, NT))
    left, slot_weight = [], []
    for slot in range(slot_count):
        cols = slice(slot * pno_count, (slot + 1) * pno_count)
        packed = coupled[slot, pno_count:]
        partner = stack([packed[:, i:i + pno_count] for i in range(0, orbital_count, pno_count)])
        left.append(dot3([x[:, cols] for x in overlap], halves(partner), NN))
        named = jnp.where(couple[...] == slot, couple_weight[...], 0.0)
        slot_weight.append(jnp.sum(named, axis=1, keepdims=True))
    dressed[:, half:, :] = jnp.zeros((pair_count, dressed.shape[1] - half, 2 * pno_count), jnp.float32)
    for pair in range(pair_count):
        rows = slice(pair * pno_count, (pair + 1) * pno_count)
        scaled = stack([x[rows] * w[pair:pair + 1] for x, w in zip(left, slot_weight)], 1)
        turned[pair] = amps[pair] + dot3(halves(scaled), [x[rows] for x in overlap], NT)
        dressed[pair, :half] = two_to_one(turned, pair, half)
        dressed[pair, half:half + 1, : fit_weight.shape[1]] = fit_weight[pair:pair + 1, :]


def two_to_one(ref, pair, half):
    return stack([ref[pair, pl.ds(i, half, stride=2), :] for i in range(2)], 1)


def dress(couple, couple_weight, fit_weight, basis, amps, coupled):
    pair_count, pno_count, _ = basis.shape
    return pl.pallas_call(
        dress_kernel,
        out_shape=jax.ShapeDtypeStruct((pair_count, pno_count // 2 + 8, 2 * pno_count), jnp.float32),
        in_specs=vmem(6),
        out_specs=vmem(1)[0],
        scratch_shapes=[pltpu.VMEM((pair_count, pno_count, pno_count), jnp.float32)],
        compiler_params=pltpu.CompilerParams(vmem_limit_bytes=10 * 2**20),
        cost_estimate=pl.CostEstimate(flops=4 * 10**9, bytes_accessed=8 * basis.size, transcendentals=0),
    )(couple, couple_weight, fit_weight, basis, amps, coupled)


def fold(x):
    return x + pltpu.roll(x, x.shape[1] // 2, 1)


def left_lanes(x):
    return lax.broadcasted_iota(jnp.int32, x.shape, 1) < x.shape[1] // 2


def split(x):
    high = x.astype(jnp.bfloat16)
    wide = high.astype(jnp.float32)
    return high, wide, x - wide


def high_low(x):
    _, high, low = split(x)
    return jnp.where(left_lanes(x), high, low).astype(jnp.bfloat16)


def project_kernel(*refs):
    bases, refs = refs[:SET], refs[SET:]
    *pieces, inner_left, inner_right, block_cat, wide, cat, projected = refs
    pair_count, pno_count, orbital_count = bases[0].shape
    block_count, part_count, row_count, _ = pieces[0].shape
    dom_count = len(pieces)
    place = lax.axis_index("dom")
    for shift, piece in enumerate(pieces):
        start = lax.rem(place + dom_count - shift, dom_count) * row_count
        for b in range(block_count):
            for m in range(part_count):
                high, low = halves(piece[b, m])
                for i, x in enumerate((high, high, low)):
                    at = pl.multiple_of(start + i * orbital_count, row_count)
                    block_cat[m, b, pl.ds(at, row_count), :] = x
    size = block_count * pno_count
    for member in range(SET):
        slot = member % 2
        high, low = halves(bases[member][...])
        for i, x in enumerate((high, low, high)):
            wide[slot, :, :, i * orbital_count:(i + 1) * orbital_count] = x
        for i, (upper, lower) in enumerate(((high, low), (high, jnp.zeros_like(low)))):
            lanes = slice(i * orbital_count, (i + 1) * orbital_count)
            cat[slot, :, :pno_count, lanes] = upper
            cat[slot, :, pno_count:, lanes] = lower
        basis = wide[slot].reshape(pair_count * pno_count, 3 * orbital_count)
        for m in range(part_count):
            for b in range(block_count):
                product = halves(dot(basis, block_cat[m, b], NN).reshape(pair_count, pno_count, orbital_count))
                at = (m * block_count + b) * pno_count
                for i in range(2):
                    projected[slot, :, at:at + pno_count, i * orbital_count:(i + 1) * orbital_count] = product[i]
        for pair in range(pair_count):
            here = member * pair_count + pair
            inner = fold(dot(projected[slot, pair], cat[slot, pair], NT))
            inner_left[here] = high_low(inner[:size])
            high, _, low = split(inner[size:])
            low = jnp.where(left_lanes(low), low, 0.0).astype(jnp.bfloat16)
            for b in range(block_count):
                rows = slice(b * pno_count, (b + 1) * pno_count)
                lanes = slice(b * 2 * pno_count, (b + 1) * 2 * pno_count)
                inner_right[here, :pno_count, lanes] = high[rows]
                inner_right[here, pno_count:, lanes] = low[rows]


def project(bases, pieces):
    pair_count, pno_count, _ = bases[0].shape
    block_count, part_count, _, orbital_count = pieces[0].shape
    pairs = SET * pair_count
    products = block_count * part_count * pairs * pno_count * orbital_count * (orbital_count + pno_count)
    return pl.pallas_call(
        project_kernel,
        out_shape=(
            jax.ShapeDtypeStruct((pairs, block_count * pno_count, 2 * pno_count), jnp.bfloat16),
            jax.ShapeDtypeStruct((pairs, 2 * pno_count, block_count * 2 * pno_count), jnp.bfloat16),
        ),
        in_specs=vmem(SET + len(pieces)),
        out_specs=tuple(vmem(2)),
        scratch_shapes=[
            pltpu.VMEM((part_count, block_count, 3 * orbital_count, orbital_count), jnp.bfloat16),
            pltpu.VMEM((2, pair_count, pno_count, 3 * orbital_count), jnp.bfloat16),
            pltpu.VMEM((2, pair_count, 2 * pno_count, 2 * orbital_count), jnp.bfloat16),
            pltpu.VMEM((2, pair_count, part_count * block_count * pno_count, 2 * orbital_count), jnp.bfloat16),
        ],
        compiler_params=pltpu.CompilerParams(vmem_limit_bytes=20 * 2**20),
        cost_estimate=pl.CostEstimate(flops=6 * products, bytes_accessed=2**20, transcendentals=0),
    )(*bases, *pieces)


def update_kernel(members, group_count, *refs):
    groups, refs = refs[:2 * group_count], refs[2 * group_count:]
    dressed, after, (turned, total) = refs[:len(members)], refs[len(members):2 * len(members)], refs[2 * len(members):]
    pair_count, _, lane_count = dressed[0].shape
    pno_count = lane_count // 2
    half = pno_count // 2
    block_count = groups[0].shape[1] // pno_count
    group_total = lax.axis_size("blk")
    me = lax.axis_index("blk")
    for index, member in enumerate(members):
        row = dressed[index][:, half:half + 1, :]
        lane = lax.broadcasted_iota(jnp.int32, row.shape, 2)
        weights = []
        for group in range(group_count):
            stop = lax.rem((me ^ member) + 2 * group_total + group * SET - me, group_total)
            for b in range(block_count):
                kept = jnp.where(lane == stop * block_count + b, row, 0.0)
                weights.append(jnp.sum(kept, axis=2, keepdims=True))
        for pair in range(pair_count):
            packed = dressed[index][pair, :half]
            other = pltpu.roll(packed, pno_count, 1)
            at = index * pair_count + pair
            turned[at, pl.ds(0, half, stride=2), :] = jnp.where(left_lanes(packed), packed, other)
            turned[at, pl.ds(1, half, stride=2), :] = jnp.where(left_lanes(packed), other, packed)
            twice = turned[at]
            _, high, _ = split(twice)
            square = stack([high_low(twice), jnp.where(left_lanes(twice), high, 0.0).astype(jnp.bfloat16)])
            here = member * pair_count + pair
            terms = []
            for group in range(group_count):
                moved = fold(dot(groups[2 * group][here], square, NN))
                blocks = [
                    high_low(moved[b * pno_count:(b + 1) * pno_count] * weights[group * block_count + b][pair])
                    for b in range(block_count)
                ]
                terms.append(dot(stack(blocks, 1), groups[2 * group + 1][here], NT))
            total[at] = fold(sum(terms[1:], terms[0]))
        for pair in range(pair_count):
            at = index * pair_count + pair
            rows = [total[at, pl.ds(i, half, stride=2), :] for i in range(2)]
            result = jnp.where(left_lanes(rows[0]), *rows)
            if member == 0:
                result += dressed[index][pair, :half]
            after[index][pair] = result


def update(members, groups, dressed):
    pair_count, _, lane_count = dressed[0].shape
    pno_count = lane_count // 2
    pairs = len(members) * pair_count
    operands = [x for group in groups for x in group] + dressed
    products = pairs * pno_count**3 * 2 * len(groups) * (groups[0][0].shape[1] // pno_count)
    return pl.pallas_call(
        lambda *refs: update_kernel(members, len(groups), *refs),
        out_shape=[jax.ShapeDtypeStruct((pair_count, pno_count // 2, lane_count), jnp.float32)] * len(members),
        in_specs=vmem(len(operands)),
        out_specs=vmem(len(members)),
        scratch_shapes=[pltpu.VMEM((pairs, pno_count, lane_count), jnp.float32)] * 2,
        compiler_params=pltpu.CompilerParams(vmem_limit_bytes=12 * 2**20),
        cost_estimate=pl.CostEstimate(flops=6 * products, bytes_accessed=2**20, transcendentals=0),
    )(*operands)


def gather_pieces(mine, axis):
    count = lax.axis_size(axis)
    up, down = [mine], []
    for shift in range(1, count):
        if shift <= count // 2:
            up.append(from_behind(up[-1], axis, 1))
        else:
            down.append(from_behind(down[-1] if down else mine, axis, count - 1))
    return up + down[::-1]


def on_device_shared(pno_basis, amplitudes, send_list, couple, couple_weight, fit_weight, fit_blocks):
    pair_count, pno_count, _ = pno_basis.shape
    group_total = lax.axis_size("blk")
    pieces = gather_pieces(fit_blocks, "dom")
    across = from_partner(pno_basis, "blk", 2)
    groups = [pieces, *[[from_behind(x, "blk", by) for x in pieces] for by in range(SET, group_total, SET)]]
    pair_amps = amplitudes.reshape(pair_count, pno_count, pno_count)
    sent = pack_pairs(send_list.reshape(-1), pno_basis, pair_amps)
    ahead = [pieces[1], pieces[-1], across, *[group[0] for group in groups[1:]]]
    sent, pieces[1], pieces[-1], across, *heads = lax.optimization_barrier((sent, *ahead))
    for group, head in zip(groups[1:], heads):
        group[0] = head
    coupled = lax.all_to_all(sent, "blk", split_axis=0, concat_axis=0, tiled=True)
    bases = [pno_basis, from_partner(pno_basis, "blk", 1), across, from_partner(across, "blk", 1)]
    own = dress(couple, couple_weight, fit_weight, pno_basis, pair_amps, coupled)
    dressed = [own, *[from_partner(own, "blk", flip) for flip in range(1, SET)]]
    inner = [project(bases, group) for group in groups]
    updated = None
    for members in ((3, 2), (1, 0)):
        partial = update(members, inner, [dressed[member] for member in members])
        if members[-1]:
            partial, inner = lax.optimization_barrier((partial, inner))
        for member, x in zip(members, partial):
            x = from_partner(x, "blk", member) if member else x
            updated = x if updated is None else updated + x
    return updated.reshape(pair_count, pno_count * pno_count)


def dress_with(pair_amps, intersection, partner_amps, weights):
    half_product = jnp.einsum("pcab,pcbe->pcae", intersection, partner_amps, precision=HIGHEST)
    sandwich = jnp.einsum("pcae,pcfe->pcaf", half_product, intersection, precision=HIGHEST)
    return pair_amps + jnp.einsum("pc,pcaf->paf", weights, sandwich, precision=HIGHEST)


def fit_term(pair_basis, dressed, blocks, weights):
    pair_count, pno_count, orbital_count = pair_basis.shape
    flat_basis = pair_basis.reshape(pair_count * pno_count, orbital_count)
    stacked = blocks.reshape(2 * orbital_count, orbital_count)
    projected = jnp.dot(
        flat_basis, stacked.T, precision=HIGHEST, preferred_element_type=jnp.float32
    )
    projected = projected.reshape(pair_count, pno_count, 2, orbital_count)
    inner_blocks = jnp.einsum("par,pbmr->mpab", pair_basis, projected, precision=HIGHEST)
    left_product = jnp.einsum("pai,pij->paj", inner_blocks[0], dressed, precision=HIGHEST)
    fit_contrib = jnp.einsum("paj,pbj->pab", left_product, inner_blocks[1], precision=HIGHEST)
    return weights[:, None, None] * fit_contrib


def on_device_ring(pno_basis, amplitudes, send_list, couple, couple_weight, fit_weight, fit_blocks):
    pair_count, pno_count, _ = pno_basis.shape
    block_count = fit_blocks.shape[0]
    pair_amps = amplitudes.reshape(pair_count, pno_count, pno_count)
    send_order = send_list.reshape(-1)
    basis_in = lax.all_to_all(jnp.take(pno_basis, send_order, axis=0), "blk", split_axis=0, concat_axis=0, tiled=True)
    amps_in = lax.all_to_all(jnp.take(pair_amps, send_order, axis=0), "blk", split_axis=0, concat_axis=0, tiled=True)
    partner_basis = jnp.take(basis_in, couple, axis=0)
    intersection = jnp.einsum("par,pcbr->pcab", pno_basis, partner_basis, precision=HIGHEST)
    dressed = dress_with(pair_amps, intersection, jnp.take(amps_in, couple, axis=0), couple_weight)
    updated = dressed
    current = lax.all_gather(fit_blocks, "dom", axis=2, tiled=True)
    for stop in range(fit_weight.shape[1] // block_count):
        if stop > 0:
            current = from_behind(current, "blk", 1)
        for b in range(block_count):
            updated = updated + fit_term(pno_basis, dressed, current[b], fit_weight[:, stop * block_count + b])
    return updated.reshape(pair_count, pno_count * pno_count)


def solution(mesh):
    placed = (
        P(("blk", "dom"), None, None),
        P(("blk", "dom"), None),
        P("blk", "dom", None, None),
        P(("blk", "dom"), None),
        P(("blk", "dom"), None),
        P(("blk", "dom"), None),
        P("blk", None, "dom", None),
    )

    def on_device(*args):
        send_list, fit_weight, fit_blocks = args[2], args[5], args[6]
        group_total = mesh.shape["blk"]
        meets_all = fit_weight.shape[1] == group_total * fit_blocks.shape[0]
        if meets_all and group_total % SET == 0 and group_total & (group_total - 1) == 0 and send_list.shape[3] == 1:
            return on_device_shared(*args)
        return on_device_ring(*args)

    return jax.shard_map(
        on_device, mesh=mesh, in_specs=placed, out_specs=P(("blk", "dom"), None), check_vma=False
    )
```

```python
import jax
import jax.numpy as jnp
from jax import lax
from jax.experimental import pallas as pl
from jax.experimental.pallas import tpu as pltpu
from jax.sharding import PartitionSpec as P

HIGHEST = lax.Precision.HIGHEST
SET = 4
NN = (((1,), (0,)), ((), ()))
NT = (((1,), (1,)), ((), ()))


def halves(x):
    high = x.astype(jnp.bfloat16)
    return high, (x - high.astype(jnp.float32)).astype(jnp.bfloat16)


def dot(a, b, dims):
    return lax.dot_general(a, b, dims, preferred_element_type=jnp.float32)


def dot3(a, b, dims):
    (a_high, a_low), (b_high, b_low) = a, b
    return dot(a_high, b_high, dims) + (dot(a_high, b_low, dims) + dot(a_low, b_high, dims))


def stack(parts, axis=0):
    return jnp.concatenate(parts, axis=axis)


def from_partner(x, axis, flip):
    return lax.ppermute(x, axis, [(i, i ^ flip) for i in range(lax.axis_size(axis))])


def from_behind(x, axis, by):
    count = lax.axis_size(axis)
    return lax.ppermute(x, axis, [(i, (i + by) % count) for i in range(count)])


def vmem(count):
    return [pl.BlockSpec(memory_space=pltpu.VMEM)] * count


def pack_kernel(send, basis, amps, out):
    pno_count = amps.shape[1]
    lanes = basis.shape[2] // pno_count
    step = pno_count // lanes
    for peer in range(out.shape[0]):
        pair = send[peer]
        out[peer, :pno_count] = basis[pair]
        listed = amps[pair]
        out[peer, pno_count:] = stack([listed[i * step:(i + 1) * step] for i in range(lanes)], 1)


def pack_pairs(send_order, basis, amps):
    _, pno_count, orbital_count = basis.shape
    rows = pno_count + pno_count * pno_count // orbital_count
    return pl.pallas_call(
        pack_kernel,
        out_shape=jax.ShapeDtypeStruct((send_order.shape[0], rows, orbital_count), jnp.float32),
        in_specs=[pl.BlockSpec(memory_space=pltpu.SMEM), *vmem(2)],
        out_specs=vmem(1)[0],
        compiler_params=pltpu.CompilerParams(vmem_limit_bytes=4 * 2**20),
        cost_estimate=pl.CostEstimate(flops=0, bytes_accessed=4 * basis.size, transcendentals=0),
    )(send_order, basis, amps)


def dress_kernel(couple, couple_weight, fit_weight, basis, amps, coupled, dressed, turned):
    pair_count, pno_count, orbital_count = basis.shape
    half = pno_count // 2
    slot_count = coupled.shape[0]
    own = halves(basis[...].reshape(pair_count * pno_count, orbital_count))
    others = halves(coupled[:, :pno_count].reshape(slot_count * pno_count, orbital_count))
    overlap = halves(dot3(own, others, NT))
    left, slot_weight = [], []
    for slot in range(slot_count):
        cols = slice(slot * pno_count, (slot + 1) * pno_count)
        packed = coupled[slot, pno_count:]
        partner = stack([packed[:, i:i + pno_count] for i in range(0, orbital_count, pno_count)])
        left.append(dot3([x[:, cols] for x in overlap], halves(partner), NN))
        named = jnp.where(couple[...] == slot, couple_weight[...], 0.0)
        slot_weight.append(jnp.sum(named, axis=1, keepdims=True))
    dressed[:, half:, :] = jnp.zeros((pair_count, dressed.shape[1] - half, 2 * pno_count), jnp.float32)
    for pair in range(pair_count):
        rows = slice(pair * pno_count, (pair + 1) * pno_count)
        scaled = stack([x[rows] * w[pair:pair + 1] for x, w in zip(left, slot_weight)], 1)
        turned[pair] = amps[pair] + dot3(halves(scaled), [x[rows] for x in overlap], NT)
        dressed[pair, :half] = two_to_one(turned, pair, half)
        dressed[pair, half:half + 1, : fit_weight.shape[1]] = fit_weight[pair:pair + 1, :]


def two_to_one(ref, pair, half):
    return stack([ref[pair, pl.ds(i, half, stride=2), :] for i in range(2)], 1)


def dress(couple, couple_weight, fit_weight, basis, amps, coupled):
    pair_count, pno_count, _ = basis.shape
    return pl.pallas_call(
        dress_kernel,
        out_shape=jax.ShapeDtypeStruct((pair_count, pno_count // 2 + 8, 2 * pno_count), jnp.float32),
        in_specs=vmem(6),
        out_specs=vmem(1)[0],
        scratch_shapes=[pltpu.VMEM((pair_count, pno_count, pno_count), jnp.float32)],
        compiler_params=pltpu.CompilerParams(vmem_limit_bytes=10 * 2**20),
        cost_estimate=pl.CostEstimate(flops=4 * 10**9, bytes_accessed=8 * basis.size, transcendentals=0),
    )(couple, couple_weight, fit_weight, basis, amps, coupled)


def fold(x):
    return x + pltpu.roll(x, x.shape[1] // 2, 1)


def left_lanes(x):
    return lax.broadcasted_iota(jnp.int32, x.shape, 1) < x.shape[1] // 2


def split(x):
    high = x.astype(jnp.bfloat16)
    wide = high.astype(jnp.float32)
    return high, wide, x - wide


def high_low(x):
    _, high, low = split(x)
    return jnp.where(left_lanes(x), high, low).astype(jnp.bfloat16)


def project_kernel(*refs):
    bases, refs = refs[:SET], refs[SET:]
    *pieces, inner_left, inner_right, block_cat, wide, cat, projected = refs
    pair_count, pno_count, orbital_count = bases[0].shape
    block_count, part_count, row_count, _ = pieces[0].shape
    dom_count = len(pieces)
    place = lax.axis_index("dom")
    for shift, piece in enumerate(pieces):
        start = lax.rem(place + dom_count - shift, dom_count) * row_count
        for b in range(block_count):
            for m in range(part_count):
                high, low = halves(piece[b, m])
                for i, x in enumerate((high, high, low)):
                    at = pl.multiple_of(start + i * orbital_count, row_count)
                    block_cat[m, b, pl.ds(at, row_count), :] = x
    size = block_count * pno_count
    for member in range(SET):
        slot = member % 2
        high, low = halves(bases[member][...])
        for i, x in enumerate((high, low, high)):
            wide[slot, :, :, i * orbital_count:(i + 1) * orbital_count] = x
        for i, (upper, lower) in enumerate(((high, low), (high, jnp.zeros_like(low)))):
            lanes = slice(i * orbital_count, (i + 1) * orbital_count)
            cat[slot, :, :pno_count, lanes] = upper
            cat[slot, :, pno_count:, lanes] = lower
        basis = wide[slot].reshape(pair_count * pno_count, 3 * orbital_count)
        for m in range(part_count):
            for b in range(block_count):
                product = halves(dot(basis, block_cat[m, b], NN).reshape(pair_count, pno_count, orbital_count))
                at = (m * block_count + b) * pno_count
                for i in range(2):
                    projected[slot, :, at:at + pno_count, i * orbital_count:(i + 1) * orbital_count] = product[i]
        for pair in range(pair_count):
            here = member * pair_count + pair
            inner = fold(dot(projected[slot, pair], cat[slot, pair], NT))
            inner_left[here] = high_low(inner[:size])
            high, _, low = split(inner[size:])
            low = jnp.where(left_lanes(low), low, 0.0).astype(jnp.bfloat16)
            for b in range(block_count):
                rows = slice(b * pno_count, (b + 1) * pno_count)
                lanes = slice(b * 2 * pno_count, (b + 1) * 2 * pno_count)
                inner_right[here, :pno_count, lanes] = high[rows]
                inner_right[here, pno_count:, lanes] = low[rows]


def project(bases, pieces):
    pair_count, pno_count, _ = bases[0].shape
    block_count, part_count, _, orbital_count = pieces[0].shape
    pairs = SET * pair_count
    products = block_count * part_count * pairs * pno_count * orbital_count * (orbital_count + pno_count)
    return pl.pallas_call(
        project_kernel,
        out_shape=(
            jax.ShapeDtypeStruct((pairs, block_count * pno_count, 2 * pno_count), jnp.bfloat16),
            jax.ShapeDtypeStruct((pairs, 2 * pno_count, block_count * 2 * pno_count), jnp.bfloat16),
        ),
        in_specs=vmem(SET + len(pieces)),
        out_specs=tuple(vmem(2)),
        scratch_shapes=[
            pltpu.VMEM((part_count, block_count, 3 * orbital_count, orbital_count), jnp.bfloat16),
            pltpu.VMEM((2, pair_count, pno_count, 3 * orbital_count), jnp.bfloat16),
            pltpu.VMEM((2, pair_count, 2 * pno_count, 2 * orbital_count), jnp.bfloat16),
            pltpu.VMEM((2, pair_count, part_count * block_count * pno_count, 2 * orbital_count), jnp.bfloat16),
        ],
        compiler_params=pltpu.CompilerParams(vmem_limit_bytes=20 * 2**20),
        cost_estimate=pl.CostEstimate(flops=6 * products, bytes_accessed=2**20, transcendentals=0),
    )(*bases, *pieces)


def update_kernel(members, group_count, *refs):
    groups, refs = refs[:2 * group_count], refs[2 * group_count:]
    dressed, after, (turned, total) = refs[:len(members)], refs[len(members):2 * len(members)], refs[2 * len(members):]
    pair_count, _, lane_count = dressed[0].shape
    pno_count = lane_count // 2
    half = pno_count // 2
    block_count = groups[0].shape[1] // pno_count
    group_total = lax.axis_size("blk")
    me = lax.axis_index("blk")
    for index, member in enumerate(members):
        row = dressed[index][:, half:half + 1, :]
        lane = lax.broadcasted_iota(jnp.int32, row.shape, 2)
        weights = []
        for group in range(group_count):
            stop = lax.rem((me ^ member) + 2 * group_total + group * SET - me, group_total)
            for b in range(block_count):
                kept = jnp.where(lane == stop * block_count + b, row, 0.0)
                weights.append(jnp.sum(kept, axis=2, keepdims=True))
        for pair in range(pair_count):
            packed = dressed[index][pair, :half]
            other = pltpu.roll(packed, pno_count, 1)
            at = index * pair_count + pair
            turned[at, pl.ds(0, half, stride=2), :] = jnp.where(left_lanes(packed), packed, other)
            turned[at, pl.ds(1, half, stride=2), :] = jnp.where(left_lanes(packed), other, packed)
            twice = turned[at]
            _, high, _ = split(twice)
            square = stack([high_low(twice), jnp.where(left_lanes(twice), high, 0.0).astype(jnp.bfloat16)])
            here = member * pair_count + pair
            terms = []
            for group in range(group_count):
                moved = fold(dot(groups[2 * group][here], square, NN))
                blocks = [
                    high_low(moved[b * pno_count:(b + 1) * pno_count] * weights[group * block_count + b][pair])
                    for b in range(block_count)
                ]
                terms.append(dot(stack(blocks, 1), groups[2 * group + 1][here], NT))
            total[at] = fold(sum(terms[1:], terms[0]))
        for pair in range(pair_count):
            at = index * pair_count + pair
            rows = [total[at, pl.ds(i, half, stride=2), :] for i in range(2)]
            result = jnp.where(left_lanes(rows[0]), *rows)
            if member == 0:
                result += dressed[index][pair, :half]
            after[index][pair] = result


def update(members, groups, dressed):
    pair_count, _, lane_count = dressed[0].shape
    pno_count = lane_count // 2
    pairs = len(members) * pair_count
    operands = [x for group in groups for x in group] + dressed
    products = pairs * pno_count**3 * 2 * len(groups) * (groups[0][0].shape[1] // pno_count)
    return pl.pallas_call(
        lambda *refs: update_kernel(members, len(groups), *refs),
        out_shape=[jax.ShapeDtypeStruct((pair_count, pno_count // 2, lane_count), jnp.float32)] * len(members),
        in_specs=vmem(len(operands)),
        out_specs=vmem(len(members)),
        scratch_shapes=[pltpu.VMEM((pairs, pno_count, lane_count), jnp.float32)] * 2,
        compiler_params=pltpu.CompilerParams(vmem_limit_bytes=12 * 2**20),
        cost_estimate=pl.CostEstimate(flops=6 * products, bytes_accessed=2**20, transcendentals=0),
    )(*operands)


def gather_pieces(mine, axis):
    count = lax.axis_size(axis)
    up, down = [mine], []
    for shift in range(1, count):
        if shift <= count // 2:
            up.append(from_behind(up[-1], axis, 1))
        else:
            down.append(from_behind(down[-1] if down else mine, axis, count - 1))
    return up + down[::-1]


def on_device_shared(pno_basis, amplitudes, send_list, couple, couple_weight, fit_weight, fit_blocks):
    pair_count, pno_count, _ = pno_basis.shape
    group_total = lax.axis_size("blk")
    pieces = gather_pieces(fit_blocks, "dom")
    across = from_partner(pno_basis, "blk", 2)
    groups = [pieces, *[[from_behind(x, "blk", by) for x in pieces] for by in range(SET, group_total, SET)]]
    pair_amps = amplitudes.reshape(pair_count, pno_count, pno_count)
    sent = pack_pairs(send_list.reshape(-1), pno_basis, pair_amps)
    sent, pieces[1], *heads = lax.optimization_barrier((sent, pieces[1], *[group[0] for group in groups[1:]]))
    for group, head in zip(groups[1:], heads):
        group[0] = head
    coupled = lax.all_to_all(sent, "blk", split_axis=0, concat_axis=0, tiled=True)
    bases = [pno_basis, from_partner(pno_basis, "blk", 1), across, from_partner(across, "blk", 1)]
    own = dress(couple, couple_weight, fit_weight, pno_basis, pair_amps, coupled)
    dressed = [own, *[from_partner(own, "blk", flip) for flip in range(1, SET)]]
    inner = [project(bases, group) for group in groups]
    updated = None
    for members in ((3, 2), (1, 0)):
        partial = update(members, inner, [dressed[member] for member in members])
        if members[-1]:
            partial, inner = lax.optimization_barrier((partial, inner))
        for member, x in zip(members, partial):
            x = from_partner(x, "blk", member) if member else x
            updated = x if updated is None else updated + x
    return updated.reshape(pair_count, pno_count * pno_count)


def dress_with(pair_amps, intersection, partner_amps, weights):
    half_product = jnp.einsum("pcab,pcbe->pcae", intersection, partner_amps, precision=HIGHEST)
    sandwich = jnp.einsum("pcae,pcfe->pcaf", half_product, intersection, precision=HIGHEST)
    return pair_amps + jnp.einsum("pc,pcaf->paf", weights, sandwich, precision=HIGHEST)


def fit_term(pair_basis, dressed, blocks, weights):
    pair_count, pno_count, orbital_count = pair_basis.shape
    flat_basis = pair_basis.reshape(pair_count * pno_count, orbital_count)
    stacked = blocks.reshape(2 * orbital_count, orbital_count)
    projected = jnp.dot(
        flat_basis, stacked.T, precision=HIGHEST, preferred_element_type=jnp.float32
    )
    projected = projected.reshape(pair_count, pno_count, 2, orbital_count)
    inner_blocks = jnp.einsum("par,pbmr->mpab", pair_basis, projected, precision=HIGHEST)
    left_product = jnp.einsum("pai,pij->paj", inner_blocks[0], dressed, precision=HIGHEST)
    fit_contrib = jnp.einsum("paj,pbj->pab", left_product, inner_blocks[1], precision=HIGHEST)
    return weights[:, None, None] * fit_contrib


def on_device_ring(pno_basis, amplitudes, send_list, couple, couple_weight, fit_weight, fit_blocks):
    pair_count, pno_count, _ = pno_basis.shape
    block_count = fit_blocks.shape[0]
    pair_amps = amplitudes.reshape(pair_count, pno_count, pno_count)
    send_order = send_list.reshape(-1)
    basis_in = lax.all_to_all(jnp.take(pno_basis, send_order, axis=0), "blk", split_axis=0, concat_axis=0, tiled=True)
    amps_in = lax.all_to_all(jnp.take(pair_amps, send_order, axis=0), "blk", split_axis=0, concat_axis=0, tiled=True)
    partner_basis = jnp.take(basis_in, couple, axis=0)
    intersection = jnp.einsum("par,pcbr->pcab", pno_basis, partner_basis, precision=HIGHEST)
    dressed = dress_with(pair_amps, intersection, jnp.take(amps_in, couple, axis=0), couple_weight)
    updated = dressed
    current = lax.all_gather(fit_blocks, "dom", axis=2, tiled=True)
    for stop in range(fit_weight.shape[1] // block_count):
        if stop > 0:
            current = from_behind(current, "blk", 1)
        for b in range(block_count):
            updated = updated + fit_term(pno_basis, dressed, current[b], fit_weight[:, stop * block_count + b])
    return updated.reshape(pair_count, pno_count * pno_count)


def solution(mesh):
    placed = (
        P(("blk", "dom"), None, None),
        P(("blk", "dom"), None),
        P("blk", "dom", None, None),
        P(("blk", "dom"), None),
        P(("blk", "dom"), None),
        P(("blk", "dom"), None),
        P("blk", None, "dom", None),
    )

    def on_device(*args):
        send_list, fit_weight, fit_blocks = args[2], args[5], args[6]
        group_total = mesh.shape["blk"]
        meets_all = fit_weight.shape[1] == group_total * fit_blocks.shape[0]
        if meets_all and group_total % SET == 0 and group_total & (group_total - 1) == 0 and send_list.shape[3] == 1:
            return on_device_shared(*args)
        return on_device_ring(*args)

    return jax.shard_map(
        on_device, mesh=mesh, in_specs=placed, out_specs=P(("blk", "dom"), None), check_vma=False
    )
```

```python
import jax
import jax.numpy as jnp
from jax import lax
from jax.experimental import pallas as pl
from jax.experimental.pallas import tpu as pltpu
from jax.sharding import PartitionSpec as P

HIGHEST = lax.Precision.HIGHEST
SET = 4
NN = (((1,), (0,)), ((), ()))
NT = (((1,), (1,)), ((), ()))


def halves(x):
    high = x.astype(jnp.bfloat16)
    return high, (x - high.astype(jnp.float32)).astype(jnp.bfloat16)


def dot(a, b, dims):
    return lax.dot_general(a, b, dims, preferred_element_type=jnp.float32)


def dot3(a, b, dims):
    (a_high, a_low), (b_high, b_low) = a, b
    return dot(a_high, b_high, dims) + (dot(a_high, b_low, dims) + dot(a_low, b_high, dims))


def stack(parts, axis=0):
    return jnp.concatenate(parts, axis=axis)


def from_partner(x, axis, flip):
    return lax.ppermute(x, axis, [(i, i ^ flip) for i in range(lax.axis_size(axis))])


def from_behind(x, axis, by):
    count = lax.axis_size(axis)
    return lax.ppermute(x, axis, [(i, (i + by) % count) for i in range(count)])


def vmem(count):
    return [pl.BlockSpec(memory_space=pltpu.VMEM)] * count


def pack_kernel(send, basis, amps, out):
    pno_count = amps.shape[1]
    lanes = basis.shape[2] // pno_count
    step = pno_count // lanes
    for peer in range(out.shape[0]):
        pair = send[peer]
        out[peer, :pno_count] = basis[pair]
        listed = amps[pair]
        out[peer, pno_count:] = stack([listed[i * step:(i + 1) * step] for i in range(lanes)], 1)


def pack_pairs(send_order, basis, amps):
    _, pno_count, orbital_count = basis.shape
    rows = pno_count + pno_count * pno_count // orbital_count
    return pl.pallas_call(
        pack_kernel,
        out_shape=jax.ShapeDtypeStruct((send_order.shape[0], rows, orbital_count), jnp.float32),
        in_specs=[pl.BlockSpec(memory_space=pltpu.SMEM), *vmem(2)],
        out_specs=vmem(1)[0],
        compiler_params=pltpu.CompilerParams(vmem_limit_bytes=4 * 2**20),
        cost_estimate=pl.CostEstimate(flops=0, bytes_accessed=4 * basis.size, transcendentals=0),
    )(send_order, basis, amps)


def dress_kernel(couple, couple_weight, fit_weight, basis, amps, coupled, dressed, result, turned):
    pair_count, pno_count, orbital_count = basis.shape
    half = pno_count // 2
    slot_count = coupled.shape[0]
    own = halves(basis[...].reshape(pair_count * pno_count, orbital_count))
    others = halves(coupled[:, :pno_count].reshape(slot_count * pno_count, orbital_count))
    overlap = halves(dot3(own, others, NT))
    left, slot_weight = [], []
    for slot in range(slot_count):
        cols = slice(slot * pno_count, (slot + 1) * pno_count)
        packed = coupled[slot, pno_count:]
        partner = stack([packed[:, i:i + pno_count] for i in range(0, orbital_count, pno_count)])
        left.append(dot3([x[:, cols] for x in overlap], halves(partner), NN))
        named = jnp.where(couple[...] == slot, couple_weight[...], 0.0)
        slot_weight.append(jnp.sum(named, axis=1, keepdims=True))
    dressed[:, half:, :] = jnp.zeros((pair_count, dressed.shape[1] - half, 2 * pno_count), jnp.float32)
    for pair in range(pair_count):
        rows = slice(pair * pno_count, (pair + 1) * pno_count)
        scaled = stack([x[rows] * w[pair:pair + 1] for x, w in zip(left, slot_weight)], 1)
        total = amps[pair] + dot3(halves(scaled), [x[rows] for x in overlap], NT)
        dressed[pair, :half] = stack([total[:half], total[half:]], 1)
        turned[pair] = total
        result[pair] = two_to_one(turned, pair, half)
        dressed[pair, half:half + 1, : fit_weight.shape[1]] = fit_weight[pair:pair + 1, :]


def two_to_one(ref, pair, half):
    return stack([ref[pair, pl.ds(i, half, stride=2), :] for i in range(2)], 1)


def dress(couple, couple_weight, fit_weight, basis, amps, coupled):
    pair_count, pno_count, _ = basis.shape
    return pl.pallas_call(
        dress_kernel,
        out_shape=tuple(
            jax.ShapeDtypeStruct((pair_count, pno_count // 2 + more, 2 * pno_count), jnp.float32) for more in (8, 0)
        ),
        in_specs=vmem(6),
        out_specs=tuple(vmem(2)),
        scratch_shapes=[pltpu.VMEM((pair_count, pno_count, pno_count), jnp.float32)],
        compiler_params=pltpu.CompilerParams(vmem_limit_bytes=10 * 2**20),
        cost_estimate=pl.CostEstimate(flops=4 * 10**9, bytes_accessed=8 * basis.size, transcendentals=0),
    )(couple, couple_weight, fit_weight, basis, amps, coupled)


def fold(x):
    return x + pltpu.roll(x, x.shape[1] // 2, 1)


def left_lanes(x):
    return lax.broadcasted_iota(jnp.int32, x.shape, 1) < x.shape[1] // 2


def split(x):
    high = x.astype(jnp.bfloat16)
    wide = high.astype(jnp.float32)
    return high, wide, x - wide


def high_low(x):
    _, high, low = split(x)
    return jnp.where(left_lanes(x), high, low).astype(jnp.bfloat16)


def project_kernel(*refs):
    bases, refs = refs[:SET], refs[SET:]
    *pieces, inner_left, inner_right, block_cat, wide, projected = refs
    pair_count, pno_count, orbital_count = bases[0].shape
    block_count, part_count, row_count, _ = pieces[0].shape
    dom_count = len(pieces)
    place = lax.axis_index("dom")
    for shift, piece in enumerate(pieces):
        start = lax.rem(place + dom_count - shift, dom_count) * row_count
        for b in range(block_count):
            for m in range(part_count):
                high, low = halves(piece[b, m])
                for i, x in enumerate((high, high, low)):
                    at = pl.multiple_of(start + i * orbital_count, row_count)
                    block_cat[m, b, pl.ds(at, row_count), :] = x
    size = block_count * pno_count
    for member in range(SET):
        slot = member % 2
        high, low = halves(bases[member][...])
        for i, x in enumerate((high, low, high)):
            wide[slot, :, :, i * orbital_count:(i + 1) * orbital_count] = x
        basis = wide[slot].reshape(pair_count * pno_count, 3 * orbital_count)
        for m in range(part_count):
            for b in range(block_count):
                product = halves(dot(basis, block_cat[m, b], NN).reshape(pair_count, pno_count, orbital_count))
                at = (m * block_count + b) * pno_count
                for i in range(2):
                    projected[slot, :, at:at + pno_count, i * orbital_count:(i + 1) * orbital_count] = product[i]
        for pair in range(pair_count):
            here = member * pair_count + pair
            both = stack([wide[slot, pair, :, i * orbital_count:(i + 1) * orbital_count] for i in range(2)])
            product = [projected[slot, pair, :, i * orbital_count:(i + 1) * orbital_count] for i in range(2)]
            inner = fold(dot(product[0], both, NT) + dot(product[1], both, NT))
            inner_left[here] = high_low(inner[:size])
            high, _, low = split(inner[size:])
            low = jnp.where(left_lanes(low), low, 0.0).astype(jnp.bfloat16)
            for b in range(block_count):
                rows = slice(b * pno_count, (b + 1) * pno_count)
                lanes = slice(b * 2 * pno_count, (b + 1) * 2 * pno_count)
                inner_right[here, :pno_count, lanes] = high[rows]
                inner_right[here, pno_count:, lanes] = low[rows]


def project(bases, pieces):
    pair_count, pno_count, _ = bases[0].shape
    block_count, part_count, _, orbital_count = pieces[0].shape
    pairs = SET * pair_count
    products = block_count * part_count * pairs * pno_count * orbital_count * (orbital_count + pno_count)
    return pl.pallas_call(
        project_kernel,
        out_shape=(
            jax.ShapeDtypeStruct((pairs, block_count * pno_count, 2 * pno_count), jnp.bfloat16),
            jax.ShapeDtypeStruct((pairs, 2 * pno_count, block_count * 2 * pno_count), jnp.bfloat16),
        ),
        in_specs=vmem(SET + len(pieces)),
        out_specs=tuple(vmem(2)),
        scratch_shapes=[
            pltpu.VMEM((part_count, block_count, 3 * orbital_count, orbital_count), jnp.bfloat16),
            pltpu.VMEM((2, pair_count, pno_count, 3 * orbital_count), jnp.bfloat16),
            pltpu.VMEM((2, pair_count, part_count * block_count * pno_count, 2 * orbital_count), jnp.bfloat16),
        ],
        compiler_params=pltpu.CompilerParams(vmem_limit_bytes=20 * 2**20),
        cost_estimate=pl.CostEstimate(flops=6 * products, bytes_accessed=2**20, transcendentals=0),
    )(*bases, *pieces)


def update_kernel(members, group_count, *refs):
    groups, refs = refs[:2 * group_count], refs[2 * group_count:]
    dressed, after, (square, moved, total) = refs[:len(members)], refs[len(members):2 * len(members)], refs[2 * len(members):]
    pair_count, _, lane_count = dressed[0].shape
    pno_count = lane_count // 2
    half = pno_count // 2
    block_count = groups[0].shape[1] // pno_count
    group_total = lax.axis_size("blk")
    me = lax.axis_index("blk")
    pairs = [(index, pair) for index in range(len(members)) for pair in range(pair_count)]
    weights = []
    for index, member in enumerate(members):
        row = dressed[index][:, half:half + 1, :]
        lane = lax.broadcasted_iota(jnp.int32, row.shape, 2)
        for group in range(group_count):
            stop = lax.rem((me ^ member) + 2 * group_total + group * SET - me, group_total)
            for b in range(block_count):
                kept = jnp.where(lane == stop * block_count + b, row, 0.0)
                weights.append(jnp.sum(kept, axis=2, keepdims=True))
    for at, (index, pair) in enumerate(pairs):
        packed = dressed[index][pair, :half]
        other = pltpu.roll(packed, pno_count, 1)
        keep = left_lanes(packed)
        _, high, low = split(stack([jnp.where(keep, packed, other), jnp.where(keep, other, packed)]))
        square[at, :pno_count] = jnp.where(left_lanes(low), high, low).astype(jnp.bfloat16)
        square[at, pno_count:] = jnp.where(left_lanes(low), high, 0.0).astype(jnp.bfloat16)
    for at, (index, pair) in enumerate(pairs):
        here = members[index] * pair_count + pair
        for group in range(group_count):
            product = fold(dot(groups[2 * group][here], square[at], NN))
            for b in range(block_count):
                weight = weights[(index * group_count + group) * block_count + b][pair]
                lanes = slice(b * lane_count, (b + 1) * lane_count)
                moved[at, group, :, lanes] = high_low(product[b * pno_count:(b + 1) * pno_count] * weight)
    for at, (index, pair) in enumerate(pairs):
        here = members[index] * pair_count + pair
        terms = [dot(moved[at, group], groups[2 * group + 1][here], NT) for group in range(group_count)]
        total[at] = fold(sum(terms[1:], terms[0]))
    for at, (index, pair) in enumerate(pairs):
        rows = [total[at, pl.ds(i, half, stride=2), :] for i in range(2)]
        after[index][pair] = jnp.where(left_lanes(rows[0]), *rows)


def update(members, groups, dressed):
    pair_count, _, lane_count = dressed[0].shape
    pno_count = lane_count // 2
    pairs = len(members) * pair_count
    operands = [x for group in groups for x in group] + dressed
    products = pairs * pno_count**3 * 2 * len(groups) * (groups[0][0].shape[1] // pno_count)
    return pl.pallas_call(
        lambda *refs: update_kernel(members, len(groups), *refs),
        out_shape=[jax.ShapeDtypeStruct((pair_count, pno_count // 2, lane_count), jnp.float32)] * len(members),
        in_specs=vmem(len(operands)),
        out_specs=vmem(len(members)),
        scratch_shapes=[
            pltpu.VMEM((pairs, lane_count, lane_count), jnp.bfloat16),
            pltpu.VMEM((pairs, len(groups), pno_count, groups[0][1].shape[2]), jnp.bfloat16),
            pltpu.VMEM((pairs, pno_count, lane_count), jnp.float32),
        ],
        compiler_params=pltpu.CompilerParams(vmem_limit_bytes=12 * 2**20),
        cost_estimate=pl.CostEstimate(flops=6 * products, bytes_accessed=2**20, transcendentals=0),
    )(*operands)


def gather_pieces(mine, axis):
    count = lax.axis_size(axis)
    up, down = [mine], []
    for shift in range(1, count):
        if shift <= count // 2:
            up.append(from_behind(up[-1], axis, 1))
        else:
            down.append(from_behind(down[-1] if down else mine, axis, count - 1))
    return up + down[::-1]


def on_device_shared(pno_basis, amplitudes, send_list, couple, couple_weight, fit_weight, fit_blocks):
    pair_count, pno_count, _ = pno_basis.shape
    group_total = lax.axis_size("blk")
    pieces = gather_pieces(fit_blocks, "dom")
    across = from_partner(pno_basis, "blk", 2)
    far = [([from_behind(fit_blocks, "blk", by)], by) for by in range(SET, group_total, SET)]
    pair_amps = amplitudes.reshape(pair_count, pno_count, pno_count)
    sent = pack_pairs(send_list.reshape(-1), pno_basis, pair_amps)
    sent, pieces[1], *heads = lax.optimization_barrier((sent, pieces[1], *[group[0] for group, _ in far]))
    far = [([head], by) for head, (_, by) in zip(heads, far)]
    coupled = lax.all_to_all(sent, "blk", split_axis=0, concat_axis=0, tiled=True)
    bases = [pno_basis, from_partner(pno_basis, "blk", 1), across, from_partner(across, "blk", 1)]
    own, updated = dress(couple, couple_weight, fit_weight, pno_basis, pair_amps, coupled)
    last = len(pieces) // 2
    _, pieces[last] = lax.optimization_barrier((own, pieces[last]))
    dressed = [own, *[from_partner(own, "blk", flip) for flip in range(1, SET)]]
    groups = [pieces, *[[group[0], *[from_behind(x, "blk", by) for x in pieces[1:]]] for group, by in far]]
    inner = [project(bases, group) for group in groups]
    for members in ((3, 2), (1, 0)):
        partial = update(members, inner, [dressed[member] for member in members])
        if members[-1]:
            partial, inner = lax.optimization_barrier((partial, inner))
        for member, x in zip(members, partial):
            updated = updated + (from_partner(x, "blk", member) if member else x)
    return updated.reshape(pair_count, pno_count * pno_count)


def dress_with(pair_amps, intersection, partner_amps, weights):
    half_product = jnp.einsum("pcab,pcbe->pcae", intersection, partner_amps, precision=HIGHEST)
    sandwich = jnp.einsum("pcae,pcfe->pcaf", half_product, intersection, precision=HIGHEST)
    return pair_amps + jnp.einsum("pc,pcaf->paf", weights, sandwich, precision=HIGHEST)


def fit_term(pair_basis, dressed, blocks, weights):
    pair_count, pno_count, orbital_count = pair_basis.shape
    flat_basis = pair_basis.reshape(pair_count * pno_count, orbital_count)
    stacked = blocks.reshape(2 * orbital_count, orbital_count)
    projected = jnp.dot(
        flat_basis, stacked.T, precision=HIGHEST, preferred_element_type=jnp.float32
    )
    projected = projected.reshape(pair_count, pno_count, 2, orbital_count)
    inner_blocks = jnp.einsum("par,pbmr->mpab", pair_basis, projected, precision=HIGHEST)
    left_product = jnp.einsum("pai,pij->paj", inner_blocks[0], dressed, precision=HIGHEST)
    fit_contrib = jnp.einsum("paj,pbj->pab", left_product, inner_blocks[1], precision=HIGHEST)
    return weights[:, None, None] * fit_contrib


def on_device_ring(pno_basis, amplitudes, send_list, couple, couple_weight, fit_weight, fit_blocks):
    pair_count, pno_count, _ = pno_basis.shape
    block_count = fit_blocks.shape[0]
    pair_amps = amplitudes.reshape(pair_count, pno_count, pno_count)
    send_order = send_list.reshape(-1)
    basis_in = lax.all_to_all(jnp.take(pno_basis, send_order, axis=0), "blk", split_axis=0, concat_axis=0, tiled=True)
    amps_in = lax.all_to_all(jnp.take(pair_amps, send_order, axis=0), "blk", split_axis=0, concat_axis=0, tiled=True)
    partner_basis = jnp.take(basis_in, couple, axis=0)
    intersection = jnp.einsum("par,pcbr->pcab", pno_basis, partner_basis, precision=HIGHEST)
    dressed = dress_with(pair_amps, intersection, jnp.take(amps_in, couple, axis=0), couple_weight)
    updated = dressed
    current = lax.all_gather(fit_blocks, "dom", axis=2, tiled=True)
    for stop in range(fit_weight.shape[1] // block_count):
        if stop > 0:
            current = from_behind(current, "blk", 1)
        for b in range(block_count):
            updated = updated + fit_term(pno_basis, dressed, current[b], fit_weight[:, stop * block_count + b])
    return updated.reshape(pair_count, pno_count * pno_count)


def solution(mesh):
    placed = (
        P(("blk", "dom"), None, None),
        P(("blk", "dom"), None),
        P("blk", "dom", None, None),
        P(("blk", "dom"), None),
        P(("blk", "dom"), None),
        P(("blk", "dom"), None),
        P("blk", None, "dom", None),
    )

    def on_device(*args):
        send_list, fit_weight, fit_blocks = args[2], args[5], args[6]
        group_total = mesh.shape["blk"]
        meets_all = fit_weight.shape[1] == group_total * fit_blocks.shape[0]
        if meets_all and group_total % SET == 0 and group_total & (group_total - 1) == 0 and send_list.shape[3] == 1:
            return on_device_shared(*args)
        return on_device_ring(*args)

    return jax.shard_map(
        on_device, mesh=mesh, in_specs=placed, out_specs=P(("blk", "dom"), None), check_vma=False
    )
```

```python
import jax
import jax.numpy as jnp
from jax import lax
from jax.experimental import pallas as pl
from jax.experimental.pallas import tpu as pltpu
from jax.sharding import PartitionSpec as P

HIGHEST = lax.Precision.HIGHEST
SET = 4
NN = (((1,), (0,)), ((), ()))
NT = (((1,), (1,)), ((), ()))


def halves(x):
    high = x.astype(jnp.bfloat16)
    return high, (x - high.astype(jnp.float32)).astype(jnp.bfloat16)


def dot(a, b, dims):
    return lax.dot_general(a, b, dims, preferred_element_type=jnp.float32)


def dot3(a, b, dims):
    (a_high, a_low), (b_high, b_low) = a, b
    return dot(a_high, b_high, dims) + (dot(a_high, b_low, dims) + dot(a_low, b_high, dims))


def stack(parts, axis=0):
    return jnp.concatenate(parts, axis=axis)


def from_partner(x, axis, flip):
    return lax.ppermute(x, axis, [(i, i ^ flip) for i in range(lax.axis_size(axis))])


def from_behind(x, axis, by):
    count = lax.axis_size(axis)
    return lax.ppermute(x, axis, [(i, (i + by) % count) for i in range(count)])


def vmem(count):
    return [pl.BlockSpec(memory_space=pltpu.VMEM)] * count


def pack_kernel(send, basis, amps, out):
    pno_count = amps.shape[1]
    lanes = basis.shape[2] // pno_count
    step = pno_count // lanes
    for peer in range(out.shape[0]):
        pair = send[peer]
        out[peer, :pno_count] = basis[pair]
        listed = amps[pair]
        out[peer, pno_count:] = stack([listed[i * step:(i + 1) * step] for i in range(lanes)], 1)


def pack_pairs(send_order, basis, amps):
    _, pno_count, orbital_count = basis.shape
    rows = pno_count + pno_count * pno_count // orbital_count
    return pl.pallas_call(
        pack_kernel,
        out_shape=jax.ShapeDtypeStruct((send_order.shape[0], rows, orbital_count), jnp.float32),
        in_specs=[pl.BlockSpec(memory_space=pltpu.SMEM), *vmem(2)],
        out_specs=vmem(1)[0],
        compiler_params=pltpu.CompilerParams(vmem_limit_bytes=4 * 2**20),
        cost_estimate=pl.CostEstimate(flops=0, bytes_accessed=4 * basis.size, transcendentals=0),
    )(send_order, basis, amps)


def dress_kernel(couple, couple_weight, fit_weight, basis, amps, coupled, dressed, result, turned):
    pair_count, pno_count, orbital_count = basis.shape
    half = pno_count // 2
    slot_count = coupled.shape[0]
    own = halves(basis[...].reshape(pair_count * pno_count, orbital_count))
    others = halves(coupled[:, :pno_count].reshape(slot_count * pno_count, orbital_count))
    overlap = halves(dot3(own, others, NT))
    left, slot_weight = [], []
    for slot in range(slot_count):
        cols = slice(slot * pno_count, (slot + 1) * pno_count)
        packed = coupled[slot, pno_count:]
        partner = stack([packed[:, i:i + pno_count] for i in range(0, orbital_count, pno_count)])
        left.append(dot3([x[:, cols] for x in overlap], halves(partner), NN))
        named = jnp.where(couple[...] == slot, couple_weight[...], 0.0)
        slot_weight.append(jnp.sum(named, axis=1, keepdims=True))
    dressed[:, half:, :] = jnp.zeros((pair_count, dressed.shape[1] - half, 2 * pno_count), jnp.float32)
    for pair in range(pair_count):
        rows = slice(pair * pno_count, (pair + 1) * pno_count)
        scaled = stack([x[rows] * w[pair:pair + 1] for x, w in zip(left, slot_weight)], 1)
        total = amps[pair] + dot3(halves(scaled), [x[rows] for x in overlap], NT)
        dressed[pair, :half] = stack([total[:half], total[half:]], 1)
        turned[pair] = total
        result[pair] = two_to_one(turned, pair, half)
        dressed[pair, half:half + 1, : fit_weight.shape[1]] = fit_weight[pair:pair + 1, :]


def two_to_one(ref, pair, half):
    return stack([ref[pair, pl.ds(i, half, stride=2), :] for i in range(2)], 1)


def dress(couple, couple_weight, fit_weight, basis, amps, coupled):
    pair_count, pno_count, _ = basis.shape
    return pl.pallas_call(
        dress_kernel,
        out_shape=tuple(
            jax.ShapeDtypeStruct((pair_count, pno_count // 2 + more, 2 * pno_count), jnp.float32) for more in (8, 0)
        ),
        in_specs=vmem(6),
        out_specs=tuple(vmem(2)),
        scratch_shapes=[pltpu.VMEM((pair_count, pno_count, pno_count), jnp.float32)],
        compiler_params=pltpu.CompilerParams(vmem_limit_bytes=10 * 2**20),
        cost_estimate=pl.CostEstimate(flops=4 * 10**9, bytes_accessed=8 * basis.size, transcendentals=0),
    )(couple, couple_weight, fit_weight, basis, amps, coupled)


def fold(x):
    return x + pltpu.roll(x, x.shape[1] // 2, 1)


def left_lanes(x):
    return lax.broadcasted_iota(jnp.int32, x.shape, 1) < x.shape[1] // 2


def split(x):
    high = x.astype(jnp.bfloat16)
    wide = high.astype(jnp.float32)
    return high, wide, x - wide


def high_low(x):
    _, high, low = split(x)
    return jnp.where(left_lanes(x), high, low).astype(jnp.bfloat16)


def project_kernel(member_count, *refs):
    bases, refs = refs[:member_count], refs[member_count:]
    *pieces, inner_left, inner_right, block_cat, wide, projected = refs
    pair_count, pno_count, orbital_count = bases[0].shape
    block_count, part_count, row_count, _ = pieces[0].shape
    dom_count = len(pieces)
    place = lax.axis_index("dom")
    for shift, piece in enumerate(pieces):
        start = lax.rem(place + dom_count - shift, dom_count) * row_count
        for b in range(block_count):
            for m in range(part_count):
                high, low = halves(piece[b, m])
                for i, x in enumerate((high, high, low)):
                    at = pl.multiple_of(start + i * orbital_count, row_count)
                    block_cat[m, b, pl.ds(at, row_count), :] = x
    size = block_count * pno_count
    for member in range(member_count):
        slot = member % 2
        high, low = halves(bases[member][...])
        for i, x in enumerate((high, low, high)):
            wide[slot, :, :, i * orbital_count:(i + 1) * orbital_count] = x
        basis = wide[slot].reshape(pair_count * pno_count, 3 * orbital_count)
        for m in range(part_count):
            for b in range(block_count):
                product = halves(dot(basis, block_cat[m, b], NN).reshape(pair_count, pno_count, orbital_count))
                at = (m * block_count + b) * pno_count
                for i in range(2):
                    projected[slot, :, at:at + pno_count, i * orbital_count:(i + 1) * orbital_count] = product[i]
        for pair in range(pair_count):
            here = member * pair_count + pair
            both = stack([wide[slot, pair, :, i * orbital_count:(i + 1) * orbital_count] for i in range(2)])
            product = [projected[slot, pair, :, i * orbital_count:(i + 1) * orbital_count] for i in range(2)]
            inner = fold(dot(product[0], both, NT) + dot(product[1], both, NT))
            inner_left[here] = high_low(inner[:size])
            high, _, low = split(inner[size:])
            low = jnp.where(left_lanes(low), low, 0.0).astype(jnp.bfloat16)
            for b in range(block_count):
                rows = slice(b * pno_count, (b + 1) * pno_count)
                lanes = slice(b * 2 * pno_count, (b + 1) * 2 * pno_count)
                inner_right[here, :pno_count, lanes] = high[rows]
                inner_right[here, pno_count:, lanes] = low[rows]


def project(bases, pieces):
    pair_count, pno_count, _ = bases[0].shape
    block_count, part_count, _, orbital_count = pieces[0].shape
    pairs = len(bases) * pair_count
    products = block_count * part_count * pairs * pno_count * orbital_count * (orbital_count + pno_count)
    return pl.pallas_call(
        lambda *refs: project_kernel(len(bases), *refs),
        out_shape=(
            jax.ShapeDtypeStruct((pairs, block_count * pno_count, 2 * pno_count), jnp.bfloat16),
            jax.ShapeDtypeStruct((pairs, 2 * pno_count, block_count * 2 * pno_count), jnp.bfloat16),
        ),
        in_specs=vmem(len(bases) + len(pieces)),
        out_specs=tuple(vmem(2)),
        scratch_shapes=[
            pltpu.VMEM((part_count, block_count, 3 * orbital_count, orbital_count), jnp.bfloat16),
            pltpu.VMEM((2, pair_count, pno_count, 3 * orbital_count), jnp.bfloat16),
            pltpu.VMEM((2, pair_count, part_count * block_count * pno_count, 2 * orbital_count), jnp.bfloat16),
        ],
        compiler_params=pltpu.CompilerParams(vmem_limit_bytes=20 * 2**20),
        cost_estimate=pl.CostEstimate(flops=6 * products, bytes_accessed=2**20, transcendentals=0),
    )(*bases, *pieces)


def update_kernel(members, group_count, *refs):
    groups, refs = refs[:2 * group_count], refs[2 * group_count:]
    dressed, after, (square, moved, total) = refs[:len(members)], refs[len(members):2 * len(members)], refs[2 * len(members):]
    pair_count, _, lane_count = dressed[0].shape
    pno_count = lane_count // 2
    half = pno_count // 2
    block_count = groups[0].shape[1] // pno_count
    group_total = lax.axis_size("blk")
    me = lax.axis_index("blk")
    pairs = [(index, pair) for index in range(len(members)) for pair in range(pair_count)]

    def row_of(group, at):
        full = groups[2 * group].shape[0] > len(pairs)
        return members[at // pair_count] * pair_count + at % pair_count if full else at

    weights = []
    for index, member in enumerate(members):
        row = dressed[index][:, half:half + 1, :]
        lane = lax.broadcasted_iota(jnp.int32, row.shape, 2)
        for group in range(group_count):
            stop = lax.rem((me ^ member) + 2 * group_total + group * SET - me, group_total)
            for b in range(block_count):
                kept = jnp.where(lane == stop * block_count + b, row, 0.0)
                weights.append(jnp.sum(kept, axis=2, keepdims=True))
    for at, (index, pair) in enumerate(pairs):
        packed = dressed[index][pair, :half]
        other = pltpu.roll(packed, pno_count, 1)
        keep = left_lanes(packed)
        _, high, low = split(stack([jnp.where(keep, packed, other), jnp.where(keep, other, packed)]))
        square[at, :pno_count] = jnp.where(left_lanes(low), high, low).astype(jnp.bfloat16)
        square[at, pno_count:] = jnp.where(left_lanes(low), high, 0.0).astype(jnp.bfloat16)
    for at, (index, pair) in enumerate(pairs):
        for group in range(group_count):
            product = fold(dot(groups[2 * group][row_of(group, at)], square[at], NN))
            for b in range(block_count):
                weight = weights[(index * group_count + group) * block_count + b][pair]
                lanes = slice(b * lane_count, (b + 1) * lane_count)
                moved[at, group, :, lanes] = high_low(product[b * pno_count:(b + 1) * pno_count] * weight)
    for at, (index, pair) in enumerate(pairs):
        terms = [dot(moved[at, group], groups[2 * group + 1][row_of(group, at)], NT) for group in range(group_count)]
        total[at] = fold(sum(terms[1:], terms[0]))
    for at, (index, pair) in enumerate(pairs):
        rows = [total[at, pl.ds(i, half, stride=2), :] for i in range(2)]
        after[index][pair] = jnp.where(left_lanes(rows[0]), *rows)


def update(members, groups, dressed):
    pair_count, _, lane_count = dressed[0].shape
    pno_count = lane_count // 2
    pairs = len(members) * pair_count
    operands = [x for group in groups for x in group] + dressed
    products = pairs * pno_count**3 * 2 * len(groups) * (groups[0][0].shape[1] // pno_count)
    return pl.pallas_call(
        lambda *refs: update_kernel(members, len(groups), *refs),
        out_shape=[jax.ShapeDtypeStruct((pair_count, pno_count // 2, lane_count), jnp.float32)] * len(members),
        in_specs=vmem(len(operands)),
        out_specs=vmem(len(members)),
        scratch_shapes=[
            pltpu.VMEM((pairs, lane_count, lane_count), jnp.bfloat16),
            pltpu.VMEM((pairs, len(groups), pno_count, groups[0][1].shape[2]), jnp.bfloat16),
            pltpu.VMEM((pairs, pno_count, lane_count), jnp.float32),
        ],
        compiler_params=pltpu.CompilerParams(vmem_limit_bytes=12 * 2**20),
        cost_estimate=pl.CostEstimate(flops=6 * products, bytes_accessed=2**20, transcendentals=0),
    )(*operands)


def gather_pieces(mine, axis):
    count = lax.axis_size(axis)
    up, down = [mine], []
    for shift in range(1, count):
        if shift <= count // 2:
            up.append(from_behind(up[-1], axis, 1))
        else:
            down.append(from_behind(down[-1] if down else mine, axis, count - 1))
    return up + down[::-1]


def on_device_shared(pno_basis, amplitudes, send_list, couple, couple_weight, fit_weight, fit_blocks):
    pair_count, pno_count, _ = pno_basis.shape
    group_total = lax.axis_size("blk")
    pieces = gather_pieces(fit_blocks, "dom")
    across = from_partner(pno_basis, "blk", 2)
    far = [([from_behind(fit_blocks, "blk", by)], by) for by in range(SET, group_total, SET)]
    pair_amps = amplitudes.reshape(pair_count, pno_count, pno_count)
    sent = pack_pairs(send_list.reshape(-1), pno_basis, pair_amps)
    sent, pieces[1], *heads = lax.optimization_barrier((sent, pieces[1], *[group[0] for group, _ in far]))
    far = [([head], by) for head, (_, by) in zip(heads, far)]
    coupled = lax.all_to_all(sent, "blk", split_axis=0, concat_axis=0, tiled=True)
    bases = [pno_basis, from_partner(pno_basis, "blk", 1), across, from_partner(across, "blk", 1)]
    coupled, *bases = lax.optimization_barrier((coupled, *bases))
    own, updated = dress(couple, couple_weight, fit_weight, pno_basis, pair_amps, coupled)
    last = len(pieces) // 2
    _, pieces[last] = lax.optimization_barrier((own, pieces[last]))
    dressed = [own, *[from_partner(own, "blk", flip) for flip in range(1, SET)]]
    groups = [pieces]
    for group, by in far:
        for shift in range(1, len(pieces)):
            near = shift == last and last > 1
            group.append(from_behind(group[-1], "dom", 1) if near else from_behind(pieces[shift], "blk", by))
        groups.append(group)
    nearest = project(bases, groups[0])
    for members in ((1, 2, 3), (0,)):
        inner = [nearest, *[project([bases[member] for member in members], group) for group in groups[1:]]]
        partial = update(members, inner, [dressed[member] for member in members])
        if members[0]:
            partial, *rest = lax.optimization_barrier((partial, *[x for group in groups[1:] for x in group]))
            size = len(pieces)
            groups[1:] = [rest[i:i + size] for i in range(0, len(rest), size)]
        for member, x in zip(members, partial):
            updated = updated + (from_partner(x, "blk", member) if member else x)
    return updated.reshape(pair_count, pno_count * pno_count)


def dress_with(pair_amps, intersection, partner_amps, weights):
    half_product = jnp.einsum("pcab,pcbe->pcae", intersection, partner_amps, precision=HIGHEST)
    sandwich = jnp.einsum("pcae,pcfe->pcaf", half_product, intersection, precision=HIGHEST)
    return pair_amps + jnp.einsum("pc,pcaf->paf", weights, sandwich, precision=HIGHEST)


def fit_term(pair_basis, dressed, blocks, weights):
    pair_count, pno_count, orbital_count = pair_basis.shape
    flat_basis = pair_basis.reshape(pair_count * pno_count, orbital_count)
    stacked = blocks.reshape(2 * orbital_count, orbital_count)
    projected = jnp.dot(
        flat_basis, stacked.T, precision=HIGHEST, preferred_element_type=jnp.float32
    )
    projected = projected.reshape(pair_count, pno_count, 2, orbital_count)
    inner_blocks = jnp.einsum("par,pbmr->mpab", pair_basis, projected, precision=HIGHEST)
    left_product = jnp.einsum("pai,pij->paj", inner_blocks[0], dressed, precision=HIGHEST)
    fit_contrib = jnp.einsum("paj,pbj->pab", left_product, inner_blocks[1], precision=HIGHEST)
    return weights[:, None, None] * fit_contrib


def on_device_ring(pno_basis, amplitudes, send_list, couple, couple_weight, fit_weight, fit_blocks):
    pair_count, pno_count, _ = pno_basis.shape
    block_count = fit_blocks.shape[0]
    pair_amps = amplitudes.reshape(pair_count, pno_count, pno_count)
    send_order = send_list.reshape(-1)
    basis_in = lax.all_to_all(jnp.take(pno_basis, send_order, axis=0), "blk", split_axis=0, concat_axis=0, tiled=True)
    amps_in = lax.all_to_all(jnp.take(pair_amps, send_order, axis=0), "blk", split_axis=0, concat_axis=0, tiled=True)
    partner_basis = jnp.take(basis_in, couple, axis=0)
    intersection = jnp.einsum("par,pcbr->pcab", pno_basis, partner_basis, precision=HIGHEST)
    dressed = dress_with(pair_amps, intersection, jnp.take(amps_in, couple, axis=0), couple_weight)
    updated = dressed
    current = lax.all_gather(fit_blocks, "dom", axis=2, tiled=True)
    for stop in range(fit_weight.shape[1] // block_count):
        if stop > 0:
            current = from_behind(current, "blk", 1)
        for b in range(block_count):
            updated = updated + fit_term(pno_basis, dressed, current[b], fit_weight[:, stop * block_count + b])
    return updated.reshape(pair_count, pno_count * pno_count)


def solution(mesh):
    placed = (
        P(("blk", "dom"), None, None),
        P(("blk", "dom"), None),
        P("blk", "dom", None, None),
        P(("blk", "dom"), None),
        P(("blk", "dom"), None),
        P(("blk", "dom"), None),
        P("blk", None, "dom", None),
    )

    def on_device(*args):
        send_list, fit_weight, fit_blocks = args[2], args[5], args[6]
        group_total = mesh.shape["blk"]
        meets_all = fit_weight.shape[1] == group_total * fit_blocks.shape[0]
        if meets_all and group_total % SET == 0 and group_total & (group_total - 1) == 0 and send_list.shape[3] == 1:
            return on_device_shared(*args)
        return on_device_ring(*args)

    return jax.shard_map(
        on_device, mesh=mesh, in_specs=placed, out_specs=P(("blk", "dom"), None), check_vma=False
    )
```

```python
import jax
import jax.numpy as jnp
from jax import lax
from jax.experimental import pallas as pl
from jax.experimental.pallas import tpu as pltpu
from jax.sharding import PartitionSpec as P

HIGHEST = lax.Precision.HIGHEST
SET = 4
NN = (((1,), (0,)), ((), ()))
NT = (((1,), (1,)), ((), ()))


def halves(x):
    high = x.astype(jnp.bfloat16)
    return high, (x - high.astype(jnp.float32)).astype(jnp.bfloat16)


def dot(a, b, dims):
    return lax.dot_general(a, b, dims, preferred_element_type=jnp.float32)


def dot3(a, b, dims):
    (a_high, a_low), (b_high, b_low) = a, b
    return dot(a_high, b_high, dims) + (dot(a_high, b_low, dims) + dot(a_low, b_high, dims))


def stack(parts, axis=0):
    return jnp.concatenate(parts, axis=axis)


def from_partner(x, axis, flip):
    return lax.ppermute(x, axis, [(i, i ^ flip) for i in range(lax.axis_size(axis))])


def from_behind(x, axis, by):
    count = lax.axis_size(axis)
    return lax.ppermute(x, axis, [(i, (i + by) % count) for i in range(count)])


def vmem(count):
    return [pl.BlockSpec(memory_space=pltpu.VMEM)] * count


def pack_kernel(send, basis, amps, out):
    pno_count = amps.shape[1]
    lanes = basis.shape[2] // pno_count
    step = pno_count // lanes
    for peer in range(out.shape[0]):
        pair = send[peer]
        out[peer, :pno_count] = basis[pair]
        listed = amps[pair]
        out[peer, pno_count:] = stack([listed[i * step:(i + 1) * step] for i in range(lanes)], 1)


def pack_pairs(send_order, basis, amps):
    _, pno_count, orbital_count = basis.shape
    rows = pno_count + pno_count * pno_count // orbital_count
    return pl.pallas_call(
        pack_kernel,
        out_shape=jax.ShapeDtypeStruct((send_order.shape[0], rows, orbital_count), jnp.float32),
        in_specs=[pl.BlockSpec(memory_space=pltpu.SMEM), *vmem(2)],
        out_specs=vmem(1)[0],
        compiler_params=pltpu.CompilerParams(vmem_limit_bytes=4 * 2**20),
        cost_estimate=pl.CostEstimate(flops=0, bytes_accessed=4 * basis.size, transcendentals=0),
    )(send_order, basis, amps)


def dress_kernel(couple, couple_weight, fit_weight, basis, amps, coupled, dressed, result, turned):
    pair_count, pno_count, orbital_count = basis.shape
    half = pno_count // 2
    slot_count = coupled.shape[0]
    own = halves(basis[...].reshape(pair_count * pno_count, orbital_count))
    others = halves(coupled[:, :pno_count].reshape(slot_count * pno_count, orbital_count))
    overlap = halves(dot3(own, others, NT))
    left, slot_weight = [], []
    for slot in range(slot_count):
        cols = slice(slot * pno_count, (slot + 1) * pno_count)
        packed = coupled[slot, pno_count:]
        partner = stack([packed[:, i:i + pno_count] for i in range(0, orbital_count, pno_count)])
        left.append(dot3([x[:, cols] for x in overlap], halves(partner), NN))
        named = jnp.where(couple[...] == slot, couple_weight[...], 0.0)
        slot_weight.append(jnp.sum(named, axis=1, keepdims=True))
    dressed[:, half:, :] = jnp.zeros((pair_count, dressed.shape[1] - half, 2 * pno_count), jnp.float32)
    for pair in range(pair_count):
        rows = slice(pair * pno_count, (pair + 1) * pno_count)
        scaled = stack([x[rows] * w[pair:pair + 1] for x, w in zip(left, slot_weight)], 1)
        total = amps[pair] + dot3(halves(scaled), [x[rows] for x in overlap], NT)
        dressed[pair, :half] = stack([total[:half], total[half:]], 1)
        turned[pair] = total
        result[pair] = two_to_one(turned, pair, half)
        dressed[pair, half:half + 1, : fit_weight.shape[1]] = fit_weight[pair:pair + 1, :]


def two_to_one(ref, pair, half):
    return stack([ref[pair, pl.ds(i, half, stride=2), :] for i in range(2)], 1)


def dress(couple, couple_weight, fit_weight, basis, amps, coupled):
    pair_count, pno_count, _ = basis.shape
    return pl.pallas_call(
        dress_kernel,
        out_shape=tuple(
            jax.ShapeDtypeStruct((pair_count, pno_count // 2 + more, 2 * pno_count), jnp.float32) for more in (8, 0)
        ),
        in_specs=vmem(6),
        out_specs=tuple(vmem(2)),
        scratch_shapes=[pltpu.VMEM((pair_count, pno_count, pno_count), jnp.float32)],
        compiler_params=pltpu.CompilerParams(vmem_limit_bytes=10 * 2**20),
        cost_estimate=pl.CostEstimate(flops=4 * 10**9, bytes_accessed=8 * basis.size, transcendentals=0),
    )(couple, couple_weight, fit_weight, basis, amps, coupled)


def fold(x):
    return x + pltpu.roll(x, x.shape[1] // 2, 1)


def left_lanes(x):
    return lax.broadcasted_iota(jnp.int32, x.shape, 1) < x.shape[1] // 2


def split(x):
    high = x.astype(jnp.bfloat16)
    wide = high.astype(jnp.float32)
    return high, wide, x - wide


def high_low(x):
    _, high, low = split(x)
    return jnp.where(left_lanes(x), high, low).astype(jnp.bfloat16)


def fetch_blocks(pieces, landed, arrived):
    copies = [pltpu.make_async_copy(x, landed.at[i], arrived.at[i]) for i, x in enumerate(pieces)]
    for copy in copies:
        copy.start()
    return copies


def split_blocks(copies, landed, block_cat):
    dom_count, block_count, part_count, row_count, orbital_count = landed.shape
    place = lax.axis_index("dom")
    for shift, copy in enumerate(copies):
        copy.wait()
        start = lax.rem(place + dom_count - shift, dom_count) * row_count
        for b in range(block_count):
            for m in range(part_count):
                high, low = halves(landed[shift, b, m])
                for i, x in enumerate((high, high, low)):
                    at = pl.multiple_of(start + i * orbital_count, row_count)
                    block_cat[m, b, pl.ds(at, row_count), :] = x


def split_basis(basis, wide):
    orbital_count = basis.shape[2]
    high, low = halves(basis[...])
    for i, x in enumerate((high, low, high)):
        wide[:, :, i * orbital_count:(i + 1) * orbital_count] = x


def project_member(wide, block_cat, projected, inner_left, inner_right, first_pair):
    pair_count, pno_count, _ = wide.shape
    part_count, block_count, _, orbital_count = block_cat.shape
    size = block_count * pno_count
    basis = wide[...].reshape(pair_count * pno_count, 3 * orbital_count)
    for m in range(part_count):
        for b in range(block_count):
            product = halves(dot(basis, block_cat[m, b], NN).reshape(pair_count, pno_count, orbital_count))
            at = (m * block_count + b) * pno_count
            for i in range(2):
                projected[:, at:at + pno_count, i * orbital_count:(i + 1) * orbital_count] = product[i]
    for pair in range(pair_count):
        here = first_pair + pair
        both = stack([wide[pair, :, i * orbital_count:(i + 1) * orbital_count] for i in range(2)])
        product = [projected[pair, :, i * orbital_count:(i + 1) * orbital_count] for i in range(2)]
        inner = fold(dot(product[0], both, NT) + dot(product[1], both, NT))
        inner_left[here] = high_low(inner[:size])
        high, _, low = split(inner[size:])
        low = jnp.where(left_lanes(low), low, 0.0).astype(jnp.bfloat16)
        for b in range(block_count):
            rows = slice(b * pno_count, (b + 1) * pno_count)
            lanes = slice(b * 2 * pno_count, (b + 1) * 2 * pno_count)
            inner_right[here, :pno_count, lanes] = high[rows]
            inner_right[here, pno_count:, lanes] = low[rows]


def project_all(bases, pieces, inner_left, inner_right, scratch):
    block_cat, wide, projected, landed, arrived = scratch
    pair_count = bases[0].shape[0]
    copies = fetch_blocks(pieces, landed, arrived)
    split_basis(bases[0], wide.at[0])
    split_blocks(copies, landed, block_cat)
    for member, basis in enumerate(bases):
        slot = member % 2
        if member:
            split_basis(basis, wide.at[slot])
        project_member(
            wide.at[slot], block_cat, projected.at[slot], inner_left, inner_right, member * pair_count
        )


def project_kernel(member_count, *refs):
    bases, refs = refs[:member_count], refs[member_count:]
    *pieces, inner_left, inner_right = refs[:-5]
    project_all(bases, pieces, inner_left, inner_right, refs[-5:])


def inner_shapes(pairs, pno_count, block_count):
    return (
        ((pairs, block_count * pno_count, 2 * pno_count), jnp.bfloat16),
        ((pairs, 2 * pno_count, block_count * 2 * pno_count), jnp.bfloat16),
    )


def project_scratch(bases, pieces):
    pair_count, pno_count, _ = bases[0].shape
    block_count, part_count, _, orbital_count = pieces[0].shape
    return [
        pltpu.VMEM((part_count, block_count, 3 * orbital_count, orbital_count), jnp.bfloat16),
        pltpu.VMEM((2, pair_count, pno_count, 3 * orbital_count), jnp.bfloat16),
        pltpu.VMEM((2, pair_count, part_count * block_count * pno_count, 2 * orbital_count), jnp.bfloat16),
        pltpu.VMEM((len(pieces), *pieces[0].shape), jnp.float32),
        pltpu.SemaphoreType.DMA((len(pieces),)),
    ]


def project_flops(bases, pieces):
    pair_count, pno_count, _ = bases[0].shape
    block_count, part_count, _, orbital_count = pieces[0].shape
    rows = len(bases) * pair_count * pno_count * block_count * part_count
    return 6 * rows * orbital_count * (orbital_count + pno_count)


def project(bases, pieces):
    pair_count, pno_count, _ = bases[0].shape
    shapes = inner_shapes(len(bases) * pair_count, pno_count, pieces[0].shape[0])
    return pl.pallas_call(
        lambda *refs: project_kernel(len(bases), *refs),
        out_shape=tuple(jax.ShapeDtypeStruct(*x) for x in shapes),
        in_specs=vmem(len(bases)) + [pl.BlockSpec(memory_space=pl.ANY)] * len(pieces),
        out_specs=tuple(vmem(2)),
        scratch_shapes=project_scratch(bases, pieces),
        compiler_params=pltpu.CompilerParams(vmem_limit_bytes=20 * 2**20),
        cost_estimate=pl.CostEstimate(flops=project_flops(bases, pieces), bytes_accessed=2**20, transcendentals=0),
    )(*bases, *pieces)


def finish_kernel(members, group_count, dom_count, *refs):
    count = len(members)
    groups, refs = refs[:2 * group_count], refs[2 * group_count:]
    bases, pieces, refs = refs[:count], refs[count:count + dom_count], refs[count + dom_count:]
    dressed, after, scratch = refs[:count], refs[count:2 * count], refs[2 * count:]
    inner_left, inner_right, square, moved, total = scratch[:5]
    project_all(bases, pieces, inner_left, inner_right, scratch[5:])
    groups = [*groups, inner_left, inner_right]
    group_count += 1
    pair_count, _, lane_count = dressed[0].shape
    pno_count = lane_count // 2
    half = pno_count // 2
    block_count = inner_left.shape[1] // pno_count
    group_total = lax.axis_size("blk")
    me = lax.axis_index("blk")
    pairs = [(index, pair) for index in range(count) for pair in range(pair_count)]

    def row_of(group, at):
        full = group < group_count - 1
        return members[at // pair_count] * pair_count + at % pair_count if full else at

    weights = []
    for index, member in enumerate(members):
        row = dressed[index][:, half:half + 1, :]
        lane = lax.broadcasted_iota(jnp.int32, row.shape, 2)
        for group in range(group_count):
            stop = lax.rem((me ^ member) + 2 * group_total + group * SET - me, group_total)
            for b in range(block_count):
                kept = jnp.where(lane == stop * block_count + b, row, 0.0)
                weights.append(jnp.sum(kept, axis=2, keepdims=True))
    for at, (index, pair) in enumerate(pairs):
        packed = dressed[index][pair, :half]
        other = pltpu.roll(packed, pno_count, 1)
        keep = left_lanes(packed)
        _, high, low = split(stack([jnp.where(keep, packed, other), jnp.where(keep, other, packed)]))
        square[at, :pno_count] = jnp.where(left_lanes(low), high, low).astype(jnp.bfloat16)
        square[at, pno_count:] = jnp.where(left_lanes(low), high, 0.0).astype(jnp.bfloat16)
    for at, (index, pair) in enumerate(pairs):
        for group in range(group_count):
            product = fold(dot(groups[2 * group][row_of(group, at)], square[at], NN))
            for b in range(block_count):
                weight = weights[(index * group_count + group) * block_count + b][pair]
                lanes = slice(b * lane_count, (b + 1) * lane_count)
                moved[at, group, :, lanes] = high_low(product[b * pno_count:(b + 1) * pno_count] * weight)
    for at, (index, pair) in enumerate(pairs):
        terms = [dot(moved[at, group], groups[2 * group + 1][row_of(group, at)], NT) for group in range(group_count)]
        total[at] = fold(sum(terms[1:], terms[0]))
    for at, (index, pair) in enumerate(pairs):
        rows = [total[at, pl.ds(i, half, stride=2), :] for i in range(2)]
        after[index][pair] = jnp.where(left_lanes(rows[0]), *rows)


def finish(members, groups, bases, pieces, dressed):
    pair_count, _, lane_count = dressed[0].shape
    pno_count = lane_count // 2
    pairs = len(members) * pair_count
    group_count = len(groups)
    block_count = pieces[0].shape[0]
    operands = [x for group in groups for x in group] + bases + pieces + dressed
    products = pairs * pno_count**3 * 2 * (group_count + 1) * block_count
    shapes = inner_shapes(pairs, pno_count, block_count)
    return pl.pallas_call(
        lambda *refs: finish_kernel(members, group_count, len(pieces), *refs),
        out_shape=[jax.ShapeDtypeStruct((pair_count, pno_count // 2, lane_count), jnp.float32)] * len(members),
        in_specs=[
            *vmem(2 * group_count + len(bases)),
            *[pl.BlockSpec(memory_space=pl.ANY)] * len(pieces),
            *vmem(len(dressed)),
        ],
        out_specs=vmem(len(members)),
        scratch_shapes=[
            *[pltpu.VMEM(*x) for x in shapes],
            pltpu.VMEM((pairs, lane_count, lane_count), jnp.bfloat16),
            pltpu.VMEM((pairs, group_count + 1, pno_count, block_count * lane_count), jnp.bfloat16),
            pltpu.VMEM((pairs, pno_count, lane_count), jnp.float32),
            *project_scratch(bases, pieces),
        ],
        compiler_params=pltpu.CompilerParams(vmem_limit_bytes=24 * 2**20),
        cost_estimate=pl.CostEstimate(
            flops=project_flops(bases, pieces) + 6 * products, bytes_accessed=2**20, transcendentals=0
        ),
    )(*operands)


def gather_pieces(mine, axis):
    count = lax.axis_size(axis)
    up, down = [mine], []
    for shift in range(1, count):
        if shift <= count // 2:
            up.append(from_behind(up[-1], axis, 1))
        else:
            down.append(from_behind(down[-1] if down else mine, axis, count - 1))
    return up + down[::-1]


def on_device_shared(pno_basis, amplitudes, send_list, couple, couple_weight, fit_weight, fit_blocks):
    pair_count, pno_count, _ = pno_basis.shape
    group_total = lax.axis_size("blk")
    pieces = gather_pieces(fit_blocks, "dom")
    across = from_partner(pno_basis, "blk", 2)
    far = [([from_behind(fit_blocks, "blk", by)], by) for by in range(SET, group_total, SET)]
    pair_amps = amplitudes.reshape(pair_count, pno_count, pno_count)
    sent = pack_pairs(send_list.reshape(-1), pno_basis, pair_amps)
    sent, pieces[1], *heads = lax.optimization_barrier((sent, pieces[1], *[group[0] for group, _ in far]))
    far = [([head], by) for head, (_, by) in zip(heads, far)]
    coupled = lax.all_to_all(sent, "blk", split_axis=0, concat_axis=0, tiled=True)
    bases = [pno_basis, from_partner(pno_basis, "blk", 1), across, from_partner(across, "blk", 1)]
    coupled, *bases = lax.optimization_barrier((coupled, *bases))
    own, updated = dress(couple, couple_weight, fit_weight, pno_basis, pair_amps, coupled)
    last = len(pieces) // 2
    _, pieces[last] = lax.optimization_barrier((own, pieces[last]))
    groups = [pieces, *[[group[0], *[from_behind(x, "blk", by) for x in pieces[1:]]] for group, by in far]]
    inner = [project(bases, group) for group in groups[:-1]]
    final = groups[-1]
    near, inner = lax.optimization_barrier((own, inner))
    dressed = [own, *[from_partner(near if flip == 1 else own, "blk", flip) for flip in range(1, SET)]]
    for members in ((1, 2, 3), (0,)):
        partial = finish(
            members, inner, [bases[member] for member in members], final, [dressed[member] for member in members]
        )
        if members[0]:
            partial, *final = lax.optimization_barrier((partial, *final))
        for member, x in zip(members, partial):
            updated = updated + (from_partner(x, "blk", member) if member else x)
    return updated.reshape(pair_count, pno_count * pno_count)


def dress_with(pair_amps, intersection, partner_amps, weights):
    half_product = jnp.einsum("pcab,pcbe->pcae", intersection, partner_amps, precision=HIGHEST)
    sandwich = jnp.einsum("pcae,pcfe->pcaf", half_product, intersection, precision=HIGHEST)
    return pair_amps + jnp.einsum("pc,pcaf->paf", weights, sandwich, precision=HIGHEST)


def fit_term(pair_basis, dressed, blocks, weights):
    pair_count, pno_count, orbital_count = pair_basis.shape
    flat_basis = pair_basis.reshape(pair_count * pno_count, orbital_count)
    stacked = blocks.reshape(2 * orbital_count, orbital_count)
    projected = jnp.dot(
        flat_basis, stacked.T, precision=HIGHEST, preferred_element_type=jnp.float32
    )
    projected = projected.reshape(pair_count, pno_count, 2, orbital_count)
    inner_blocks = jnp.einsum("par,pbmr->mpab", pair_basis, projected, precision=HIGHEST)
    left_product = jnp.einsum("pai,pij->paj", inner_blocks[0], dressed, precision=HIGHEST)
    fit_contrib = jnp.einsum("paj,pbj->pab", left_product, inner_blocks[1], precision=HIGHEST)
    return weights[:, None, None] * fit_contrib


def on_device_ring(pno_basis, amplitudes, send_list, couple, couple_weight, fit_weight, fit_blocks):
    pair_count, pno_count, _ = pno_basis.shape
    block_count = fit_blocks.shape[0]
    pair_amps = amplitudes.reshape(pair_count, pno_count, pno_count)
    send_order = send_list.reshape(-1)
    basis_in = lax.all_to_all(jnp.take(pno_basis, send_order, axis=0), "blk", split_axis=0, concat_axis=0, tiled=True)
    amps_in = lax.all_to_all(jnp.take(pair_amps, send_order, axis=0), "blk", split_axis=0, concat_axis=0, tiled=True)
    partner_basis = jnp.take(basis_in, couple, axis=0)
    intersection = jnp.einsum("par,pcbr->pcab", pno_basis, partner_basis, precision=HIGHEST)
    dressed = dress_with(pair_amps, intersection, jnp.take(amps_in, couple, axis=0), couple_weight)
    updated = dressed
    current = lax.all_gather(fit_blocks, "dom", axis=2, tiled=True)
    for stop in range(fit_weight.shape[1] // block_count):
        if stop > 0:
            current = from_behind(current, "blk", 1)
        for b in range(block_count):
            updated = updated + fit_term(pno_basis, dressed, current[b], fit_weight[:, stop * block_count + b])
    return updated.reshape(pair_count, pno_count * pno_count)


def solution(mesh):
    placed = (
        P(("blk", "dom"), None, None),
        P(("blk", "dom"), None),
        P("blk", "dom", None, None),
        P(("blk", "dom"), None),
        P(("blk", "dom"), None),
        P(("blk", "dom"), None),
        P("blk", None, "dom", None),
    )

    def on_device(*args):
        send_list, fit_weight, fit_blocks = args[2], args[5], args[6]
        group_total = mesh.shape["blk"]
        meets_all = fit_weight.shape[1] == group_total * fit_blocks.shape[0]
        if meets_all and group_total % SET == 0 and group_total > SET and group_total & (group_total - 1) == 0 and send_list.shape[3] == 1:
            return on_device_shared(*args)
        return on_device_ring(*args)

    return jax.shard_map(
        on_device, mesh=mesh, in_specs=placed, out_specs=P(("blk", "dom"), None), check_vma=False
    )
```

```python
import jax
import jax.numpy as jnp
from jax import lax
from jax.experimental import pallas as pl
from jax.experimental.pallas import tpu as pltpu
from jax.sharding import PartitionSpec as P

HIGHEST = lax.Precision.HIGHEST
SET = 4
NN = (((1,), (0,)), ((), ()))
NT = (((1,), (1,)), ((), ()))


def halves(x):
    high = x.astype(jnp.bfloat16)
    return high, (x - high.astype(jnp.float32)).astype(jnp.bfloat16)


def dot(a, b, dims):
    return lax.dot_general(a, b, dims, preferred_element_type=jnp.float32)


def dot3(a, b, dims):
    (a_high, a_low), (b_high, b_low) = a, b
    return dot(a_high, b_high, dims) + (dot(a_high, b_low, dims) + dot(a_low, b_high, dims))


def stack(parts, axis=0):
    return jnp.concatenate(parts, axis=axis)


def from_partner(x, axis, flip):
    return lax.ppermute(x, axis, [(i, i ^ flip) for i in range(lax.axis_size(axis))])


def from_behind(x, axis, by):
    count = lax.axis_size(axis)
    return lax.ppermute(x, axis, [(i, (i + by) % count) for i in range(count)])


def vmem(count):
    return [pl.BlockSpec(memory_space=pltpu.VMEM)] * count


def pack_kernel(send, basis, amps, out):
    pno_count = amps.shape[1]
    lanes = basis.shape[2] // pno_count
    step = pno_count // lanes
    for peer in range(out.shape[0]):
        pair = send[peer]
        out[peer, :pno_count] = basis[pair]
        listed = amps[pair]
        out[peer, pno_count:] = stack([listed[i * step:(i + 1) * step] for i in range(lanes)], 1)


def pack_pairs(send_order, basis, amps):
    _, pno_count, orbital_count = basis.shape
    rows = pno_count + pno_count * pno_count // orbital_count
    return pl.pallas_call(
        pack_kernel,
        out_shape=jax.ShapeDtypeStruct((send_order.shape[0], rows, orbital_count), jnp.float32),
        in_specs=[pl.BlockSpec(memory_space=pltpu.SMEM), *vmem(2)],
        out_specs=vmem(1)[0],
        compiler_params=pltpu.CompilerParams(vmem_limit_bytes=4 * 2**20),
        cost_estimate=pl.CostEstimate(flops=0, bytes_accessed=4 * basis.size, transcendentals=0),
    )(send_order, basis, amps)


def dress_kernel(couple, couple_weight, fit_weight, basis, amps, coupled, dressed, result, turned):
    pair_count, pno_count, orbital_count = basis.shape
    half = pno_count // 2
    slot_count = coupled.shape[0]
    own = halves(basis[...].reshape(pair_count * pno_count, orbital_count))
    others = halves(coupled[:, :pno_count].reshape(slot_count * pno_count, orbital_count))
    overlap = halves(dot3(own, others, NT))
    left, slot_weight = [], []
    for slot in range(slot_count):
        cols = slice(slot * pno_count, (slot + 1) * pno_count)
        packed = coupled[slot, pno_count:]
        partner = stack([packed[:, i:i + pno_count] for i in range(0, orbital_count, pno_count)])
        left.append(dot3([x[:, cols] for x in overlap], halves(partner), NN))
        named = jnp.where(couple[...] == slot, couple_weight[...], 0.0)
        slot_weight.append(jnp.sum(named, axis=1, keepdims=True))
    dressed[:, half:, :] = jnp.zeros((pair_count, dressed.shape[1] - half, 2 * pno_count), jnp.float32)
    for pair in range(pair_count):
        rows = slice(pair * pno_count, (pair + 1) * pno_count)
        scaled = stack([x[rows] * w[pair:pair + 1] for x, w in zip(left, slot_weight)], 1)
        total = amps[pair] + dot3(halves(scaled), [x[rows] for x in overlap], NT)
        dressed[pair, :half] = stack([total[:half], total[half:]], 1)
        turned[pair] = total
        result[pair] = two_to_one(turned, pair, half)
        dressed[pair, half:half + 1, : fit_weight.shape[1]] = fit_weight[pair:pair + 1, :]


def two_to_one(ref, pair, half):
    return stack([ref[pair, pl.ds(i, half, stride=2), :] for i in range(2)], 1)


def dress(couple, couple_weight, fit_weight, basis, amps, coupled):
    pair_count, pno_count, _ = basis.shape
    return pl.pallas_call(
        dress_kernel,
        out_shape=tuple(
            jax.ShapeDtypeStruct((pair_count, pno_count // 2 + more, 2 * pno_count), jnp.float32) for more in (8, 0)
        ),
        in_specs=vmem(6),
        out_specs=tuple(vmem(2)),
        scratch_shapes=[pltpu.VMEM((pair_count, pno_count, pno_count), jnp.float32)],
        compiler_params=pltpu.CompilerParams(vmem_limit_bytes=10 * 2**20),
        cost_estimate=pl.CostEstimate(flops=4 * 10**9, bytes_accessed=8 * basis.size, transcendentals=0),
    )(couple, couple_weight, fit_weight, basis, amps, coupled)


def fold(x):
    return x + pltpu.roll(x, x.shape[1] // 2, 1)


def left_lanes(x):
    return lax.broadcasted_iota(jnp.int32, x.shape, 1) < x.shape[1] // 2


def split(x):
    high = x.astype(jnp.bfloat16)
    wide = high.astype(jnp.float32)
    return high, wide, x - wide


def high_low(x):
    _, high, low = split(x)
    return jnp.where(left_lanes(x), high, low).astype(jnp.bfloat16)


def split_blocks(pieces, block_cat):
    dom_count = len(pieces)
    block_count, part_count, row_count, orbital_count = pieces[0].shape
    place = lax.axis_index("dom")
    for shift, piece in enumerate(pieces):
        start = lax.rem(place + dom_count - shift, dom_count) * row_count
        for b in range(block_count):
            for m in range(part_count):
                high, low = halves(piece[b, m])
                for i, x in enumerate((high, high, low)):
                    at = pl.multiple_of(start + i * orbital_count, row_count)
                    block_cat[m, b, pl.ds(at, row_count), :] = x


def split_basis(basis, wide):
    orbital_count = basis.shape[2]
    high, low = halves(basis[...])
    for i, x in enumerate((high, low, high)):
        wide[:, :, i * orbital_count:(i + 1) * orbital_count] = x


def project_member(wide, block_cat, projected, inner_left, inner_right, first_pair):
    pair_count, pno_count, _ = wide.shape
    part_count, block_count, _, orbital_count = block_cat.shape
    size = block_count * pno_count
    basis = wide[...].reshape(pair_count * pno_count, 3 * orbital_count)
    for m in range(part_count):
        for b in range(block_count):
            product = halves(dot(basis, block_cat[m, b], NN).reshape(pair_count, pno_count, orbital_count))
            at = (m * block_count + b) * pno_count
            for i in range(2):
                projected[:, at:at + pno_count, i * orbital_count:(i + 1) * orbital_count] = product[i]
    for pair in range(pair_count):
        here = first_pair + pair
        both = stack([wide[pair, :, i * orbital_count:(i + 1) * orbital_count] for i in range(2)])
        product = [projected[pair, :, i * orbital_count:(i + 1) * orbital_count] for i in range(2)]
        inner = fold(dot(product[0], both, NT) + dot(product[1], both, NT))
        inner_left[here] = high_low(inner[:size])
        high, _, low = split(inner[size:])
        low = jnp.where(left_lanes(low), low, 0.0).astype(jnp.bfloat16)
        for b in range(block_count):
            rows = slice(b * pno_count, (b + 1) * pno_count)
            lanes = slice(b * 2 * pno_count, (b + 1) * 2 * pno_count)
            inner_right[here, :pno_count, lanes] = high[rows]
            inner_right[here, pno_count:, lanes] = low[rows]


def project_all(bases, pieces, inner_left, inner_right, scratch):
    block_cat, wide, projected = scratch
    pair_count = bases[0].shape[0]
    split_blocks(pieces, block_cat)
    for member, basis in enumerate(bases):
        slot = member % 2
        split_basis(basis, wide.at[slot])
        project_member(
            wide.at[slot], block_cat, projected.at[slot], inner_left, inner_right, member * pair_count
        )


def project_kernel(member_count, *refs):
    bases, refs = refs[:member_count], refs[member_count:]
    *pieces, inner_left, inner_right = refs[:-3]
    project_all(bases, pieces, inner_left, inner_right, refs[-3:])


def inner_shapes(pairs, pno_count, block_count):
    return (
        ((pairs, block_count * pno_count, 2 * pno_count), jnp.bfloat16),
        ((pairs, 2 * pno_count, block_count * 2 * pno_count), jnp.bfloat16),
    )


def project_scratch(bases, pieces):
    pair_count, pno_count, _ = bases[0].shape
    block_count, part_count, _, orbital_count = pieces[0].shape
    return [
        pltpu.VMEM((part_count, block_count, 3 * orbital_count, orbital_count), jnp.bfloat16),
        pltpu.VMEM((2, pair_count, pno_count, 3 * orbital_count), jnp.bfloat16),
        pltpu.VMEM((2, pair_count, part_count * block_count * pno_count, 2 * orbital_count), jnp.bfloat16),
    ]


def project_flops(bases, pieces):
    pair_count, pno_count, _ = bases[0].shape
    block_count, part_count, _, orbital_count = pieces[0].shape
    rows = len(bases) * pair_count * pno_count * block_count * part_count
    return 6 * rows * orbital_count * (orbital_count + pno_count)


def project(bases, pieces):
    pair_count, pno_count, _ = bases[0].shape
    shapes = inner_shapes(len(bases) * pair_count, pno_count, pieces[0].shape[0])
    return pl.pallas_call(
        lambda *refs: project_kernel(len(bases), *refs),
        out_shape=tuple(jax.ShapeDtypeStruct(*x) for x in shapes),
        in_specs=vmem(len(bases) + len(pieces)),
        out_specs=tuple(vmem(2)),
        scratch_shapes=project_scratch(bases, pieces),
        compiler_params=pltpu.CompilerParams(vmem_limit_bytes=20 * 2**20),
        cost_estimate=pl.CostEstimate(flops=project_flops(bases, pieces), bytes_accessed=2**20, transcendentals=0),
    )(*bases, *pieces)


def finish_kernel(members, group_count, dom_count, *refs):
    count = len(members)
    groups, refs = refs[:2 * group_count], refs[2 * group_count:]
    bases, pieces, refs = refs[:count], refs[count:count + dom_count], refs[count + dom_count:]
    dressed, after, scratch = refs[:count], refs[count:2 * count], refs[2 * count:]
    inner_left, inner_right, square, moved, total = scratch[:5]
    project_all(bases, pieces, inner_left, inner_right, scratch[5:])
    groups = [*groups, inner_left, inner_right]
    group_count += 1
    pair_count, _, lane_count = dressed[0].shape
    pno_count = lane_count // 2
    half = pno_count // 2
    block_count = inner_left.shape[1] // pno_count
    group_total = lax.axis_size("blk")
    me = lax.axis_index("blk")
    pairs = [(index, pair) for index in range(count) for pair in range(pair_count)]

    def row_of(group, at):
        full = group < group_count - 1
        return members[at // pair_count] * pair_count + at % pair_count if full else at

    weights = []
    for index, member in enumerate(members):
        row = dressed[index][:, half:half + 1, :]
        lane = lax.broadcasted_iota(jnp.int32, row.shape, 2)
        for group in range(group_count):
            stop = lax.rem((me ^ member) + 2 * group_total + group * SET - me, group_total)
            for b in range(block_count):
                kept = jnp.where(lane == stop * block_count + b, row, 0.0)
                weights.append(jnp.sum(kept, axis=2, keepdims=True))
    for at, (index, pair) in enumerate(pairs):
        packed = dressed[index][pair, :half]
        other = pltpu.roll(packed, pno_count, 1)
        keep = left_lanes(packed)
        _, high, low = split(stack([jnp.where(keep, packed, other), jnp.where(keep, other, packed)]))
        square[at, :pno_count] = jnp.where(left_lanes(low), high, low).astype(jnp.bfloat16)
        square[at, pno_count:] = jnp.where(left_lanes(low), high, 0.0).astype(jnp.bfloat16)
    for at, (index, pair) in enumerate(pairs):
        for group in range(group_count):
            product = fold(dot(groups[2 * group][row_of(group, at)], square[at], NN))
            for b in range(block_count):
                weight = weights[(index * group_count + group) * block_count + b][pair]
                lanes = slice(b * lane_count, (b + 1) * lane_count)
                moved[at, group, :, lanes] = high_low(product[b * pno_count:(b + 1) * pno_count] * weight)
    for at, (index, pair) in enumerate(pairs):
        terms = [dot(moved[at, group], groups[2 * group + 1][row_of(group, at)], NT) for group in range(group_count)]
        total[at] = fold(sum(terms[1:], terms[0]))
    for at, (index, pair) in enumerate(pairs):
        rows = [total[at, pl.ds(i, half, stride=2), :] for i in range(2)]
        after[index][pair] = jnp.where(left_lanes(rows[0]), *rows)


def finish(members, groups, bases, pieces, dressed):
    pair_count, _, lane_count = dressed[0].shape
    pno_count = lane_count // 2
    pairs = len(members) * pair_count
    group_count = len(groups)
    block_count = pieces[0].shape[0]
    operands = [x for group in groups for x in group] + bases + pieces + dressed
    products = pairs * pno_count**3 * 2 * (group_count + 1) * block_count
    shapes = inner_shapes(pairs, pno_count, block_count)
    return pl.pallas_call(
        lambda *refs: finish_kernel(members, group_count, len(pieces), *refs),
        out_shape=[jax.ShapeDtypeStruct((pair_count, pno_count // 2, lane_count), jnp.float32)] * len(members),
        in_specs=vmem(len(operands)),
        out_specs=vmem(len(members)),
        scratch_shapes=[
            *[pltpu.VMEM(*x) for x in shapes],
            pltpu.VMEM((pairs, lane_count, lane_count), jnp.bfloat16),
            pltpu.VMEM((pairs, group_count + 1, pno_count, block_count * lane_count), jnp.bfloat16),
            pltpu.VMEM((pairs, pno_count, lane_count), jnp.float32),
            *project_scratch(bases, pieces),
        ],
        compiler_params=pltpu.CompilerParams(vmem_limit_bytes=24 * 2**20),
        cost_estimate=pl.CostEstimate(
            flops=project_flops(bases, pieces) + 6 * products, bytes_accessed=2**20, transcendentals=0
        ),
    )(*operands)


def gather_pieces(mine, axis):
    count = lax.axis_size(axis)
    up, down = [mine], []
    for shift in range(1, count):
        if shift <= count // 2:
            up.append(from_behind(up[-1], axis, 1))
        else:
            down.append(from_behind(down[-1] if down else mine, axis, count - 1))
    return up + down[::-1]


def on_device_shared(pno_basis, amplitudes, send_list, couple, couple_weight, fit_weight, fit_blocks):
    pair_count, pno_count, _ = pno_basis.shape
    group_total = lax.axis_size("blk")
    pieces = gather_pieces(fit_blocks, "dom")
    across = from_partner(pno_basis, "blk", 2)
    far = [([from_behind(fit_blocks, "blk", by)], by) for by in range(SET, group_total, SET)]
    pair_amps = amplitudes.reshape(pair_count, pno_count, pno_count)
    sent = pack_pairs(send_list.reshape(-1), pno_basis, pair_amps)
    sent, pieces[1], *heads = lax.optimization_barrier((sent, pieces[1], *[group[0] for group, _ in far]))
    far = [([head], by) for head, (_, by) in zip(heads, far)]
    coupled = lax.all_to_all(sent, "blk", split_axis=0, concat_axis=0, tiled=True)
    bases = [pno_basis, from_partner(pno_basis, "blk", 1), across, from_partner(across, "blk", 1)]
    coupled, *bases = lax.optimization_barrier((coupled, *bases))
    own, updated = dress(couple, couple_weight, fit_weight, pno_basis, pair_amps, coupled)
    last = len(pieces) // 2
    _, pieces[last] = lax.optimization_barrier((own, pieces[last]))
    groups = [pieces, *[[group[0], *[from_behind(x, "blk", by) for x in pieces[1:]]] for group, by in far]]
    inner = [project(bases, group) for group in groups[:-1]]
    final = groups[-1]
    dressed = [own, *[from_partner(own, "blk", flip) for flip in range(1, SET)]]
    for members in ((2, 3), (0, 1)):
        partial = finish(
            members, inner, [bases[member] for member in members], final, [dressed[member] for member in members]
        )
        if members[0]:
            partial, *final = lax.optimization_barrier((partial, *final))
            for member, x in zip(members, partial):
                updated = updated + from_partner(x, "blk", member)
        else:
            mine, beside = partial
            updated, mine, beside = lax.optimization_barrier((updated, mine, from_partner(beside, "blk", 1)))
            updated = updated + mine + beside
    return updated.reshape(pair_count, pno_count * pno_count)


def dress_with(pair_amps, intersection, partner_amps, weights):
    half_product = jnp.einsum("pcab,pcbe->pcae", intersection, partner_amps, precision=HIGHEST)
    sandwich = jnp.einsum("pcae,pcfe->pcaf", half_product, intersection, precision=HIGHEST)
    return pair_amps + jnp.einsum("pc,pcaf->paf", weights, sandwich, precision=HIGHEST)


def fit_term(pair_basis, dressed, blocks, weights):
    pair_count, pno_count, orbital_count = pair_basis.shape
    flat_basis = pair_basis.reshape(pair_count * pno_count, orbital_count)
    stacked = blocks.reshape(2 * orbital_count, orbital_count)
    projected = jnp.dot(
        flat_basis, stacked.T, precision=HIGHEST, preferred_element_type=jnp.float32
    )
    projected = projected.reshape(pair_count, pno_count, 2, orbital_count)
    inner_blocks = jnp.einsum("par,pbmr->mpab", pair_basis, projected, precision=HIGHEST)
    left_product = jnp.einsum("pai,pij->paj", inner_blocks[0], dressed, precision=HIGHEST)
    fit_contrib = jnp.einsum("paj,pbj->pab", left_product, inner_blocks[1], precision=HIGHEST)
    return weights[:, None, None] * fit_contrib


def on_device_ring(pno_basis, amplitudes, send_list, couple, couple_weight, fit_weight, fit_blocks):
    pair_count, pno_count, _ = pno_basis.shape
    block_count = fit_blocks.shape[0]
    pair_amps = amplitudes.reshape(pair_count, pno_count, pno_count)
    send_order = send_list.reshape(-1)
    basis_in = lax.all_to_all(jnp.take(pno_basis, send_order, axis=0), "blk", split_axis=0, concat_axis=0, tiled=True)
    amps_in = lax.all_to_all(jnp.take(pair_amps, send_order, axis=0), "blk", split_axis=0, concat_axis=0, tiled=True)
    partner_basis = jnp.take(basis_in, couple, axis=0)
    intersection = jnp.einsum("par,pcbr->pcab", pno_basis, partner_basis, precision=HIGHEST)
    dressed = dress_with(pair_amps, intersection, jnp.take(amps_in, couple, axis=0), couple_weight)
    updated = dressed
    current = lax.all_gather(fit_blocks, "dom", axis=2, tiled=True)
    for stop in range(fit_weight.shape[1] // block_count):
        if stop > 0:
            current = from_behind(current, "blk", 1)
        for b in range(block_count):
            updated = updated + fit_term(pno_basis, dressed, current[b], fit_weight[:, stop * block_count + b])
    return updated.reshape(pair_count, pno_count * pno_count)


def solution(mesh):
    placed = (
        P(("blk", "dom"), None, None),
        P(("blk", "dom"), None),
        P("blk", "dom", None, None),
        P(("blk", "dom"), None),
        P(("blk", "dom"), None),
        P(("blk", "dom"), None),
        P("blk", None, "dom", None),
    )

    def on_device(*args):
        send_list, fit_weight, fit_blocks = args[2], args[5], args[6]
        group_total = mesh.shape["blk"]
        meets_all = fit_weight.shape[1] == group_total * fit_blocks.shape[0]
        if meets_all and group_total % SET == 0 and group_total > SET and group_total & (group_total - 1) == 0 and send_list.shape[3] == 1:
            return on_device_shared(*args)
        return on_device_ring(*args)

    return jax.shard_map(
        on_device, mesh=mesh, in_specs=placed, out_specs=P(("blk", "dom"), None), check_vma=False
    )
```

```python
import jax
import jax.numpy as jnp
from jax import lax
from jax.experimental import pallas as pl
from jax.experimental.pallas import tpu as pltpu
from jax.sharding import PartitionSpec as P

HIGHEST = lax.Precision.HIGHEST
SET = 4
NN = (((1,), (0,)), ((), ()))
NT = (((1,), (1,)), ((), ()))


def halves(x):
    high = x.astype(jnp.bfloat16)
    return high, (x - high.astype(jnp.float32)).astype(jnp.bfloat16)


def dot(a, b, dims):
    return lax.dot_general(a, b, dims, preferred_element_type=jnp.float32)


def dot3(a, b, dims):
    (a_high, a_low), (b_high, b_low) = a, b
    return dot(a_high, b_high, dims) + (dot(a_high, b_low, dims) + dot(a_low, b_high, dims))


def stack(parts, axis=0):
    return jnp.concatenate(parts, axis=axis)


def from_partner(x, axis, flip):
    return lax.ppermute(x, axis, [(i, i ^ flip) for i in range(lax.axis_size(axis))])


def from_behind(x, axis, by):
    count = lax.axis_size(axis)
    return lax.ppermute(x, axis, [(i, (i + by) % count) for i in range(count)])


def vmem(count):
    return [pl.BlockSpec(memory_space=pltpu.VMEM)] * count


def pack_kernel(send, basis, amps, out):
    pno_count = amps.shape[1]
    lanes = basis.shape[2] // pno_count
    step = pno_count // lanes
    for peer in range(out.shape[0]):
        pair = send[peer]
        out[peer, :pno_count] = basis[pair]
        listed = amps[pair]
        out[peer, pno_count:] = stack([listed[i * step:(i + 1) * step] for i in range(lanes)], 1)


def pack_pairs(send_order, basis, amps):
    _, pno_count, orbital_count = basis.shape
    rows = pno_count + pno_count * pno_count // orbital_count
    return pl.pallas_call(
        pack_kernel,
        out_shape=jax.ShapeDtypeStruct((send_order.shape[0], rows, orbital_count), jnp.float32),
        in_specs=[pl.BlockSpec(memory_space=pltpu.SMEM), *vmem(2)],
        out_specs=vmem(1)[0],
        compiler_params=pltpu.CompilerParams(vmem_limit_bytes=4 * 2**20),
        cost_estimate=pl.CostEstimate(flops=0, bytes_accessed=4 * basis.size, transcendentals=0),
    )(send_order, basis, amps)


def dress_kernel(couple, couple_weight, fit_weight, basis, amps, coupled, dressed, result, turned):
    pair_count, pno_count, orbital_count = basis.shape
    half = pno_count // 2
    slot_count = coupled.shape[0]
    own = halves(basis[...].reshape(pair_count * pno_count, orbital_count))
    others = halves(coupled[:, :pno_count].reshape(slot_count * pno_count, orbital_count))
    overlap = halves(dot3(own, others, NT))
    left, slot_weight = [], []
    for slot in range(slot_count):
        cols = slice(slot * pno_count, (slot + 1) * pno_count)
        packed = coupled[slot, pno_count:]
        partner = stack([packed[:, i:i + pno_count] for i in range(0, orbital_count, pno_count)])
        left.append(dot3([x[:, cols] for x in overlap], halves(partner), NN))
        named = jnp.where(couple[...] == slot, couple_weight[...], 0.0)
        slot_weight.append(jnp.sum(named, axis=1, keepdims=True))
    dressed[:, half:, :] = jnp.zeros((pair_count, dressed.shape[1] - half, 2 * pno_count), jnp.float32)
    for pair in range(pair_count):
        rows = slice(pair * pno_count, (pair + 1) * pno_count)
        scaled = stack([x[rows] * w[pair:pair + 1] for x, w in zip(left, slot_weight)], 1)
        total = amps[pair] + dot3(halves(scaled), [x[rows] for x in overlap], NT)
        dressed[pair, :half] = stack([total[:half], total[half:]], 1)
        turned[pair] = total
        result[pair] = two_to_one(turned, pair, half)
        dressed[pair, half:half + 1, : fit_weight.shape[1]] = fit_weight[pair:pair + 1, :]


def two_to_one(ref, pair, half):
    return stack([ref[pair, pl.ds(i, half, stride=2), :] for i in range(2)], 1)


def dress(couple, couple_weight, fit_weight, basis, amps, coupled):
    pair_count, pno_count, _ = basis.shape
    return pl.pallas_call(
        dress_kernel,
        out_shape=tuple(
            jax.ShapeDtypeStruct((pair_count, pno_count // 2 + more, 2 * pno_count), jnp.float32) for more in (8, 0)
        ),
        in_specs=vmem(6),
        out_specs=tuple(vmem(2)),
        scratch_shapes=[pltpu.VMEM((pair_count, pno_count, pno_count), jnp.float32)],
        compiler_params=pltpu.CompilerParams(vmem_limit_bytes=10 * 2**20),
        cost_estimate=pl.CostEstimate(flops=4 * 10**9, bytes_accessed=8 * basis.size, transcendentals=0),
    )(couple, couple_weight, fit_weight, basis, amps, coupled)


def fold(x):
    return x + pltpu.roll(x, x.shape[1] // 2, 1)


def left_lanes(x):
    return lax.broadcasted_iota(jnp.int32, x.shape, 1) < x.shape[1] // 2


def split(x):
    high = x.astype(jnp.bfloat16)
    wide = high.astype(jnp.float32)
    return high, wide, x - wide


def high_low(x):
    _, high, low = split(x)
    return jnp.where(left_lanes(x), high, low).astype(jnp.bfloat16)


def split_blocks(pieces, block_cat):
    dom_count = len(pieces)
    block_count, part_count, row_count, orbital_count = pieces[0].shape
    place = lax.axis_index("dom")
    for shift, piece in enumerate(pieces):
        start = lax.rem(place + dom_count - shift, dom_count) * row_count
        for b in range(block_count):
            for m in range(part_count):
                high, low = halves(piece[b, m])
                for i, x in enumerate((high, high, low)):
                    at = pl.multiple_of(start + i * orbital_count, row_count)
                    block_cat[m, b, pl.ds(at, row_count), :] = x


def split_basis(basis, wide):
    orbital_count = basis.shape[2]
    high, low = halves(basis[...])
    for i, x in enumerate((high, low, high)):
        wide[:, :, i * orbital_count:(i + 1) * orbital_count] = x


def project_member(wide, block_cat, projected, inner_left, inner_right, first_pair):
    pair_count, pno_count, _ = wide.shape
    part_count, block_count, _, orbital_count = block_cat.shape
    size = block_count * pno_count
    basis = wide[...].reshape(pair_count * pno_count, 3 * orbital_count)
    for m in range(part_count):
        for b in range(block_count):
            product = halves(dot(basis, block_cat[m, b], NN).reshape(pair_count, pno_count, orbital_count))
            at = (m * block_count + b) * pno_count
            for i in range(2):
                projected[:, at:at + pno_count, i * orbital_count:(i + 1) * orbital_count] = product[i]
    for pair in range(pair_count):
        here = first_pair + pair
        both = stack([wide[pair, :, i * orbital_count:(i + 1) * orbital_count] for i in range(2)])
        product = [projected[pair, :, i * orbital_count:(i + 1) * orbital_count] for i in range(2)]
        inner = fold(dot(product[0], both, NT) + dot(product[1], both, NT))
        inner_left[here] = high_low(inner[:size])
        high, _, low = split(inner[size:])
        low = jnp.where(left_lanes(low), low, 0.0).astype(jnp.bfloat16)
        for b in range(block_count):
            rows = slice(b * pno_count, (b + 1) * pno_count)
            lanes = slice(b * 2 * pno_count, (b + 1) * 2 * pno_count)
            inner_right[here, :pno_count, lanes] = high[rows]
            inner_right[here, pno_count:, lanes] = low[rows]


def project_all(bases, pieces, inner_left, inner_right, scratch):
    block_cat, wide, projected = scratch
    pair_count = bases[0].shape[0]
    split_blocks(pieces, block_cat)
    for member, basis in enumerate(bases):
        slot = member % 2
        split_basis(basis, wide.at[slot])
        project_member(
            wide.at[slot], block_cat, projected.at[slot], inner_left, inner_right, member * pair_count
        )


def project_kernel(member_count, *refs):
    bases, refs = refs[:member_count], refs[member_count:]
    *pieces, inner_left, inner_right = refs[:-3]
    project_all(bases, pieces, inner_left, inner_right, refs[-3:])


def inner_shapes(pairs, pno_count, block_count):
    return (
        ((pairs, block_count * pno_count, 2 * pno_count), jnp.bfloat16),
        ((pairs, 2 * pno_count, block_count * 2 * pno_count), jnp.bfloat16),
    )


def project_scratch(bases, pieces):
    pair_count, pno_count, _ = bases[0].shape
    block_count, part_count, _, orbital_count = pieces[0].shape
    return [
        pltpu.VMEM((part_count, block_count, 3 * orbital_count, orbital_count), jnp.bfloat16),
        pltpu.VMEM((2, pair_count, pno_count, 3 * orbital_count), jnp.bfloat16),
        pltpu.VMEM((2, pair_count, part_count * block_count * pno_count, 2 * orbital_count), jnp.bfloat16),
    ]


def project_flops(bases, pieces):
    pair_count, pno_count, _ = bases[0].shape
    block_count, part_count, _, orbital_count = pieces[0].shape
    rows = len(bases) * pair_count * pno_count * block_count * part_count
    return 6 * rows * orbital_count * (orbital_count + pno_count)


def project(bases, pieces):
    pair_count, pno_count, _ = bases[0].shape
    shapes = inner_shapes(len(bases) * pair_count, pno_count, pieces[0].shape[0])
    return pl.pallas_call(
        lambda *refs: project_kernel(len(bases), *refs),
        out_shape=tuple(jax.ShapeDtypeStruct(*x) for x in shapes),
        in_specs=vmem(len(bases) + len(pieces)),
        out_specs=tuple(vmem(2)),
        scratch_shapes=project_scratch(bases, pieces),
        compiler_params=pltpu.CompilerParams(vmem_limit_bytes=20 * 2**20),
        cost_estimate=pl.CostEstimate(flops=project_flops(bases, pieces), bytes_accessed=2**20, transcendentals=0),
    )(*bases, *pieces)


def finish_kernel(members, group_count, dom_count, *refs):
    count = len(members)
    groups, refs = refs[:2 * group_count], refs[2 * group_count:]
    bases, pieces, refs = refs[:count], refs[count:count + dom_count], refs[count + dom_count:]
    dressed, after, scratch = refs[:count], refs[count:2 * count], refs[2 * count:]
    inner_left, inner_right, square, moved, total = scratch[:5]
    project_all(bases, pieces, inner_left, inner_right, scratch[5:])
    groups = [*groups, inner_left, inner_right]
    group_count += 1
    pair_count, _, lane_count = dressed[0].shape
    pno_count = lane_count // 2
    half = pno_count // 2
    block_count = inner_left.shape[1] // pno_count
    group_total = lax.axis_size("blk")
    me = lax.axis_index("blk")
    pairs = [(index, pair) for index in range(count) for pair in range(pair_count)]

    def row_of(group, at):
        full = group < group_count - 1
        return members[at // pair_count] * pair_count + at % pair_count if full else at

    weights = []
    for index, member in enumerate(members):
        row = dressed[index][:, half:half + 1, :]
        lane = lax.broadcasted_iota(jnp.int32, row.shape, 2)
        for group in range(group_count):
            stop = lax.rem((me ^ member) + 2 * group_total + group * SET - me, group_total)
            for b in range(block_count):
                kept = jnp.where(lane == stop * block_count + b, row, 0.0)
                weights.append(jnp.sum(kept, axis=2, keepdims=True))
    for at, (index, pair) in enumerate(pairs):
        packed = dressed[index][pair, :half]
        other = pltpu.roll(packed, pno_count, 1)
        keep = left_lanes(packed)
        _, high, low = split(stack([jnp.where(keep, packed, other), jnp.where(keep, other, packed)]))
        square[at, :pno_count] = jnp.where(left_lanes(low), high, low).astype(jnp.bfloat16)
        square[at, pno_count:] = jnp.where(left_lanes(low), high, 0.0).astype(jnp.bfloat16)
    for at, (index, pair) in enumerate(pairs):
        for group in range(group_count):
            product = fold(dot(groups[2 * group][row_of(group, at)], square[at], NN))
            for b in range(block_count):
                weight = weights[(index * group_count + group) * block_count + b][pair]
                lanes = slice(b * lane_count, (b + 1) * lane_count)
                moved[at, group, :, lanes] = high_low(product[b * pno_count:(b + 1) * pno_count] * weight)
    for at, (index, pair) in enumerate(pairs):
        terms = [dot(moved[at, group], groups[2 * group + 1][row_of(group, at)], NT) for group in range(group_count)]
        total[at] = fold(sum(terms[1:], terms[0]))
    for at, (index, pair) in enumerate(pairs):
        rows = [total[at, pl.ds(i, half, stride=2), :] for i in range(2)]
        after[index][pair] = jnp.where(left_lanes(rows[0]), *rows)


def finish(members, groups, bases, pieces, dressed):
    pair_count, _, lane_count = dressed[0].shape
    pno_count = lane_count // 2
    pairs = len(members) * pair_count
    group_count = len(groups)
    block_count = pieces[0].shape[0]
    operands = [x for group in groups for x in group] + bases + pieces + dressed
    products = pairs * pno_count**3 * 2 * (group_count + 1) * block_count
    shapes = inner_shapes(pairs, pno_count, block_count)
    return pl.pallas_call(
        lambda *refs: finish_kernel(members, group_count, len(pieces), *refs),
        out_shape=[jax.ShapeDtypeStruct((pair_count, pno_count // 2, lane_count), jnp.float32)] * len(members),
        in_specs=vmem(len(operands)),
        out_specs=vmem(len(members)),
        scratch_shapes=[
            *[pltpu.VMEM(*x) for x in shapes],
            pltpu.VMEM((pairs, lane_count, lane_count), jnp.bfloat16),
            pltpu.VMEM((pairs, group_count + 1, pno_count, block_count * lane_count), jnp.bfloat16),
            pltpu.VMEM((pairs, pno_count, lane_count), jnp.float32),
            *project_scratch(bases, pieces),
        ],
        compiler_params=pltpu.CompilerParams(vmem_limit_bytes=24 * 2**20),
        cost_estimate=pl.CostEstimate(
            flops=project_flops(bases, pieces) + 6 * products, bytes_accessed=2**20, transcendentals=0
        ),
    )(*operands)


def gather_pieces(mine, axis):
    count = lax.axis_size(axis)
    up, down = [mine], []
    for shift in range(1, count):
        if shift <= (count - 1) // 2:
            up.append(from_behind(up[-1], axis, 1))
        else:
            down.append(from_behind(down[-1] if down else mine, axis, count - 1))
    return up + down[::-1]


def on_device_shared(pno_basis, amplitudes, send_list, couple, couple_weight, fit_weight, fit_blocks):
    pair_count, pno_count, _ = pno_basis.shape
    group_total = lax.axis_size("blk")
    pieces = gather_pieces(fit_blocks, "dom")
    across = from_partner(pno_basis, "blk", 2)
    far = [([from_behind(fit_blocks, "blk", by)], by) for by in range(SET, group_total, SET)]
    pair_amps = amplitudes.reshape(pair_count, pno_count, pno_count)
    sent = pack_pairs(send_list.reshape(-1), pno_basis, pair_amps)
    sent, pieces[1], *heads = lax.optimization_barrier((sent, pieces[1], *[group[0] for group, _ in far]))
    far = [([head], by) for head, (_, by) in zip(heads, far)]
    coupled = lax.all_to_all(sent, "blk", split_axis=0, concat_axis=0, tiled=True)
    bases = [pno_basis, from_partner(pno_basis, "blk", 1), across, from_partner(across, "blk", 1)]
    coupled, *bases = lax.optimization_barrier((coupled, *bases))
    own, updated = dress(couple, couple_weight, fit_weight, pno_basis, pair_amps, coupled)
    last = len(pieces) // 2
    _, pieces[last] = lax.optimization_barrier((own, pieces[last]))
    groups = [pieces, *[[group[0], *[from_behind(x, "blk", by) for x in pieces[1:]]] for group, by in far]]
    inner = [project(bases, group) for group in groups[:-1]]
    final = groups[-1]
    dressed = [own, *[from_partner(own, "blk", flip) for flip in range(1, SET)]]
    for members in ((2, 3), (0, 1)):
        partial = finish(
            members, inner, [bases[member] for member in members], final, [dressed[member] for member in members]
        )
        if members[0]:
            partial, *final = lax.optimization_barrier((partial, *final))
            for member, x in zip(members, partial):
                updated = updated + from_partner(x, "blk", member)
        else:
            mine, beside = partial
            updated, mine, beside = lax.optimization_barrier((updated, mine, from_partner(beside, "blk", 1)))
            updated = updated + mine + beside
    return updated.reshape(pair_count, pno_count * pno_count)


def dress_with(pair_amps, intersection, partner_amps, weights):
    half_product = jnp.einsum("pcab,pcbe->pcae", intersection, partner_amps, precision=HIGHEST)
    sandwich = jnp.einsum("pcae,pcfe->pcaf", half_product, intersection, precision=HIGHEST)
    return pair_amps + jnp.einsum("pc,pcaf->paf", weights, sandwich, precision=HIGHEST)


def fit_term(pair_basis, dressed, blocks, weights):
    pair_count, pno_count, orbital_count = pair_basis.shape
    flat_basis = pair_basis.reshape(pair_count * pno_count, orbital_count)
    stacked = blocks.reshape(2 * orbital_count, orbital_count)
    projected = jnp.dot(
        flat_basis, stacked.T, precision=HIGHEST, preferred_element_type=jnp.float32
    )
    projected = projected.reshape(pair_count, pno_count, 2, orbital_count)
    inner_blocks = jnp.einsum("par,pbmr->mpab", pair_basis, projected, precision=HIGHEST)
    left_product = jnp.einsum("pai,pij->paj", inner_blocks[0], dressed, precision=HIGHEST)
    fit_contrib = jnp.einsum("paj,pbj->pab", left_product, inner_blocks[1], precision=HIGHEST)
    return weights[:, None, None] * fit_contrib


def on_device_ring(pno_basis, amplitudes, send_list, couple, couple_weight, fit_weight, fit_blocks):
    pair_count, pno_count, _ = pno_basis.shape
    block_count = fit_blocks.shape[0]
    pair_amps = amplitudes.reshape(pair_count, pno_count, pno_count)
    send_order = send_list.reshape(-1)
    basis_in = lax.all_to_all(jnp.take(pno_basis, send_order, axis=0), "blk", split_axis=0, concat_axis=0, tiled=True)
    amps_in = lax.all_to_all(jnp.take(pair_amps, send_order, axis=0), "blk", split_axis=0, concat_axis=0, tiled=True)
    partner_basis = jnp.take(basis_in, couple, axis=0)
    intersection = jnp.einsum("par,pcbr->pcab", pno_basis, partner_basis, precision=HIGHEST)
    dressed = dress_with(pair_amps, intersection, jnp.take(amps_in, couple, axis=0), couple_weight)
    updated = dressed
    current = lax.all_gather(fit_blocks, "dom", axis=2, tiled=True)
    for stop in range(fit_weight.shape[1] // block_count):
        if stop > 0:
            current = from_behind(current, "blk", 1)
        for b in range(block_count):
            updated = updated + fit_term(pno_basis, dressed, current[b], fit_weight[:, stop * block_count + b])
    return updated.reshape(pair_count, pno_count * pno_count)


def solution(mesh):
    placed = (
        P(("blk", "dom"), None, None),
        P(("blk", "dom"), None),
        P("blk", "dom", None, None),
        P(("blk", "dom"), None),
        P(("blk", "dom"), None),
        P(("blk", "dom"), None),
        P("blk", None, "dom", None),
    )

    def on_device(*args):
        send_list, fit_weight, fit_blocks = args[2], args[5], args[6]
        group_total = mesh.shape["blk"]
        meets_all = fit_weight.shape[1] == group_total * fit_blocks.shape[0]
        if meets_all and group_total % SET == 0 and group_total > SET and group_total & (group_total - 1) == 0 and send_list.shape[3] == 1:
            return on_device_shared(*args)
        return on_device_ring(*args)

    return jax.shard_map(
        on_device, mesh=mesh, in_specs=placed, out_specs=P(("blk", "dom"), None), check_vma=False
    )
```

```python
import jax
import jax.numpy as jnp
from jax import lax
from jax.experimental import pallas as pl
from jax.experimental.pallas import tpu as pltpu
from jax.sharding import PartitionSpec as P

HIGHEST = lax.Precision.HIGHEST
SET = 4
NN = (((1,), (0,)), ((), ()))
NT = (((1,), (1,)), ((), ()))


def halves(x):
    high = x.astype(jnp.bfloat16)
    return high, (x - high.astype(jnp.float32)).astype(jnp.bfloat16)


def dot(a, b, dims):
    return lax.dot_general(a, b, dims, preferred_element_type=jnp.float32)


def dot3(a, b, dims):
    (a_high, a_low), (b_high, b_low) = a, b
    return dot(a_high, b_high, dims) + (dot(a_high, b_low, dims) + dot(a_low, b_high, dims))


def stack(parts, axis=0):
    return jnp.concatenate(parts, axis=axis)


def from_partner(x, axis, flip):
    return lax.ppermute(x, axis, [(i, i ^ flip) for i in range(lax.axis_size(axis))])


def from_behind(x, axis, by):
    count = lax.axis_size(axis)
    return lax.ppermute(x, axis, [(i, (i + by) % count) for i in range(count)])


def vmem(count):
    return [pl.BlockSpec(memory_space=pltpu.VMEM)] * count


def pack_kernel(send, basis, amps, out):
    pno_count = amps.shape[1]
    lanes = basis.shape[2] // pno_count
    step = pno_count // lanes
    for peer in range(out.shape[0]):
        pair = send[peer]
        out[peer, :pno_count] = basis[pair]
        listed = amps[pair]
        out[peer, pno_count:] = stack([listed[i * step:(i + 1) * step] for i in range(lanes)], 1)


def pack_pairs(send_order, basis, amps):
    _, pno_count, orbital_count = basis.shape
    rows = pno_count + pno_count * pno_count // orbital_count
    return pl.pallas_call(
        pack_kernel,
        out_shape=jax.ShapeDtypeStruct((send_order.shape[0], rows, orbital_count), jnp.float32),
        in_specs=[pl.BlockSpec(memory_space=pltpu.SMEM), *vmem(2)],
        out_specs=vmem(1)[0],
        compiler_params=pltpu.CompilerParams(vmem_limit_bytes=4 * 2**20),
        cost_estimate=pl.CostEstimate(flops=0, bytes_accessed=4 * basis.size, transcendentals=0),
    )(send_order, basis, amps)


def dress_kernel(couple, couple_weight, fit_weight, basis, amps, coupled, dressed, result, turned):
    pair_count, pno_count, orbital_count = basis.shape
    half = pno_count // 2
    slot_count = coupled.shape[0]
    own = halves(basis[...].reshape(pair_count * pno_count, orbital_count))
    others = halves(coupled[:, :pno_count].reshape(slot_count * pno_count, orbital_count))
    overlap = halves(dot3(own, others, NT))
    left, slot_weight = [], []
    for slot in range(slot_count):
        cols = slice(slot * pno_count, (slot + 1) * pno_count)
        packed = coupled[slot, pno_count:]
        partner = stack([packed[:, i:i + pno_count] for i in range(0, orbital_count, pno_count)])
        left.append(dot3([x[:, cols] for x in overlap], halves(partner), NN))
        named = jnp.where(couple[...] == slot, couple_weight[...], 0.0)
        slot_weight.append(jnp.sum(named, axis=1, keepdims=True))
    dressed[:, half:, :] = jnp.zeros((pair_count, dressed.shape[1] - half, 2 * pno_count), jnp.float32)
    for pair in range(pair_count):
        rows = slice(pair * pno_count, (pair + 1) * pno_count)
        scaled = stack([x[rows] * w[pair:pair + 1] for x, w in zip(left, slot_weight)], 1)
        total = amps[pair] + dot3(halves(scaled), [x[rows] for x in overlap], NT)
        dressed[pair, :half] = stack([total[:half], total[half:]], 1)
        turned[pair] = total
        result[pair] = two_to_one(turned, pair, half)
        dressed[pair, half:half + 1, : fit_weight.shape[1]] = fit_weight[pair:pair + 1, :]


def two_to_one(ref, pair, half):
    return stack([ref[pair, pl.ds(i, half, stride=2), :] for i in range(2)], 1)


def dress(couple, couple_weight, fit_weight, basis, amps, coupled):
    pair_count, pno_count, _ = basis.shape
    return pl.pallas_call(
        dress_kernel,
        out_shape=tuple(
            jax.ShapeDtypeStruct((pair_count, pno_count // 2 + more, 2 * pno_count), jnp.float32) for more in (8, 0)
        ),
        in_specs=vmem(6),
        out_specs=tuple(vmem(2)),
        scratch_shapes=[pltpu.VMEM((pair_count, pno_count, pno_count), jnp.float32)],
        compiler_params=pltpu.CompilerParams(vmem_limit_bytes=10 * 2**20),
        cost_estimate=pl.CostEstimate(flops=4 * 10**9, bytes_accessed=8 * basis.size, transcendentals=0),
    )(couple, couple_weight, fit_weight, basis, amps, coupled)


def fold(x):
    return x + pltpu.roll(x, x.shape[1] // 2, 1)


def left_lanes(x):
    return lax.broadcasted_iota(jnp.int32, x.shape, 1) < x.shape[1] // 2


def split(x):
    high = x.astype(jnp.bfloat16)
    wide = high.astype(jnp.float32)
    return high, wide, x - wide


def high_low(x):
    _, high, low = split(x)
    return jnp.where(left_lanes(x), high, low).astype(jnp.bfloat16)


def split_blocks(pieces, block_cat):
    dom_count = len(pieces)
    block_count, part_count, row_count, orbital_count = pieces[0].shape
    place = lax.axis_index("dom")
    for shift, piece in enumerate(pieces):
        start = lax.rem(place + dom_count - shift, dom_count) * row_count
        for b in range(block_count):
            for m in range(part_count):
                high, low = halves(piece[b, m])
                for i, x in enumerate((high, high, low)):
                    at = pl.multiple_of(start + i * orbital_count, row_count)
                    block_cat[m, b, pl.ds(at, row_count), :] = x


def split_basis(basis, wide):
    orbital_count = basis.shape[2]
    high, low = halves(basis[...])
    for i, x in enumerate((high, low, high)):
        wide[:, :, i * orbital_count:(i + 1) * orbital_count] = x


def project_member(wide, block_cat, projected, inner_left, inner_right, first_pair):
    pair_count, pno_count, _ = wide.shape
    part_count, block_count, _, orbital_count = block_cat.shape
    size = block_count * pno_count
    basis = wide[...].reshape(pair_count * pno_count, 3 * orbital_count)
    for m in range(part_count):
        for b in range(block_count):
            product = halves(dot(basis, block_cat[m, b], NN).reshape(pair_count, pno_count, orbital_count))
            at = (m * block_count + b) * pno_count
            for i in range(2):
                projected[:, at:at + pno_count, i * orbital_count:(i + 1) * orbital_count] = product[i]
    for pair in range(pair_count):
        here = first_pair + pair
        both = stack([wide[pair, :, i * orbital_count:(i + 1) * orbital_count] for i in range(2)])
        product = [projected[pair, :, i * orbital_count:(i + 1) * orbital_count] for i in range(2)]
        inner = fold(dot(product[0], both, NT) + dot(product[1], both, NT))
        inner_left[here] = high_low(inner[:size])
        high, _, low = split(inner[size:])
        low = jnp.where(left_lanes(low), low, 0.0).astype(jnp.bfloat16)
        for b in range(block_count):
            rows = slice(b * pno_count, (b + 1) * pno_count)
            lanes = slice(b * 2 * pno_count, (b + 1) * 2 * pno_count)
            inner_right[here, :pno_count, lanes] = high[rows]
            inner_right[here, pno_count:, lanes] = low[rows]


def project_all(bases, pieces, inner_left, inner_right, scratch):
    block_cat, wide, projected = scratch
    pair_count = bases[0].shape[0]
    split_blocks(pieces, block_cat)
    for member, basis in enumerate(bases):
        slot = member % 2
        split_basis(basis, wide.at[slot])
        project_member(
            wide.at[slot], block_cat, projected.at[slot], inner_left, inner_right, member * pair_count
        )


def project_kernel(member_count, *refs):
    bases, refs = refs[:member_count], refs[member_count:]
    *pieces, inner_left, inner_right = refs[:-3]
    project_all(bases, pieces, inner_left, inner_right, refs[-3:])


def inner_shapes(pairs, pno_count, block_count):
    return (
        ((pairs, block_count * pno_count, 2 * pno_count), jnp.bfloat16),
        ((pairs, 2 * pno_count, block_count * 2 * pno_count), jnp.bfloat16),
    )


def project_scratch(bases, pieces):
    pair_count, pno_count, _ = bases[0].shape
    block_count, part_count, _, orbital_count = pieces[0].shape
    return [
        pltpu.VMEM((part_count, block_count, 3 * orbital_count, orbital_count), jnp.bfloat16),
        pltpu.VMEM((2, pair_count, pno_count, 3 * orbital_count), jnp.bfloat16),
        pltpu.VMEM((2, pair_count, part_count * block_count * pno_count, 2 * orbital_count), jnp.bfloat16),
    ]


def project_flops(bases, pieces):
    pair_count, pno_count, _ = bases[0].shape
    block_count, part_count, _, orbital_count = pieces[0].shape
    rows = len(bases) * pair_count * pno_count * block_count * part_count
    return 6 * rows * orbital_count * (orbital_count + pno_count)


def project(bases, pieces):
    pair_count, pno_count, _ = bases[0].shape
    shapes = inner_shapes(len(bases) * pair_count, pno_count, pieces[0].shape[0])
    return pl.pallas_call(
        lambda *refs: project_kernel(len(bases), *refs),
        out_shape=tuple(jax.ShapeDtypeStruct(*x) for x in shapes),
        in_specs=vmem(len(bases) + len(pieces)),
        out_specs=tuple(vmem(2)),
        scratch_shapes=project_scratch(bases, pieces),
        compiler_params=pltpu.CompilerParams(vmem_limit_bytes=20 * 2**20),
        cost_estimate=pl.CostEstimate(flops=project_flops(bases, pieces), bytes_accessed=2**20, transcendentals=0),
    )(*bases, *pieces)


def finish_kernel(members, group_count, dom_count, *refs):
    count = len(members)
    groups, refs = refs[:2 * group_count], refs[2 * group_count:]
    bases, pieces, refs = refs[:count], refs[count:count + dom_count], refs[count + dom_count:]
    dressed, after, scratch = refs[:count], refs[count:2 * count], refs[2 * count:]
    inner_left, inner_right, square, moved, total = scratch[:5]
    project_all(bases, pieces, inner_left, inner_right, scratch[5:])
    groups = [*groups, inner_left, inner_right]
    group_count += 1
    pair_count, _, lane_count = dressed[0].shape
    pno_count = lane_count // 2
    half = pno_count // 2
    block_count = inner_left.shape[1] // pno_count
    group_total = lax.axis_size("blk")
    me = lax.axis_index("blk")
    pairs = [(index, pair) for index in range(count) for pair in range(pair_count)]

    def row_of(group, at):
        full = group < group_count - 1
        return members[at // pair_count] * pair_count + at % pair_count if full else at

    weights = []
    for index, member in enumerate(members):
        row = dressed[index][:, half:half + 1, :]
        lane = lax.broadcasted_iota(jnp.int32, row.shape, 2)
        for group in range(group_count):
            stop = lax.rem((me ^ member) + 2 * group_total + group * SET - me, group_total)
            for b in range(block_count):
                kept = jnp.where(lane == stop * block_count + b, row, 0.0)
                weights.append(jnp.sum(kept, axis=2, keepdims=True))
    for at, (index, pair) in enumerate(pairs):
        packed = dressed[index][pair, :half]
        other = pltpu.roll(packed, pno_count, 1)
        keep = left_lanes(packed)
        _, high, low = split(stack([jnp.where(keep, packed, other), jnp.where(keep, other, packed)]))
        square[at, :pno_count] = jnp.where(left_lanes(low), high, low).astype(jnp.bfloat16)
        square[at, pno_count:] = jnp.where(left_lanes(low), high, 0.0).astype(jnp.bfloat16)
    for at, (index, pair) in enumerate(pairs):
        for group in range(group_count):
            product = fold(dot(groups[2 * group][row_of(group, at)], square[at], NN))
            for b in range(block_count):
                weight = weights[(index * group_count + group) * block_count + b][pair]
                lanes = slice(b * lane_count, (b + 1) * lane_count)
                moved[at, group, :, lanes] = high_low(product[b * pno_count:(b + 1) * pno_count] * weight)
    for at, (index, pair) in enumerate(pairs):
        terms = [dot(moved[at, group], groups[2 * group + 1][row_of(group, at)], NT) for group in range(group_count)]
        total[at] = fold(sum(terms[1:], terms[0]))
    for at, (index, pair) in enumerate(pairs):
        rows = [total[at, pl.ds(i, half, stride=2), :] for i in range(2)]
        after[index][pair] = jnp.where(left_lanes(rows[0]), *rows)


def finish(members, groups, bases, pieces, dressed):
    pair_count, _, lane_count = dressed[0].shape
    pno_count = lane_count // 2
    pairs = len(members) * pair_count
    group_count = len(groups)
    block_count = pieces[0].shape[0]
    operands = [x for group in groups for x in group] + bases + pieces + dressed
    products = pairs * pno_count**3 * 2 * (group_count + 1) * block_count
    shapes = inner_shapes(pairs, pno_count, block_count)
    return pl.pallas_call(
        lambda *refs: finish_kernel(members, group_count, len(pieces), *refs),
        out_shape=[jax.ShapeDtypeStruct((pair_count, pno_count // 2, lane_count), jnp.float32)] * len(members),
        in_specs=vmem(len(operands)),
        out_specs=vmem(len(members)),
        scratch_shapes=[
            *[pltpu.VMEM(*x) for x in shapes],
            pltpu.VMEM((pairs, lane_count, lane_count), jnp.bfloat16),
            pltpu.VMEM((pairs, group_count + 1, pno_count, block_count * lane_count), jnp.bfloat16),
            pltpu.VMEM((pairs, pno_count, lane_count), jnp.float32),
            *project_scratch(bases, pieces),
        ],
        compiler_params=pltpu.CompilerParams(vmem_limit_bytes=24 * 2**20),
        cost_estimate=pl.CostEstimate(
            flops=project_flops(bases, pieces) + 6 * products, bytes_accessed=2**20, transcendentals=0
        ),
    )(*operands)


def gather_pieces(mine, axis):
    count = lax.axis_size(axis)
    up, down = [mine], []
    for shift in range(1, count):
        if shift <= count // 2:
            up.append(from_behind(up[-1], axis, 1))
        else:
            down.append(from_behind(down[-1] if down else mine, axis, count - 1))
    return up + down[::-1]


def on_device_shared(pno_basis, amplitudes, send_list, couple, couple_weight, fit_weight, fit_blocks):
    pair_count, pno_count, _ = pno_basis.shape
    group_total = lax.axis_size("blk")
    pieces = gather_pieces(fit_blocks, "dom")
    across = from_partner(pno_basis, "blk", 2)
    far = [([from_behind(fit_blocks, "blk", by)], by) for by in range(SET, group_total, SET)]
    pair_amps = amplitudes.reshape(pair_count, pno_count, pno_count)
    sent = pack_pairs(send_list.reshape(-1), pno_basis, pair_amps)
    sent, pieces[1], *heads = lax.optimization_barrier((sent, pieces[1], *[group[0] for group, _ in far]))
    far = [([head], by) for head, (_, by) in zip(heads, far)]
    coupled = lax.all_to_all(sent, "blk", split_axis=0, concat_axis=0, tiled=True)
    bases = [pno_basis, from_partner(pno_basis, "blk", 1), across, from_partner(across, "blk", 1)]
    coupled, *bases = lax.optimization_barrier((coupled, *bases))
    own, updated = dress(couple, couple_weight, fit_weight, pno_basis, pair_amps, coupled)
    last = len(pieces) // 2
    _, pieces[last] = lax.optimization_barrier((own, pieces[last]))
    groups = [pieces]
    for group, by in far:
        for shift in range(1, len(pieces)):
            source = pieces[shift]
            if 1 < shift == last:
                source, pieces[last] = lax.optimization_barrier((group[-1], pieces[last]))
            group.append(from_behind(source, "dom", 1) if 1 < shift == last else from_behind(source, "blk", by))
        groups.append(group)
    inner = [project(bases, group) for group in groups[:-1]]
    final = groups[-1]
    dressed = [own, *[from_partner(own, "blk", flip) for flip in range(1, SET)]]
    for members in ((2, 3), (0, 1)):
        partial = finish(
            members, inner, [bases[member] for member in members], final, [dressed[member] for member in members]
        )
        if members[0]:
            partial, *final = lax.optimization_barrier((partial, *final))
            for member, x in zip(members, partial):
                updated = updated + from_partner(x, "blk", member)
        else:
            mine, beside = partial
            updated, mine, beside = lax.optimization_barrier((updated, mine, from_partner(beside, "blk", 1)))
            updated = updated + mine + beside
    return updated.reshape(pair_count, pno_count * pno_count)


def dress_with(pair_amps, intersection, partner_amps, weights):
    half_product = jnp.einsum("pcab,pcbe->pcae", intersection, partner_amps, precision=HIGHEST)
    sandwich = jnp.einsum("pcae,pcfe->pcaf", half_product, intersection, precision=HIGHEST)
    return pair_amps + jnp.einsum("pc,pcaf->paf", weights, sandwich, precision=HIGHEST)


def fit_term(pair_basis, dressed, blocks, weights):
    pair_count, pno_count, orbital_count = pair_basis.shape
    flat_basis = pair_basis.reshape(pair_count * pno_count, orbital_count)
    stacked = blocks.reshape(2 * orbital_count, orbital_count)
    projected = jnp.dot(
        flat_basis, stacked.T, precision=HIGHEST, preferred_element_type=jnp.float32
    )
    projected = projected.reshape(pair_count, pno_count, 2, orbital_count)
    inner_blocks = jnp.einsum("par,pbmr->mpab", pair_basis, projected, precision=HIGHEST)
    left_product = jnp.einsum("pai,pij->paj", inner_blocks[0], dressed, precision=HIGHEST)
    fit_contrib = jnp.einsum("paj,pbj->pab", left_product, inner_blocks[1], precision=HIGHEST)
    return weights[:, None, None] * fit_contrib


def on_device_ring(pno_basis, amplitudes, send_list, couple, couple_weight, fit_weight, fit_blocks):
    pair_count, pno_count, _ = pno_basis.shape
    block_count = fit_blocks.shape[0]
    pair_amps = amplitudes.reshape(pair_count, pno_count, pno_count)
    send_order = send_list.reshape(-1)
    basis_in = lax.all_to_all(jnp.take(pno_basis, send_order, axis=0), "blk", split_axis=0, concat_axis=0, tiled=True)
    amps_in = lax.all_to_all(jnp.take(pair_amps, send_order, axis=0), "blk", split_axis=0, concat_axis=0, tiled=True)
    partner_basis = jnp.take(basis_in, couple, axis=0)
    intersection = jnp.einsum("par,pcbr->pcab", pno_basis, partner_basis, precision=HIGHEST)
    dressed = dress_with(pair_amps, intersection, jnp.take(amps_in, couple, axis=0), couple_weight)
    updated = dressed
    current = lax.all_gather(fit_blocks, "dom", axis=2, tiled=True)
    for stop in range(fit_weight.shape[1] // block_count):
        if stop > 0:
            current = from_behind(current, "blk", 1)
        for b in range(block_count):
            updated = updated + fit_term(pno_basis, dressed, current[b], fit_weight[:, stop * block_count + b])
    return updated.reshape(pair_count, pno_count * pno_count)


def solution(mesh):
    placed = (
        P(("blk", "dom"), None, None),
        P(("blk", "dom"), None),
        P("blk", "dom", None, None),
        P(("blk", "dom"), None),
        P(("blk", "dom"), None),
        P(("blk", "dom"), None),
        P("blk", None, "dom", None),
    )

    def on_device(*args):
        send_list, fit_weight, fit_blocks = args[2], args[5], args[6]
        group_total = mesh.shape["blk"]
        meets_all = fit_weight.shape[1] == group_total * fit_blocks.shape[0]
        if meets_all and group_total % SET == 0 and group_total > SET and group_total & (group_total - 1) == 0 and send_list.shape[3] == 1:
            return on_device_shared(*args)
        return on_device_ring(*args)

    return jax.shard_map(
        on_device, mesh=mesh, in_specs=placed, out_specs=P(("blk", "dom"), None), check_vma=False
    )
```

```python
import jax
import jax.numpy as jnp
from jax import lax
from jax.experimental import pallas as pl
from jax.experimental.pallas import tpu as pltpu
from jax.sharding import PartitionSpec as P

HIGHEST = lax.Precision.HIGHEST
SET = 4
NN = (((1,), (0,)), ((), ()))
NT = (((1,), (1,)), ((), ()))


def halves(x):
    high = x.astype(jnp.bfloat16)
    return high, (x - high.astype(jnp.float32)).astype(jnp.bfloat16)


def dot(a, b, dims):
    return lax.dot_general(a, b, dims, preferred_element_type=jnp.float32)


def dot3(a, b, dims):
    (a_high, a_low), (b_high, b_low) = a, b
    return dot(a_high, b_high, dims) + (dot(a_high, b_low, dims) + dot(a_low, b_high, dims))


def stack(parts, axis=0):
    return jnp.concatenate(parts, axis=axis)


def from_partner(x, axis, flip):
    return lax.ppermute(x, axis, [(i, i ^ flip) for i in range(lax.axis_size(axis))])


def from_behind(x, axis, by):
    count = lax.axis_size(axis)
    return lax.ppermute(x, axis, [(i, (i + by) % count) for i in range(count)])


def vmem(count):
    return [pl.BlockSpec(memory_space=pltpu.VMEM)] * count


def pack_kernel(send, basis, amps, out):
    pno_count = amps.shape[1]
    lanes = basis.shape[2] // pno_count
    step = pno_count // lanes
    for peer in range(out.shape[0]):
        pair = send[peer]
        out[peer, :pno_count] = basis[pair]
        listed = amps[pair]
        out[peer, pno_count:] = stack([listed[i * step:(i + 1) * step] for i in range(lanes)], 1)


def pack_pairs(send_order, basis, amps):
    _, pno_count, orbital_count = basis.shape
    rows = pno_count + pno_count * pno_count // orbital_count
    return pl.pallas_call(
        pack_kernel,
        out_shape=jax.ShapeDtypeStruct((send_order.shape[0], rows, orbital_count), jnp.float32),
        in_specs=[pl.BlockSpec(memory_space=pltpu.SMEM), *vmem(2)],
        out_specs=vmem(1)[0],
        compiler_params=pltpu.CompilerParams(vmem_limit_bytes=4 * 2**20),
        cost_estimate=pl.CostEstimate(flops=0, bytes_accessed=4 * basis.size, transcendentals=0),
    )(send_order, basis, amps)


def dress_kernel(couple, couple_weight, fit_weight, basis, amps, coupled, dressed, result, turned):
    pair_count, pno_count, orbital_count = basis.shape
    half = pno_count // 2
    slot_count = coupled.shape[0]
    own = halves(basis[...].reshape(pair_count * pno_count, orbital_count))
    others = halves(coupled[:, :pno_count].reshape(slot_count * pno_count, orbital_count))
    overlap = halves(dot3(own, others, NT))
    left, slot_weight = [], []
    for slot in range(slot_count):
        cols = slice(slot * pno_count, (slot + 1) * pno_count)
        packed = coupled[slot, pno_count:]
        partner = stack([packed[:, i:i + pno_count] for i in range(0, orbital_count, pno_count)])
        left.append(dot3([x[:, cols] for x in overlap], halves(partner), NN))
        named = jnp.where(couple[...] == slot, couple_weight[...], 0.0)
        slot_weight.append(jnp.sum(named, axis=1, keepdims=True))
    dressed[:, half:, :] = jnp.zeros((pair_count, dressed.shape[1] - half, 2 * pno_count), jnp.float32)
    for pair in range(pair_count):
        rows = slice(pair * pno_count, (pair + 1) * pno_count)
        scaled = stack([x[rows] * w[pair:pair + 1] for x, w in zip(left, slot_weight)], 1)
        total = amps[pair] + dot3(halves(scaled), [x[rows] for x in overlap], NT)
        dressed[pair, :half] = stack([total[:half], total[half:]], 1)
        turned[pair] = total
        result[pair] = two_to_one(turned, pair, half)
        dressed[pair, half:half + 1, : fit_weight.shape[1]] = fit_weight[pair:pair + 1, :]


def two_to_one(ref, pair, half):
    return stack([ref[pair, pl.ds(i, half, stride=2), :] for i in range(2)], 1)


def dress(couple, couple_weight, fit_weight, basis, amps, coupled):
    pair_count, pno_count, _ = basis.shape
    return pl.pallas_call(
        dress_kernel,
        out_shape=tuple(
            jax.ShapeDtypeStruct((pair_count, pno_count // 2 + more, 2 * pno_count), jnp.float32) for more in (8, 0)
        ),
        in_specs=vmem(6),
        out_specs=tuple(vmem(2)),
        scratch_shapes=[pltpu.VMEM((pair_count, pno_count, pno_count), jnp.float32)],
        compiler_params=pltpu.CompilerParams(vmem_limit_bytes=10 * 2**20),
        cost_estimate=pl.CostEstimate(flops=4 * 10**9, bytes_accessed=8 * basis.size, transcendentals=0),
    )(couple, couple_weight, fit_weight, basis, amps, coupled)


def fold(x):
    return x + pltpu.roll(x, x.shape[1] // 2, 1)


def left_lanes(x):
    return lax.broadcasted_iota(jnp.int32, x.shape, 1) < x.shape[1] // 2


def split(x):
    high = x.astype(jnp.bfloat16)
    wide = high.astype(jnp.float32)
    return high, wide, x - wide


def high_low(x):
    _, high, low = split(x)
    return jnp.where(left_lanes(x), high, low).astype(jnp.bfloat16)


def split_blocks(pieces, block_cat):
    dom_count = len(pieces)
    block_count, part_count, row_count, orbital_count = pieces[0].shape
    place = lax.axis_index("dom")
    for shift, piece in enumerate(pieces):
        start = lax.rem(place + dom_count - shift, dom_count) * row_count
        for b in range(block_count):
            for m in range(part_count):
                high, low = halves(piece[b, m])
                for i, x in enumerate((high, high, low)):
                    at = pl.multiple_of(start + i * orbital_count, row_count)
                    block_cat[m, b, pl.ds(at, row_count), :] = x


def split_basis(basis, wide):
    orbital_count = basis.shape[2]
    high, low = halves(basis[...])
    for i, x in enumerate((high, low, high)):
        wide[:, :, i * orbital_count:(i + 1) * orbital_count] = x


def project_member(wide, block_cat, projected, inner_left, inner_right, first_pair):
    pair_count, pno_count, _ = wide.shape
    part_count, block_count, _, orbital_count = block_cat.shape
    size = block_count * pno_count
    basis = wide[...].reshape(pair_count * pno_count, 3 * orbital_count)
    for m in range(part_count):
        for b in range(block_count):
            product = halves(dot(basis, block_cat[m, b], NN).reshape(pair_count, pno_count, orbital_count))
            at = (m * block_count + b) * pno_count
            for i in range(2):
                projected[:, at:at + pno_count, i * orbital_count:(i + 1) * orbital_count] = product[i]
    for pair in range(pair_count):
        here = first_pair + pair
        both = stack([wide[pair, :, i * orbital_count:(i + 1) * orbital_count] for i in range(2)])
        product = [projected[pair, :, i * orbital_count:(i + 1) * orbital_count] for i in range(2)]
        inner = fold(dot(product[0], both, NT) + dot(product[1], both, NT))
        inner_left[here] = high_low(inner[:size])
        high, _, low = split(inner[size:])
        low = jnp.where(left_lanes(low), low, 0.0).astype(jnp.bfloat16)
        for b in range(block_count):
            rows = slice(b * pno_count, (b + 1) * pno_count)
            lanes = slice(b * 2 * pno_count, (b + 1) * 2 * pno_count)
            inner_right[here, :pno_count, lanes] = high[rows]
            inner_right[here, pno_count:, lanes] = low[rows]


def project_all(bases, pieces, inner_left, inner_right, scratch):
    block_cat, wide, projected = scratch
    pair_count = bases[0].shape[0]
    split_blocks(pieces, block_cat)
    for member, basis in enumerate(bases):
        slot = member % 2
        split_basis(basis, wide.at[slot])
        project_member(
            wide.at[slot], block_cat, projected.at[slot], inner_left, inner_right, member * pair_count
        )


def project_kernel(member_count, *refs):
    bases, refs = refs[:member_count], refs[member_count:]
    *pieces, inner_left, inner_right = refs[:-3]
    project_all(bases, pieces, inner_left, inner_right, refs[-3:])


def inner_shapes(pairs, pno_count, block_count):
    return (
        ((pairs, block_count * pno_count, 2 * pno_count), jnp.bfloat16),
        ((pairs, 2 * pno_count, block_count * 2 * pno_count), jnp.bfloat16),
    )


def project_scratch(bases, pieces):
    pair_count, pno_count, _ = bases[0].shape
    block_count, part_count, _, orbital_count = pieces[0].shape
    return [
        pltpu.VMEM((part_count, block_count, 3 * orbital_count, orbital_count), jnp.bfloat16),
        pltpu.VMEM((2, pair_count, pno_count, 3 * orbital_count), jnp.bfloat16),
        pltpu.VMEM((2, pair_count, part_count * block_count * pno_count, 2 * orbital_count), jnp.bfloat16),
    ]


def project_flops(bases, pieces):
    pair_count, pno_count, _ = bases[0].shape
    block_count, part_count, _, orbital_count = pieces[0].shape
    rows = len(bases) * pair_count * pno_count * block_count * part_count
    return 6 * rows * orbital_count * (orbital_count + pno_count)


def project(bases, pieces):
    pair_count, pno_count, _ = bases[0].shape
    shapes = inner_shapes(len(bases) * pair_count, pno_count, pieces[0].shape[0])
    return pl.pallas_call(
        lambda *refs: project_kernel(len(bases), *refs),
        out_shape=tuple(jax.ShapeDtypeStruct(*x) for x in shapes),
        in_specs=vmem(len(bases) + len(pieces)),
        out_specs=tuple(vmem(2)),
        scratch_shapes=project_scratch(bases, pieces),
        compiler_params=pltpu.CompilerParams(vmem_limit_bytes=20 * 2**20),
        cost_estimate=pl.CostEstimate(flops=project_flops(bases, pieces), bytes_accessed=2**20, transcendentals=0),
    )(*bases, *pieces)


def finish_kernel(members, group_count, dom_count, *refs):
    count = len(members)
    groups, refs = refs[:2 * group_count], refs[2 * group_count:]
    bases, pieces, refs = refs[:count], refs[count:count + dom_count], refs[count + dom_count:]
    dressed, after, scratch = refs[:count], refs[count:2 * count], refs[2 * count:]
    inner_left, inner_right, square, moved, total = scratch[:5]
    project_all(bases, pieces, inner_left, inner_right, scratch[5:])
    groups = [*groups, inner_left, inner_right]
    group_count += 1
    pair_count, _, lane_count = dressed[0].shape
    pno_count = lane_count // 2
    half = pno_count // 2
    block_count = inner_left.shape[1] // pno_count
    group_total = lax.axis_size("blk")
    me = lax.axis_index("blk")
    pairs = [(index, pair) for index in range(count) for pair in range(pair_count)]

    def row_of(group, at):
        full = group < group_count - 1
        return members[at // pair_count] * pair_count + at % pair_count if full else at

    weights = []
    for index, member in enumerate(members):
        row = dressed[index][:, half:half + 1, :]
        lane = lax.broadcasted_iota(jnp.int32, row.shape, 2)
        for group in range(group_count):
            stop = lax.rem((me ^ member) + 2 * group_total + group * SET - me, group_total)
            for b in range(block_count):
                kept = jnp.where(lane == stop * block_count + b, row, 0.0)
                weights.append(jnp.sum(kept, axis=2, keepdims=True))
    for at, (index, pair) in enumerate(pairs):
        packed = dressed[index][pair, :half]
        other = pltpu.roll(packed, pno_count, 1)
        keep = left_lanes(packed)
        _, high, low = split(stack([jnp.where(keep, packed, other), jnp.where(keep, other, packed)]))
        square[at, :pno_count] = jnp.where(left_lanes(low), high, low).astype(jnp.bfloat16)
        square[at, pno_count:] = jnp.where(left_lanes(low), high, 0.0).astype(jnp.bfloat16)
    for at, (index, pair) in enumerate(pairs):
        for group in range(group_count):
            product = fold(dot(groups[2 * group][row_of(group, at)], square[at], NN))
            for b in range(block_count):
                weight = weights[(index * group_count + group) * block_count + b][pair]
                lanes = slice(b * lane_count, (b + 1) * lane_count)
                moved[at, group, :, lanes] = high_low(product[b * pno_count:(b + 1) * pno_count] * weight)
    for at, (index, pair) in enumerate(pairs):
        terms = [dot(moved[at, group], groups[2 * group + 1][row_of(group, at)], NT) for group in range(group_count)]
        total[at] = fold(sum(terms[1:], terms[0]))
    for at, (index, pair) in enumerate(pairs):
        rows = [total[at, pl.ds(i, half, stride=2), :] for i in range(2)]
        after[index][pair] = jnp.where(left_lanes(rows[0]), *rows)


def finish(members, groups, bases, pieces, dressed):
    pair_count, _, lane_count = dressed[0].shape
    pno_count = lane_count // 2
    pairs = len(members) * pair_count
    group_count = len(groups)
    block_count = pieces[0].shape[0]
    operands = [x for group in groups for x in group] + bases + pieces + dressed
    products = pairs * pno_count**3 * 2 * (group_count + 1) * block_count
    shapes = inner_shapes(pairs, pno_count, block_count)
    return pl.pallas_call(
        lambda *refs: finish_kernel(members, group_count, len(pieces), *refs),
        out_shape=[jax.ShapeDtypeStruct((pair_count, pno_count // 2, lane_count), jnp.float32)] * len(members),
        in_specs=vmem(len(operands)),
        out_specs=vmem(len(members)),
        scratch_shapes=[
            *[pltpu.VMEM(*x) for x in shapes],
            pltpu.VMEM((pairs, lane_count, lane_count), jnp.bfloat16),
            pltpu.VMEM((pairs, group_count + 1, pno_count, block_count * lane_count), jnp.bfloat16),
            pltpu.VMEM((pairs, pno_count, lane_count), jnp.float32),
            *project_scratch(bases, pieces),
        ],
        compiler_params=pltpu.CompilerParams(vmem_limit_bytes=24 * 2**20),
        cost_estimate=pl.CostEstimate(
            flops=project_flops(bases, pieces) + 6 * products, bytes_accessed=2**20, transcendentals=0
        ),
    )(*operands)


def gather_pieces(mine, axis):
    count = lax.axis_size(axis)
    up, down = [mine], []
    for shift in range(1, count):
        if shift <= (count - 1) // 2:
            up.append(from_behind(up[-1], axis, 1))
        else:
            down.append(from_behind(down[-1] if down else mine, axis, count - 1))
    return up + down[::-1]


def on_device_shared(pno_basis, amplitudes, send_list, couple, couple_weight, fit_weight, fit_blocks):
    pair_count, pno_count, _ = pno_basis.shape
    group_total = lax.axis_size("blk")
    pieces = gather_pieces(fit_blocks, "dom")
    across = from_partner(pno_basis, "blk", 2)
    far = [([from_behind(fit_blocks, "blk", by)], by) for by in range(SET, group_total, SET)]
    pair_amps = amplitudes.reshape(pair_count, pno_count, pno_count)
    sent = pack_pairs(send_list.reshape(-1), pno_basis, pair_amps)
    sent, pieces[-1], *heads = lax.optimization_barrier((sent, pieces[-1], *[group[0] for group, _ in far]))
    far = [([head], by) for head, (_, by) in zip(heads, far)]
    coupled = lax.all_to_all(sent, "blk", split_axis=0, concat_axis=0, tiled=True)
    bases = [pno_basis, from_partner(pno_basis, "blk", 1), across, from_partner(across, "blk", 1)]
    coupled, *bases = lax.optimization_barrier((coupled, *bases))
    own, updated = dress(couple, couple_weight, fit_weight, pno_basis, pair_amps, coupled)
    last = len(pieces) // 2
    _, pieces[last] = lax.optimization_barrier((own, pieces[last]))
    groups = [pieces]
    for group, by in far:
        group += [from_behind(x, "blk", by) for x in pieces[1:]]
        if last > 1:
            source, pieces[last] = lax.optimization_barrier((group[last + 1], pieces[last]))
            group[last] = from_behind(source, "dom", len(pieces) - 1)
        groups.append(group)
    inner = [project(bases, group) for group in groups[:-1]]
    final = groups[-1]
    dressed = [own, *[from_partner(own, "blk", flip) for flip in range(1, SET)]]
    for members in ((2, 3), (0, 1)):
        partial = finish(
            members, inner, [bases[member] for member in members], final, [dressed[member] for member in members]
        )
        if members[0]:
            partial, *final = lax.optimization_barrier((partial, *final))
            for member, x in zip(members, partial):
                updated = updated + from_partner(x, "blk", member)
        else:
            mine, beside = partial
            updated, mine, beside = lax.optimization_barrier((updated, mine, from_partner(beside, "blk", 1)))
            updated = updated + mine + beside
    return updated.reshape(pair_count, pno_count * pno_count)


def dress_with(pair_amps, intersection, partner_amps, weights):
    half_product = jnp.einsum("pcab,pcbe->pcae", intersection, partner_amps, precision=HIGHEST)
    sandwich = jnp.einsum("pcae,pcfe->pcaf", half_product, intersection, precision=HIGHEST)
    return pair_amps + jnp.einsum("pc,pcaf->paf", weights, sandwich, precision=HIGHEST)


def fit_term(pair_basis, dressed, blocks, weights):
    pair_count, pno_count, orbital_count = pair_basis.shape
    flat_basis = pair_basis.reshape(pair_count * pno_count, orbital_count)
    stacked = blocks.reshape(2 * orbital_count, orbital_count)
    projected = jnp.dot(
        flat_basis, stacked.T, precision=HIGHEST, preferred_element_type=jnp.float32
    )
    projected = projected.reshape(pair_count, pno_count, 2, orbital_count)
    inner_blocks = jnp.einsum("par,pbmr->mpab", pair_basis, projected, precision=HIGHEST)
    left_product = jnp.einsum("pai,pij->paj", inner_blocks[0], dressed, precision=HIGHEST)
    fit_contrib = jnp.einsum("paj,pbj->pab", left_product, inner_blocks[1], precision=HIGHEST)
    return weights[:, None, None] * fit_contrib


def on_device_ring(pno_basis, amplitudes, send_list, couple, couple_weight, fit_weight, fit_blocks):
    pair_count, pno_count, _ = pno_basis.shape
    block_count = fit_blocks.shape[0]
    pair_amps = amplitudes.reshape(pair_count, pno_count, pno_count)
    send_order = send_list.reshape(-1)
    basis_in = lax.all_to_all(jnp.take(pno_basis, send_order, axis=0), "blk", split_axis=0, concat_axis=0, tiled=True)
    amps_in = lax.all_to_all(jnp.take(pair_amps, send_order, axis=0), "blk", split_axis=0, concat_axis=0, tiled=True)
    partner_basis = jnp.take(basis_in, couple, axis=0)
    intersection = jnp.einsum("par,pcbr->pcab", pno_basis, partner_basis, precision=HIGHEST)
    dressed = dress_with(pair_amps, intersection, jnp.take(amps_in, couple, axis=0), couple_weight)
    updated = dressed
    current = lax.all_gather(fit_blocks, "dom", axis=2, tiled=True)
    for stop in range(fit_weight.shape[1] // block_count):
        if stop > 0:
            current = from_behind(current, "blk", 1)
        for b in range(block_count):
            updated = updated + fit_term(pno_basis, dressed, current[b], fit_weight[:, stop * block_count + b])
    return updated.reshape(pair_count, pno_count * pno_count)


def solution(mesh):
    placed = (
        P(("blk", "dom"), None, None),
        P(("blk", "dom"), None),
        P("blk", "dom", None, None),
        P(("blk", "dom"), None),
        P(("blk", "dom"), None),
        P(("blk", "dom"), None),
        P("blk", None, "dom", None),
    )

    def on_device(*args):
        send_list, fit_weight, fit_blocks = args[2], args[5], args[6]
        group_total = mesh.shape["blk"]
        meets_all = fit_weight.shape[1] == group_total * fit_blocks.shape[0]
        if meets_all and group_total % SET == 0 and group_total > SET and group_total & (group_total - 1) == 0 and send_list.shape[3] == 1:
            return on_device_shared(*args)
        return on_device_ring(*args)

    return jax.shard_map(
        on_device, mesh=mesh, in_specs=placed, out_specs=P(("blk", "dom"), None), check_vma=False
    )
```

```python
import jax
import jax.numpy as jnp
from jax import lax
from jax.experimental import pallas as pl
from jax.experimental.pallas import tpu as pltpu
from jax.sharding import PartitionSpec as P

HIGHEST = lax.Precision.HIGHEST
SET = 4
NN = (((1,), (0,)), ((), ()))
NT = (((1,), (1,)), ((), ()))


def halves(x):
    high = x.astype(jnp.bfloat16)
    return high, (x - high.astype(jnp.float32)).astype(jnp.bfloat16)


def dot(a, b, dims):
    return lax.dot_general(a, b, dims, preferred_element_type=jnp.float32)


def dot3(a, b, dims):
    (a_high, a_low), (b_high, b_low) = a, b
    return dot(a_high, b_high, dims) + (dot(a_high, b_low, dims) + dot(a_low, b_high, dims))


def stack(parts, axis=0):
    return jnp.concatenate(parts, axis=axis)


def from_partner(x, axis, flip):
    return lax.ppermute(x, axis, [(i, i ^ flip) for i in range(lax.axis_size(axis))])


def from_behind(x, axis, by):
    count = lax.axis_size(axis)
    return lax.ppermute(x, axis, [(i, (i + by) % count) for i in range(count)])


def vmem(count):
    return [pl.BlockSpec(memory_space=pltpu.VMEM)] * count


def pack_kernel(send, basis, amps, out):
    pno_count = amps.shape[1]
    lanes = basis.shape[2] // pno_count
    step = pno_count // lanes
    for peer in range(out.shape[0]):
        pair = send[peer]
        out[peer, :pno_count] = basis[pair]
        listed = amps[pair]
        out[peer, pno_count:] = stack([listed[i * step:(i + 1) * step] for i in range(lanes)], 1)


def pack_pairs(send_order, basis, amps):
    _, pno_count, orbital_count = basis.shape
    rows = pno_count + pno_count * pno_count // orbital_count
    return pl.pallas_call(
        pack_kernel,
        out_shape=jax.ShapeDtypeStruct((send_order.shape[0], rows, orbital_count), jnp.float32),
        in_specs=[pl.BlockSpec(memory_space=pltpu.SMEM), *vmem(2)],
        out_specs=vmem(1)[0],
        compiler_params=pltpu.CompilerParams(vmem_limit_bytes=4 * 2**20),
        cost_estimate=pl.CostEstimate(flops=0, bytes_accessed=4 * basis.size, transcendentals=0),
    )(send_order, basis, amps)


def dress_kernel(couple, couple_weight, fit_weight, basis, amps, coupled, dressed, result, turned):
    pair_count, pno_count, orbital_count = basis.shape
    half = pno_count // 2
    slot_count = coupled.shape[0]
    own = halves(basis[...].reshape(pair_count * pno_count, orbital_count))
    others = halves(coupled[:, :pno_count].reshape(slot_count * pno_count, orbital_count))
    overlap = halves(dot3(own, others, NT))
    left, slot_weight = [], []
    for slot in range(slot_count):
        cols = slice(slot * pno_count, (slot + 1) * pno_count)
        packed = coupled[slot, pno_count:]
        partner = stack([packed[:, i:i + pno_count] for i in range(0, orbital_count, pno_count)])
        left.append(dot3([x[:, cols] for x in overlap], halves(partner), NN))
        named = jnp.where(couple[...] == slot, couple_weight[...], 0.0)
        slot_weight.append(jnp.sum(named, axis=1, keepdims=True))
    dressed[:, half:, :] = jnp.zeros((pair_count, dressed.shape[1] - half, 2 * pno_count), jnp.float32)
    for pair in range(pair_count):
        rows = slice(pair * pno_count, (pair + 1) * pno_count)
        scaled = stack([x[rows] * w[pair:pair + 1] for x, w in zip(left, slot_weight)], 1)
        total = amps[pair] + dot3(halves(scaled), [x[rows] for x in overlap], NT)
        dressed[pair, :half] = stack([total[:half], total[half:]], 1)
        turned[pair] = total
        result[pair] = two_to_one(turned, pair, half)
        dressed[pair, half:half + 1, : fit_weight.shape[1]] = fit_weight[pair:pair + 1, :]


def two_to_one(ref, pair, half):
    return stack([ref[pair, pl.ds(i, half, stride=2), :] for i in range(2)], 1)


def dress(couple, couple_weight, fit_weight, basis, amps, coupled):
    pair_count, pno_count, _ = basis.shape
    return pl.pallas_call(
        dress_kernel,
        out_shape=tuple(
            jax.ShapeDtypeStruct((pair_count, pno_count // 2 + more, 2 * pno_count), jnp.float32) for more in (8, 0)
        ),
        in_specs=vmem(6),
        out_specs=tuple(vmem(2)),
        scratch_shapes=[pltpu.VMEM((pair_count, pno_count, pno_count), jnp.float32)],
        compiler_params=pltpu.CompilerParams(vmem_limit_bytes=10 * 2**20),
        cost_estimate=pl.CostEstimate(flops=4 * 10**9, bytes_accessed=8 * basis.size, transcendentals=0),
    )(couple, couple_weight, fit_weight, basis, amps, coupled)


def fold(x):
    return x + pltpu.roll(x, x.shape[1] // 2, 1)


def left_lanes(x):
    return lax.broadcasted_iota(jnp.int32, x.shape, 1) < x.shape[1] // 2


def split(x):
    high = x.astype(jnp.bfloat16)
    wide = high.astype(jnp.float32)
    return high, wide, x - wide


def high_low(x):
    _, high, low = split(x)
    return jnp.where(left_lanes(x), high, low).astype(jnp.bfloat16)


def split_blocks(pieces, block_cat):
    dom_count = len(pieces)
    block_count, part_count, row_count, orbital_count = pieces[0].shape
    place = lax.axis_index("dom")
    for shift, piece in enumerate(pieces):
        start = lax.rem(place + dom_count - shift, dom_count) * row_count
        for b in range(block_count):
            for m in range(part_count):
                high, low = halves(piece[b, m])
                for i, x in enumerate((high, high, low)):
                    at = pl.multiple_of(start + i * orbital_count, row_count)
                    block_cat[m, b, pl.ds(at, row_count), :] = x


def split_basis(basis, wide):
    orbital_count = basis.shape[2]
    high, low = halves(basis[...])
    for i, x in enumerate((high, low, high)):
        wide[:, :, i * orbital_count:(i + 1) * orbital_count] = x


def project_member(wide, block_cat, projected, inner_left, inner_right, first_pair):
    pair_count, pno_count, _ = wide.shape
    part_count, block_count, _, orbital_count = block_cat.shape
    size = block_count * pno_count
    basis = wide[...].reshape(pair_count * pno_count, 3 * orbital_count)
    for m in range(part_count):
        for b in range(block_count):
            product = halves(dot(basis, block_cat[m, b], NN).reshape(pair_count, pno_count, orbital_count))
            at = (m * block_count + b) * pno_count
            for i in range(2):
                projected[:, at:at + pno_count, i * orbital_count:(i + 1) * orbital_count] = product[i]
    for pair in range(pair_count):
        here = first_pair + pair
        both = stack([wide[pair, :, i * orbital_count:(i + 1) * orbital_count] for i in range(2)])
        product = [projected[pair, :, i * orbital_count:(i + 1) * orbital_count] for i in range(2)]
        inner = fold(dot(product[0], both, NT) + dot(product[1], both, NT))
        inner_left[here] = high_low(inner[:size])
        high, _, low = split(inner[size:])
        low = jnp.where(left_lanes(low), low, 0.0).astype(jnp.bfloat16)
        for b in range(block_count):
            rows = slice(b * pno_count, (b + 1) * pno_count)
            lanes = slice(b * 2 * pno_count, (b + 1) * 2 * pno_count)
            inner_right[here, :pno_count, lanes] = high[rows]
            inner_right[here, pno_count:, lanes] = low[rows]


def project_all(bases, pieces, inner_left, inner_right, scratch):
    block_cat, wide, projected = scratch
    pair_count = bases[0].shape[0]
    split_blocks(pieces, block_cat)
    for member, basis in enumerate(bases):
        slot = member % 2
        split_basis(basis, wide.at[slot])
        project_member(
            wide.at[slot], block_cat, projected.at[slot], inner_left, inner_right, member * pair_count
        )


def project_kernel(member_count, *refs):
    bases, refs = refs[:member_count], refs[member_count:]
    *pieces, inner_left, inner_right = refs[:-3]
    project_all(bases, pieces, inner_left, inner_right, refs[-3:])


def inner_shapes(pairs, pno_count, block_count):
    return (
        ((pairs, block_count * pno_count, 2 * pno_count), jnp.bfloat16),
        ((pairs, 2 * pno_count, block_count * 2 * pno_count), jnp.bfloat16),
    )


def project_scratch(bases, pieces):
    pair_count, pno_count, _ = bases[0].shape
    block_count, part_count, _, orbital_count = pieces[0].shape
    return [
        pltpu.VMEM((part_count, block_count, 3 * orbital_count, orbital_count), jnp.bfloat16),
        pltpu.VMEM((2, pair_count, pno_count, 3 * orbital_count), jnp.bfloat16),
        pltpu.VMEM((2, pair_count, part_count * block_count * pno_count, 2 * orbital_count), jnp.bfloat16),
    ]


def project_flops(bases, pieces):
    pair_count, pno_count, _ = bases[0].shape
    block_count, part_count, _, orbital_count = pieces[0].shape
    rows = len(bases) * pair_count * pno_count * block_count * part_count
    return 6 * rows * orbital_count * (orbital_count + pno_count)


def project(bases, pieces):
    pair_count, pno_count, _ = bases[0].shape
    shapes = inner_shapes(len(bases) * pair_count, pno_count, pieces[0].shape[0])
    return pl.pallas_call(
        lambda *refs: project_kernel(len(bases), *refs),
        out_shape=tuple(jax.ShapeDtypeStruct(*x) for x in shapes),
        in_specs=vmem(len(bases) + len(pieces)),
        out_specs=tuple(vmem(2)),
        scratch_shapes=project_scratch(bases, pieces),
        compiler_params=pltpu.CompilerParams(vmem_limit_bytes=20 * 2**20),
        cost_estimate=pl.CostEstimate(flops=project_flops(bases, pieces), bytes_accessed=2**20, transcendentals=0),
    )(*bases, *pieces)


def finish_kernel(members, group_count, dom_count, *refs):
    count = len(members)
    groups, refs = refs[:2 * group_count], refs[2 * group_count:]
    bases, pieces, refs = refs[:count], refs[count:count + dom_count], refs[count + dom_count:]
    dressed, after, scratch = refs[:count], refs[count:2 * count], refs[2 * count:]
    inner_left, inner_right, square, moved, total = scratch[:5]
    project_all(bases, pieces, inner_left, inner_right, scratch[5:])
    groups = [*groups, inner_left, inner_right]
    group_count += 1
    pair_count, _, lane_count = dressed[0].shape
    pno_count = lane_count // 2
    half = pno_count // 2
    block_count = inner_left.shape[1] // pno_count
    group_total = lax.axis_size("blk")
    me = lax.axis_index("blk")
    pairs = [(index, pair) for index in range(count) for pair in range(pair_count)]

    def row_of(group, at):
        full = group < group_count - 1
        return members[at // pair_count] * pair_count + at % pair_count if full else at

    weights = []
    for index, member in enumerate(members):
        row = dressed[index][:, half:half + 1, :]
        lane = lax.broadcasted_iota(jnp.int32, row.shape, 2)
        for group in range(group_count):
            stop = lax.rem((me ^ member) + 2 * group_total + group * SET - me, group_total)
            for b in range(block_count):
                kept = jnp.where(lane == stop * block_count + b, row, 0.0)
                weights.append(jnp.sum(kept, axis=2, keepdims=True))
    for at, (index, pair) in enumerate(pairs):
        packed = dressed[index][pair, :half]
        other = pltpu.roll(packed, pno_count, 1)
        keep = left_lanes(packed)
        _, high, low = split(stack([jnp.where(keep, packed, other), jnp.where(keep, other, packed)]))
        square[at, :pno_count] = jnp.where(left_lanes(low), high, low).astype(jnp.bfloat16)
        square[at, pno_count:] = jnp.where(left_lanes(low), high, 0.0).astype(jnp.bfloat16)
    for at, (index, pair) in enumerate(pairs):
        for group in range(group_count):
            product = fold(dot(groups[2 * group][row_of(group, at)], square[at], NN))
            for b in range(block_count):
                weight = weights[(index * group_count + group) * block_count + b][pair]
                lanes = slice(b * lane_count, (b + 1) * lane_count)
                moved[at, group, :, lanes] = high_low(product[b * pno_count:(b + 1) * pno_count] * weight)
    for at, (index, pair) in enumerate(pairs):
        terms = [dot(moved[at, group], groups[2 * group + 1][row_of(group, at)], NT) for group in range(group_count)]
        total[at] = fold(sum(terms[1:], terms[0]))
    for at, (index, pair) in enumerate(pairs):
        rows = [total[at, pl.ds(i, half, stride=2), :] for i in range(2)]
        after[index][pair] = jnp.where(left_lanes(rows[0]), *rows)


def finish(members, groups, bases, pieces, dressed):
    pair_count, _, lane_count = dressed[0].shape
    pno_count = lane_count // 2
    pairs = len(members) * pair_count
    group_count = len(groups)
    block_count = pieces[0].shape[0]
    operands = [x for group in groups for x in group] + bases + pieces + dressed
    products = pairs * pno_count**3 * 2 * (group_count + 1) * block_count
    shapes = inner_shapes(pairs, pno_count, block_count)
    return pl.pallas_call(
        lambda *refs: finish_kernel(members, group_count, len(pieces), *refs),
        out_shape=[jax.ShapeDtypeStruct((pair_count, pno_count // 2, lane_count), jnp.float32)] * len(members),
        in_specs=vmem(len(operands)),
        out_specs=vmem(len(members)),
        scratch_shapes=[
            *[pltpu.VMEM(*x) for x in shapes],
            pltpu.VMEM((pairs, lane_count, lane_count), jnp.bfloat16),
            pltpu.VMEM((pairs, group_count + 1, pno_count, block_count * lane_count), jnp.bfloat16),
            pltpu.VMEM((pairs, pno_count, lane_count), jnp.float32),
            *project_scratch(bases, pieces),
        ],
        compiler_params=pltpu.CompilerParams(vmem_limit_bytes=24 * 2**20),
        cost_estimate=pl.CostEstimate(
            flops=project_flops(bases, pieces) + 6 * products, bytes_accessed=2**20, transcendentals=0
        ),
    )(*operands)


def gather_pieces(mine, axis):
    count = lax.axis_size(axis)
    up, down = [mine], []
    for shift in range(1, count):
        if shift <= count // 2:
            up.append(from_behind(up[-1], axis, 1))
        else:
            down.append(from_behind(down[-1] if down else mine, axis, count - 1))
    return up + down[::-1]


def on_device_shared(pno_basis, amplitudes, send_list, couple, couple_weight, fit_weight, fit_blocks):
    pair_count, pno_count, _ = pno_basis.shape
    group_total = lax.axis_size("blk")
    pieces = gather_pieces(fit_blocks, "dom")
    across = from_partner(pno_basis, "blk", 2)
    far = [([from_behind(fit_blocks, "blk", by)], by) for by in range(SET, group_total, SET)]
    pair_amps = amplitudes.reshape(pair_count, pno_count, pno_count)
    sent = pack_pairs(send_list.reshape(-1), pno_basis, pair_amps)
    sent, *heads = lax.optimization_barrier((sent, *[group[0] for group, _ in far]))
    far = [([head], by) for head, (_, by) in zip(heads, far)]
    coupled = lax.all_to_all(sent, "blk", split_axis=0, concat_axis=0, tiled=True)
    across, pieces[1], pieces[-1] = lax.optimization_barrier((across, pieces[1], pieces[-1]))
    bases = [pno_basis, from_partner(pno_basis, "blk", 1), across, from_partner(across, "blk", 1)]
    coupled, *bases = lax.optimization_barrier((coupled, *bases))
    own, updated = dress(couple, couple_weight, fit_weight, pno_basis, pair_amps, coupled)
    last = len(pieces) // 2
    _, pieces[last] = lax.optimization_barrier((own, pieces[last]))
    groups = [pieces, *[[group[0], *[from_behind(x, "blk", by) for x in pieces[1:]]] for group, by in far]]
    inner = [project(bases, group) for group in groups[:-1]]
    final = groups[-1]
    dressed = [own, *[from_partner(own, "blk", flip) for flip in range(1, SET)]]
    for members in ((2, 3), (0, 1)):
        partial = finish(
            members, inner, [bases[member] for member in members], final, [dressed[member] for member in members]
        )
        if members[0]:
            partial, *final = lax.optimization_barrier((partial, *final))
            for member, x in zip(members, partial):
                updated = updated + from_partner(x, "blk", member)
        else:
            mine, beside = partial
            updated, mine, beside = lax.optimization_barrier((updated, mine, from_partner(beside, "blk", 1)))
            updated = updated + mine + beside
    return updated.reshape(pair_count, pno_count * pno_count)


def dress_with(pair_amps, intersection, partner_amps, weights):
    half_product = jnp.einsum("pcab,pcbe->pcae", intersection, partner_amps, precision=HIGHEST)
    sandwich = jnp.einsum("pcae,pcfe->pcaf", half_product, intersection, precision=HIGHEST)
    return pair_amps + jnp.einsum("pc,pcaf->paf", weights, sandwich, precision=HIGHEST)


def fit_term(pair_basis, dressed, blocks, weights):
    pair_count, pno_count, orbital_count = pair_basis.shape
    flat_basis = pair_basis.reshape(pair_count * pno_count, orbital_count)
    stacked = blocks.reshape(2 * orbital_count, orbital_count)
    projected = jnp.dot(
        flat_basis, stacked.T, precision=HIGHEST, preferred_element_type=jnp.float32
    )
    projected = projected.reshape(pair_count, pno_count, 2, orbital_count)
    inner_blocks = jnp.einsum("par,pbmr->mpab", pair_basis, projected, precision=HIGHEST)
    left_product = jnp.einsum("pai,pij->paj", inner_blocks[0], dressed, precision=HIGHEST)
    fit_contrib = jnp.einsum("paj,pbj->pab", left_product, inner_blocks[1], precision=HIGHEST)
    return weights[:, None, None] * fit_contrib


def on_device_ring(pno_basis, amplitudes, send_list, couple, couple_weight, fit_weight, fit_blocks):
    pair_count, pno_count, _ = pno_basis.shape
    block_count = fit_blocks.shape[0]
    pair_amps = amplitudes.reshape(pair_count, pno_count, pno_count)
    send_order = send_list.reshape(-1)
    basis_in = lax.all_to_all(jnp.take(pno_basis, send_order, axis=0), "blk", split_axis=0, concat_axis=0, tiled=True)
    amps_in = lax.all_to_all(jnp.take(pair_amps, send_order, axis=0), "blk", split_axis=0, concat_axis=0, tiled=True)
    partner_basis = jnp.take(basis_in, couple, axis=0)
    intersection = jnp.einsum("par,pcbr->pcab", pno_basis, partner_basis, precision=HIGHEST)
    dressed = dress_with(pair_amps, intersection, jnp.take(amps_in, couple, axis=0), couple_weight)
    updated = dressed
    current = lax.all_gather(fit_blocks, "dom", axis=2, tiled=True)
    for stop in range(fit_weight.shape[1] // block_count):
        if stop > 0:
            current = from_behind(current, "blk", 1)
        for b in range(block_count):
            updated = updated + fit_term(pno_basis, dressed, current[b], fit_weight[:, stop * block_count + b])
    return updated.reshape(pair_count, pno_count * pno_count)


def solution(mesh):
    placed = (
        P(("blk", "dom"), None, None),
        P(("blk", "dom"), None),
        P("blk", "dom", None, None),
        P(("blk", "dom"), None),
        P(("blk", "dom"), None),
        P(("blk", "dom"), None),
        P("blk", None, "dom", None),
    )

    def on_device(*args):
        send_list, fit_weight, fit_blocks = args[2], args[5], args[6]
        group_total = mesh.shape["blk"]
        meets_all = fit_weight.shape[1] == group_total * fit_blocks.shape[0]
        if meets_all and group_total % SET == 0 and group_total > SET and group_total & (group_total - 1) == 0 and send_list.shape[3] == 1:
            return on_device_shared(*args)
        return on_device_ring(*args)

    return jax.shard_map(
        on_device, mesh=mesh, in_specs=placed, out_specs=P(("blk", "dom"), None), check_vma=False
    )
```

```python
import jax
import jax.numpy as jnp
from jax import lax
from jax.experimental import pallas as pl
from jax.experimental.pallas import tpu as pltpu
from jax.sharding import PartitionSpec as P

HIGHEST = lax.Precision.HIGHEST
SET = 4
NN = (((1,), (0,)), ((), ()))
NT = (((1,), (1,)), ((), ()))


def halves(x):
    high = x.astype(jnp.bfloat16)
    return high, (x - high.astype(jnp.float32)).astype(jnp.bfloat16)


def dot(a, b, dims):
    return lax.dot_general(a, b, dims, preferred_element_type=jnp.float32)


def dot3(a, b, dims):
    (a_high, a_low), (b_high, b_low) = a, b
    return dot(a_high, b_high, dims) + (dot(a_high, b_low, dims) + dot(a_low, b_high, dims))


def stack(parts, axis=0):
    return jnp.concatenate(parts, axis=axis)


def from_partner(x, axis, flip):
    return lax.ppermute(x, axis, [(i, i ^ flip) for i in range(lax.axis_size(axis))])


def from_behind(x, axis, by):
    count = lax.axis_size(axis)
    return lax.ppermute(x, axis, [(i, (i + by) % count) for i in range(count)])


def vmem(count):
    return [pl.BlockSpec(memory_space=pltpu.VMEM)] * count


def pack_kernel(send, basis, amps, out):
    pno_count = amps.shape[1]
    lanes = basis.shape[2] // pno_count
    step = pno_count // lanes
    for peer in range(out.shape[0]):
        pair = send[peer]
        out[peer, :pno_count] = basis[pair]
        listed = amps[pair]
        out[peer, pno_count:] = stack([listed[i * step:(i + 1) * step] for i in range(lanes)], 1)


def pack_pairs(send_order, basis, amps):
    _, pno_count, orbital_count = basis.shape
    rows = pno_count + pno_count * pno_count // orbital_count
    return pl.pallas_call(
        pack_kernel,
        out_shape=jax.ShapeDtypeStruct((send_order.shape[0], rows, orbital_count), jnp.float32),
        in_specs=[pl.BlockSpec(memory_space=pltpu.SMEM), *vmem(2)],
        out_specs=vmem(1)[0],
        compiler_params=pltpu.CompilerParams(vmem_limit_bytes=4 * 2**20),
        cost_estimate=pl.CostEstimate(flops=0, bytes_accessed=4 * basis.size, transcendentals=0),
    )(send_order, basis, amps)


def dress_kernel(couple, couple_weight, fit_weight, basis, amps, coupled, dressed, result, turned):
    pair_count, pno_count, orbital_count = basis.shape
    half = pno_count // 2
    slot_count = coupled.shape[0]
    own = halves(basis[...].reshape(pair_count * pno_count, orbital_count))
    others = halves(coupled[:, :pno_count].reshape(slot_count * pno_count, orbital_count))
    overlap = halves(dot3(own, others, NT))
    left, slot_weight = [], []
    for slot in range(slot_count):
        cols = slice(slot * pno_count, (slot + 1) * pno_count)
        packed = coupled[slot, pno_count:]
        partner = stack([packed[:, i:i + pno_count] for i in range(0, orbital_count, pno_count)])
        left.append(dot3([x[:, cols] for x in overlap], halves(partner), NN))
        named = jnp.where(couple[...] == slot, couple_weight[...], 0.0)
        slot_weight.append(jnp.sum(named, axis=1, keepdims=True))
    dressed[:, half:, :] = jnp.zeros((pair_count, dressed.shape[1] - half, 2 * pno_count), jnp.float32)
    for pair in range(pair_count):
        rows = slice(pair * pno_count, (pair + 1) * pno_count)
        scaled = stack([x[rows] * w[pair:pair + 1] for x, w in zip(left, slot_weight)], 1)
        total = amps[pair] + dot3(halves(scaled), [x[rows] for x in overlap], NT)
        dressed[pair, :half] = stack([total[:half], total[half:]], 1)
        turned[pair] = total
        result[pair] = two_to_one(turned, pair, half)
        dressed[pair, half:half + 1, : fit_weight.shape[1]] = fit_weight[pair:pair + 1, :]


def two_to_one(ref, pair, half):
    return stack([ref[pair, pl.ds(i, half, stride=2), :] for i in range(2)], 1)


def dress(couple, couple_weight, fit_weight, basis, amps, coupled):
    pair_count, pno_count, _ = basis.shape
    return pl.pallas_call(
        dress_kernel,
        out_shape=tuple(
            jax.ShapeDtypeStruct((pair_count, pno_count // 2 + more, 2 * pno_count), jnp.float32) for more in (8, 0)
        ),
        in_specs=vmem(6),
        out_specs=tuple(vmem(2)),
        scratch_shapes=[pltpu.VMEM((pair_count, pno_count, pno_count), jnp.float32)],
        compiler_params=pltpu.CompilerParams(vmem_limit_bytes=10 * 2**20),
        cost_estimate=pl.CostEstimate(flops=4 * 10**9, bytes_accessed=8 * basis.size, transcendentals=0),
    )(couple, couple_weight, fit_weight, basis, amps, coupled)


def fold(x):
    return x + pltpu.roll(x, x.shape[1] // 2, 1)


def left_lanes(x):
    return lax.broadcasted_iota(jnp.int32, x.shape, 1) < x.shape[1] // 2


def split(x):
    high = x.astype(jnp.bfloat16)
    wide = high.astype(jnp.float32)
    return high, wide, x - wide


def high_low(x):
    _, high, low = split(x)
    return jnp.where(left_lanes(x), high, low).astype(jnp.bfloat16)


def split_blocks(pieces, block_cat):
    dom_count = len(pieces)
    block_count, part_count, row_count, orbital_count = pieces[0].shape
    place = lax.axis_index("dom")
    for shift, piece in enumerate(pieces):
        start = lax.rem(place + dom_count - shift, dom_count) * row_count
        for b in range(block_count):
            for m in range(part_count):
                high, low = halves(piece[b, m])
                for i, x in enumerate((high, high, low)):
                    at = pl.multiple_of(start + i * orbital_count, row_count)
                    block_cat[m, b, pl.ds(at, row_count), :] = x


def split_basis(basis, wide):
    orbital_count = basis.shape[2]
    high, low = halves(basis[...])
    for i, x in enumerate((high, low, high)):
        wide[:, :, i * orbital_count:(i + 1) * orbital_count] = x


def project_member(wide, block_cat, projected, inner_left, inner_right, first_pair):
    pair_count, pno_count, _ = wide.shape
    part_count, block_count, _, orbital_count = block_cat.shape
    size = block_count * pno_count
    basis = wide[...].reshape(pair_count * pno_count, 3 * orbital_count)
    for m in range(part_count):
        for b in range(block_count):
            product = halves(dot(basis, block_cat[m, b], NN).reshape(pair_count, pno_count, orbital_count))
            at = (m * block_count + b) * pno_count
            for i in range(2):
                projected[:, at:at + pno_count, i * orbital_count:(i + 1) * orbital_count] = product[i]
    for pair in range(pair_count):
        here = first_pair + pair
        both = stack([wide[pair, :, i * orbital_count:(i + 1) * orbital_count] for i in range(2)])
        product = [projected[pair, :, i * orbital_count:(i + 1) * orbital_count] for i in range(2)]
        inner = fold(dot(product[0], both, NT) + dot(product[1], both, NT))
        inner_left[here] = high_low(inner[:size])
        high, _, low = split(inner[size:])
        low = jnp.where(left_lanes(low), low, 0.0).astype(jnp.bfloat16)
        for b in range(block_count):
            rows = slice(b * pno_count, (b + 1) * pno_count)
            lanes = slice(b * 2 * pno_count, (b + 1) * 2 * pno_count)
            inner_right[here, :pno_count, lanes] = high[rows]
            inner_right[here, pno_count:, lanes] = low[rows]


def project_all(bases, pieces, inner_left, inner_right, scratch):
    block_cat, wide, projected = scratch
    pair_count = bases[0].shape[0]
    split_blocks(pieces, block_cat)
    for member, basis in enumerate(bases):
        slot = member % 2
        split_basis(basis, wide.at[slot])
        project_member(
            wide.at[slot], block_cat, projected.at[slot], inner_left, inner_right, member * pair_count
        )


def project_kernel(member_count, *refs):
    bases, refs = refs[:member_count], refs[member_count:]
    *pieces, inner_left, inner_right = refs[:-3]
    project_all(bases, pieces, inner_left, inner_right, refs[-3:])


def inner_shapes(pairs, pno_count, block_count):
    return (
        ((pairs, block_count * pno_count, 2 * pno_count), jnp.bfloat16),
        ((pairs, 2 * pno_count, block_count * 2 * pno_count), jnp.bfloat16),
    )


def project_scratch(bases, pieces):
    pair_count, pno_count, _ = bases[0].shape
    block_count, part_count, _, orbital_count = pieces[0].shape
    return [
        pltpu.VMEM((part_count, block_count, 3 * orbital_count, orbital_count), jnp.bfloat16),
        pltpu.VMEM((2, pair_count, pno_count, 3 * orbital_count), jnp.bfloat16),
        pltpu.VMEM((2, pair_count, part_count * block_count * pno_count, 2 * orbital_count), jnp.bfloat16),
    ]


def project_flops(bases, pieces):
    pair_count, pno_count, _ = bases[0].shape
    block_count, part_count, _, orbital_count = pieces[0].shape
    rows = len(bases) * pair_count * pno_count * block_count * part_count
    return 6 * rows * orbital_count * (orbital_count + pno_count)


def project(bases, pieces):
    pair_count, pno_count, _ = bases[0].shape
    shapes = inner_shapes(len(bases) * pair_count, pno_count, pieces[0].shape[0])
    return pl.pallas_call(
        lambda *refs: project_kernel(len(bases), *refs),
        out_shape=tuple(jax.ShapeDtypeStruct(*x) for x in shapes),
        in_specs=vmem(len(bases) + len(pieces)),
        out_specs=tuple(vmem(2)),
        scratch_shapes=project_scratch(bases, pieces),
        compiler_params=pltpu.CompilerParams(vmem_limit_bytes=20 * 2**20),
        cost_estimate=pl.CostEstimate(flops=project_flops(bases, pieces), bytes_accessed=2**20, transcendentals=0),
    )(*bases, *pieces)


def finish_kernel(members, group_count, dom_count, *refs):
    count = len(members)
    groups, refs = refs[:2 * group_count], refs[2 * group_count:]
    bases, pieces, refs = refs[:count], refs[count:count + dom_count], refs[count + dom_count:]
    dressed, after, scratch = refs[:count], refs[count:2 * count], refs[2 * count:]
    inner_left, inner_right, square, moved, total = scratch[:5]
    project_all(bases, pieces, inner_left, inner_right, scratch[5:])
    groups = [*groups, inner_left, inner_right]
    group_count += 1
    pair_count, _, lane_count = dressed[0].shape
    pno_count = lane_count // 2
    half = pno_count // 2
    block_count = inner_left.shape[1] // pno_count
    group_total = lax.axis_size("blk")
    me = lax.axis_index("blk")
    pairs = [(index, pair) for index in range(count) for pair in range(pair_count)]

    def row_of(group, at):
        full = group < group_count - 1
        return members[at // pair_count] * pair_count + at % pair_count if full else at

    weights = []
    for index, member in enumerate(members):
        row = dressed[index][:, half:half + 1, :]
        lane = lax.broadcasted_iota(jnp.int32, row.shape, 2)
        for group in range(group_count):
            stop = lax.rem((me ^ member) + 2 * group_total + group * SET - me, group_total)
            for b in range(block_count):
                kept = jnp.where(lane == stop * block_count + b, row, 0.0)
                weights.append(jnp.sum(kept, axis=2, keepdims=True))
    for at, (index, pair) in enumerate(pairs):
        packed = dressed[index][pair, :half]
        other = pltpu.roll(packed, pno_count, 1)
        keep = left_lanes(packed)
        _, high, low = split(stack([jnp.where(keep, packed, other), jnp.where(keep, other, packed)]))
        square[at, :pno_count] = jnp.where(left_lanes(low), high, low).astype(jnp.bfloat16)
        square[at, pno_count:] = jnp.where(left_lanes(low), high, 0.0).astype(jnp.bfloat16)
    for at, (index, pair) in enumerate(pairs):
        for group in range(group_count):
            product = fold(dot(groups[2 * group][row_of(group, at)], square[at], NN))
            for b in range(block_count):
                weight = weights[(index * group_count + group) * block_count + b][pair]
                lanes = slice(b * lane_count, (b + 1) * lane_count)
                moved[at, group, :, lanes] = high_low(product[b * pno_count:(b + 1) * pno_count] * weight)
    for at, (index, pair) in enumerate(pairs):
        terms = [dot(moved[at, group], groups[2 * group + 1][row_of(group, at)], NT) for group in range(group_count)]
        total[at] = fold(sum(terms[1:], terms[0]))
    for at, (index, pair) in enumerate(pairs):
        rows = [total[at, pl.ds(i, half, stride=2), :] for i in range(2)]
        after[index][pair] = jnp.where(left_lanes(rows[0]), *rows)


def finish(members, groups, bases, pieces, dressed):
    pair_count, _, lane_count = dressed[0].shape
    pno_count = lane_count // 2
    pairs = len(members) * pair_count
    group_count = len(groups)
    block_count = pieces[0].shape[0]
    operands = [x for group in groups for x in group] + bases + pieces + dressed
    products = pairs * pno_count**3 * 2 * (group_count + 1) * block_count
    shapes = inner_shapes(pairs, pno_count, block_count)
    return pl.pallas_call(
        lambda *refs: finish_kernel(members, group_count, len(pieces), *refs),
        out_shape=[jax.ShapeDtypeStruct((pair_count, pno_count // 2, lane_count), jnp.float32)] * len(members),
        in_specs=vmem(len(operands)),
        out_specs=vmem(len(members)),
        scratch_shapes=[
            *[pltpu.VMEM(*x) for x in shapes],
            pltpu.VMEM((pairs, lane_count, lane_count), jnp.bfloat16),
            pltpu.VMEM((pairs, group_count + 1, pno_count, block_count * lane_count), jnp.bfloat16),
            pltpu.VMEM((pairs, pno_count, lane_count), jnp.float32),
            *project_scratch(bases, pieces),
        ],
        compiler_params=pltpu.CompilerParams(vmem_limit_bytes=24 * 2**20),
        cost_estimate=pl.CostEstimate(
            flops=project_flops(bases, pieces) + 6 * products, bytes_accessed=2**20, transcendentals=0
        ),
    )(*operands)


def gather_pieces(mine, axis):
    count = lax.axis_size(axis)
    up, down = [mine], []
    for shift in range(1, count):
        if shift <= count // 2:
            up.append(from_behind(up[-1], axis, 1))
        else:
            down.append(from_behind(down[-1] if down else mine, axis, count - 1))
    return up + down[::-1]


def on_device_shared(pno_basis, amplitudes, send_list, couple, couple_weight, fit_weight, fit_blocks):
    pair_count, pno_count, _ = pno_basis.shape
    group_total = lax.axis_size("blk")
    pieces = gather_pieces(fit_blocks, "dom")
    across = from_partner(pno_basis, "blk", 2)
    far = [([from_behind(fit_blocks, "blk", by)], by) for by in range(SET, group_total, SET)]
    pair_amps = amplitudes.reshape(pair_count, pno_count, pno_count)
    sent = pack_pairs(send_list.reshape(-1), pno_basis, pair_amps)
    sent, *heads = lax.optimization_barrier((sent, *[group[0] for group, _ in far]))
    far = [([head], by) for head, (_, by) in zip(heads, far)]
    coupled = lax.all_to_all(sent, "blk", split_axis=0, concat_axis=0, tiled=True)
    across, pieces[1], pieces[-1] = lax.optimization_barrier((across, pieces[1], pieces[-1]))
    bases = [pno_basis, from_partner(pno_basis, "blk", 1), across, from_partner(across, "blk", 1)]
    coupled, *bases = lax.optimization_barrier((coupled, *bases))
    own, updated = dress(couple, couple_weight, fit_weight, pno_basis, pair_amps, coupled)
    last = len(pieces) // 2
    _, pieces[last] = lax.optimization_barrier((own, pieces[last]))
    groups = [pieces]
    for group, by in far:
        group += [from_behind(x, "blk", by) for x in pieces[1:]]
        if last > 1:
            source, pieces[last] = lax.optimization_barrier((group[0], pieces[last]))
            group[-1] = from_behind(source, "dom", len(pieces) - 1)
        groups.append(group)
    inner = [project(bases, group) for group in groups[:-1]]
    final = groups[-1]
    dressed = [own, *[from_partner(own, "blk", flip) for flip in range(1, SET)]]
    for members in ((2, 3), (0, 1)):
        partial = finish(
            members, inner, [bases[member] for member in members], final, [dressed[member] for member in members]
        )
        if members[0]:
            partial, *final = lax.optimization_barrier((partial, *final))
            for member, x in zip(members, partial):
                updated = updated + from_partner(x, "blk", member)
        else:
            mine, beside = partial
            updated, mine, beside = lax.optimization_barrier((updated, mine, from_partner(beside, "blk", 1)))
            updated = updated + mine + beside
    return updated.reshape(pair_count, pno_count * pno_count)


def dress_with(pair_amps, intersection, partner_amps, weights):
    half_product = jnp.einsum("pcab,pcbe->pcae", intersection, partner_amps, precision=HIGHEST)
    sandwich = jnp.einsum("pcae,pcfe->pcaf", half_product, intersection, precision=HIGHEST)
    return pair_amps + jnp.einsum("pc,pcaf->paf", weights, sandwich, precision=HIGHEST)


def fit_term(pair_basis, dressed, blocks, weights):
    pair_count, pno_count, orbital_count = pair_basis.shape
    flat_basis = pair_basis.reshape(pair_count * pno_count, orbital_count)
    stacked = blocks.reshape(2 * orbital_count, orbital_count)
    projected = jnp.dot(
        flat_basis, stacked.T, precision=HIGHEST, preferred_element_type=jnp.float32
    )
    projected = projected.reshape(pair_count, pno_count, 2, orbital_count)
    inner_blocks = jnp.einsum("par,pbmr->mpab", pair_basis, projected, precision=HIGHEST)
    left_product = jnp.einsum("pai,pij->paj", inner_blocks[0], dressed, precision=HIGHEST)
    fit_contrib = jnp.einsum("paj,pbj->pab", left_product, inner_blocks[1], precision=HIGHEST)
    return weights[:, None, None] * fit_contrib


def on_device_ring(pno_basis, amplitudes, send_list, couple, couple_weight, fit_weight, fit_blocks):
    pair_count, pno_count, _ = pno_basis.shape
    block_count = fit_blocks.shape[0]
    pair_amps = amplitudes.reshape(pair_count, pno_count, pno_count)
    send_order = send_list.reshape(-1)
    basis_in = lax.all_to_all(jnp.take(pno_basis, send_order, axis=0), "blk", split_axis=0, concat_axis=0, tiled=True)
    amps_in = lax.all_to_all(jnp.take(pair_amps, send_order, axis=0), "blk", split_axis=0, concat_axis=0, tiled=True)
    partner_basis = jnp.take(basis_in, couple, axis=0)
    intersection = jnp.einsum("par,pcbr->pcab", pno_basis, partner_basis, precision=HIGHEST)
    dressed = dress_with(pair_amps, intersection, jnp.take(amps_in, couple, axis=0), couple_weight)
    updated = dressed
    current = lax.all_gather(fit_blocks, "dom", axis=2, tiled=True)
    for stop in range(fit_weight.shape[1] // block_count):
        if stop > 0:
            current = from_behind(current, "blk", 1)
        for b in range(block_count):
            updated = updated + fit_term(pno_basis, dressed, current[b], fit_weight[:, stop * block_count + b])
    return updated.reshape(pair_count, pno_count * pno_count)


def solution(mesh):
    placed = (
        P(("blk", "dom"), None, None),
        P(("blk", "dom"), None),
        P("blk", "dom", None, None),
        P(("blk", "dom"), None),
        P(("blk", "dom"), None),
        P(("blk", "dom"), None),
        P("blk", None, "dom", None),
    )

    def on_device(*args):
        send_list, fit_weight, fit_blocks = args[2], args[5], args[6]
        group_total = mesh.shape["blk"]
        meets_all = fit_weight.shape[1] == group_total * fit_blocks.shape[0]
        if meets_all and group_total % SET == 0 and group_total > SET and group_total & (group_total - 1) == 0 and send_list.shape[3] == 1:
            return on_device_shared(*args)
        return on_device_ring(*args)

    return jax.shard_map(
        on_device, mesh=mesh, in_specs=placed, out_specs=P(("blk", "dom"), None), check_vma=False
    )
```

```python
import jax
import jax.numpy as jnp
from jax import lax
from jax.experimental import pallas as pl
from jax.experimental.pallas import tpu as pltpu
from jax.sharding import PartitionSpec as P

HIGHEST = lax.Precision.HIGHEST
SET = 4
NN = (((1,), (0,)), ((), ()))
NT = (((1,), (1,)), ((), ()))


def halves(x):
    high = x.astype(jnp.bfloat16)
    return high, (x - high.astype(jnp.float32)).astype(jnp.bfloat16)


def dot(a, b, dims):
    return lax.dot_general(a, b, dims, preferred_element_type=jnp.float32)


def dot3(a, b, dims):
    (a_high, a_low), (b_high, b_low) = a, b
    return dot(a_high, b_high, dims) + (dot(a_high, b_low, dims) + dot(a_low, b_high, dims))


def stack(parts, axis=0):
    return jnp.concatenate(parts, axis=axis)


def from_partner(x, axis, flip):
    return lax.ppermute(x, axis, [(i, i ^ flip) for i in range(lax.axis_size(axis))])


def from_behind(x, axis, by):
    count = lax.axis_size(axis)
    return lax.ppermute(x, axis, [(i, (i + by) % count) for i in range(count)])


def vmem(count):
    return [pl.BlockSpec(memory_space=pltpu.VMEM)] * count


def pack_kernel(send, basis, amps, out, rows, sent):
    peer_count, row_count, lane_count = rows.shape
    pno_count = out.shape[1] - row_count
    copies = []
    for peer in range(peer_count):
        copies.append(pltpu.make_async_copy(basis.at[send[peer]], out.at[peer, pl.ds(0, pno_count)], sent.at[0, peer]))
        copies[-1].start()
    for peer in range(peer_count):
        for i in range(row_count):
            rows[peer, i:i + 1, :] = amps[pl.ds(send[peer], 1), i * lane_count:(i + 1) * lane_count]
        copies.append(pltpu.make_async_copy(rows.at[peer], out.at[peer, pl.ds(pno_count, row_count)], sent.at[1, peer]))
        copies[-1].start()
    for copy in copies:
        copy.wait()


def pack_pairs(send_order, basis, amps):
    _, pno_count, orbital_count = basis.shape
    peer_count, rows = send_order.shape[0], amps.shape[1] // orbital_count
    return pl.pallas_call(
        pack_kernel,
        out_shape=jax.ShapeDtypeStruct((peer_count, pno_count + rows, orbital_count), jnp.float32),
        in_specs=[
            pl.BlockSpec(memory_space=pltpu.SMEM),
            pl.BlockSpec(memory_space=pl.ANY),
            *vmem(1),
        ],
        out_specs=pl.BlockSpec(memory_space=pl.ANY),
        scratch_shapes=[
            pltpu.VMEM((peer_count, rows, orbital_count), jnp.float32),
            pltpu.SemaphoreType.DMA((2, peer_count)),
        ],
        compiler_params=pltpu.CompilerParams(vmem_limit_bytes=4 * 2**20),
        cost_estimate=pl.CostEstimate(flops=0, bytes_accessed=4 * basis.size, transcendentals=0),
    )(send_order, basis, amps)


def dress_kernel(couple, couple_weight, fit_weight, basis, amps, coupled, dressed, result, turned, paired, partners):
    pair_count, pno_count, orbital_count = basis.shape
    half = pno_count // 2
    slot_count = coupled.shape[0]
    width = 2 * pno_count
    for i in range(half):
        paired[pl.ds(i, pair_count, stride=half), :] = amps[:, i * width:(i + 1) * width]
    for pair in range(pair_count):
        packed = paired[pair * half:(pair + 1) * half]
        for i in range(2):
            turned[pair, pl.ds(i, half, stride=2), :] = packed[:, i * pno_count:(i + 1) * pno_count]
    own = halves(basis[...].reshape(pair_count * pno_count, orbital_count))
    others = halves(coupled[:, :pno_count].reshape(slot_count * pno_count, orbital_count))
    overlap = halves(dot3(own, others, NT))
    left, slot_weight = [], []
    for slot in range(slot_count):
        cols = slice(slot * pno_count, (slot + 1) * pno_count)
        packed = coupled[slot, pno_count:]
        step = orbital_count // pno_count
        for i in range(step):
            lanes = slice(i * pno_count, (i + 1) * pno_count)
            partners[slot, pl.ds(i, packed.shape[0], stride=step), :] = packed[:, lanes]
        left.append(dot3([x[:, cols] for x in overlap], halves(partners[slot]), NN))
        named = jnp.where(couple[...] == slot, couple_weight[...], 0.0)
        slot_weight.append(jnp.sum(named, axis=1, keepdims=True))
    dressed[:, half:, :] = jnp.zeros((pair_count, dressed.shape[1] - half, 2 * pno_count), jnp.float32)
    for pair in range(pair_count):
        rows = slice(pair * pno_count, (pair + 1) * pno_count)
        scaled = stack([x[rows] * w[pair:pair + 1] for x, w in zip(left, slot_weight)], 1)
        total = turned[pair] + dot3(halves(scaled), [x[rows] for x in overlap], NT)
        dressed[pair, :half] = stack([total[:half], total[half:]], 1)
        turned[pair] = total
        result[pair] = two_to_one(turned, pair, half)
        dressed[pair, half:half + 1, : fit_weight.shape[1]] = fit_weight[pair:pair + 1, :]


def two_to_one(ref, pair, half):
    return stack([ref[pair, pl.ds(i, half, stride=2), :] for i in range(2)], 1)


def dress(couple, couple_weight, fit_weight, basis, amps, coupled):
    pair_count, pno_count, _ = basis.shape
    return pl.pallas_call(
        dress_kernel,
        out_shape=tuple(
            jax.ShapeDtypeStruct((pair_count, pno_count // 2 + more, 2 * pno_count), jnp.float32) for more in (8, 0)
        ),
        in_specs=vmem(6),
        out_specs=tuple(vmem(2)),
        scratch_shapes=[
            pltpu.VMEM((pair_count, pno_count, pno_count), jnp.float32),
            pltpu.VMEM((pair_count * pno_count // 2, 2 * pno_count), jnp.float32),
            pltpu.VMEM((coupled.shape[0], pno_count, pno_count), jnp.float32),
        ],
        compiler_params=pltpu.CompilerParams(vmem_limit_bytes=10 * 2**20),
        cost_estimate=pl.CostEstimate(flops=4 * 10**9, bytes_accessed=8 * basis.size, transcendentals=0),
    )(couple, couple_weight, fit_weight, basis, amps, coupled)


def fold(x):
    return x + pltpu.roll(x, x.shape[1] // 2, 1)


def left_lanes(x):
    return lax.broadcasted_iota(jnp.int32, x.shape, 1) < x.shape[1] // 2


def split(x):
    high = x.astype(jnp.bfloat16)
    wide = high.astype(jnp.float32)
    return high, wide, x - wide


def high_low(x):
    _, high, low = split(x)
    return jnp.where(left_lanes(x), high, low).astype(jnp.bfloat16)


def split_blocks(pieces, block_cat):
    dom_count = len(pieces)
    block_count, part_count, row_count, orbital_count = pieces[0].shape
    place = lax.axis_index("dom")
    for shift, piece in enumerate(pieces):
        start = lax.rem(place + dom_count - shift, dom_count) * row_count
        for b in range(block_count):
            for m in range(part_count):
                high, low = halves(piece[b, m])
                for i, x in enumerate((high, high, low)):
                    at = pl.multiple_of(start + i * orbital_count, row_count)
                    block_cat[m, b, pl.ds(at, row_count), :] = x


def split_basis(basis, wide):
    orbital_count = basis.shape[2]
    high, low = halves(basis[...])
    for i, x in enumerate((high, low, high)):
        wide[:, :, i * orbital_count:(i + 1) * orbital_count] = x


def project_member(wide, block_cat, projected, inner_left, inner_right, first_pair):
    pair_count, pno_count, _ = wide.shape
    part_count, block_count, _, orbital_count = block_cat.shape
    size = block_count * pno_count
    basis = wide[...].reshape(pair_count * pno_count, 3 * orbital_count)
    for m in range(part_count):
        for b in range(block_count):
            product = halves(dot(basis, block_cat[m, b], NN).reshape(pair_count, pno_count, orbital_count))
            at = (m * block_count + b) * pno_count
            for i in range(2):
                projected[:, at:at + pno_count, i * orbital_count:(i + 1) * orbital_count] = product[i]
    for pair in range(pair_count):
        here = first_pair + pair
        both = stack([wide[pair, :, i * orbital_count:(i + 1) * orbital_count] for i in range(2)])
        product = [projected[pair, :, i * orbital_count:(i + 1) * orbital_count] for i in range(2)]
        inner = fold(dot(product[0], both, NT) + dot(product[1], both, NT))
        inner_left[here] = high_low(inner[:size])
        high, _, low = split(inner[size:])
        low = jnp.where(left_lanes(low), low, 0.0).astype(jnp.bfloat16)
        for b in range(block_count):
            rows = slice(b * pno_count, (b + 1) * pno_count)
            lanes = slice(b * 2 * pno_count, (b + 1) * 2 * pno_count)
            inner_right[here, :pno_count, lanes] = high[rows]
            inner_right[here, pno_count:, lanes] = low[rows]


def project_all(bases, pieces, inner_left, inner_right, scratch):
    block_cat, wide, projected = scratch
    pair_count = bases[0].shape[0]
    split_blocks(pieces, block_cat)
    for member, basis in enumerate(bases):
        slot = member % 2
        split_basis(basis, wide.at[slot])
        project_member(
            wide.at[slot], block_cat, projected.at[slot], inner_left, inner_right, member * pair_count
        )


def project_kernel(member_count, *refs):
    bases, refs = refs[:member_count], refs[member_count:]
    *pieces, inner_left, inner_right = refs[:-3]
    project_all(bases, pieces, inner_left, inner_right, refs[-3:])


def inner_shapes(pairs, pno_count, block_count):
    return (
        ((pairs, block_count * pno_count, 2 * pno_count), jnp.bfloat16),
        ((pairs, 2 * pno_count, block_count * 2 * pno_count), jnp.bfloat16),
    )


def project_scratch(bases, pieces):
    pair_count, pno_count, _ = bases[0].shape
    block_count, part_count, _, orbital_count = pieces[0].shape
    return [
        pltpu.VMEM((part_count, block_count, 3 * orbital_count, orbital_count), jnp.bfloat16),
        pltpu.VMEM((2, pair_count, pno_count, 3 * orbital_count), jnp.bfloat16),
        pltpu.VMEM((2, pair_count, part_count * block_count * pno_count, 2 * orbital_count), jnp.bfloat16),
    ]


def project_flops(bases, pieces):
    pair_count, pno_count, _ = bases[0].shape
    block_count, part_count, _, orbital_count = pieces[0].shape
    rows = len(bases) * pair_count * pno_count * block_count * part_count
    return 6 * rows * orbital_count * (orbital_count + pno_count)


def project(bases, pieces):
    pair_count, pno_count, _ = bases[0].shape
    shapes = inner_shapes(len(bases) * pair_count, pno_count, pieces[0].shape[0])
    return pl.pallas_call(
        lambda *refs: project_kernel(len(bases), *refs),
        out_shape=tuple(jax.ShapeDtypeStruct(*x) for x in shapes),
        in_specs=vmem(len(bases) + len(pieces)),
        out_specs=tuple(vmem(2)),
        scratch_shapes=project_scratch(bases, pieces),
        compiler_params=pltpu.CompilerParams(vmem_limit_bytes=20 * 2**20),
        cost_estimate=pl.CostEstimate(flops=project_flops(bases, pieces), bytes_accessed=2**20, transcendentals=0),
    )(*bases, *pieces)


def finish_kernel(members, group_count, dom_count, *refs):
    count = len(members)
    groups, refs = refs[:2 * group_count], refs[2 * group_count:]
    bases, pieces, refs = refs[:count], refs[count:count + dom_count], refs[count + dom_count:]
    dressed, after, scratch = refs[:count], refs[count:2 * count], refs[2 * count:]
    inner_left, inner_right, square, moved, total = scratch[:5]
    project_all(bases, pieces, inner_left, inner_right, scratch[5:])
    groups = [*groups, inner_left, inner_right]
    group_count += 1
    pair_count, _, lane_count = dressed[0].shape
    pno_count = lane_count // 2
    half = pno_count // 2
    block_count = inner_left.shape[1] // pno_count
    group_total = lax.axis_size("blk")
    me = lax.axis_index("blk")
    pairs = [(index, pair) for index in range(count) for pair in range(pair_count)]

    def row_of(group, at):
        full = group < group_count - 1
        return members[at // pair_count] * pair_count + at % pair_count if full else at

    weights = []
    for index, member in enumerate(members):
        row = dressed[index][:, half:half + 1, :]
        lane = lax.broadcasted_iota(jnp.int32, row.shape, 2)
        for group in range(group_count):
            stop = lax.rem((me ^ member) + 2 * group_total + group * SET - me, group_total)
            for b in range(block_count):
                kept = jnp.where(lane == stop * block_count + b, row, 0.0)
                weights.append(jnp.sum(kept, axis=2, keepdims=True))
    for at, (index, pair) in enumerate(pairs):
        packed = dressed[index][pair, :half]
        other = pltpu.roll(packed, pno_count, 1)
        keep = left_lanes(packed)
        _, high, low = split(stack([jnp.where(keep, packed, other), jnp.where(keep, other, packed)]))
        square[at, :pno_count] = jnp.where(left_lanes(low), high, low).astype(jnp.bfloat16)
        square[at, pno_count:] = jnp.where(left_lanes(low), high, 0.0).astype(jnp.bfloat16)
    for at, (index, pair) in enumerate(pairs):
        for group in range(group_count):
            product = fold(dot(groups[2 * group][row_of(group, at)], square[at], NN))
            for b in range(block_count):
                weight = weights[(index * group_count + group) * block_count + b][pair]
                lanes = slice(b * lane_count, (b + 1) * lane_count)
                moved[at, group, :, lanes] = high_low(product[b * pno_count:(b + 1) * pno_count] * weight)
    for at, (index, pair) in enumerate(pairs):
        terms = [dot(moved[at, group], groups[2 * group + 1][row_of(group, at)], NT) for group in range(group_count)]
        total[at] = fold(sum(terms[1:], terms[0]))
    for at, (index, pair) in enumerate(pairs):
        rows = [total[at, pl.ds(i, half, stride=2), :] for i in range(2)]
        after[index][pair] = jnp.where(left_lanes(rows[0]), *rows)


def finish(members, groups, bases, pieces, dressed):
    pair_count, _, lane_count = dressed[0].shape
    pno_count = lane_count // 2
    pairs = len(members) * pair_count
    group_count = len(groups)
    block_count = pieces[0].shape[0]
    operands = [x for group in groups for x in group] + bases + pieces + dressed
    products = pairs * pno_count**3 * 2 * (group_count + 1) * block_count
    shapes = inner_shapes(pairs, pno_count, block_count)
    return pl.pallas_call(
        lambda *refs: finish_kernel(members, group_count, len(pieces), *refs),
        out_shape=[jax.ShapeDtypeStruct((pair_count, pno_count // 2, lane_count), jnp.float32)] * len(members),
        in_specs=vmem(len(operands)),
        out_specs=vmem(len(members)),
        scratch_shapes=[
            *[pltpu.VMEM(*x) for x in shapes],
            pltpu.VMEM((pairs, lane_count, lane_count), jnp.bfloat16),
            pltpu.VMEM((pairs, group_count + 1, pno_count, block_count * lane_count), jnp.bfloat16),
            pltpu.VMEM((pairs, pno_count, lane_count), jnp.float32),
            *project_scratch(bases, pieces),
        ],
        compiler_params=pltpu.CompilerParams(vmem_limit_bytes=24 * 2**20),
        cost_estimate=pl.CostEstimate(
            flops=project_flops(bases, pieces) + 6 * products, bytes_accessed=2**20, transcendentals=0
        ),
    )(*operands)


def gather_pieces(mine, axis):
    count = lax.axis_size(axis)
    up, down = [mine], []
    for shift in range(1, count):
        if shift <= count // 2:
            up.append(from_behind(up[-1], axis, 1))
        else:
            down.append(from_behind(down[-1] if down else mine, axis, count - 1))
    return up + down[::-1]


def on_device_shared(pno_basis, amplitudes, send_list, couple, couple_weight, fit_weight, fit_blocks):
    pair_count, pno_count, _ = pno_basis.shape
    group_total = lax.axis_size("blk")
    pieces = gather_pieces(fit_blocks, "dom")
    across = from_partner(pno_basis, "blk", 2)
    far = [([from_behind(fit_blocks, "blk", by)], by) for by in range(SET, group_total, SET)]
    sent = pack_pairs(send_list.reshape(-1), pno_basis, amplitudes)
    sent, *heads = lax.optimization_barrier((sent, *[group[0] for group, _ in far]))
    far = [([head], by) for head, (_, by) in zip(heads, far)]
    coupled = lax.all_to_all(sent, "blk", split_axis=0, concat_axis=0, tiled=True)
    across, pieces[1], pieces[-1] = lax.optimization_barrier((across, pieces[1], pieces[-1]))
    bases = [pno_basis, from_partner(pno_basis, "blk", 1), across, from_partner(across, "blk", 1)]
    coupled, *bases = lax.optimization_barrier((coupled, *bases))
    own, updated = dress(couple, couple_weight, fit_weight, pno_basis, amplitudes, coupled)
    last = len(pieces) // 2
    _, pieces[last] = lax.optimization_barrier((own, pieces[last]))
    groups = [pieces]
    for group, by in far:
        group += [from_behind(x, "blk", by) for x in pieces[1:]]
        if last > 1:
            source, pieces[-1] = lax.optimization_barrier((group[0], pieces[-1]))
            group[-1] = from_behind(source, "dom", len(pieces) - 1)
        groups.append(group)
    inner = [project(bases, group) for group in groups[:-1]]
    final = groups[-1]
    dressed = [own, *[from_partner(own, "blk", flip) for flip in range(1, SET)]]
    for members in ((2, 3), (0, 1)):
        partial = finish(
            members, inner, [bases[member] for member in members], final, [dressed[member] for member in members]
        )
        if members[0]:
            partial, *final = lax.optimization_barrier((partial, *final))
            for member, x in zip(members, partial):
                updated = updated + from_partner(x, "blk", member)
        else:
            mine, beside = partial
            updated, mine, beside = lax.optimization_barrier((updated, mine, from_partner(beside, "blk", 1)))
            updated = updated + mine + beside
    return updated.reshape(pair_count, pno_count * pno_count)


def dress_with(pair_amps, intersection, partner_amps, weights):
    half_product = jnp.einsum("pcab,pcbe->pcae", intersection, partner_amps, precision=HIGHEST)
    sandwich = jnp.einsum("pcae,pcfe->pcaf", half_product, intersection, precision=HIGHEST)
    return pair_amps + jnp.einsum("pc,pcaf->paf", weights, sandwich, precision=HIGHEST)


def fit_term(pair_basis, dressed, blocks, weights):
    pair_count, pno_count, orbital_count = pair_basis.shape
    flat_basis = pair_basis.reshape(pair_count * pno_count, orbital_count)
    stacked = blocks.reshape(2 * orbital_count, orbital_count)
    projected = jnp.dot(
        flat_basis, stacked.T, precision=HIGHEST, preferred_element_type=jnp.float32
    )
    projected = projected.reshape(pair_count, pno_count, 2, orbital_count)
    inner_blocks = jnp.einsum("par,pbmr->mpab", pair_basis, projected, precision=HIGHEST)
    left_product = jnp.einsum("pai,pij->paj", inner_blocks[0], dressed, precision=HIGHEST)
    fit_contrib = jnp.einsum("paj,pbj->pab", left_product, inner_blocks[1], precision=HIGHEST)
    return weights[:, None, None] * fit_contrib


def on_device_ring(pno_basis, amplitudes, send_list, couple, couple_weight, fit_weight, fit_blocks):
    pair_count, pno_count, _ = pno_basis.shape
    block_count = fit_blocks.shape[0]
    pair_amps = amplitudes.reshape(pair_count, pno_count, pno_count)
    send_order = send_list.reshape(-1)
    basis_in = lax.all_to_all(jnp.take(pno_basis, send_order, axis=0), "blk", split_axis=0, concat_axis=0, tiled=True)
    amps_in = lax.all_to_all(jnp.take(pair_amps, send_order, axis=0), "blk", split_axis=0, concat_axis=0, tiled=True)
    partner_basis = jnp.take(basis_in, couple, axis=0)
    intersection = jnp.einsum("par,pcbr->pcab", pno_basis, partner_basis, precision=HIGHEST)
    dressed = dress_with(pair_amps, intersection, jnp.take(amps_in, couple, axis=0), couple_weight)
    updated = dressed
    current = lax.all_gather(fit_blocks, "dom", axis=2, tiled=True)
    for stop in range(fit_weight.shape[1] // block_count):
        if stop > 0:
            current = from_behind(current, "blk", 1)
        for b in range(block_count):
            updated = updated + fit_term(pno_basis, dressed, current[b], fit_weight[:, stop * block_count + b])
    return updated.reshape(pair_count, pno_count * pno_count)


def solution(mesh):
    placed = (
        P(("blk", "dom"), None, None),
        P(("blk", "dom"), None),
        P("blk", "dom", None, None),
        P(("blk", "dom"), None),
        P(("blk", "dom"), None),
        P(("blk", "dom"), None),
        P("blk", None, "dom", None),
    )

    def on_device(*args):
        send_list, fit_weight, fit_blocks = args[2], args[5], args[6]
        group_total = mesh.shape["blk"]
        meets_all = fit_weight.shape[1] == group_total * fit_blocks.shape[0]
        if meets_all and group_total % SET == 0 and group_total > SET and group_total & (group_total - 1) == 0 and send_list.shape[3] == 1:
            return on_device_shared(*args)
        return on_device_ring(*args)

    return jax.shard_map(
        on_device, mesh=mesh, in_specs=placed, out_specs=P(("blk", "dom"), None), check_vma=False
    )
```

```python
import functools

import jax
import jax.numpy as jnp
from jax import lax
from jax.experimental import pallas as pl
from jax.experimental.pallas import tpu as pltpu
from jax.sharding import PartitionSpec as P

HIGHEST = lax.Precision.HIGHEST
SET = 4
NN = (((1,), (0,)), ((), ()))
NT = (((1,), (1,)), ((), ()))


def halves(x):
    high = x.astype(jnp.bfloat16)
    return high, (x - high.astype(jnp.float32)).astype(jnp.bfloat16)


def dot(a, b, dims):
    return lax.dot_general(a, b, dims, preferred_element_type=jnp.float32)


def dot3(a, b, dims):
    (a_high, a_low), (b_high, b_low) = a, b
    return dot(a_high, b_high, dims) + (dot(a_high, b_low, dims) + dot(a_low, b_high, dims))


def stack(parts, axis=0):
    return jnp.concatenate(parts, axis=axis)


def from_partner(x, axis, flip):
    return lax.ppermute(x, axis, [(i, i ^ flip) for i in range(lax.axis_size(axis))])


def from_behind(x, axis, by):
    count = lax.axis_size(axis)
    return lax.ppermute(x, axis, [(i, (i + by) % count) for i in range(count)])


def vmem(count):
    return [pl.BlockSpec(memory_space=pltpu.VMEM)] * count


def pack_kernel(send, basis, amps, out, rows, sent):
    peer_count, row_count, lane_count = rows.shape
    pno_count = out.shape[1] - row_count
    copies = []
    for peer in range(peer_count):
        copies.append(pltpu.make_async_copy(basis.at[send[peer]], out.at[peer, pl.ds(0, pno_count)], sent.at[0, peer]))
        copies[-1].start()
    for peer in range(peer_count):
        for i in range(row_count):
            rows[peer, i:i + 1, :] = amps[pl.ds(send[peer], 1), i * lane_count:(i + 1) * lane_count]
        copies.append(pltpu.make_async_copy(rows.at[peer], out.at[peer, pl.ds(pno_count, row_count)], sent.at[1, peer]))
        copies[-1].start()
    for copy in copies:
        copy.wait()


def pack_pairs(send_order, basis, amps):
    _, pno_count, orbital_count = basis.shape
    peer_count, rows = send_order.shape[0], amps.shape[1] // orbital_count
    return pl.pallas_call(
        pack_kernel,
        out_shape=jax.ShapeDtypeStruct((peer_count, pno_count + rows, orbital_count), jnp.float32),
        in_specs=[
            pl.BlockSpec(memory_space=pltpu.SMEM),
            pl.BlockSpec(memory_space=pl.ANY),
            *vmem(1),
        ],
        out_specs=pl.BlockSpec(memory_space=pl.ANY),
        scratch_shapes=[
            pltpu.VMEM((peer_count, rows, orbital_count), jnp.float32),
            pltpu.SemaphoreType.DMA((2, peer_count)),
        ],
        compiler_params=pltpu.CompilerParams(vmem_limit_bytes=60 * 2**20),
        cost_estimate=pl.CostEstimate(flops=0, bytes_accessed=4 * basis.size, transcendentals=0),
    )(send_order, basis, amps)


def dress_kernel(couple, couple_weight, fit_weight, basis, amps, coupled, dressed, result, turned, paired, partners):
    pair_count, pno_count, orbital_count = basis.shape
    half = pno_count // 2
    slot_count = coupled.shape[0]
    width = 2 * pno_count
    for i in range(half):
        paired[pl.ds(i, pair_count, stride=half), :] = amps[:, i * width:(i + 1) * width]
    for pair in range(pair_count):
        packed = paired[pair * half:(pair + 1) * half]
        for i in range(2):
            turned[pair, pl.ds(i, half, stride=2), :] = packed[:, i * pno_count:(i + 1) * pno_count]
    own = halves(basis[...].reshape(pair_count * pno_count, orbital_count))
    others = halves(coupled[:, :pno_count].reshape(slot_count * pno_count, orbital_count))
    overlap = halves(dot3(own, others, NT))
    left, slot_weight = [], []
    for slot in range(slot_count):
        cols = slice(slot * pno_count, (slot + 1) * pno_count)
        packed = coupled[slot, pno_count:]
        step = orbital_count // pno_count
        for i in range(step):
            lanes = slice(i * pno_count, (i + 1) * pno_count)
            partners[slot, pl.ds(i, packed.shape[0], stride=step), :] = packed[:, lanes]
        left.append(dot3([x[:, cols] for x in overlap], halves(partners[slot]), NN))
        named = jnp.where(couple[...] == slot, couple_weight[...], 0.0)
        slot_weight.append(jnp.sum(named, axis=1, keepdims=True))
    dressed[:, half:, :] = jnp.zeros((pair_count, dressed.shape[1] - half, 2 * pno_count), jnp.float32)
    for pair in range(pair_count):
        rows = slice(pair * pno_count, (pair + 1) * pno_count)
        scaled = stack([x[rows] * w[pair:pair + 1] for x, w in zip(left, slot_weight)], 1)
        total = turned[pair] + dot3(halves(scaled), [x[rows] for x in overlap], NT)
        dressed[pair, :half] = stack([total[:half], total[half:]], 1)
        turned[pair] = total
        result[pair] = two_to_one(turned, pair, half)
        dressed[pair, half:half + 1, : fit_weight.shape[1]] = fit_weight[pair:pair + 1, :]


def two_to_one(ref, pair, half):
    return stack([ref[pair, pl.ds(i, half, stride=2), :] for i in range(2)], 1)


def dress(couple, couple_weight, fit_weight, basis, amps, coupled):
    pair_count, pno_count, _ = basis.shape
    return pl.pallas_call(
        dress_kernel,
        out_shape=tuple(
            jax.ShapeDtypeStruct((pair_count, pno_count // 2 + more, 2 * pno_count), jnp.float32) for more in (8, 0)
        ),
        in_specs=vmem(6),
        out_specs=tuple(vmem(2)),
        scratch_shapes=[
            pltpu.VMEM((pair_count, pno_count, pno_count), jnp.float32),
            pltpu.VMEM((pair_count * pno_count // 2, 2 * pno_count), jnp.float32),
            pltpu.VMEM((coupled.shape[0], pno_count, pno_count), jnp.float32),
        ],
        compiler_params=pltpu.CompilerParams(vmem_limit_bytes=10 * 2**20),
        cost_estimate=pl.CostEstimate(flops=4 * 10**9, bytes_accessed=8 * basis.size, transcendentals=0),
    )(couple, couple_weight, fit_weight, basis, amps, coupled)


def fold(x):
    return x + pltpu.roll(x, x.shape[1] // 2, 1)


def left_lanes(x):
    return lax.broadcasted_iota(jnp.int32, x.shape, 1) < x.shape[1] // 2


def split(x):
    high = x.astype(jnp.bfloat16)
    wide = high.astype(jnp.float32)
    return high, wide, x - wide


def high_low(x):
    _, high, low = split(x)
    return jnp.where(left_lanes(x), high, low).astype(jnp.bfloat16)


def split_blocks(pieces, block_cat):
    dom_count = len(pieces)
    block_count, part_count, row_count, orbital_count = pieces[0].shape
    place = lax.axis_index("dom")
    for shift, piece in enumerate(pieces):
        start = lax.rem(place + dom_count - shift, dom_count) * row_count
        for b in range(block_count):
            for m in range(part_count):
                high, low = halves(piece[b, m])
                for i, x in enumerate((high, high, low)):
                    at = pl.multiple_of(start + i * orbital_count, row_count)
                    block_cat[m, b, pl.ds(at, row_count), :] = x


def split_basis(basis, wide):
    orbital_count = basis.shape[2]
    high, low = halves(basis[...])
    for i, x in enumerate((high, low, high)):
        wide[:, :, i * orbital_count:(i + 1) * orbital_count] = x


def project_slice(wide, block, projected, at):
    pair_count, pno_count, lane_count = wide.shape
    orbital_count = block.shape[1]
    basis = wide[...].reshape(pair_count * pno_count, lane_count)
    product = halves(dot(basis, block[...], NN).reshape(pair_count, pno_count, orbital_count))
    for i in range(2):
        projected[:, at:at + pno_count, i * orbital_count:(i + 1) * orbital_count] = product[i]


def inner_pair(wide, projected, inner_left, inner_right, pair, here):
    _, pno_count, lane_count = wide.shape
    orbital_count = lane_count // 3
    size = inner_left.shape[1]
    both = stack([wide[pair, :, i * orbital_count:(i + 1) * orbital_count] for i in range(2)])
    product = [projected[pair, :, i * orbital_count:(i + 1) * orbital_count] for i in range(2)]
    inner = fold(dot(product[0], both, NT) + dot(product[1], both, NT))
    inner_left[here] = high_low(inner[:size])
    high, _, low = split(inner[size:])
    low = jnp.where(left_lanes(low), low, 0.0).astype(jnp.bfloat16)
    for b in range(size // pno_count):
        rows = slice(b * pno_count, (b + 1) * pno_count)
        lanes = slice(b * 2 * pno_count, (b + 1) * 2 * pno_count)
        inner_right[here, :pno_count, lanes] = high[rows]
        inner_right[here, pno_count:, lanes] = low[rows]


def project_all(bases, pieces, inner_left, inner_right, scratch, meanwhile=()):
    block_cat, wide, projected = scratch
    pair_count, pno_count, _ = bases[0].shape
    part_count, block_count = block_cat.shape[:2]
    slices = [(m, b) for m in range(part_count) for b in range(block_count)]
    meanwhile = list(meanwhile)
    split_blocks(pieces, block_cat)
    for member in range(len(bases) + 1):
        if member < len(bases):
            split_basis(bases[member], wide.at[member % 2])
        for index, (m, b) in enumerate(slices):
            if member < len(bases):
                slot = member % 2
                project_slice(wide.at[slot], block_cat.at[m, b], projected.at[slot], index * pno_count)
            if member:
                slot, share = (member - 1) % 2, pair_count // len(slices)
                pairs = range(index * share, (index + 1) * share if index < len(slices) - 1 else pair_count)
                for pair in pairs:
                    here = (member - 1) * pair_count + pair
                    inner_pair(wide.at[slot], projected.at[slot], inner_left, inner_right, pair, here)
            else:
                share = -(-len(meanwhile) // len(slices))
                for work in meanwhile[index * share:(index + 1) * share]:
                    work()


def project_kernel(member_count, *refs):
    bases, refs = refs[:member_count], refs[member_count:]
    *pieces, inner_left, inner_right = refs[:-3]
    project_all(bases, pieces, inner_left, inner_right, refs[-3:])


def inner_shapes(pairs, pno_count, block_count):
    return (
        ((pairs, block_count * pno_count, 2 * pno_count), jnp.bfloat16),
        ((pairs, 2 * pno_count, block_count * 2 * pno_count), jnp.bfloat16),
    )


def project_scratch(bases, pieces):
    pair_count, pno_count, _ = bases[0].shape
    block_count, part_count, _, orbital_count = pieces[0].shape
    return [
        pltpu.VMEM((part_count, block_count, 3 * orbital_count, orbital_count), jnp.bfloat16),
        pltpu.VMEM((2, pair_count, pno_count, 3 * orbital_count), jnp.bfloat16),
        pltpu.VMEM((2, pair_count, part_count * block_count * pno_count, 2 * orbital_count), jnp.bfloat16),
    ]


def project_flops(bases, pieces):
    pair_count, pno_count, _ = bases[0].shape
    block_count, part_count, _, orbital_count = pieces[0].shape
    rows = len(bases) * pair_count * pno_count * block_count * part_count
    return 6 * rows * orbital_count * (orbital_count + pno_count)


def project(bases, pieces):
    pair_count, pno_count, _ = bases[0].shape
    shapes = inner_shapes(len(bases) * pair_count, pno_count, pieces[0].shape[0])
    return pl.pallas_call(
        lambda *refs: project_kernel(len(bases), *refs),
        out_shape=tuple(jax.ShapeDtypeStruct(*x) for x in shapes),
        in_specs=vmem(len(bases) + len(pieces)),
        out_specs=tuple(vmem(2)),
        scratch_shapes=project_scratch(bases, pieces),
        compiler_params=pltpu.CompilerParams(vmem_limit_bytes=20 * 2**20),
        cost_estimate=pl.CostEstimate(flops=project_flops(bases, pieces), bytes_accessed=2**20, transcendentals=0),
    )(*bases, *pieces)


def finish_kernel(members, group_count, dom_count, *refs):
    count = len(members)
    groups, refs = refs[:2 * group_count], refs[2 * group_count:]
    bases, pieces, refs = refs[:count], refs[count:count + dom_count], refs[count + dom_count:]
    dressed, after, scratch = refs[:count], refs[count:2 * count], refs[2 * count:]
    inner_left, inner_right, square, moved, total = scratch[:5]
    groups = [*groups, inner_left, inner_right]
    group_count += 1
    pair_count, _, lane_count = dressed[0].shape
    pno_count = lane_count // 2
    half = pno_count // 2
    block_count = inner_left.shape[1] // pno_count
    group_total = lax.axis_size("blk")
    me = lax.axis_index("blk")
    pairs = [(index, pair) for index in range(count) for pair in range(pair_count)]

    def row_of(group, at):
        full = group < group_count - 1
        return members[at // pair_count] * pair_count + at % pair_count if full else at

    weights = []
    for index, member in enumerate(members):
        row = dressed[index][:, half:half + 1, :]
        lane = lax.broadcasted_iota(jnp.int32, row.shape, 2)
        for group in range(group_count):
            stop = lax.rem((me ^ member) + 2 * group_total + group * SET - me, group_total)
            for b in range(block_count):
                kept = jnp.where(lane == stop * block_count + b, row, 0.0)
                weights.append(jnp.sum(kept, axis=2, keepdims=True))

    def square_of(at, index, pair):
        packed = dressed[index][pair, :half]
        other = pltpu.roll(packed, pno_count, 1)
        keep = left_lanes(packed)
        _, high, low = split(stack([jnp.where(keep, packed, other), jnp.where(keep, other, packed)]))
        square[at, :pno_count] = jnp.where(left_lanes(low), high, low).astype(jnp.bfloat16)
        square[at, pno_count:] = jnp.where(left_lanes(low), high, 0.0).astype(jnp.bfloat16)

    meanwhile = [functools.partial(square_of, at, *x) for at, x in enumerate(pairs)]
    project_all(bases, pieces, inner_left, inner_right, scratch[5:], meanwhile)
    for at, (index, pair) in enumerate(pairs):
        for group in range(group_count):
            product = fold(dot(groups[2 * group][row_of(group, at)], square[at], NN))
            for b in range(block_count):
                weight = weights[(index * group_count + group) * block_count + b][pair]
                lanes = slice(b * lane_count, (b + 1) * lane_count)
                moved[at, group, :, lanes] = high_low(product[b * pno_count:(b + 1) * pno_count] * weight)
    for at, (index, pair) in enumerate(pairs):
        terms = [dot(moved[at, group], groups[2 * group + 1][row_of(group, at)], NT) for group in range(group_count)]
        total[at] = fold(sum(terms[1:], terms[0]))
    for at, (index, pair) in enumerate(pairs):
        rows = [total[at, pl.ds(i, half, stride=2), :] for i in range(2)]
        after[index][pair] = jnp.where(left_lanes(rows[0]), *rows)


def finish(members, groups, bases, pieces, dressed):
    pair_count, _, lane_count = dressed[0].shape
    pno_count = lane_count // 2
    pairs = len(members) * pair_count
    group_count = len(groups)
    block_count = pieces[0].shape[0]
    operands = [x for group in groups for x in group] + bases + pieces + dressed
    products = pairs * pno_count**3 * 2 * (group_count + 1) * block_count
    shapes = inner_shapes(pairs, pno_count, block_count)
    return pl.pallas_call(
        lambda *refs: finish_kernel(members, group_count, len(pieces), *refs),
        out_shape=[jax.ShapeDtypeStruct((pair_count, pno_count // 2, lane_count), jnp.float32)] * len(members),
        in_specs=vmem(len(operands)),
        out_specs=vmem(len(members)),
        scratch_shapes=[
            *[pltpu.VMEM(*x) for x in shapes],
            pltpu.VMEM((pairs, lane_count, lane_count), jnp.bfloat16),
            pltpu.VMEM((pairs, group_count + 1, pno_count, block_count * lane_count), jnp.bfloat16),
            pltpu.VMEM((pairs, pno_count, lane_count), jnp.float32),
            *project_scratch(bases, pieces),
        ],
        compiler_params=pltpu.CompilerParams(vmem_limit_bytes=24 * 2**20),
        cost_estimate=pl.CostEstimate(
            flops=project_flops(bases, pieces) + 6 * products, bytes_accessed=2**20, transcendentals=0
        ),
    )(*operands)


def gather_pieces(mine, axis):
    count = lax.axis_size(axis)
    up, down = [mine], []
    for shift in range(1, count):
        if shift <= count // 2:
            up.append(from_behind(up[-1], axis, 1))
        else:
            down.append(from_behind(down[-1] if down else mine, axis, count - 1))
    return up + down[::-1]


def on_device_shared(pno_basis, amplitudes, send_list, couple, couple_weight, fit_weight, fit_blocks):
    pair_count, pno_count, _ = pno_basis.shape
    group_total = lax.axis_size("blk")
    pieces = gather_pieces(fit_blocks, "dom")
    across = from_partner(pno_basis, "blk", 2)
    far = [([from_behind(fit_blocks, "blk", by)], by) for by in range(SET, group_total, SET)]
    sent = pack_pairs(send_list.reshape(-1), pno_basis, amplitudes)
    sent, *heads = lax.optimization_barrier((sent, *[group[0] for group, _ in far]))
    far = [([head], by) for head, (_, by) in zip(heads, far)]
    coupled = lax.all_to_all(sent, "blk", split_axis=0, concat_axis=0, tiled=True)
    across, pieces[1], pieces[-1] = lax.optimization_barrier((across, pieces[1], pieces[-1]))
    bases = [pno_basis, from_partner(pno_basis, "blk", 1), across, from_partner(across, "blk", 1)]
    coupled, *bases = lax.optimization_barrier((coupled, *bases))
    own, updated = dress(couple, couple_weight, fit_weight, pno_basis, amplitudes, coupled)
    last = len(pieces) // 2
    _, pieces[last] = lax.optimization_barrier((own, pieces[last]))
    groups = [pieces]
    for group, by in far:
        group += [from_behind(x, "blk", by) for x in pieces[1:]]
        if last > 1:
            source, pieces[-1] = lax.optimization_barrier((group[0], pieces[-1]))
            group[-1] = from_behind(source, "dom", len(pieces) - 1)
        groups.append(group)
    inner = [project(bases, group) for group in groups[:-1]]
    final = groups[-1]
    dressed = [own, *[from_partner(own, "blk", flip) for flip in range(1, SET)]]
    for members in ((2, 3), (0, 1)):
        partial = finish(
            members, inner, [bases[member] for member in members], final, [dressed[member] for member in members]
        )
        if members[0]:
            partial, *final = lax.optimization_barrier((partial, *final))
            for member, x in zip(members, partial):
                updated = updated + from_partner(x, "blk", member)
        else:
            mine, beside = partial
            updated, mine, beside = lax.optimization_barrier((updated, mine, from_partner(beside, "blk", 1)))
            updated = updated + mine + beside
    return updated.reshape(pair_count, pno_count * pno_count)


def dress_with(pair_amps, intersection, partner_amps, weights):
    half_product = jnp.einsum("pcab,pcbe->pcae", intersection, partner_amps, precision=HIGHEST)
    sandwich = jnp.einsum("pcae,pcfe->pcaf", half_product, intersection, precision=HIGHEST)
    return pair_amps + jnp.einsum("pc,pcaf->paf", weights, sandwich, precision=HIGHEST)


def fit_term(pair_basis, dressed, blocks, weights):
    pair_count, pno_count, orbital_count = pair_basis.shape
    flat_basis = pair_basis.reshape(pair_count * pno_count, orbital_count)
    stacked = blocks.reshape(2 * orbital_count, orbital_count)
    projected = jnp.dot(
        flat_basis, stacked.T, precision=HIGHEST, preferred_element_type=jnp.float32
    )
    projected = projected.reshape(pair_count, pno_count, 2, orbital_count)
    inner_blocks = jnp.einsum("par,pbmr->mpab", pair_basis, projected, precision=HIGHEST)
    left_product = jnp.einsum("pai,pij->paj", inner_blocks[0], dressed, precision=HIGHEST)
    fit_contrib = jnp.einsum("paj,pbj->pab", left_product, inner_blocks[1], precision=HIGHEST)
    return weights[:, None, None] * fit_contrib


def on_device_ring(pno_basis, amplitudes, send_list, couple, couple_weight, fit_weight, fit_blocks):
    pair_count, pno_count, _ = pno_basis.shape
    block_count = fit_blocks.shape[0]
    pair_amps = amplitudes.reshape(pair_count, pno_count, pno_count)
    send_order = send_list.reshape(-1)
    basis_in = lax.all_to_all(jnp.take(pno_basis, send_order, axis=0), "blk", split_axis=0, concat_axis=0, tiled=True)
    amps_in = lax.all_to_all(jnp.take(pair_amps, send_order, axis=0), "blk", split_axis=0, concat_axis=0, tiled=True)
    partner_basis = jnp.take(basis_in, couple, axis=0)
    intersection = jnp.einsum("par,pcbr->pcab", pno_basis, partner_basis, precision=HIGHEST)
    dressed = dress_with(pair_amps, intersection, jnp.take(amps_in, couple, axis=0), couple_weight)
    updated = dressed
    current = lax.all_gather(fit_blocks, "dom", axis=2, tiled=True)
    for stop in range(fit_weight.shape[1] // block_count):
        if stop > 0:
            current = from_behind(current, "blk", 1)
        for b in range(block_count):
            updated = updated + fit_term(pno_basis, dressed, current[b], fit_weight[:, stop * block_count + b])
    return updated.reshape(pair_count, pno_count * pno_count)


def solution(mesh):
    placed = (
        P(("blk", "dom"), None, None),
        P(("blk", "dom"), None),
        P("blk", "dom", None, None),
        P(("blk", "dom"), None),
        P(("blk", "dom"), None),
        P(("blk", "dom"), None),
        P("blk", None, "dom", None),
    )

    def on_device(*args):
        send_list, fit_weight, fit_blocks = args[2], args[5], args[6]
        group_total = mesh.shape["blk"]
        meets_all = fit_weight.shape[1] == group_total * fit_blocks.shape[0]
        if meets_all and group_total % SET == 0 and group_total > SET and group_total & (group_total - 1) == 0 and send_list.shape[3] == 1:
            return on_device_shared(*args)
        return on_device_ring(*args)

    return jax.shard_map(
        on_device, mesh=mesh, in_specs=placed, out_specs=P(("blk", "dom"), None), check_vma=False
    )
```

```python
import jax
import jax.numpy as jnp
from jax import lax
from jax.experimental import pallas as pl
from jax.experimental.pallas import tpu as pltpu
from jax.sharding import PartitionSpec as P

HIGHEST = lax.Precision.HIGHEST
SET = 4
NN = (((1,), (0,)), ((), ()))
NT = (((1,), (1,)), ((), ()))


def halves(x):
    high = x.astype(jnp.bfloat16)
    return high, (x - high.astype(jnp.float32)).astype(jnp.bfloat16)


def dot(a, b, dims):
    return lax.dot_general(a, b, dims, preferred_element_type=jnp.float32)


def dot3(a, b, dims):
    (a_high, a_low), (b_high, b_low) = a, b
    return dot(a_high, b_high, dims) + (dot(a_high, b_low, dims) + dot(a_low, b_high, dims))


def stack(parts, axis=0):
    return jnp.concatenate(parts, axis=axis)


def from_partner(x, axis, flip):
    return lax.ppermute(x, axis, [(i, i ^ flip) for i in range(lax.axis_size(axis))])


def from_behind(x, axis, by):
    count = lax.axis_size(axis)
    return lax.ppermute(x, axis, [(i, (i + by) % count) for i in range(count)])


def vmem(count):
    return [pl.BlockSpec(memory_space=pltpu.VMEM)] * count


def pack_kernel(send, basis, amps, out):
    peer_count, row_count, lane_count = out.shape
    pno_count = basis.shape[1]
    for peer in range(peer_count):
        pair = send[peer]
        out[peer, :pno_count] = basis[pair]
        for i in range(row_count - pno_count):
            at = pno_count + i
            out[peer, at:at + 1, :] = amps[pl.ds(pair, 1), i * lane_count:(i + 1) * lane_count]


def pack_pairs(send_order, basis, amps):
    _, pno_count, orbital_count = basis.shape
    rows = pno_count + amps.shape[1] // orbital_count
    return pl.pallas_call(
        pack_kernel,
        out_shape=jax.ShapeDtypeStruct((send_order.shape[0], rows, orbital_count), jnp.float32),
        in_specs=[pl.BlockSpec(memory_space=pltpu.SMEM), *vmem(2)],
        out_specs=vmem(1)[0],
        compiler_params=pltpu.CompilerParams(vmem_limit_bytes=60 * 2**20),
        cost_estimate=pl.CostEstimate(flops=0, bytes_accessed=4 * basis.size, transcendentals=0),
    )(send_order, basis, amps)


def dress_kernel(couple, couple_weight, fit_weight, basis, amps, coupled, dressed, result, turned, paired, partners):
    pair_count, pno_count, orbital_count = basis.shape
    half = pno_count // 2
    slot_count = coupled.shape[0]
    width = 2 * pno_count
    for i in range(half):
        paired[pl.ds(i, pair_count, stride=half), :] = amps[:, i * width:(i + 1) * width]
    for pair in range(pair_count):
        packed = paired[pair * half:(pair + 1) * half]
        for i in range(2):
            turned[pair, pl.ds(i, half, stride=2), :] = packed[:, i * pno_count:(i + 1) * pno_count]
    own = halves(basis[...].reshape(pair_count * pno_count, orbital_count))
    others = halves(coupled[:, :pno_count].reshape(slot_count * pno_count, orbital_count))
    overlap = halves(dot3(own, others, NT))
    left, slot_weight = [], []
    for slot in range(slot_count):
        cols = slice(slot * pno_count, (slot + 1) * pno_count)
        packed = coupled[slot, pno_count:]
        step = orbital_count // pno_count
        for i in range(step):
            lanes = slice(i * pno_count, (i + 1) * pno_count)
            partners[slot, pl.ds(i, packed.shape[0], stride=step), :] = packed[:, lanes]
        left.append(dot3([x[:, cols] for x in overlap], halves(partners[slot]), NN))
        named = jnp.where(couple[...] == slot, couple_weight[...], 0.0)
        slot_weight.append(jnp.sum(named, axis=1, keepdims=True))
    dressed[:, half:, :] = jnp.zeros((pair_count, dressed.shape[1] - half, 2 * pno_count), jnp.float32)
    for pair in range(pair_count):
        rows = slice(pair * pno_count, (pair + 1) * pno_count)
        scaled = stack([x[rows] * w[pair:pair + 1] for x, w in zip(left, slot_weight)], 1)
        total = turned[pair] + dot3(halves(scaled), [x[rows] for x in overlap], NT)
        dressed[pair, :half] = stack([total[:half], total[half:]], 1)
        turned[pair] = total
        result[pair] = two_to_one(turned, pair, half)
        dressed[pair, half:half + 1, : fit_weight.shape[1]] = fit_weight[pair:pair + 1, :]


def two_to_one(ref, pair, half):
    return stack([ref[pair, pl.ds(i, half, stride=2), :] for i in range(2)], 1)


def dress(couple, couple_weight, fit_weight, basis, amps, coupled):
    pair_count, pno_count, _ = basis.shape
    return pl.pallas_call(
        dress_kernel,
        out_shape=tuple(
            jax.ShapeDtypeStruct((pair_count, pno_count // 2 + more, 2 * pno_count), jnp.float32) for more in (8, 0)
        ),
        in_specs=vmem(6),
        out_specs=tuple(vmem(2)),
        scratch_shapes=[
            pltpu.VMEM((pair_count, pno_count, pno_count), jnp.float32),
            pltpu.VMEM((pair_count * pno_count // 2, 2 * pno_count), jnp.float32),
            pltpu.VMEM((coupled.shape[0], pno_count, pno_count), jnp.float32),
        ],
        compiler_params=pltpu.CompilerParams(vmem_limit_bytes=10 * 2**20),
        cost_estimate=pl.CostEstimate(flops=4 * 10**9, bytes_accessed=8 * basis.size, transcendentals=0),
    )(couple, couple_weight, fit_weight, basis, amps, coupled)


def fold(x):
    return x + pltpu.roll(x, x.shape[1] // 2, 1)


def left_lanes(x):
    return lax.broadcasted_iota(jnp.int32, x.shape, 1) < x.shape[1] // 2


def split(x):
    high = x.astype(jnp.bfloat16)
    wide = high.astype(jnp.float32)
    return high, wide, x - wide


def high_low(x):
    _, high, low = split(x)
    return jnp.where(left_lanes(x), high, low).astype(jnp.bfloat16)


def split_blocks(pieces, block_cat):
    dom_count = len(pieces)
    block_count, part_count, row_count, orbital_count = pieces[0].shape
    place = lax.axis_index("dom")
    for shift, piece in enumerate(pieces):
        start = lax.rem(place + dom_count - shift, dom_count) * row_count
        for b in range(block_count):
            for m in range(part_count):
                high, low = halves(piece[b, m])
                for i, x in enumerate((high, high, low)):
                    at = pl.multiple_of(start + i * orbital_count, row_count)
                    block_cat[m, b, pl.ds(at, row_count), :] = x


def split_basis(basis, wide):
    orbital_count = basis.shape[2]
    high, low = halves(basis[...])
    for i, x in enumerate((high, low, high)):
        wide[:, :, i * orbital_count:(i + 1) * orbital_count] = x


def project_slice(wide, block, projected, at):
    pair_count, pno_count, lane_count = wide.shape
    orbital_count = block.shape[1]
    basis = wide[...].reshape(pair_count * pno_count, lane_count)
    product = halves(dot(basis, block[...], NN).reshape(pair_count, pno_count, orbital_count))
    for i in range(2):
        projected[:, at:at + pno_count, i * orbital_count:(i + 1) * orbital_count] = product[i]


def inner_pair(wide, projected, inner_left, inner_right, pair, here):
    _, pno_count, lane_count = wide.shape
    orbital_count = lane_count // 3
    size = inner_left.shape[1]
    both = stack([wide[pair, :, i * orbital_count:(i + 1) * orbital_count] for i in range(2)])
    product = [projected[pair, :, i * orbital_count:(i + 1) * orbital_count] for i in range(2)]
    inner = fold(dot(product[0], both, NT) + dot(product[1], both, NT))
    inner_left[here] = high_low(inner[:size])
    high, _, low = split(inner[size:])
    low = jnp.where(left_lanes(low), low, 0.0).astype(jnp.bfloat16)
    for b in range(size // pno_count):
        rows = slice(b * pno_count, (b + 1) * pno_count)
        lanes = slice(b * 2 * pno_count, (b + 1) * 2 * pno_count)
        inner_right[here, :pno_count, lanes] = high[rows]
        inner_right[here, pno_count:, lanes] = low[rows]


def project_all(bases, pieces, inner_left, inner_right, scratch):
    block_cat, wide, projected = scratch
    pair_count, pno_count, _ = bases[0].shape
    part_count, block_count = block_cat.shape[:2]
    split_blocks(pieces, block_cat)
    for member, basis in enumerate(bases):
        split_basis(basis, wide.at[pl.ds(member * pair_count, pair_count)])
    for m in range(part_count):
        for b in range(block_count):
            project_slice(wide, block_cat.at[m, b], projected, (m * block_count + b) * pno_count)
    for pair in range(len(bases) * pair_count):
        inner_pair(wide, projected, inner_left, inner_right, pair, pair)


def project_kernel(member_count, *refs):
    bases, refs = refs[:member_count], refs[member_count:]
    *pieces, inner_left, inner_right = refs[:-3]
    project_all(bases, pieces, inner_left, inner_right, refs[-3:])


def inner_shapes(pairs, pno_count, block_count):
    return (
        ((pairs, block_count * pno_count, 2 * pno_count), jnp.bfloat16),
        ((pairs, 2 * pno_count, block_count * 2 * pno_count), jnp.bfloat16),
    )


def project_scratch(bases, pieces):
    pair_count, pno_count, _ = bases[0].shape
    block_count, part_count, _, orbital_count = pieces[0].shape
    return [
        pltpu.VMEM((part_count, block_count, 3 * orbital_count, orbital_count), jnp.bfloat16),
        pltpu.VMEM((len(bases) * pair_count, pno_count, 3 * orbital_count), jnp.bfloat16),
        pltpu.VMEM((len(bases) * pair_count, part_count * block_count * pno_count, 2 * orbital_count), jnp.bfloat16),
    ]


def project_flops(bases, pieces):
    pair_count, pno_count, _ = bases[0].shape
    block_count, part_count, _, orbital_count = pieces[0].shape
    rows = len(bases) * pair_count * pno_count * block_count * part_count
    return 6 * rows * orbital_count * (orbital_count + pno_count)


def project(bases, pieces):
    pair_count, pno_count, _ = bases[0].shape
    shapes = inner_shapes(len(bases) * pair_count, pno_count, pieces[0].shape[0])
    return pl.pallas_call(
        lambda *refs: project_kernel(len(bases), *refs),
        out_shape=tuple(jax.ShapeDtypeStruct(*x) for x in shapes),
        in_specs=vmem(len(bases) + len(pieces)),
        out_specs=tuple(vmem(2)),
        scratch_shapes=project_scratch(bases, pieces),
        compiler_params=pltpu.CompilerParams(vmem_limit_bytes=28 * 2**20),
        cost_estimate=pl.CostEstimate(flops=project_flops(bases, pieces), bytes_accessed=2**20, transcendentals=0),
    )(*bases, *pieces)


def finish_kernel(members, group_count, dom_count, *refs):
    count = len(members)
    groups, refs = refs[:2 * group_count], refs[2 * group_count:]
    bases, pieces, refs = refs[:count], refs[count:count + dom_count], refs[count + dom_count:]
    dressed, after, scratch = refs[:count], refs[count:2 * count], refs[2 * count:]
    inner_left, inner_right, square, moved, total = scratch[:5]
    groups = [*groups, inner_left, inner_right]
    group_count += 1
    pair_count, _, lane_count = dressed[0].shape
    pno_count = lane_count // 2
    half = pno_count // 2
    block_count = inner_left.shape[1] // pno_count
    group_total = lax.axis_size("blk")
    me = lax.axis_index("blk")
    pairs = [(index, pair) for index in range(count) for pair in range(pair_count)]

    def row_of(group, at):
        full = group < group_count - 1
        return members[at // pair_count] * pair_count + at % pair_count if full else at

    weights = []
    for index, member in enumerate(members):
        row = dressed[index][:, half:half + 1, :]
        lane = lax.broadcasted_iota(jnp.int32, row.shape, 2)
        for group in range(group_count):
            stop = lax.rem((me ^ member) + 2 * group_total + group * SET - me, group_total)
            for b in range(block_count):
                kept = jnp.where(lane == stop * block_count + b, row, 0.0)
                weights.append(jnp.sum(kept, axis=2, keepdims=True))
    project_all(bases, pieces, inner_left, inner_right, scratch[5:])
    for at, (index, pair) in enumerate(pairs):
        packed = dressed[index][pair, :half]
        other = pltpu.roll(packed, pno_count, 1)
        keep = left_lanes(packed)
        _, high, low = split(stack([jnp.where(keep, packed, other), jnp.where(keep, other, packed)]))
        square[at, :pno_count] = jnp.where(left_lanes(low), high, low).astype(jnp.bfloat16)
        square[at, pno_count:] = jnp.where(left_lanes(low), high, 0.0).astype(jnp.bfloat16)
    for at, (index, pair) in enumerate(pairs):
        for group in range(group_count):
            product = fold(dot(groups[2 * group][row_of(group, at)], square[at], NN))
            for b in range(block_count):
                weight = weights[(index * group_count + group) * block_count + b][pair]
                lanes = slice(b * lane_count, (b + 1) * lane_count)
                moved[at, group, :, lanes] = high_low(product[b * pno_count:(b + 1) * pno_count] * weight)
    for at, (index, pair) in enumerate(pairs):
        terms = [dot(moved[at, group], groups[2 * group + 1][row_of(group, at)], NT) for group in range(group_count)]
        total[at] = fold(sum(terms[1:], terms[0]))
    for at, (index, pair) in enumerate(pairs):
        rows = [total[at, pl.ds(i, half, stride=2), :] for i in range(2)]
        after[index][pair] = jnp.where(left_lanes(rows[0]), *rows)


def finish(members, groups, bases, pieces, dressed):
    pair_count, _, lane_count = dressed[0].shape
    pno_count = lane_count // 2
    pairs = len(members) * pair_count
    group_count = len(groups)
    block_count = pieces[0].shape[0]
    operands = [x for group in groups for x in group] + bases + pieces + dressed
    products = pairs * pno_count**3 * 2 * (group_count + 1) * block_count
    shapes = inner_shapes(pairs, pno_count, block_count)
    return pl.pallas_call(
        lambda *refs: finish_kernel(members, group_count, len(pieces), *refs),
        out_shape=[jax.ShapeDtypeStruct((pair_count, pno_count // 2, lane_count), jnp.float32)] * len(members),
        in_specs=vmem(len(operands)),
        out_specs=vmem(len(members)),
        scratch_shapes=[
            *[pltpu.VMEM(*x) for x in shapes],
            pltpu.VMEM((pairs, lane_count, lane_count), jnp.bfloat16),
            pltpu.VMEM((pairs, group_count + 1, pno_count, block_count * lane_count), jnp.bfloat16),
            pltpu.VMEM((pairs, pno_count, lane_count), jnp.float32),
            *project_scratch(bases, pieces),
        ],
        compiler_params=pltpu.CompilerParams(vmem_limit_bytes=24 * 2**20),
        cost_estimate=pl.CostEstimate(
            flops=project_flops(bases, pieces) + 6 * products, bytes_accessed=2**20, transcendentals=0
        ),
    )(*operands)


def gather_pieces(mine, axis):
    count = lax.axis_size(axis)
    up, down = [mine], []
    for shift in range(1, count):
        if shift <= (count - 1) // 2:
            up.append(from_behind(up[-1], axis, 1))
        else:
            down.append(from_behind(down[-1] if down else mine, axis, count - 1))
    return up + down[::-1]


def on_device_shared(pno_basis, amplitudes, send_list, couple, couple_weight, fit_weight, fit_blocks):
    pair_count, pno_count, _ = pno_basis.shape
    group_total = lax.axis_size("blk")
    pieces = gather_pieces(fit_blocks, "dom")
    across = from_partner(pno_basis, "blk", 2)
    far = [([from_behind(fit_blocks, "blk", by)], by) for by in range(SET, group_total, SET)]
    sent = pack_pairs(send_list.reshape(-1), pno_basis, amplitudes)
    sent, *heads = lax.optimization_barrier((sent, *[group[0] for group, _ in far]))
    far = [([head], by) for head, (_, by) in zip(heads, far)]
    coupled = lax.all_to_all(sent, "blk", split_axis=0, concat_axis=0, tiled=True)
    across, pieces[1], pieces[-1] = lax.optimization_barrier((across, pieces[1], pieces[-1]))
    bases = [pno_basis, from_partner(pno_basis, "blk", 1), across, from_partner(across, "blk", 1)]
    coupled, *bases = lax.optimization_barrier((coupled, *bases))
    own, updated = dress(couple, couple_weight, fit_weight, pno_basis, amplitudes, coupled)
    last = len(pieces) // 2
    _, pieces[last] = lax.optimization_barrier((own, pieces[last]))
    groups = [pieces]
    for group, by in far:
        group += [from_behind(x, "blk", by) for x in pieces[1:]]
        if last > 1:
            source, pieces[-1] = lax.optimization_barrier((group[0], pieces[-1]))
            group[-1] = from_behind(source, "dom", len(pieces) - 1)
        groups.append(group)
    inner = [project(bases, group) for group in groups[:-1]]
    final = groups[-1]
    dressed = [own, *[from_partner(own, "blk", flip) for flip in range(1, SET)]]
    for members in ((2, 3), (0, 1)):
        partial = finish(
            members, inner, [bases[member] for member in members], final, [dressed[member] for member in members]
        )
        if members[0]:
            partial, *final = lax.optimization_barrier((partial, *final))
            for member, x in zip(members, partial):
                updated = updated + from_partner(x, "blk", member)
        else:
            mine, beside = partial
            updated, mine, beside = lax.optimization_barrier((updated, mine, from_partner(beside, "blk", 1)))
            updated = updated + mine + beside
    return updated.reshape(pair_count, pno_count * pno_count)


def dress_with(pair_amps, intersection, partner_amps, weights):
    half_product = jnp.einsum("pcab,pcbe->pcae", intersection, partner_amps, precision=HIGHEST)
    sandwich = jnp.einsum("pcae,pcfe->pcaf", half_product, intersection, precision=HIGHEST)
    return pair_amps + jnp.einsum("pc,pcaf->paf", weights, sandwich, precision=HIGHEST)


def fit_term(pair_basis, dressed, blocks, weights):
    pair_count, pno_count, orbital_count = pair_basis.shape
    flat_basis = pair_basis.reshape(pair_count * pno_count, orbital_count)
    stacked = blocks.reshape(2 * orbital_count, orbital_count)
    projected = jnp.dot(
        flat_basis, stacked.T, precision=HIGHEST, preferred_element_type=jnp.float32
    )
    projected = projected.reshape(pair_count, pno_count, 2, orbital_count)
    inner_blocks = jnp.einsum("par,pbmr->mpab", pair_basis, projected, precision=HIGHEST)
    left_product = jnp.einsum("pai,pij->paj", inner_blocks[0], dressed, precision=HIGHEST)
    fit_contrib = jnp.einsum("paj,pbj->pab", left_product, inner_blocks[1], precision=HIGHEST)
    return weights[:, None, None] * fit_contrib


def on_device_ring(pno_basis, amplitudes, send_list, couple, couple_weight, fit_weight, fit_blocks):
    pair_count, pno_count, _ = pno_basis.shape
    block_count = fit_blocks.shape[0]
    pair_amps = amplitudes.reshape(pair_count, pno_count, pno_count)
    send_order = send_list.reshape(-1)
    basis_in = lax.all_to_all(jnp.take(pno_basis, send_order, axis=0), "blk", split_axis=0, concat_axis=0, tiled=True)
    amps_in = lax.all_to_all(jnp.take(pair_amps, send_order, axis=0), "blk", split_axis=0, concat_axis=0, tiled=True)
    partner_basis = jnp.take(basis_in, couple, axis=0)
    intersection = jnp.einsum("par,pcbr->pcab", pno_basis, partner_basis, precision=HIGHEST)
    dressed = dress_with(pair_amps, intersection, jnp.take(amps_in, couple, axis=0), couple_weight)
    updated = dressed
    current = lax.all_gather(fit_blocks, "dom", axis=2, tiled=True)
    for stop in range(fit_weight.shape[1] // block_count):
        if stop > 0:
            current = from_behind(current, "blk", 1)
        for b in range(block_count):
            updated = updated + fit_term(pno_basis, dressed, current[b], fit_weight[:, stop * block_count + b])
    return updated.reshape(pair_count, pno_count * pno_count)


def solution(mesh):
    placed = (
        P(("blk", "dom"), None, None),
        P(("blk", "dom"), None),
        P("blk", "dom", None, None),
        P(("blk", "dom"), None),
        P(("blk", "dom"), None),
        P(("blk", "dom"), None),
        P("blk", None, "dom", None),
    )

    def on_device(*args):
        send_list, fit_weight, fit_blocks = args[2], args[5], args[6]
        group_total = mesh.shape["blk"]
        meets_all = fit_weight.shape[1] == group_total * fit_blocks.shape[0]
        if meets_all and group_total % SET == 0 and group_total > SET and group_total & (group_total - 1) == 0 and send_list.shape[3] == 1:
            return on_device_shared(*args)
        return on_device_ring(*args)

    return jax.shard_map(
        on_device, mesh=mesh, in_specs=placed, out_specs=P(("blk", "dom"), None), check_vma=False
    )
```

```python
import jax
import jax.numpy as jnp
from jax import lax
from jax.experimental import pallas as pl
from jax.experimental.pallas import tpu as pltpu
from jax.sharding import PartitionSpec as P

HIGHEST = lax.Precision.HIGHEST
SET = 4
NN = (((1,), (0,)), ((), ()))
NT = (((1,), (1,)), ((), ()))


def halves(x):
    high = x.astype(jnp.bfloat16)
    return high, (x - high.astype(jnp.float32)).astype(jnp.bfloat16)


def dot(a, b, dims):
    return lax.dot_general(a, b, dims, preferred_element_type=jnp.float32)


def dot3(a, b, dims):
    (a_high, a_low), (b_high, b_low) = a, b
    return dot(a_high, b_high, dims) + (dot(a_high, b_low, dims) + dot(a_low, b_high, dims))


def stack(parts, axis=0):
    return jnp.concatenate(parts, axis=axis)


def from_partner(x, axis, flip):
    return lax.ppermute(x, axis, [(i, i ^ flip) for i in range(lax.axis_size(axis))])


def from_behind(x, axis, by):
    count = lax.axis_size(axis)
    return lax.ppermute(x, axis, [(i, (i + by) % count) for i in range(count)])


def vmem(count):
    return [pl.BlockSpec(memory_space=pltpu.VMEM)] * count


def pack_kernel(send, basis, amps, out):
    peer_count, row_count, lane_count = out.shape
    pno_count = basis.shape[1]
    for peer in range(peer_count):
        pair = send[peer]
        out[peer, :pno_count] = basis[pair]
        for i in range(row_count - pno_count):
            at = pno_count + i
            out[peer, at:at + 1, :] = amps[pl.ds(pair, 1), i * lane_count:(i + 1) * lane_count]


def pack_pairs(send_order, basis, amps):
    _, pno_count, orbital_count = basis.shape
    rows = pno_count + amps.shape[1] // orbital_count
    return pl.pallas_call(
        pack_kernel,
        out_shape=jax.ShapeDtypeStruct((send_order.shape[0], rows, orbital_count), jnp.float32),
        in_specs=[pl.BlockSpec(memory_space=pltpu.SMEM), *vmem(2)],
        out_specs=vmem(1)[0],
        compiler_params=pltpu.CompilerParams(vmem_limit_bytes=60 * 2**20),
        cost_estimate=pl.CostEstimate(flops=0, bytes_accessed=4 * basis.size, transcendentals=0),
    )(send_order, basis, amps)


def dress_kernel(couple, couple_weight, fit_weight, basis, amps, coupled, dressed, result, turned, paired, partners):
    pair_count, pno_count, orbital_count = basis.shape
    half = pno_count // 2
    slot_count = coupled.shape[0]
    width = 2 * pno_count
    for i in range(half):
        paired[pl.ds(i, pair_count, stride=half), :] = amps[:, i * width:(i + 1) * width]
    for pair in range(pair_count):
        packed = paired[pair * half:(pair + 1) * half]
        for i in range(2):
            turned[pair, pl.ds(i, half, stride=2), :] = packed[:, i * pno_count:(i + 1) * pno_count]
    own = halves(basis[...].reshape(pair_count * pno_count, orbital_count))
    others = halves(coupled[:, :pno_count].reshape(slot_count * pno_count, orbital_count))
    overlap = halves(dot3(own, others, NT))
    left, slot_weight = [], []
    for slot in range(slot_count):
        cols = slice(slot * pno_count, (slot + 1) * pno_count)
        packed = coupled[slot, pno_count:]
        step = orbital_count // pno_count
        for i in range(step):
            lanes = slice(i * pno_count, (i + 1) * pno_count)
            partners[slot, pl.ds(i, packed.shape[0], stride=step), :] = packed[:, lanes]
        left.append(dot3([x[:, cols] for x in overlap], halves(partners[slot]), NN))
        named = jnp.where(couple[...] == slot, couple_weight[...], 0.0)
        slot_weight.append(jnp.sum(named, axis=1, keepdims=True))
    dressed[:, half:, :] = jnp.zeros((pair_count, dressed.shape[1] - half, 2 * pno_count), jnp.float32)
    for pair in range(pair_count):
        rows = slice(pair * pno_count, (pair + 1) * pno_count)
        scaled = stack([x[rows] * w[pair:pair + 1] for x, w in zip(left, slot_weight)], 1)
        total = turned[pair] + dot3(halves(scaled), [x[rows] for x in overlap], NT)
        dressed[pair, :half] = stack([total[:half], total[half:]], 1)
        turned[pair] = total
        result[pair] = two_to_one(turned, pair, half)
        dressed[pair, half:half + 1, : fit_weight.shape[1]] = fit_weight[pair:pair + 1, :]


def two_to_one(ref, pair, half):
    return stack([ref[pair, pl.ds(i, half, stride=2), :] for i in range(2)], 1)


def dress(couple, couple_weight, fit_weight, basis, amps, coupled):
    pair_count, pno_count, _ = basis.shape
    return pl.pallas_call(
        dress_kernel,
        out_shape=tuple(
            jax.ShapeDtypeStruct((pair_count, pno_count // 2 + more, 2 * pno_count), jnp.float32) for more in (8, 0)
        ),
        in_specs=vmem(6),
        out_specs=tuple(vmem(2)),
        scratch_shapes=[
            pltpu.VMEM((pair_count, pno_count, pno_count), jnp.float32),
            pltpu.VMEM((pair_count * pno_count // 2, 2 * pno_count), jnp.float32),
            pltpu.VMEM((coupled.shape[0], pno_count, pno_count), jnp.float32),
        ],
        compiler_params=pltpu.CompilerParams(vmem_limit_bytes=10 * 2**20),
        cost_estimate=pl.CostEstimate(flops=4 * 10**9, bytes_accessed=8 * basis.size, transcendentals=0),
    )(couple, couple_weight, fit_weight, basis, amps, coupled)


def fold(x):
    return x + pltpu.roll(x, x.shape[1] // 2, 1)


def left_lanes(x):
    return lax.broadcasted_iota(jnp.int32, x.shape, 1) < x.shape[1] // 2


def split(x):
    high = x.astype(jnp.bfloat16)
    wide = high.astype(jnp.float32)
    return high, wide, x - wide


def high_low(x):
    _, high, low = split(x)
    return jnp.where(left_lanes(x), high, low).astype(jnp.bfloat16)


def split_blocks(pieces, block_cat):
    dom_count = len(pieces)
    block_count, part_count, row_count, orbital_count = pieces[0].shape
    place = lax.axis_index("dom")
    for shift, piece in enumerate(pieces):
        start = lax.rem(place + dom_count - shift, dom_count) * row_count
        for b in range(block_count):
            for m in range(part_count):
                high, low = halves(piece[b, m])
                for i, x in enumerate((high, high, low)):
                    at = pl.multiple_of(start + i * orbital_count, row_count)
                    block_cat[m, b, pl.ds(at, row_count), :] = x


def split_basis(basis, wide):
    orbital_count = basis.shape[2]
    high, low = halves(basis[...])
    for i, x in enumerate((high, low, high)):
        wide[:, :, i * orbital_count:(i + 1) * orbital_count] = x


def project_slice(wide, block, projected, at):
    pair_count, pno_count, lane_count = wide.shape
    orbital_count = block.shape[1]
    basis = wide[...].reshape(pair_count * pno_count, lane_count)
    product = halves(dot(basis, block[...], NN).reshape(pair_count, pno_count, orbital_count))
    for i in range(2):
        projected[:, at:at + pno_count, i * orbital_count:(i + 1) * orbital_count] = product[i]


def inner_pair(wide, projected, inner_left, inner_right, pair, here):
    _, pno_count, lane_count = wide.shape
    orbital_count = lane_count // 3
    size = inner_left.shape[1]
    both = stack([wide[pair, :, i * orbital_count:(i + 1) * orbital_count] for i in range(2)])
    product = [projected[pair, :, i * orbital_count:(i + 1) * orbital_count] for i in range(2)]
    inner = fold(dot(product[0], both, NT) + dot(product[1], both, NT))
    inner_left[here] = high_low(inner[:size])
    high, _, low = split(inner[size:])
    low = jnp.where(left_lanes(low), low, 0.0).astype(jnp.bfloat16)
    for b in range(size // pno_count):
        rows = slice(b * pno_count, (b + 1) * pno_count)
        lanes = slice(b * 2 * pno_count, (b + 1) * 2 * pno_count)
        inner_right[here, :pno_count, lanes] = high[rows]
        inner_right[here, pno_count:, lanes] = low[rows]


def project_all(bases, pieces, inner_left, inner_right, scratch):
    block_cat, wide, projected = scratch
    pair_count, pno_count, _ = bases[0].shape
    part_count, block_count = block_cat.shape[:2]
    split_blocks(pieces, block_cat)
    for member, basis in enumerate(bases):
        split_basis(basis, wide.at[pl.ds(member * pair_count, pair_count)])
    for m in range(part_count):
        for b in range(block_count):
            project_slice(wide, block_cat.at[m, b], projected, (m * block_count + b) * pno_count)
    for pair in range(len(bases) * pair_count):
        inner_pair(wide, projected, inner_left, inner_right, pair, pair)


def project_kernel(member_count, *refs):
    bases, refs = refs[:member_count], refs[member_count:]
    *pieces, inner_left, inner_right = refs[:-3]
    project_all(bases, pieces, inner_left, inner_right, refs[-3:])


def inner_shapes(pairs, pno_count, block_count):
    return (
        ((pairs, block_count * pno_count, 2 * pno_count), jnp.bfloat16),
        ((pairs, 2 * pno_count, block_count * 2 * pno_count), jnp.bfloat16),
    )


def project_scratch(bases, pieces):
    pair_count, pno_count, _ = bases[0].shape
    block_count, part_count, _, orbital_count = pieces[0].shape
    return [
        pltpu.VMEM((part_count, block_count, 3 * orbital_count, orbital_count), jnp.bfloat16),
        pltpu.VMEM((len(bases) * pair_count, pno_count, 3 * orbital_count), jnp.bfloat16),
        pltpu.VMEM((len(bases) * pair_count, part_count * block_count * pno_count, 2 * orbital_count), jnp.bfloat16),
    ]


def project_flops(bases, pieces):
    pair_count, pno_count, _ = bases[0].shape
    block_count, part_count, _, orbital_count = pieces[0].shape
    rows = len(bases) * pair_count * pno_count * block_count * part_count
    return 6 * rows * orbital_count * (orbital_count + pno_count)


def project(bases, pieces):
    pair_count, pno_count, _ = bases[0].shape
    shapes = inner_shapes(len(bases) * pair_count, pno_count, pieces[0].shape[0])
    return pl.pallas_call(
        lambda *refs: project_kernel(len(bases), *refs),
        out_shape=tuple(jax.ShapeDtypeStruct(*x) for x in shapes),
        in_specs=vmem(len(bases) + len(pieces)),
        out_specs=tuple(vmem(2)),
        scratch_shapes=project_scratch(bases, pieces),
        compiler_params=pltpu.CompilerParams(vmem_limit_bytes=28 * 2**20),
        cost_estimate=pl.CostEstimate(flops=project_flops(bases, pieces), bytes_accessed=2**20, transcendentals=0),
    )(*bases, *pieces)


def finish_kernel(members, group_count, dom_count, *refs):
    count = len(members)
    groups, refs = refs[:2 * group_count], refs[2 * group_count:]
    bases, pieces, refs = refs[:count], refs[count:count + dom_count], refs[count + dom_count:]
    dressed, after, scratch = refs[:count], refs[count:2 * count], refs[2 * count:]
    inner_left, inner_right, square, moved, total = scratch[:5]
    groups = [*groups, inner_left, inner_right]
    group_count += 1
    pair_count, _, lane_count = dressed[0].shape
    pno_count = lane_count // 2
    half = pno_count // 2
    block_count = inner_left.shape[1] // pno_count
    group_total = lax.axis_size("blk")
    me = lax.axis_index("blk")
    pairs = [(index, pair) for index in range(count) for pair in range(pair_count)]

    def row_of(group, at):
        full = group < group_count - 1
        return members[at // pair_count] * pair_count + at % pair_count if full else at

    weights = []
    for index, member in enumerate(members):
        row = dressed[index][:, half:half + 1, :]
        lane = lax.broadcasted_iota(jnp.int32, row.shape, 2)
        for group in range(group_count):
            stop = lax.rem((me ^ member) + 2 * group_total + group * SET - me, group_total)
            for b in range(block_count):
                kept = jnp.where(lane == stop * block_count + b, row, 0.0)
                weights.append(jnp.sum(kept, axis=2, keepdims=True))
    project_all(bases, pieces, inner_left, inner_right, scratch[5:])
    for at, (index, pair) in enumerate(pairs):
        packed = dressed[index][pair, :half]
        other = pltpu.roll(packed, pno_count, 1)
        keep = left_lanes(packed)
        _, high, low = split(stack([jnp.where(keep, packed, other), jnp.where(keep, other, packed)]))
        square[at, :pno_count] = jnp.where(left_lanes(low), high, low).astype(jnp.bfloat16)
        square[at, pno_count:] = jnp.where(left_lanes(low), high, 0.0).astype(jnp.bfloat16)
    for at, (index, pair) in enumerate(pairs):
        for group in range(group_count):
            product = fold(dot(groups[2 * group][row_of(group, at)], square[at], NN))
            for b in range(block_count):
                weight = weights[(index * group_count + group) * block_count + b][pair]
                lanes = slice(b * lane_count, (b + 1) * lane_count)
                moved[at, group, :, lanes] = high_low(product[b * pno_count:(b + 1) * pno_count] * weight)
    for at, (index, pair) in enumerate(pairs):
        terms = [dot(moved[at, group], groups[2 * group + 1][row_of(group, at)], NT) for group in range(group_count)]
        total[at] = fold(sum(terms[1:], terms[0]))
    for at, (index, pair) in enumerate(pairs):
        rows = [total[at, pl.ds(i, half, stride=2), :] for i in range(2)]
        after[index][pair] = jnp.where(left_lanes(rows[0]), *rows)


def finish(members, groups, bases, pieces, dressed):
    pair_count, _, lane_count = dressed[0].shape
    pno_count = lane_count // 2
    pairs = len(members) * pair_count
    group_count = len(groups)
    block_count = pieces[0].shape[0]
    operands = [x for group in groups for x in group] + bases + pieces + dressed
    products = pairs * pno_count**3 * 2 * (group_count + 1) * block_count
    shapes = inner_shapes(pairs, pno_count, block_count)
    return pl.pallas_call(
        lambda *refs: finish_kernel(members, group_count, len(pieces), *refs),
        out_shape=[jax.ShapeDtypeStruct((pair_count, pno_count // 2, lane_count), jnp.float32)] * len(members),
        in_specs=vmem(len(operands)),
        out_specs=vmem(len(members)),
        scratch_shapes=[
            *[pltpu.VMEM(*x) for x in shapes],
            pltpu.VMEM((pairs, lane_count, lane_count), jnp.bfloat16),
            pltpu.VMEM((pairs, group_count + 1, pno_count, block_count * lane_count), jnp.bfloat16),
            pltpu.VMEM((pairs, pno_count, lane_count), jnp.float32),
            *project_scratch(bases, pieces),
        ],
        compiler_params=pltpu.CompilerParams(vmem_limit_bytes=24 * 2**20),
        cost_estimate=pl.CostEstimate(
            flops=project_flops(bases, pieces) + 6 * products, bytes_accessed=2**20, transcendentals=0
        ),
    )(*operands)


def gather_pieces(mine, axis):
    count = lax.axis_size(axis)
    up, down = [mine], []
    for shift in range(1, count):
        if shift <= count // 2:
            up.append(from_behind(up[-1], axis, 1))
        else:
            down.append(from_behind(down[-1] if down else mine, axis, count - 1))
    return up + down[::-1]


def on_device_shared(pno_basis, amplitudes, send_list, couple, couple_weight, fit_weight, fit_blocks):
    pair_count, pno_count, _ = pno_basis.shape
    group_total = lax.axis_size("blk")
    pieces = gather_pieces(fit_blocks, "dom")
    across = from_partner(pno_basis, "blk", 2)
    far = [([from_behind(fit_blocks, "blk", by)], by) for by in range(SET, group_total, SET)]
    sent = pack_pairs(send_list.reshape(-1), pno_basis, amplitudes)
    sent, *heads = lax.optimization_barrier((sent, *[group[0] for group, _ in far]))
    far = [([head], by) for head, (_, by) in zip(heads, far)]
    coupled = lax.all_to_all(sent, "blk", split_axis=0, concat_axis=0, tiled=True)
    across, pieces[1] = lax.optimization_barrier((across, pieces[1]))
    bases = [pno_basis, from_partner(pno_basis, "blk", 1), across, from_partner(across, "blk", 1)]
    coupled, *bases = lax.optimization_barrier((coupled, *bases))
    own, updated = dress(couple, couple_weight, fit_weight, pno_basis, amplitudes, coupled)
    last = len(pieces) // 2
    _, pieces[last] = lax.optimization_barrier((own, pieces[last]))
    groups = [pieces]
    for group, by in far:
        group += [from_behind(x, "blk", by) for x in pieces[1:]]
        if last > 1:
            source, pieces[-1] = lax.optimization_barrier((group[0], pieces[-1]))
            group[-1] = from_behind(source, "dom", len(pieces) - 1)
        groups.append(group)
    inner = [project(bases, group) for group in groups[:-1]]
    final = groups[-1]
    dressed = [own, *[from_partner(own, "blk", flip) for flip in range(1, SET)]]
    for members in ((2, 3), (0, 1)):
        partial = finish(
            members, inner, [bases[member] for member in members], final, [dressed[member] for member in members]
        )
        if members[0]:
            partial, *final = lax.optimization_barrier((partial, *final))
            for member, x in zip(members, partial):
                updated = updated + from_partner(x, "blk", member)
        else:
            mine, beside = partial
            updated, mine, beside = lax.optimization_barrier((updated, mine, from_partner(beside, "blk", 1)))
            updated = updated + mine + beside
    return updated.reshape(pair_count, pno_count * pno_count)


def dress_with(pair_amps, intersection, partner_amps, weights):
    half_product = jnp.einsum("pcab,pcbe->pcae", intersection, partner_amps, precision=HIGHEST)
    sandwich = jnp.einsum("pcae,pcfe->pcaf", half_product, intersection, precision=HIGHEST)
    return pair_amps + jnp.einsum("pc,pcaf->paf", weights, sandwich, precision=HIGHEST)


def fit_term(pair_basis, dressed, blocks, weights):
    pair_count, pno_count, orbital_count = pair_basis.shape
    flat_basis = pair_basis.reshape(pair_count * pno_count, orbital_count)
    stacked = blocks.reshape(2 * orbital_count, orbital_count)
    projected = jnp.dot(
        flat_basis, stacked.T, precision=HIGHEST, preferred_element_type=jnp.float32
    )
    projected = projected.reshape(pair_count, pno_count, 2, orbital_count)
    inner_blocks = jnp.einsum("par,pbmr->mpab", pair_basis, projected, precision=HIGHEST)
    left_product = jnp.einsum("pai,pij->paj", inner_blocks[0], dressed, precision=HIGHEST)
    fit_contrib = jnp.einsum("paj,pbj->pab", left_product, inner_blocks[1], precision=HIGHEST)
    return weights[:, None, None] * fit_contrib


def on_device_ring(pno_basis, amplitudes, send_list, couple, couple_weight, fit_weight, fit_blocks):
    pair_count, pno_count, _ = pno_basis.shape
    block_count = fit_blocks.shape[0]
    pair_amps = amplitudes.reshape(pair_count, pno_count, pno_count)
    send_order = send_list.reshape(-1)
    basis_in = lax.all_to_all(jnp.take(pno_basis, send_order, axis=0), "blk", split_axis=0, concat_axis=0, tiled=True)
    amps_in = lax.all_to_all(jnp.take(pair_amps, send_order, axis=0), "blk", split_axis=0, concat_axis=0, tiled=True)
    partner_basis = jnp.take(basis_in, couple, axis=0)
    intersection = jnp.einsum("par,pcbr->pcab", pno_basis, partner_basis, precision=HIGHEST)
    dressed = dress_with(pair_amps, intersection, jnp.take(amps_in, couple, axis=0), couple_weight)
    updated = dressed
    current = lax.all_gather(fit_blocks, "dom", axis=2, tiled=True)
    for stop in range(fit_weight.shape[1] // block_count):
        if stop > 0:
            current = from_behind(current, "blk", 1)
        for b in range(block_count):
            updated = updated + fit_term(pno_basis, dressed, current[b], fit_weight[:, stop * block_count + b])
    return updated.reshape(pair_count, pno_count * pno_count)


def solution(mesh):
    placed = (
        P(("blk", "dom"), None, None),
        P(("blk", "dom"), None),
        P("blk", "dom", None, None),
        P(("blk", "dom"), None),
        P(("blk", "dom"), None),
        P(("blk", "dom"), None),
        P("blk", None, "dom", None),
    )

    def on_device(*args):
        send_list, fit_weight, fit_blocks = args[2], args[5], args[6]
        group_total = mesh.shape["blk"]
        meets_all = fit_weight.shape[1] == group_total * fit_blocks.shape[0]
        if meets_all and group_total % SET == 0 and group_total > SET and group_total & (group_total - 1) == 0 and send_list.shape[3] == 1:
            return on_device_shared(*args)
        return on_device_ring(*args)

    return jax.shard_map(
        on_device, mesh=mesh, in_specs=placed, out_specs=P(("blk", "dom"), None), check_vma=False
    )
```

```python
import jax
import jax.numpy as jnp
from jax import lax
from jax.experimental import pallas as pl
from jax.experimental.pallas import tpu as pltpu
from jax.sharding import PartitionSpec as P

HIGHEST = lax.Precision.HIGHEST
SET = 4
NN = (((1,), (0,)), ((), ()))
NT = (((1,), (1,)), ((), ()))


def halves(x):
    high = x.astype(jnp.bfloat16)
    return high, (x - high.astype(jnp.float32)).astype(jnp.bfloat16)


def dot(a, b, dims):
    return lax.dot_general(a, b, dims, preferred_element_type=jnp.float32)


def dot3(a, b, dims):
    (a_high, a_low), (b_high, b_low) = a, b
    return dot(a_high, b_high, dims) + (dot(a_high, b_low, dims) + dot(a_low, b_high, dims))


def stack(parts, axis=0):
    return jnp.concatenate(parts, axis=axis)


def from_partner(x, axis, flip):
    return lax.ppermute(x, axis, [(i, i ^ flip) for i in range(lax.axis_size(axis))])


def from_behind(x, axis, by):
    count = lax.axis_size(axis)
    return lax.ppermute(x, axis, [(i, (i + by) % count) for i in range(count)])


def vmem(count):
    return [pl.BlockSpec(memory_space=pltpu.VMEM)] * count


def pack_kernel(send, basis, amps, out):
    peer_count, row_count, lane_count = out.shape
    pno_count = basis.shape[1]
    for peer in range(peer_count):
        pair = send[peer]
        out[peer, :pno_count] = basis[pair]
        for i in range(row_count - pno_count):
            at = pno_count + i
            out[peer, at:at + 1, :] = amps[pl.ds(pair, 1), i * lane_count:(i + 1) * lane_count]


def pack_pairs(send_order, basis, amps):
    _, pno_count, orbital_count = basis.shape
    rows = pno_count + amps.shape[1] // orbital_count
    return pl.pallas_call(
        pack_kernel,
        out_shape=jax.ShapeDtypeStruct((send_order.shape[0], rows, orbital_count), jnp.float32),
        in_specs=[pl.BlockSpec(memory_space=pltpu.SMEM), *vmem(2)],
        out_specs=vmem(1)[0],
        compiler_params=pltpu.CompilerParams(vmem_limit_bytes=62 * 2**20),
        cost_estimate=pl.CostEstimate(flops=0, bytes_accessed=4 * basis.size, transcendentals=0),
    )(send_order, basis, amps)


def dress_kernel(couple, couple_weight, fit_weight, basis, amps, coupled, dressed, result, turned, paired, partners):
    pair_count, pno_count, orbital_count = basis.shape
    half = pno_count // 2
    slot_count = coupled.shape[0]
    width = 2 * pno_count
    for i in range(half):
        paired[pl.ds(i, pair_count, stride=half), :] = amps[:, i * width:(i + 1) * width]
    for pair in range(pair_count):
        packed = paired[pair * half:(pair + 1) * half]
        for i in range(2):
            turned[pair, pl.ds(i, half, stride=2), :] = packed[:, i * pno_count:(i + 1) * pno_count]
    own = halves(basis[...].reshape(pair_count * pno_count, orbital_count))
    others = halves(coupled[:, :pno_count].reshape(slot_count * pno_count, orbital_count))
    overlap = halves(dot3(own, others, NT))
    left, slot_weight = [], []
    for slot in range(slot_count):
        cols = slice(slot * pno_count, (slot + 1) * pno_count)
        packed = coupled[slot, pno_count:]
        step = orbital_count // pno_count
        for i in range(step):
            lanes = slice(i * pno_count, (i + 1) * pno_count)
            partners[slot, pl.ds(i, packed.shape[0], stride=step), :] = packed[:, lanes]
        left.append(dot3([x[:, cols] for x in overlap], halves(partners[slot]), NN))
        named = jnp.where(couple[...] == slot, couple_weight[...], 0.0)
        slot_weight.append(jnp.sum(named, axis=1, keepdims=True))
    dressed[:, half:, :] = jnp.zeros((pair_count, dressed.shape[1] - half, 2 * pno_count), jnp.float32)
    for pair in range(pair_count):
        rows = slice(pair * pno_count, (pair + 1) * pno_count)
        scaled = stack([x[rows] * w[pair:pair + 1] for x, w in zip(left, slot_weight)], 1)
        total = turned[pair] + dot3(halves(scaled), [x[rows] for x in overlap], NT)
        dressed[pair, :half] = stack([total[:half], total[half:]], 1)
        turned[pair] = total
        result[pair] = two_to_one(turned, pair, half)
        dressed[pair, half:half + 1, : fit_weight.shape[1]] = fit_weight[pair:pair + 1, :]


def two_to_one(ref, pair, half):
    return stack([ref[pair, pl.ds(i, half, stride=2), :] for i in range(2)], 1)


def dress(couple, couple_weight, fit_weight, basis, amps, coupled):
    pair_count, pno_count, _ = basis.shape
    return pl.pallas_call(
        dress_kernel,
        out_shape=tuple(
            jax.ShapeDtypeStruct((pair_count, pno_count // 2 + more, 2 * pno_count), jnp.float32) for more in (8, 0)
        ),
        in_specs=vmem(6),
        out_specs=tuple(vmem(2)),
        scratch_shapes=[
            pltpu.VMEM((pair_count, pno_count, pno_count), jnp.float32),
            pltpu.VMEM((pair_count * pno_count // 2, 2 * pno_count), jnp.float32),
            pltpu.VMEM((coupled.shape[0], pno_count, pno_count), jnp.float32),
        ],
        compiler_params=pltpu.CompilerParams(vmem_limit_bytes=10 * 2**20),
        cost_estimate=pl.CostEstimate(flops=4 * 10**9, bytes_accessed=8 * basis.size, transcendentals=0),
    )(couple, couple_weight, fit_weight, basis, amps, coupled)


def fold(x):
    return x + pltpu.roll(x, x.shape[1] // 2, 1)


def left_lanes(x):
    return lax.broadcasted_iota(jnp.int32, x.shape, 1) < x.shape[1] // 2


def split(x):
    high = x.astype(jnp.bfloat16)
    wide = high.astype(jnp.float32)
    return high, wide, x - wide


def high_low(x):
    _, high, low = split(x)
    return jnp.where(left_lanes(x), high, low).astype(jnp.bfloat16)


def split_blocks(pieces, block_cat):
    dom_count = len(pieces)
    block_count, part_count, row_count, orbital_count = pieces[0].shape
    place = lax.axis_index("dom")
    for shift, piece in enumerate(pieces):
        start = lax.rem(place + dom_count - shift, dom_count) * row_count
        for b in range(block_count):
            for m in range(part_count):
                high, low = halves(piece[b, m])
                for i, x in enumerate((high, high, low)):
                    at = pl.multiple_of(start + i * orbital_count, row_count)
                    block_cat[m, b, pl.ds(at, row_count), :] = x


def split_basis(basis, wide):
    orbital_count = basis.shape[2]
    high, low = halves(basis[...])
    for i, x in enumerate((high, low, high)):
        wide[:, :, i * orbital_count:(i + 1) * orbital_count] = x


def project_slice(wide, block, projected, at):
    pair_count, pno_count, lane_count = wide.shape
    orbital_count = block.shape[1]
    basis = wide[...].reshape(pair_count * pno_count, lane_count)
    product = halves(dot(basis, block[...], NN).reshape(pair_count, pno_count, orbital_count))
    for i in range(2):
        projected[:, at:at + pno_count, i * orbital_count:(i + 1) * orbital_count] = product[i]


def inner_pair(wide, projected, inner_left, inner_right, pair, here):
    _, pno_count, lane_count = wide.shape
    orbital_count = lane_count // 3
    size = inner_left.shape[1]
    both = stack([wide[pair, :, i * orbital_count:(i + 1) * orbital_count] for i in range(2)])
    product = [projected[pair, :, i * orbital_count:(i + 1) * orbital_count] for i in range(2)]
    inner = fold(dot(product[0], both, NT) + dot(product[1], both, NT))
    inner_left[here] = high_low(inner[:size])
    high, _, low = split(inner[size:])
    low = jnp.where(left_lanes(low), low, 0.0).astype(jnp.bfloat16)
    for b in range(size // pno_count):
        rows = slice(b * pno_count, (b + 1) * pno_count)
        lanes = slice(b * 2 * pno_count, (b + 1) * 2 * pno_count)
        inner_right[here, :pno_count, lanes] = high[rows]
        inner_right[here, pno_count:, lanes] = low[rows]


def project_all(bases, pieces, inner_left, inner_right, scratch):
    block_cat, wide, projected = scratch
    pair_count, pno_count, _ = bases[0].shape
    part_count, block_count = block_cat.shape[:2]
    split_blocks(pieces, block_cat)
    for member, basis in enumerate(bases):
        split_basis(basis, wide.at[pl.ds(member * pair_count, pair_count)])
    for m in range(part_count):
        for b in range(block_count):
            project_slice(wide, block_cat.at[m, b], projected, (m * block_count + b) * pno_count)
    for pair in range(len(bases) * pair_count):
        inner_pair(wide, projected, inner_left, inner_right, pair, pair)


def project_kernel(member_count, *refs):
    bases, refs = refs[:member_count], refs[member_count:]
    *pieces, inner_left, inner_right = refs[:-3]
    project_all(bases, pieces, inner_left, inner_right, refs[-3:])


def inner_shapes(pairs, pno_count, block_count):
    return (
        ((pairs, block_count * pno_count, 2 * pno_count), jnp.bfloat16),
        ((pairs, 2 * pno_count, block_count * 2 * pno_count), jnp.bfloat16),
    )


def project_scratch(bases, pieces):
    pair_count, pno_count, _ = bases[0].shape
    block_count, part_count, _, orbital_count = pieces[0].shape
    return [
        pltpu.VMEM((part_count, block_count, 3 * orbital_count, orbital_count), jnp.bfloat16),
        pltpu.VMEM((len(bases) * pair_count, pno_count, 3 * orbital_count), jnp.bfloat16),
        pltpu.VMEM((len(bases) * pair_count, part_count * block_count * pno_count, 2 * orbital_count), jnp.bfloat16),
    ]


def project_flops(bases, pieces):
    pair_count, pno_count, _ = bases[0].shape
    block_count, part_count, _, orbital_count = pieces[0].shape
    rows = len(bases) * pair_count * pno_count * block_count * part_count
    return 6 * rows * orbital_count * (orbital_count + pno_count)


def project(bases, pieces):
    pair_count, pno_count, _ = bases[0].shape
    shapes = inner_shapes(len(bases) * pair_count, pno_count, pieces[0].shape[0])
    return pl.pallas_call(
        lambda *refs: project_kernel(len(bases), *refs),
        out_shape=tuple(jax.ShapeDtypeStruct(*x) for x in shapes),
        in_specs=vmem(len(bases) + len(pieces)),
        out_specs=tuple(vmem(2)),
        scratch_shapes=project_scratch(bases, pieces),
        compiler_params=pltpu.CompilerParams(vmem_limit_bytes=28 * 2**20),
        cost_estimate=pl.CostEstimate(flops=project_flops(bases, pieces), bytes_accessed=2**20, transcendentals=0),
    )(*bases, *pieces)


def finish_kernel(members, group_count, dom_count, *refs):
    count = len(members)
    groups, refs = refs[:2 * group_count], refs[2 * group_count:]
    bases, pieces, refs = refs[:count], refs[count:count + dom_count], refs[count + dom_count:]
    dressed, after, scratch = refs[:count], refs[count:2 * count], refs[2 * count:]
    inner_left, inner_right, square, moved, total = scratch[:5]
    groups = [*groups, inner_left, inner_right]
    group_count += 1
    pair_count, _, lane_count = dressed[0].shape
    pno_count = lane_count // 2
    half = pno_count // 2
    block_count = inner_left.shape[1] // pno_count
    group_total = lax.axis_size("blk")
    me = lax.axis_index("blk")
    pairs = [(index, pair) for index in range(count) for pair in range(pair_count)]

    def row_of(group, at):
        full = group < group_count - 1
        return members[at // pair_count] * pair_count + at % pair_count if full else at

    weights = []
    for index, member in enumerate(members):
        row = dressed[index][:, half:half + 1, :]
        lane = lax.broadcasted_iota(jnp.int32, row.shape, 2)
        for group in range(group_count):
            stop = lax.rem((me ^ member) + 2 * group_total + group * SET - me, group_total)
            for b in range(block_count):
                kept = jnp.where(lane == stop * block_count + b, row, 0.0)
                weights.append(jnp.sum(kept, axis=2, keepdims=True))
    project_all(bases, pieces, inner_left, inner_right, scratch[5:])
    for at, (index, pair) in enumerate(pairs):
        packed = dressed[index][pair, :half]
        other = pltpu.roll(packed, pno_count, 1)
        keep = left_lanes(packed)
        _, high, low = split(stack([jnp.where(keep, packed, other), jnp.where(keep, other, packed)]))
        square[at, :pno_count] = jnp.where(left_lanes(low), high, low).astype(jnp.bfloat16)
        square[at, pno_count:] = jnp.where(left_lanes(low), high, 0.0).astype(jnp.bfloat16)
    for at, (index, pair) in enumerate(pairs):
        for group in range(group_count):
            product = fold(dot(groups[2 * group][row_of(group, at)], square[at], NN))
            for b in range(block_count):
                weight = weights[(index * group_count + group) * block_count + b][pair]
                lanes = slice(b * lane_count, (b + 1) * lane_count)
                moved[at, group, :, lanes] = high_low(product[b * pno_count:(b + 1) * pno_count] * weight)
    for at, (index, pair) in enumerate(pairs):
        terms = [dot(moved[at, group], groups[2 * group + 1][row_of(group, at)], NT) for group in range(group_count)]
        total[at] = fold(sum(terms[1:], terms[0]))
    for at, (index, pair) in enumerate(pairs):
        rows = [total[at, pl.ds(i, half, stride=2), :] for i in range(2)]
        after[index][pair] = jnp.where(left_lanes(rows[0]), *rows)


def finish(members, groups, bases, pieces, dressed):
    pair_count, _, lane_count = dressed[0].shape
    pno_count = lane_count // 2
    pairs = len(members) * pair_count
    group_count = len(groups)
    block_count = pieces[0].shape[0]
    operands = [x for group in groups for x in group] + bases + pieces + dressed
    products = pairs * pno_count**3 * 2 * (group_count + 1) * block_count
    shapes = inner_shapes(pairs, pno_count, block_count)
    return pl.pallas_call(
        lambda *refs: finish_kernel(members, group_count, len(pieces), *refs),
        out_shape=[jax.ShapeDtypeStruct((pair_count, pno_count // 2, lane_count), jnp.float32)] * len(members),
        in_specs=vmem(len(operands)),
        out_specs=vmem(len(members)),
        scratch_shapes=[
            *[pltpu.VMEM(*x) for x in shapes],
            pltpu.VMEM((pairs, lane_count, lane_count), jnp.bfloat16),
            pltpu.VMEM((pairs, group_count + 1, pno_count, block_count * lane_count), jnp.bfloat16),
            pltpu.VMEM((pairs, pno_count, lane_count), jnp.float32),
            *project_scratch(bases, pieces),
        ],
        compiler_params=pltpu.CompilerParams(vmem_limit_bytes=24 * 2**20),
        cost_estimate=pl.CostEstimate(
            flops=project_flops(bases, pieces) + 6 * products, bytes_accessed=2**20, transcendentals=0
        ),
    )(*operands)


def gather_pieces(mine, axis):
    count = lax.axis_size(axis)
    up, down = [mine], []
    for shift in range(1, count):
        if shift <= (count - 1) // 2:
            up.append(from_behind(up[-1], axis, 1))
        else:
            down.append(from_behind(down[-1] if down else mine, axis, count - 1))
    return up + down[::-1]


def on_device_shared(pno_basis, amplitudes, send_list, couple, couple_weight, fit_weight, fit_blocks):
    pair_count, pno_count, _ = pno_basis.shape
    group_total = lax.axis_size("blk")
    pieces = gather_pieces(fit_blocks, "dom")
    across = from_partner(pno_basis, "blk", 2)
    far = [([from_behind(fit_blocks, "blk", by)], by) for by in range(SET, group_total, SET)]
    sent = pack_pairs(send_list.reshape(-1), pno_basis, amplitudes)
    sent, *heads = lax.optimization_barrier((sent, *[group[0] for group, _ in far]))
    far = [([head], by) for head, (_, by) in zip(heads, far)]
    coupled = lax.all_to_all(sent, "blk", split_axis=0, concat_axis=0, tiled=True)
    across, pieces[1], pieces[-1] = lax.optimization_barrier((across, pieces[1], pieces[-1]))
    bases = [pno_basis, from_partner(pno_basis, "blk", 1), across, from_partner(across, "blk", 1)]
    coupled, *bases = lax.optimization_barrier((coupled, *bases))
    own, updated = dress(couple, couple_weight, fit_weight, pno_basis, amplitudes, coupled)
    last = len(pieces) // 2
    _, pieces[last] = lax.optimization_barrier((own, pieces[last]))
    groups = [pieces]
    for group, by in far:
        group += [from_behind(x, "blk", by) for x in pieces[1:]]
        if last > 1:
            source, _ = lax.optimization_barrier((group[0], own))
            group[-1] = from_behind(source, "dom", len(pieces) - 1)
        groups.append(group)
    inner = [project(bases, group) for group in groups[:-1]]
    final = groups[-1]
    dressed = [own, *[from_partner(own, "blk", flip) for flip in range(1, SET)]]
    for members in ((2, 3), (0, 1)):
        partial = finish(
            members, inner, [bases[member] for member in members], final, [dressed[member] for member in members]
        )
        if members[0]:
            partial, *final = lax.optimization_barrier((partial, *final))
            for member, x in zip(members, partial):
                updated = updated + from_partner(x, "blk", member)
        else:
            mine, beside = partial
            updated, mine, beside = lax.optimization_barrier((updated, mine, from_partner(beside, "blk", 1)))
            updated = updated + mine + beside
    return updated.reshape(pair_count, pno_count * pno_count)


def dress_with(pair_amps, intersection, partner_amps, weights):
    half_product = jnp.einsum("pcab,pcbe->pcae", intersection, partner_amps, precision=HIGHEST)
    sandwich = jnp.einsum("pcae,pcfe->pcaf", half_product, intersection, precision=HIGHEST)
    return pair_amps + jnp.einsum("pc,pcaf->paf", weights, sandwich, precision=HIGHEST)


def fit_term(pair_basis, dressed, blocks, weights):
    pair_count, pno_count, orbital_count = pair_basis.shape
    flat_basis = pair_basis.reshape(pair_count * pno_count, orbital_count)
    stacked = blocks.reshape(2 * orbital_count, orbital_count)
    projected = jnp.dot(
        flat_basis, stacked.T, precision=HIGHEST, preferred_element_type=jnp.float32
    )
    projected = projected.reshape(pair_count, pno_count, 2, orbital_count)
    inner_blocks = jnp.einsum("par,pbmr->mpab", pair_basis, projected, precision=HIGHEST)
    left_product = jnp.einsum("pai,pij->paj", inner_blocks[0], dressed, precision=HIGHEST)
    fit_contrib = jnp.einsum("paj,pbj->pab", left_product, inner_blocks[1], precision=HIGHEST)
    return weights[:, None, None] * fit_contrib


def on_device_ring(pno_basis, amplitudes, send_list, couple, couple_weight, fit_weight, fit_blocks):
    pair_count, pno_count, _ = pno_basis.shape
    block_count = fit_blocks.shape[0]
    pair_amps = amplitudes.reshape(pair_count, pno_count, pno_count)
    send_order = send_list.reshape(-1)
    basis_in = lax.all_to_all(jnp.take(pno_basis, send_order, axis=0), "blk", split_axis=0, concat_axis=0, tiled=True)
    amps_in = lax.all_to_all(jnp.take(pair_amps, send_order, axis=0), "blk", split_axis=0, concat_axis=0, tiled=True)
    partner_basis = jnp.take(basis_in, couple, axis=0)
    intersection = jnp.einsum("par,pcbr->pcab", pno_basis, partner_basis, precision=HIGHEST)
    dressed = dress_with(pair_amps, intersection, jnp.take(amps_in, couple, axis=0), couple_weight)
    updated = dressed
    current = lax.all_gather(fit_blocks, "dom", axis=2, tiled=True)
    for stop in range(fit_weight.shape[1] // block_count):
        if stop > 0:
            current = from_behind(current, "blk", 1)
        for b in range(block_count):
            updated = updated + fit_term(pno_basis, dressed, current[b], fit_weight[:, stop * block_count + b])
    return updated.reshape(pair_count, pno_count * pno_count)


def solution(mesh):
    placed = (
        P(("blk", "dom"), None, None),
        P(("blk", "dom"), None),
        P("blk", "dom", None, None),
        P(("blk", "dom"), None),
        P(("blk", "dom"), None),
        P(("blk", "dom"), None),
        P("blk", None, "dom", None),
    )

    def on_device(*args):
        send_list, fit_weight, fit_blocks = args[2], args[5], args[6]
        group_total = mesh.shape["blk"]
        meets_all = fit_weight.shape[1] == group_total * fit_blocks.shape[0]
        if meets_all and group_total % SET == 0 and group_total > SET and group_total & (group_total - 1) == 0 and send_list.shape[3] == 1:
            return on_device_shared(*args)
        return on_device_ring(*args)

    return jax.shard_map(
        on_device, mesh=mesh, in_specs=placed, out_specs=P(("blk", "dom"), None), check_vma=False
    )
```

```python
import jax
import jax.numpy as jnp
from jax import lax
from jax.experimental import pallas as pl
from jax.experimental.pallas import tpu as pltpu
from jax.sharding import PartitionSpec as P

HIGHEST = lax.Precision.HIGHEST
SET = 4
NN = (((1,), (0,)), ((), ()))
NT = (((1,), (1,)), ((), ()))


def halves(x):
    high = x.astype(jnp.bfloat16)
    return high, (x - high.astype(jnp.float32)).astype(jnp.bfloat16)


def dot(a, b, dims):
    return lax.dot_general(a, b, dims, preferred_element_type=jnp.float32)


def dot3(a, b, dims):
    (a_high, a_low), (b_high, b_low) = a, b
    return dot(a_high, b_high, dims) + (dot(a_high, b_low, dims) + dot(a_low, b_high, dims))


def stack(parts, axis=0):
    return jnp.concatenate(parts, axis=axis)


def from_partner(x, axis, flip):
    return lax.ppermute(x, axis, [(i, i ^ flip) for i in range(lax.axis_size(axis))])


def from_behind(x, axis, by):
    count = lax.axis_size(axis)
    return lax.ppermute(x, axis, [(i, (i + by) % count) for i in range(count)])


def vmem(count):
    return [pl.BlockSpec(memory_space=pltpu.VMEM)] * count


def pack_kernel(send, basis, amps, out):
    peer_count, row_count, lane_count = out.shape
    pno_count = basis.shape[1]
    for peer in range(peer_count):
        pair = send[peer]
        out[peer, :pno_count] = basis[pair]
        for i in range(row_count - pno_count):
            at = pno_count + i
            out[peer, at:at + 1, :] = amps[pl.ds(pair, 1), i * lane_count:(i + 1) * lane_count]


def pack_pairs(send_order, basis, amps):
    _, pno_count, orbital_count = basis.shape
    rows = pno_count + amps.shape[1] // orbital_count
    return pl.pallas_call(
        pack_kernel,
        out_shape=jax.ShapeDtypeStruct((send_order.shape[0], rows, orbital_count), jnp.float32),
        in_specs=[pl.BlockSpec(memory_space=pltpu.SMEM), *vmem(2)],
        out_specs=vmem(1)[0],
        compiler_params=pltpu.CompilerParams(vmem_limit_bytes=62 * 2**20),
        cost_estimate=pl.CostEstimate(flops=0, bytes_accessed=4 * basis.size, transcendentals=0),
    )(send_order, basis, amps)


def dress_kernel(couple, couple_weight, fit_weight, basis, amps, coupled, dressed, result, turned, paired, partners):
    pair_count, pno_count, orbital_count = basis.shape
    half = pno_count // 2
    slot_count = coupled.shape[0]
    width = 2 * pno_count
    for i in range(half):
        paired[pl.ds(i, pair_count, stride=half), :] = amps[:, i * width:(i + 1) * width]
    for pair in range(pair_count):
        packed = paired[pair * half:(pair + 1) * half]
        for i in range(2):
            turned[pair, pl.ds(i, half, stride=2), :] = packed[:, i * pno_count:(i + 1) * pno_count]
    own = halves(basis[...].reshape(pair_count * pno_count, orbital_count))
    others = halves(coupled[:, :pno_count].reshape(slot_count * pno_count, orbital_count))
    overlap = halves(dot3(own, others, NT))
    left, slot_weight = [], []
    for slot in range(slot_count):
        cols = slice(slot * pno_count, (slot + 1) * pno_count)
        packed = coupled[slot, pno_count:]
        step = orbital_count // pno_count
        for i in range(step):
            lanes = slice(i * pno_count, (i + 1) * pno_count)
            partners[slot, pl.ds(i, packed.shape[0], stride=step), :] = packed[:, lanes]
        left.append(dot3([x[:, cols] for x in overlap], halves(partners[slot]), NN))
        named = jnp.where(couple[...] == slot, couple_weight[...], 0.0)
        slot_weight.append(jnp.sum(named, axis=1, keepdims=True))
    dressed[:, half:, :] = jnp.zeros((pair_count, dressed.shape[1] - half, 2 * pno_count), jnp.float32)
    for pair in range(pair_count):
        rows = slice(pair * pno_count, (pair + 1) * pno_count)
        scaled = stack([x[rows] * w[pair:pair + 1] for x, w in zip(left, slot_weight)], 1)
        total = turned[pair] + dot3(halves(scaled), [x[rows] for x in overlap], NT)
        dressed[pair, :half] = stack([total[:half], total[half:]], 1)
        turned[pair] = total
        result[pair] = two_to_one(turned, pair, half)
        dressed[pair, half:half + 1, : fit_weight.shape[1]] = fit_weight[pair:pair + 1, :]


def two_to_one(ref, pair, half):
    return stack([ref[pair, pl.ds(i, half, stride=2), :] for i in range(2)], 1)


def dress(couple, couple_weight, fit_weight, basis, amps, coupled):
    pair_count, pno_count, _ = basis.shape
    return pl.pallas_call(
        dress_kernel,
        out_shape=tuple(
            jax.ShapeDtypeStruct((pair_count, pno_count // 2 + more, 2 * pno_count), jnp.float32) for more in (8, 0)
        ),
        in_specs=vmem(6),
        out_specs=tuple(vmem(2)),
        scratch_shapes=[
            pltpu.VMEM((pair_count, pno_count, pno_count), jnp.float32),
            pltpu.VMEM((pair_count * pno_count // 2, 2 * pno_count), jnp.float32),
            pltpu.VMEM((coupled.shape[0], pno_count, pno_count), jnp.float32),
        ],
        compiler_params=pltpu.CompilerParams(vmem_limit_bytes=10 * 2**20),
        cost_estimate=pl.CostEstimate(flops=4 * 10**9, bytes_accessed=8 * basis.size, transcendentals=0),
    )(couple, couple_weight, fit_weight, basis, amps, coupled)


def fold(x):
    return x + pltpu.roll(x, x.shape[1] // 2, 1)


def left_lanes(x):
    return lax.broadcasted_iota(jnp.int32, x.shape, 1) < x.shape[1] // 2


def split(x):
    high = x.astype(jnp.bfloat16)
    wide = high.astype(jnp.float32)
    return high, wide, x - wide


def high_low(x):
    _, high, low = split(x)
    return jnp.where(left_lanes(x), high, low).astype(jnp.bfloat16)


def split_blocks(pieces, block_cat):
    dom_count = len(pieces)
    block_count, part_count, row_count, orbital_count = pieces[0].shape
    place = lax.axis_index("dom")
    for shift, piece in enumerate(pieces):
        start = lax.rem(place + dom_count - shift, dom_count) * row_count
        for b in range(block_count):
            for m in range(part_count):
                high, low = halves(piece[b, m])
                for i, x in enumerate((high, high, low)):
                    at = pl.multiple_of(start + i * orbital_count, row_count)
                    block_cat[m, b, pl.ds(at, row_count), :] = x


def split_basis(basis, wide):
    orbital_count = basis.shape[2]
    high, low = halves(basis[...])
    for i, x in enumerate((high, low, high)):
        wide[:, :, i * orbital_count:(i + 1) * orbital_count] = x


def project_slice(wide, block, projected, at):
    pair_count, pno_count, lane_count = wide.shape
    orbital_count = block.shape[1]
    basis = wide[...].reshape(pair_count * pno_count, lane_count)
    product = halves(dot(basis, block[...], NN).reshape(pair_count, pno_count, orbital_count))
    for i in range(2):
        projected[:, at:at + pno_count, i * orbital_count:(i + 1) * orbital_count] = product[i]


def inner_pair(wide, projected, inner_left, inner_right, pair, here):
    _, pno_count, lane_count = wide.shape
    orbital_count = lane_count // 3
    size = inner_left.shape[1]
    both = stack([wide[pair, :, i * orbital_count:(i + 1) * orbital_count] for i in range(2)])
    product = [projected[pair, :, i * orbital_count:(i + 1) * orbital_count] for i in range(2)]
    inner = fold(dot(product[0], both, NT) + dot(product[1], both, NT))
    inner_left[here] = high_low(inner[:size])
    high, _, low = split(inner[size:])
    low = jnp.where(left_lanes(low), low, 0.0).astype(jnp.bfloat16)
    for b in range(size // pno_count):
        rows = slice(b * pno_count, (b + 1) * pno_count)
        lanes = slice(b * 2 * pno_count, (b + 1) * 2 * pno_count)
        inner_right[here, :pno_count, lanes] = high[rows]
        inner_right[here, pno_count:, lanes] = low[rows]


def project_all(bases, pieces, inner_left, inner_right, scratch):
    block_cat, wide, projected = scratch
    pair_count, pno_count, _ = bases[0].shape
    part_count, block_count = block_cat.shape[:2]
    split_blocks(pieces, block_cat)
    for member, basis in enumerate(bases):
        split_basis(basis, wide.at[pl.ds(member * pair_count, pair_count)])
    for m in range(part_count):
        for b in range(block_count):
            project_slice(wide, block_cat.at[m, b], projected, (m * block_count + b) * pno_count)
    for pair in range(len(bases) * pair_count):
        inner_pair(wide, projected, inner_left, inner_right, pair, pair)


def project_kernel(member_count, *refs):
    bases, refs = refs[:member_count], refs[member_count:]
    *pieces, inner_left, inner_right = refs[:-3]
    project_all(bases, pieces, inner_left, inner_right, refs[-3:])


def inner_shapes(pairs, pno_count, block_count):
    return (
        ((pairs, block_count * pno_count, 2 * pno_count), jnp.bfloat16),
        ((pairs, 2 * pno_count, block_count * 2 * pno_count), jnp.bfloat16),
    )


def project_scratch(bases, pieces):
    pair_count, pno_count, _ = bases[0].shape
    block_count, part_count, _, orbital_count = pieces[0].shape
    return [
        pltpu.VMEM((part_count, block_count, 3 * orbital_count, orbital_count), jnp.bfloat16),
        pltpu.VMEM((len(bases) * pair_count, pno_count, 3 * orbital_count), jnp.bfloat16),
        pltpu.VMEM((len(bases) * pair_count, part_count * block_count * pno_count, 2 * orbital_count), jnp.bfloat16),
    ]


def project_flops(bases, pieces):
    pair_count, pno_count, _ = bases[0].shape
    block_count, part_count, _, orbital_count = pieces[0].shape
    rows = len(bases) * pair_count * pno_count * block_count * part_count
    return 6 * rows * orbital_count * (orbital_count + pno_count)


def project(bases, pieces):
    pair_count, pno_count, _ = bases[0].shape
    shapes = inner_shapes(len(bases) * pair_count, pno_count, pieces[0].shape[0])
    return pl.pallas_call(
        lambda *refs: project_kernel(len(bases), *refs),
        out_shape=tuple(jax.ShapeDtypeStruct(*x) for x in shapes),
        in_specs=vmem(len(bases) + len(pieces)),
        out_specs=tuple(vmem(2)),
        scratch_shapes=project_scratch(bases, pieces),
        compiler_params=pltpu.CompilerParams(vmem_limit_bytes=28 * 2**20),
        cost_estimate=pl.CostEstimate(flops=project_flops(bases, pieces), bytes_accessed=2**20, transcendentals=0),
    )(*bases, *pieces)


def finish_kernel(members, group_count, dom_count, *refs):
    count = len(members)
    groups, refs = refs[:2 * group_count], refs[2 * group_count:]
    bases, pieces, refs = refs[:count], refs[count:count + dom_count], refs[count + dom_count:]
    dressed, after, scratch = refs[:count], refs[count:2 * count], refs[2 * count:]
    inner_left, inner_right, square, moved, total = scratch[:5]
    groups = [*groups, inner_left, inner_right]
    group_count += 1
    pair_count, _, lane_count = dressed[0].shape
    pno_count = lane_count // 2
    half = pno_count // 2
    block_count = inner_left.shape[1] // pno_count
    group_total = lax.axis_size("blk")
    me = lax.axis_index("blk")
    pairs = [(index, pair) for index in range(count) for pair in range(pair_count)]

    def row_of(group, at):
        full = group < group_count - 1
        return members[at // pair_count] * pair_count + at % pair_count if full else at

    weights = []
    for index, member in enumerate(members):
        row = dressed[index][:, half:half + 1, :]
        lane = lax.broadcasted_iota(jnp.int32, row.shape, 2)
        for group in range(group_count):
            stop = lax.rem((me ^ member) + 2 * group_total + group * SET - me, group_total)
            for b in range(block_count):
                kept = jnp.where(lane == stop * block_count + b, row, 0.0)
                weights.append(jnp.sum(kept, axis=2, keepdims=True))
    project_all(bases, pieces, inner_left, inner_right, scratch[5:])
    for at, (index, pair) in enumerate(pairs):
        packed = dressed[index][pair, :half]
        other = pltpu.roll(packed, pno_count, 1)
        keep = left_lanes(packed)
        _, high, low = split(stack([jnp.where(keep, packed, other), jnp.where(keep, other, packed)]))
        square[at, :pno_count] = jnp.where(left_lanes(low), high, low).astype(jnp.bfloat16)
        square[at, pno_count:] = jnp.where(left_lanes(low), high, 0.0).astype(jnp.bfloat16)
    for at, (index, pair) in enumerate(pairs):
        for group in range(group_count):
            product = fold(dot(groups[2 * group][row_of(group, at)], square[at], NN))
            for b in range(block_count):
                weight = weights[(index * group_count + group) * block_count + b][pair]
                lanes = slice(b * lane_count, (b + 1) * lane_count)
                moved[at, group, :, lanes] = high_low(product[b * pno_count:(b + 1) * pno_count] * weight)
    for at, (index, pair) in enumerate(pairs):
        terms = [dot(moved[at, group], groups[2 * group + 1][row_of(group, at)], NT) for group in range(group_count)]
        total[at] = fold(sum(terms[1:], terms[0]))
    for at, (index, pair) in enumerate(pairs):
        rows = [total[at, pl.ds(i, half, stride=2), :] for i in range(2)]
        after[index][pair] = jnp.where(left_lanes(rows[0]), *rows)


def finish(members, groups, bases, pieces, dressed):
    pair_count, _, lane_count = dressed[0].shape
    pno_count = lane_count // 2
    pairs = len(members) * pair_count
    group_count = len(groups)
    block_count = pieces[0].shape[0]
    operands = [x for group in groups for x in group] + bases + pieces + dressed
    products = pairs * pno_count**3 * 2 * (group_count + 1) * block_count
    shapes = inner_shapes(pairs, pno_count, block_count)
    return pl.pallas_call(
        lambda *refs: finish_kernel(members, group_count, len(pieces), *refs),
        out_shape=[jax.ShapeDtypeStruct((pair_count, pno_count // 2, lane_count), jnp.float32)] * len(members),
        in_specs=vmem(len(operands)),
        out_specs=vmem(len(members)),
        scratch_shapes=[
            *[pltpu.VMEM(*x) for x in shapes],
            pltpu.VMEM((pairs, lane_count, lane_count), jnp.bfloat16),
            pltpu.VMEM((pairs, group_count + 1, pno_count, block_count * lane_count), jnp.bfloat16),
            pltpu.VMEM((pairs, pno_count, lane_count), jnp.float32),
            *project_scratch(bases, pieces),
        ],
        compiler_params=pltpu.CompilerParams(vmem_limit_bytes=24 * 2**20),
        cost_estimate=pl.CostEstimate(
            flops=project_flops(bases, pieces) + 6 * products, bytes_accessed=2**20, transcendentals=0
        ),
    )(*operands)


def gather_pieces(mine, axis):
    count = lax.axis_size(axis)
    up, down = [mine], []
    for shift in range(1, count):
        if shift <= (count - 1) // 2:
            up.append(from_behind(up[-1], axis, 1))
        else:
            down.append(from_behind(down[-1] if down else mine, axis, count - 1))
    return up + down[::-1]


def on_device_shared(pno_basis, amplitudes, send_list, couple, couple_weight, fit_weight, fit_blocks):
    pair_count, pno_count, _ = pno_basis.shape
    group_total = lax.axis_size("blk")
    pieces = gather_pieces(fit_blocks, "dom")
    across = from_partner(pno_basis, "blk", 2)
    far = [([from_behind(fit_blocks, "blk", by)], by) for by in range(SET, group_total, SET)]
    sent = pack_pairs(send_list.reshape(-1), pno_basis, amplitudes)
    sent, *heads = lax.optimization_barrier((sent, *[group[0] for group, _ in far]))
    far = [([head], by) for head, (_, by) in zip(heads, far)]
    coupled = lax.all_to_all(sent, "blk", split_axis=0, concat_axis=0, tiled=True)
    across, pieces[1], pieces[-1] = lax.optimization_barrier((across, pieces[1], pieces[-1]))
    bases = [pno_basis, from_partner(pno_basis, "blk", 1), across, from_partner(across, "blk", 1)]
    coupled, *bases = lax.optimization_barrier((coupled, *bases))
    own, updated = dress(couple, couple_weight, fit_weight, pno_basis, amplitudes, coupled)
    last = len(pieces) // 2
    _, pieces[last] = lax.optimization_barrier((own, pieces[last]))
    groups = [pieces]
    for group, by in far:
        group += [from_behind(x, "blk", by) for x in pieces[1:]]
        if last > 1:
            source, pieces[-1] = lax.optimization_barrier((group[0], pieces[-1]))
            group[-1] = from_behind(source, "dom", len(pieces) - 1)
        groups.append(group)
    inner = [project(bases, group) for group in groups[:-1]]
    final = groups[-1]
    dressed = [own, *[from_partner(own, "blk", flip) for flip in range(1, SET)]]
    for members in ((2, 3), (0, 1)):
        partial = finish(
            members, inner, [bases[member] for member in members], final, [dressed[member] for member in members]
        )
        if members[0]:
            partial, *final = lax.optimization_barrier((partial, *final))
            for member, x in zip(members, partial):
                updated = updated + from_partner(x, "blk", member)
        else:
            mine, beside = partial
            updated, mine, beside = lax.optimization_barrier((updated, mine, from_partner(beside, "blk", 1)))
            updated = updated + mine + beside
    return updated.reshape(pair_count, pno_count * pno_count)


def dress_with(pair_amps, intersection, partner_amps, weights):
    half_product = jnp.einsum("pcab,pcbe->pcae", intersection, partner_amps, precision=HIGHEST)
    sandwich = jnp.einsum("pcae,pcfe->pcaf", half_product, intersection, precision=HIGHEST)
    return pair_amps + jnp.einsum("pc,pcaf->paf", weights, sandwich, precision=HIGHEST)


def fit_term(pair_basis, dressed, blocks, weights):
    pair_count, pno_count, orbital_count = pair_basis.shape
    flat_basis = pair_basis.reshape(pair_count * pno_count, orbital_count)
    stacked = blocks.reshape(2 * orbital_count, orbital_count)
    projected = jnp.dot(
        flat_basis, stacked.T, precision=HIGHEST, preferred_element_type=jnp.float32
    )
    projected = projected.reshape(pair_count, pno_count, 2, orbital_count)
    inner_blocks = jnp.einsum("par,pbmr->mpab", pair_basis, projected, precision=HIGHEST)
    left_product = jnp.einsum("pai,pij->paj", inner_blocks[0], dressed, precision=HIGHEST)
    fit_contrib = jnp.einsum("paj,pbj->pab", left_product, inner_blocks[1], precision=HIGHEST)
    return weights[:, None, None] * fit_contrib


def on_device_ring(pno_basis, amplitudes, send_list, couple, couple_weight, fit_weight, fit_blocks):
    pair_count, pno_count, _ = pno_basis.shape
    block_count = fit_blocks.shape[0]
    pair_amps = amplitudes.reshape(pair_count, pno_count, pno_count)
    send_order = send_list.reshape(-1)
    basis_in = lax.all_to_all(jnp.take(pno_basis, send_order, axis=0), "blk", split_axis=0, concat_axis=0, tiled=True)
    amps_in = lax.all_to_all(jnp.take(pair_amps, send_order, axis=0), "blk", split_axis=0, concat_axis=0, tiled=True)
    partner_basis = jnp.take(basis_in, couple, axis=0)
    intersection = jnp.einsum("par,pcbr->pcab", pno_basis, partner_basis, precision=HIGHEST)
    dressed = dress_with(pair_amps, intersection, jnp.take(amps_in, couple, axis=0), couple_weight)
    updated = dressed
    current = lax.all_gather(fit_blocks, "dom", axis=2, tiled=True)
    for stop in range(fit_weight.shape[1] // block_count):
        if stop > 0:
            current = from_behind(current, "blk", 1)
        for b in range(block_count):
            updated = updated + fit_term(pno_basis, dressed, current[b], fit_weight[:, stop * block_count + b])
    return updated.reshape(pair_count, pno_count * pno_count)


def solution(mesh):
    placed = (
        P(("blk", "dom"), None, None),
        P(("blk", "dom"), None),
        P("blk", "dom", None, None),
        P(("blk", "dom"), None),
        P(("blk", "dom"), None),
        P(("blk", "dom"), None),
        P("blk", None, "dom", None),
    )

    def on_device(*args):
        send_list, fit_weight, fit_blocks = args[2], args[5], args[6]
        group_total = mesh.shape["blk"]
        meets_all = fit_weight.shape[1] == group_total * fit_blocks.shape[0]
        if meets_all and group_total % SET == 0 and group_total > SET and group_total & (group_total - 1) == 0 and send_list.shape[3] == 1:
            return on_device_shared(*args)
        return on_device_ring(*args)

    return jax.shard_map(
        on_device, mesh=mesh, in_specs=placed, out_specs=P(("blk", "dom"), None), check_vma=False
    )
```

```python
import jax
import jax.numpy as jnp
from jax import lax
from jax.experimental import pallas as pl
from jax.experimental.pallas import tpu as pltpu
from jax.sharding import PartitionSpec as P

HIGHEST = lax.Precision.HIGHEST
SET = 4
NN = (((1,), (0,)), ((), ()))
NT = (((1,), (1,)), ((), ()))


def halves(x):
    high = x.astype(jnp.bfloat16)
    return high, (x - high.astype(jnp.float32)).astype(jnp.bfloat16)


def dot(a, b, dims):
    return lax.dot_general(a, b, dims, preferred_element_type=jnp.float32)


def dot3(a, b, dims):
    (a_high, a_low), (b_high, b_low) = a, b
    return dot(a_high, b_high, dims) + (dot(a_high, b_low, dims) + dot(a_low, b_high, dims))


def stack(parts, axis=0):
    return jnp.concatenate(parts, axis=axis)


def from_partner(x, axis, flip):
    return lax.ppermute(x, axis, [(i, i ^ flip) for i in range(lax.axis_size(axis))])


def from_behind(x, axis, by):
    count = lax.axis_size(axis)
    return lax.ppermute(x, axis, [(i, (i + by) % count) for i in range(count)])


def vmem(count):
    return [pl.BlockSpec(memory_space=pltpu.VMEM)] * count


def pack_kernel(send, basis, amps, out):
    peer_count, row_count, lane_count = out.shape
    pno_count = basis.shape[1]
    for peer in range(peer_count):
        pair = send[peer]
        out[peer, :pno_count] = basis[pair]
        for i in range(row_count - pno_count):
            at = pno_count + i
            out[peer, at:at + 1, :] = amps[pl.ds(pair, 1), i * lane_count:(i + 1) * lane_count]


def pack_pairs(send_order, basis, amps):
    _, pno_count, orbital_count = basis.shape
    rows = pno_count + amps.shape[1] // orbital_count
    return pl.pallas_call(
        pack_kernel,
        out_shape=jax.ShapeDtypeStruct((send_order.shape[0], rows, orbital_count), jnp.float32),
        in_specs=[pl.BlockSpec(memory_space=pltpu.SMEM), *vmem(2)],
        out_specs=vmem(1)[0],
        compiler_params=pltpu.CompilerParams(vmem_limit_bytes=62 * 2**20),
        cost_estimate=pl.CostEstimate(flops=0, bytes_accessed=4 * basis.size, transcendentals=0),
    )(send_order, basis, amps)


def dress_kernel(couple, couple_weight, fit_weight, basis, amps, coupled, dressed, result, turned, paired, partners):
    pair_count, pno_count, orbital_count = basis.shape
    half = pno_count // 2
    slot_count = coupled.shape[0]
    width = 2 * pno_count
    for i in range(half):
        paired[pl.ds(i, pair_count, stride=half), :] = amps[:, i * width:(i + 1) * width]
    for pair in range(pair_count):
        packed = paired[pair * half:(pair + 1) * half]
        for i in range(2):
            turned[pair, pl.ds(i, half, stride=2), :] = packed[:, i * pno_count:(i + 1) * pno_count]
    own = halves(basis[...].reshape(pair_count * pno_count, orbital_count))
    others = halves(coupled[:, :pno_count].reshape(slot_count * pno_count, orbital_count))
    overlap = halves(dot3(own, others, NT))
    step = orbital_count // pno_count
    left, slot_weight = [], []
    for both in range(slot_count // 2):
        named = []
        for j in range(2):
            packed = coupled[2 * both + j, pno_count:]
            for i in range(step):
                rows = pl.ds(j * pno_count + i, packed.shape[0], stride=step)
                block = packed[:, i * pno_count:(i + 1) * pno_count]
                none = jnp.zeros_like(block)
                partners[both, rows, :] = stack([none, block] if j else [block, none], 1)
            weight = jnp.where(couple[...] == 2 * both + j, couple_weight[...], 0.0)
            named.append(jnp.sum(weight, axis=1, keepdims=True))
        lane = lax.broadcasted_iota(jnp.int32, (pair_count, width), 1)
        slot_weight.append(jnp.where(lane < pno_count, *named))
        high, low = [x[:, both * width:(both + 1) * width] for x in overlap]
        diagonal = halves(partners[both])
        product = dot(high, stack(diagonal, 1), NN)
        left.append(product[:, :width] + (product[:, width:] + dot(low, diagonal[0], NN)))
    dressed[:, half:, :] = jnp.zeros((pair_count, dressed.shape[1] - half, 2 * pno_count), jnp.float32)
    for pair in range(pair_count):
        rows = slice(pair * pno_count, (pair + 1) * pno_count)
        high, low = halves(stack([x[rows] * w[pair:pair + 1] for x, w in zip(left, slot_weight)], 1))
        right = [x[rows] for x in overlap]
        product = dot(high, stack(right), NT)
        total = turned[pair] + product[:, :pno_count] + (product[:, pno_count:] + dot(low, right[0], NT))
        dressed[pair, :half] = stack([total[:half], total[half:]], 1)
        turned[pair] = total
        result[pair] = two_to_one(turned, pair, half)
        dressed[pair, half:half + 1, : fit_weight.shape[1]] = fit_weight[pair:pair + 1, :]


def two_to_one(ref, pair, half):
    return stack([ref[pair, pl.ds(i, half, stride=2), :] for i in range(2)], 1)


def dress(couple, couple_weight, fit_weight, basis, amps, coupled):
    pair_count, pno_count, _ = basis.shape
    return pl.pallas_call(
        dress_kernel,
        out_shape=tuple(
            jax.ShapeDtypeStruct((pair_count, pno_count // 2 + more, 2 * pno_count), jnp.float32) for more in (8, 0)
        ),
        in_specs=vmem(6),
        out_specs=tuple(vmem(2)),
        scratch_shapes=[
            pltpu.VMEM((pair_count, pno_count, pno_count), jnp.float32),
            pltpu.VMEM((pair_count * pno_count // 2, 2 * pno_count), jnp.float32),
            pltpu.VMEM((coupled.shape[0] // 2, 2 * pno_count, 2 * pno_count), jnp.float32),
        ],
        compiler_params=pltpu.CompilerParams(vmem_limit_bytes=10 * 2**20),
        cost_estimate=pl.CostEstimate(flops=4 * 10**9, bytes_accessed=8 * basis.size, transcendentals=0),
    )(couple, couple_weight, fit_weight, basis, amps, coupled)


def fold(x):
    return x + pltpu.roll(x, x.shape[1] // 2, 1)


def left_lanes(x):
    return lax.broadcasted_iota(jnp.int32, x.shape, 1) < x.shape[1] // 2


def split(x):
    high = x.astype(jnp.bfloat16)
    wide = high.astype(jnp.float32)
    return high, wide, x - wide


def high_low(x):
    _, high, low = split(x)
    return jnp.where(left_lanes(x), high, low).astype(jnp.bfloat16)


def split_blocks(pieces, block_cat):
    dom_count = len(pieces)
    block_count, part_count, row_count, orbital_count = pieces[0].shape
    place = lax.axis_index("dom")
    for shift, piece in enumerate(pieces):
        start = lax.rem(place + dom_count - shift, dom_count) * row_count
        for b in range(block_count):
            for m in range(part_count):
                high, low = halves(piece[b, m])
                for i, x in enumerate((high, high, low)):
                    at = pl.multiple_of(start + i * orbital_count, row_count)
                    block_cat[m, b, pl.ds(at, row_count), :] = x


def split_basis(basis, wide):
    orbital_count = basis.shape[2]
    high, low = halves(basis[...])
    for i, x in enumerate((high, low, high)):
        wide[:, :, i * orbital_count:(i + 1) * orbital_count] = x


def project_slice(wide, block, projected, at):
    pair_count, pno_count, lane_count = wide.shape
    orbital_count = block.shape[1]
    basis = wide[...].reshape(pair_count * pno_count, lane_count)
    product = halves(dot(basis, block[...], NN).reshape(pair_count, pno_count, orbital_count))
    for i in range(2):
        projected[:, at:at + pno_count, i * orbital_count:(i + 1) * orbital_count] = product[i]


def inner_pair(wide, projected, inner_left, inner_right, pair, here):
    _, pno_count, lane_count = wide.shape
    orbital_count = lane_count // 3
    size = inner_left.shape[1]
    both = stack([wide[pair, :, i * orbital_count:(i + 1) * orbital_count] for i in range(2)])
    product = [projected[pair, :, i * orbital_count:(i + 1) * orbital_count] for i in range(2)]
    inner = fold(dot(product[0], both, NT) + dot(product[1], both, NT))
    inner_left[here] = high_low(inner[:size])
    high, _, low = split(inner[size:])
    low = jnp.where(left_lanes(low), low, 0.0).astype(jnp.bfloat16)
    for b in range(size // pno_count):
        rows = slice(b * pno_count, (b + 1) * pno_count)
        lanes = slice(b * 2 * pno_count, (b + 1) * 2 * pno_count)
        inner_right[here, :pno_count, lanes] = high[rows]
        inner_right[here, pno_count:, lanes] = low[rows]


def project_all(bases, pieces, inner_left, inner_right, scratch):
    block_cat, wide, projected = scratch
    pair_count, pno_count, _ = bases[0].shape
    part_count, block_count = block_cat.shape[:2]
    split_blocks(pieces, block_cat)
    for member, basis in enumerate(bases):
        split_basis(basis, wide.at[pl.ds(member * pair_count, pair_count)])
    for m in range(part_count):
        for b in range(block_count):
            project_slice(wide, block_cat.at[m, b], projected, (m * block_count + b) * pno_count)
    for pair in range(len(bases) * pair_count):
        inner_pair(wide, projected, inner_left, inner_right, pair, pair)


def project_kernel(member_count, *refs):
    bases, refs = refs[:member_count], refs[member_count:]
    *pieces, inner_left, inner_right = refs[:-3]
    project_all(bases, pieces, inner_left, inner_right, refs[-3:])


def inner_shapes(pairs, pno_count, block_count):
    return (
        ((pairs, block_count * pno_count, 2 * pno_count), jnp.bfloat16),
        ((pairs, 2 * pno_count, block_count * 2 * pno_count), jnp.bfloat16),
    )


def project_scratch(bases, pieces):
    pair_count, pno_count, _ = bases[0].shape
    block_count, part_count, _, orbital_count = pieces[0].shape
    return [
        pltpu.VMEM((part_count, block_count, 3 * orbital_count, orbital_count), jnp.bfloat16),
        pltpu.VMEM((len(bases) * pair_count, pno_count, 3 * orbital_count), jnp.bfloat16),
        pltpu.VMEM((len(bases) * pair_count, part_count * block_count * pno_count, 2 * orbital_count), jnp.bfloat16),
    ]


def project_flops(bases, pieces):
    pair_count, pno_count, _ = bases[0].shape
    block_count, part_count, _, orbital_count = pieces[0].shape
    rows = len(bases) * pair_count * pno_count * block_count * part_count
    return 6 * rows * orbital_count * (orbital_count + pno_count)


def project(bases, pieces):
    pair_count, pno_count, _ = bases[0].shape
    shapes = inner_shapes(len(bases) * pair_count, pno_count, pieces[0].shape[0])
    return pl.pallas_call(
        lambda *refs: project_kernel(len(bases), *refs),
        out_shape=tuple(jax.ShapeDtypeStruct(*x) for x in shapes),
        in_specs=vmem(len(bases) + len(pieces)),
        out_specs=tuple(vmem(2)),
        scratch_shapes=project_scratch(bases, pieces),
        compiler_params=pltpu.CompilerParams(vmem_limit_bytes=28 * 2**20),
        cost_estimate=pl.CostEstimate(flops=project_flops(bases, pieces), bytes_accessed=2**20, transcendentals=0),
    )(*bases, *pieces)


def finish_kernel(members, group_count, dom_count, *refs):
    count = len(members)
    groups, refs = refs[:2 * group_count], refs[2 * group_count:]
    bases, pieces, refs = refs[:count], refs[count:count + dom_count], refs[count + dom_count:]
    dressed, after, scratch = refs[:count], refs[count:2 * count], refs[2 * count:]
    inner_left, inner_right, square, moved, total = scratch[:5]
    groups = [*groups, inner_left, inner_right]
    group_count += 1
    pair_count, _, lane_count = dressed[0].shape
    pno_count = lane_count // 2
    half = pno_count // 2
    block_count = inner_left.shape[1] // pno_count
    group_total = lax.axis_size("blk")
    me = lax.axis_index("blk")
    pairs = [(index, pair) for index in range(count) for pair in range(pair_count)]

    def row_of(group, at):
        full = group < group_count - 1
        return members[at // pair_count] * pair_count + at % pair_count if full else at

    weights = []
    for index, member in enumerate(members):
        row = dressed[index][:, half:half + 1, :]
        lane = lax.broadcasted_iota(jnp.int32, row.shape, 2)
        for group in range(group_count):
            stop = lax.rem((me ^ member) + 2 * group_total + group * SET - me, group_total)
            for b in range(block_count):
                kept = jnp.where(lane == stop * block_count + b, row, 0.0)
                weights.append(jnp.sum(kept, axis=2, keepdims=True))
    project_all(bases, pieces, inner_left, inner_right, scratch[5:])
    for at, (index, pair) in enumerate(pairs):
        packed = dressed[index][pair, :half]
        other = pltpu.roll(packed, pno_count, 1)
        keep = left_lanes(packed)
        _, high, low = split(stack([jnp.where(keep, packed, other), jnp.where(keep, other, packed)]))
        square[at, :pno_count] = jnp.where(left_lanes(low), high, low).astype(jnp.bfloat16)
        square[at, pno_count:] = jnp.where(left_lanes(low), high, 0.0).astype(jnp.bfloat16)
    for at, (index, pair) in enumerate(pairs):
        for group in range(group_count):
            product = fold(dot(groups[2 * group][row_of(group, at)], square[at], NN))
            for b in range(block_count):
                weight = weights[(index * group_count + group) * block_count + b][pair]
                lanes = slice(b * lane_count, (b + 1) * lane_count)
                moved[at, group, :, lanes] = high_low(product[b * pno_count:(b + 1) * pno_count] * weight)
    for at, (index, pair) in enumerate(pairs):
        terms = [dot(moved[at, group], groups[2 * group + 1][row_of(group, at)], NT) for group in range(group_count)]
        total[at] = fold(sum(terms[1:], terms[0]))
    for at, (index, pair) in enumerate(pairs):
        rows = [total[at, pl.ds(i, half, stride=2), :] for i in range(2)]
        after[index][pair] = jnp.where(left_lanes(rows[0]), *rows)


def finish(members, groups, bases, pieces, dressed):
    pair_count, _, lane_count = dressed[0].shape
    pno_count = lane_count // 2
    pairs = len(members) * pair_count
    group_count = len(groups)
    block_count = pieces[0].shape[0]
    operands = [x for group in groups for x in group] + bases + pieces + dressed
    products = pairs * pno_count**3 * 2 * (group_count + 1) * block_count
    shapes = inner_shapes(pairs, pno_count, block_count)
    return pl.pallas_call(
        lambda *refs: finish_kernel(members, group_count, len(pieces), *refs),
        out_shape=[jax.ShapeDtypeStruct((pair_count, pno_count // 2, lane_count), jnp.float32)] * len(members),
        in_specs=vmem(len(operands)),
        out_specs=vmem(len(members)),
        scratch_shapes=[
            *[pltpu.VMEM(*x) for x in shapes],
            pltpu.VMEM((pairs, lane_count, lane_count), jnp.bfloat16),
            pltpu.VMEM((pairs, group_count + 1, pno_count, block_count * lane_count), jnp.bfloat16),
            pltpu.VMEM((pairs, pno_count, lane_count), jnp.float32),
            *project_scratch(bases, pieces),
        ],
        compiler_params=pltpu.CompilerParams(vmem_limit_bytes=24 * 2**20),
        cost_estimate=pl.CostEstimate(
            flops=project_flops(bases, pieces) + 6 * products, bytes_accessed=2**20, transcendentals=0
        ),
    )(*operands)


def gather_pieces(mine, axis):
    count = lax.axis_size(axis)
    up, down = [mine], []
    for shift in range(1, count):
        if shift <= (count - 1) // 2:
            up.append(from_behind(up[-1], axis, 1))
        else:
            down.append(from_behind(down[-1] if down else mine, axis, count - 1))
    return up + down[::-1]


def on_device_shared(pno_basis, amplitudes, send_list, couple, couple_weight, fit_weight, fit_blocks):
    pair_count, pno_count, _ = pno_basis.shape
    group_total = lax.axis_size("blk")
    pieces = gather_pieces(fit_blocks, "dom")
    across = from_partner(pno_basis, "blk", 2)
    far = [([from_behind(fit_blocks, "blk", by)], by) for by in range(SET, group_total, SET)]
    sent = pack_pairs(send_list.reshape(-1), pno_basis, amplitudes)
    sent, *heads = lax.optimization_barrier((sent, *[group[0] for group, _ in far]))
    far = [([head], by) for head, (_, by) in zip(heads, far)]
    coupled = lax.all_to_all(sent, "blk", split_axis=0, concat_axis=0, tiled=True)
    across, pieces[1], pieces[-1] = lax.optimization_barrier((across, pieces[1], pieces[-1]))
    bases = [pno_basis, from_partner(pno_basis, "blk", 1), across, from_partner(across, "blk", 1)]
    coupled, *bases = lax.optimization_barrier((coupled, *bases))
    own, updated = dress(couple, couple_weight, fit_weight, pno_basis, amplitudes, coupled)
    last = len(pieces) // 2
    _, pieces[last] = lax.optimization_barrier((own, pieces[last]))
    groups = [pieces]
    for group, by in far:
        group += [from_behind(x, "blk", by) for x in pieces[1:]]
        if last > 1:
            source, pieces[-1] = lax.optimization_barrier((group[0], pieces[-1]))
            group[-1] = from_behind(source, "dom", len(pieces) - 1)
        groups.append(group)
    inner = [project(bases, group) for group in groups[:-1]]
    final = groups[-1]
    dressed = [own, *[from_partner(own, "blk", flip) for flip in range(1, SET)]]
    for members in ((2, 3), (0, 1)):
        partial = finish(
            members, inner, [bases[member] for member in members], final, [dressed[member] for member in members]
        )
        if members[0]:
            partial, *final = lax.optimization_barrier((partial, *final))
            for member, x in zip(members, partial):
                updated = updated + from_partner(x, "blk", member)
        else:
            mine, beside = partial
            updated, mine, beside = lax.optimization_barrier((updated, mine, from_partner(beside, "blk", 1)))
            updated = updated + mine + beside
    return updated.reshape(pair_count, pno_count * pno_count)


def dress_with(pair_amps, intersection, partner_amps, weights):
    half_product = jnp.einsum("pcab,pcbe->pcae", intersection, partner_amps, precision=HIGHEST)
    sandwich = jnp.einsum("pcae,pcfe->pcaf", half_product, intersection, precision=HIGHEST)
    return pair_amps + jnp.einsum("pc,pcaf->paf", weights, sandwich, precision=HIGHEST)


def fit_term(pair_basis, dressed, blocks, weights):
    pair_count, pno_count, orbital_count = pair_basis.shape
    flat_basis = pair_basis.reshape(pair_count * pno_count, orbital_count)
    stacked = blocks.reshape(2 * orbital_count, orbital_count)
    projected = jnp.dot(
        flat_basis, stacked.T, precision=HIGHEST, preferred_element_type=jnp.float32
    )
    projected = projected.reshape(pair_count, pno_count, 2, orbital_count)
    inner_blocks = jnp.einsum("par,pbmr->mpab", pair_basis, projected, precision=HIGHEST)
    left_product = jnp.einsum("pai,pij->paj", inner_blocks[0], dressed, precision=HIGHEST)
    fit_contrib = jnp.einsum("paj,pbj->pab", left_product, inner_blocks[1], precision=HIGHEST)
    return weights[:, None, None] * fit_contrib


def on_device_ring(pno_basis, amplitudes, send_list, couple, couple_weight, fit_weight, fit_blocks):
    pair_count, pno_count, _ = pno_basis.shape
    block_count = fit_blocks.shape[0]
    pair_amps = amplitudes.reshape(pair_count, pno_count, pno_count)
    send_order = send_list.reshape(-1)
    basis_in = lax.all_to_all(jnp.take(pno_basis, send_order, axis=0), "blk", split_axis=0, concat_axis=0, tiled=True)
    amps_in = lax.all_to_all(jnp.take(pair_amps, send_order, axis=0), "blk", split_axis=0, concat_axis=0, tiled=True)
    partner_basis = jnp.take(basis_in, couple, axis=0)
    intersection = jnp.einsum("par,pcbr->pcab", pno_basis, partner_basis, precision=HIGHEST)
    dressed = dress_with(pair_amps, intersection, jnp.take(amps_in, couple, axis=0), couple_weight)
    updated = dressed
    current = lax.all_gather(fit_blocks, "dom", axis=2, tiled=True)
    for stop in range(fit_weight.shape[1] // block_count):
        if stop > 0:
            current = from_behind(current, "blk", 1)
        for b in range(block_count):
            updated = updated + fit_term(pno_basis, dressed, current[b], fit_weight[:, stop * block_count + b])
    return updated.reshape(pair_count, pno_count * pno_count)


def solution(mesh):
    placed = (
        P(("blk", "dom"), None, None),
        P(("blk", "dom"), None),
        P("blk", "dom", None, None),
        P(("blk", "dom"), None),
        P(("blk", "dom"), None),
        P(("blk", "dom"), None),
        P("blk", None, "dom", None),
    )

    def on_device(*args):
        send_list, fit_weight, fit_blocks = args[2], args[5], args[6]
        group_total = mesh.shape["blk"]
        meets_all = fit_weight.shape[1] == group_total * fit_blocks.shape[0]
        if meets_all and group_total % SET == 0 and group_total > SET and group_total & (group_total - 1) == 0 and send_list.shape[3] == 1:
            return on_device_shared(*args)
        return on_device_ring(*args)

    return jax.shard_map(
        on_device, mesh=mesh, in_specs=placed, out_specs=P(("blk", "dom"), None), check_vma=False
    )
```

```python
import jax
import jax.numpy as jnp
from jax import lax
from jax.experimental import pallas as pl
from jax.experimental.pallas import tpu as pltpu
from jax.sharding import PartitionSpec as P

HIGHEST = lax.Precision.HIGHEST
SET = 4
NN = (((1,), (0,)), ((), ()))
NT = (((1,), (1,)), ((), ()))


def halves(x):
    high = x.astype(jnp.bfloat16)
    return high, (x - high.astype(jnp.float32)).astype(jnp.bfloat16)


def dot(a, b, dims):
    return lax.dot_general(a, b, dims, preferred_element_type=jnp.float32)


def dot3(a, b, dims):
    (a_high, a_low), (b_high, b_low) = a, b
    return dot(a_high, b_high, dims) + (dot(a_high, b_low, dims) + dot(a_low, b_high, dims))


def stack(parts, axis=0):
    return jnp.concatenate(parts, axis=axis)


def from_partner(x, axis, flip):
    return lax.ppermute(x, axis, [(i, i ^ flip) for i in range(lax.axis_size(axis))])


def from_behind(x, axis, by):
    count = lax.axis_size(axis)
    return lax.ppermute(x, axis, [(i, (i + by) % count) for i in range(count)])


def vmem(count):
    return [pl.BlockSpec(memory_space=pltpu.VMEM)] * count


def pack_kernel(send, basis, amps, out):
    peer_count, row_count, lane_count = out.shape
    pno_count = basis.shape[1]
    for peer in range(peer_count):
        pair = send[peer]
        out[peer, :pno_count] = basis[pair]
        for i in range(row_count - pno_count):
            at = pno_count + i
            out[peer, at:at + 1, :] = amps[pl.ds(pair, 1), i * lane_count:(i + 1) * lane_count]


def pack_pairs(send_order, basis, amps):
    _, pno_count, orbital_count = basis.shape
    rows = pno_count + amps.shape[1] // orbital_count
    return pl.pallas_call(
        pack_kernel,
        out_shape=jax.ShapeDtypeStruct((send_order.shape[0], rows, orbital_count), jnp.float32),
        in_specs=[pl.BlockSpec(memory_space=pltpu.SMEM), *vmem(2)],
        out_specs=vmem(1)[0],
        compiler_params=pltpu.CompilerParams(vmem_limit_bytes=62 * 2**20),
        cost_estimate=pl.CostEstimate(flops=0, bytes_accessed=4 * basis.size, transcendentals=0),
    )(send_order, basis, amps)


def dress_kernel(couple, couple_weight, fit_weight, basis, amps, coupled, dressed, result, turned, paired, partners):
    pair_count, pno_count, orbital_count = basis.shape
    half = pno_count // 2
    slot_count = coupled.shape[0]
    width = 2 * pno_count
    for i in range(half):
        paired[pl.ds(i, pair_count, stride=half), :] = amps[:, i * width:(i + 1) * width]
    for pair in range(pair_count):
        packed = paired[pair * half:(pair + 1) * half]
        for i in range(2):
            turned[pair, pl.ds(i, half, stride=2), :] = packed[:, i * pno_count:(i + 1) * pno_count]
    own = halves(basis[...].reshape(pair_count * pno_count, orbital_count))
    others = halves(coupled[:, :pno_count].reshape(slot_count * pno_count, orbital_count))
    overlap = halves(dot3(own, others, NT))
    step = orbital_count // pno_count
    left, slot_weight = [], []
    for both in range(slot_count // 2):
        named = []
        for j in range(2):
            packed = coupled[2 * both + j, pno_count:]
            for i in range(step):
                rows = pl.ds(j * pno_count + i, packed.shape[0], stride=step)
                block = packed[:, i * pno_count:(i + 1) * pno_count]
                none = jnp.zeros_like(block)
                partners[both, rows, :] = stack([none, block] if j else [block, none], 1)
            weight = jnp.where(couple[...] == 2 * both + j, couple_weight[...], 0.0)
            named.append(jnp.sum(weight, axis=1, keepdims=True))
        lane = lax.broadcasted_iota(jnp.int32, (pair_count, width), 1)
        slot_weight.append(jnp.where(lane < pno_count, *named))
        high, low = [x[:, both * width:(both + 1) * width] for x in overlap]
        diagonal = halves(partners[both])
        product = dot(high, stack(diagonal, 1), NN)
        left.append(product[:, :width] + (product[:, width:] + dot(low, diagonal[0], NN)))
    dressed[:, half:, :] = jnp.zeros((pair_count, dressed.shape[1] - half, 2 * pno_count), jnp.float32)
    for pair in range(pair_count):
        rows = slice(pair * pno_count, (pair + 1) * pno_count)
        high, low = halves(stack([x[rows] * w[pair:pair + 1] for x, w in zip(left, slot_weight)], 1))
        right = [x[rows] for x in overlap]
        product = dot(high, stack(right), NT)
        total = turned[pair] + product[:, :pno_count] + (product[:, pno_count:] + dot(low, right[0], NT))
        dressed[pair, :half] = stack([total[:half], total[half:]], 1)
        turned[pair] = total
        result[pair] = two_to_one(turned, pair, half)
        dressed[pair, half:half + 1, : fit_weight.shape[1]] = fit_weight[pair:pair + 1, :]


def two_to_one(ref, pair, half):
    return stack([ref[pair, pl.ds(i, half, stride=2), :] for i in range(2)], 1)


def dress(couple, couple_weight, fit_weight, basis, amps, coupled):
    pair_count, pno_count, _ = basis.shape
    return pl.pallas_call(
        dress_kernel,
        out_shape=tuple(
            jax.ShapeDtypeStruct((pair_count, pno_count // 2 + more, 2 * pno_count), jnp.float32) for more in (8, 0)
        ),
        in_specs=vmem(6),
        out_specs=tuple(vmem(2)),
        scratch_shapes=[
            pltpu.VMEM((pair_count, pno_count, pno_count), jnp.float32),
            pltpu.VMEM((pair_count * pno_count // 2, 2 * pno_count), jnp.float32),
            pltpu.VMEM((coupled.shape[0] // 2, 2 * pno_count, 2 * pno_count), jnp.float32),
        ],
        compiler_params=pltpu.CompilerParams(vmem_limit_bytes=10 * 2**20),
        cost_estimate=pl.CostEstimate(flops=4 * 10**9, bytes_accessed=8 * basis.size, transcendentals=0),
    )(couple, couple_weight, fit_weight, basis, amps, coupled)


def fold(x):
    return x + pltpu.roll(x, x.shape[1] // 2, 1)


def left_lanes(x):
    return lax.broadcasted_iota(jnp.int32, x.shape, 1) < x.shape[1] // 2


def split(x):
    high = x.astype(jnp.bfloat16)
    wide = high.astype(jnp.float32)
    return high, wide, x - wide


def high_low(x):
    _, high, low = split(x)
    return jnp.where(left_lanes(x), high, low).astype(jnp.bfloat16)


def split_blocks(pieces, block_cat):
    dom_count = len(pieces)
    block_count, part_count, row_count, orbital_count = pieces[0].shape
    place = lax.axis_index("dom")
    for shift, piece in enumerate(pieces):
        start = lax.rem(place + dom_count - shift, dom_count) * row_count
        for b in range(block_count):
            for m in range(part_count):
                high, low = halves(piece[b, m])
                for i, x in enumerate((high, high, low)):
                    at = pl.multiple_of(start + i * orbital_count, row_count)
                    block_cat[m, b, pl.ds(at, row_count), :] = x


def split_basis(basis, wide):
    orbital_count = basis.shape[2]
    high, low = halves(basis[...])
    for i, x in enumerate((high, low, high)):
        wide[:, :, i * orbital_count:(i + 1) * orbital_count] = x


def project_slice(wide, block, projected, at, together=4):
    pair_count, pno_count, lane_count = wide.shape
    orbital_count = block.shape[1]
    for first in range(0, pair_count, together):
        span = slice(first, min(first + together, pair_count))
        basis = wide[span]
        shape = (basis.shape[0], pno_count, orbital_count)
        product = halves(dot(basis.reshape(shape[0] * pno_count, lane_count), block[...], NN).reshape(shape))
        for i in range(2):
            projected[span, at:at + pno_count, i * orbital_count:(i + 1) * orbital_count] = product[i]


def inner_pair(wide, projected, inner_left, inner_right, pair, here):
    _, pno_count, lane_count = wide.shape
    orbital_count = lane_count // 3
    size = inner_left.shape[1]
    both = stack([wide[pair, :, i * orbital_count:(i + 1) * orbital_count] for i in range(2)])
    product = [projected[pair, :, i * orbital_count:(i + 1) * orbital_count] for i in range(2)]
    inner = fold(dot(product[0], both, NT) + dot(product[1], both, NT))
    inner_left[here] = high_low(inner[:size])
    high, _, low = split(inner[size:])
    low = jnp.where(left_lanes(low), low, 0.0).astype(jnp.bfloat16)
    for b in range(size // pno_count):
        rows = slice(b * pno_count, (b + 1) * pno_count)
        lanes = slice(b * 2 * pno_count, (b + 1) * 2 * pno_count)
        inner_right[here, :pno_count, lanes] = high[rows]
        inner_right[here, pno_count:, lanes] = low[rows]


def project_all(bases, pieces, inner_left, inner_right, scratch):
    block_cat, wide, projected = scratch
    pair_count, pno_count, _ = bases[0].shape
    part_count, block_count = block_cat.shape[:2]
    split_blocks(pieces, block_cat)
    for member, basis in enumerate(bases):
        split_basis(basis, wide.at[pl.ds(member * pair_count, pair_count)])
    for m in range(part_count):
        for b in range(block_count):
            project_slice(wide, block_cat.at[m, b], projected, (m * block_count + b) * pno_count)
    for pair in range(len(bases) * pair_count):
        inner_pair(wide, projected, inner_left, inner_right, pair, pair)


def project_kernel(member_count, *refs):
    bases, refs = refs[:member_count], refs[member_count:]
    *pieces, inner_left, inner_right = refs[:-3]
    project_all(bases, pieces, inner_left, inner_right, refs[-3:])


def inner_shapes(pairs, pno_count, block_count):
    return (
        ((pairs, block_count * pno_count, 2 * pno_count), jnp.bfloat16),
        ((pairs, 2 * pno_count, block_count * 2 * pno_count), jnp.bfloat16),
    )


def project_scratch(bases, pieces):
    pair_count, pno_count, _ = bases[0].shape
    block_count, part_count, _, orbital_count = pieces[0].shape
    return [
        pltpu.VMEM((part_count, block_count, 3 * orbital_count, orbital_count), jnp.bfloat16),
        pltpu.VMEM((len(bases) * pair_count, pno_count, 3 * orbital_count), jnp.bfloat16),
        pltpu.VMEM((len(bases) * pair_count, part_count * block_count * pno_count, 2 * orbital_count), jnp.bfloat16),
    ]


def project_flops(bases, pieces):
    pair_count, pno_count, _ = bases[0].shape
    block_count, part_count, _, orbital_count = pieces[0].shape
    rows = len(bases) * pair_count * pno_count * block_count * part_count
    return 6 * rows * orbital_count * (orbital_count + pno_count)


def project(bases, pieces):
    pair_count, pno_count, _ = bases[0].shape
    shapes = inner_shapes(len(bases) * pair_count, pno_count, pieces[0].shape[0])
    return pl.pallas_call(
        lambda *refs: project_kernel(len(bases), *refs),
        out_shape=tuple(jax.ShapeDtypeStruct(*x) for x in shapes),
        in_specs=vmem(len(bases) + len(pieces)),
        out_specs=tuple(vmem(2)),
        scratch_shapes=project_scratch(bases, pieces),
        compiler_params=pltpu.CompilerParams(vmem_limit_bytes=28 * 2**20),
        cost_estimate=pl.CostEstimate(flops=project_flops(bases, pieces), bytes_accessed=2**20, transcendentals=0),
    )(*bases, *pieces)


def finish_kernel(members, group_count, dom_count, *refs):
    count = len(members)
    groups, refs = refs[:2 * group_count], refs[2 * group_count:]
    bases, pieces, refs = refs[:count], refs[count:count + dom_count], refs[count + dom_count:]
    dressed, after, scratch = refs[:count], refs[count:2 * count], refs[2 * count:]
    inner_left, inner_right, square, moved, total = scratch[:5]
    groups = [*groups, inner_left, inner_right]
    group_count += 1
    pair_count, _, lane_count = dressed[0].shape
    pno_count = lane_count // 2
    half = pno_count // 2
    block_count = inner_left.shape[1] // pno_count
    group_total = lax.axis_size("blk")
    me = lax.axis_index("blk")
    pairs = [(index, pair) for index in range(count) for pair in range(pair_count)]

    def row_of(group, at):
        full = group < group_count - 1
        return members[at // pair_count] * pair_count + at % pair_count if full else at

    weights = []
    for index, member in enumerate(members):
        row = dressed[index][:, half:half + 1, :]
        lane = lax.broadcasted_iota(jnp.int32, row.shape, 2)
        for group in range(group_count):
            stop = lax.rem((me ^ member) + 2 * group_total + group * SET - me, group_total)
            for b in range(block_count):
                kept = jnp.where(lane == stop * block_count + b, row, 0.0)
                weights.append(jnp.sum(kept, axis=2, keepdims=True))
    project_all(bases, pieces, inner_left, inner_right, scratch[5:])
    for at, (index, pair) in enumerate(pairs):
        packed = dressed[index][pair, :half]
        other = pltpu.roll(packed, pno_count, 1)
        keep = left_lanes(packed)
        _, high, low = split(stack([jnp.where(keep, packed, other), jnp.where(keep, other, packed)]))
        square[at, :pno_count] = jnp.where(left_lanes(low), high, low).astype(jnp.bfloat16)
        square[at, pno_count:] = jnp.where(left_lanes(low), high, 0.0).astype(jnp.bfloat16)
    for at, (index, pair) in enumerate(pairs):
        lefts = [groups[2 * group][row_of(group, at)] for group in range(group_count)]
        product = fold(dot(stack(lefts), square[at], NN))
        for term in range(group_count * block_count):
            weight = weights[index * group_count * block_count + term][pair]
            rows, lanes = (slice(term * size, (term + 1) * size) for size in (pno_count, lane_count))
            moved[at, :, lanes] = high_low(product[rows] * weight)
    for at, (index, pair) in enumerate(pairs):
        rights = [groups[2 * group + 1][row_of(group, at)] for group in range(group_count)]
        total[at] = fold(dot(moved[at], stack(rights, 1), NT))
    for at, (index, pair) in enumerate(pairs):
        rows = [total[at, pl.ds(i, half, stride=2), :] for i in range(2)]
        after[index][pair] = jnp.where(left_lanes(rows[0]), *rows)


def finish(members, groups, bases, pieces, dressed):
    pair_count, _, lane_count = dressed[0].shape
    pno_count = lane_count // 2
    pairs = len(members) * pair_count
    group_count = len(groups)
    block_count = pieces[0].shape[0]
    operands = [x for group in groups for x in group] + bases + pieces + dressed
    products = pairs * pno_count**3 * 2 * (group_count + 1) * block_count
    shapes = inner_shapes(pairs, pno_count, block_count)
    return pl.pallas_call(
        lambda *refs: finish_kernel(members, group_count, len(pieces), *refs),
        out_shape=[jax.ShapeDtypeStruct((pair_count, pno_count // 2, lane_count), jnp.float32)] * len(members),
        in_specs=vmem(len(operands)),
        out_specs=vmem(len(members)),
        scratch_shapes=[
            *[pltpu.VMEM(*x) for x in shapes],
            pltpu.VMEM((pairs, lane_count, lane_count), jnp.bfloat16),
            pltpu.VMEM((pairs, pno_count, (group_count + 1) * block_count * lane_count), jnp.bfloat16),
            pltpu.VMEM((pairs, pno_count, lane_count), jnp.float32),
            *project_scratch(bases, pieces),
        ],
        compiler_params=pltpu.CompilerParams(vmem_limit_bytes=24 * 2**20),
        cost_estimate=pl.CostEstimate(
            flops=project_flops(bases, pieces) + 6 * products, bytes_accessed=2**20, transcendentals=0
        ),
    )(*operands)


def gather_pieces(mine, axis):
    count = lax.axis_size(axis)
    up, down = [mine], []
    for shift in range(1, count):
        if shift <= (count - 1) // 2:
            up.append(from_behind(up[-1], axis, 1))
        else:
            down.append(from_behind(down[-1] if down else mine, axis, count - 1))
    return up + down[::-1]


def on_device_shared(pno_basis, amplitudes, send_list, couple, couple_weight, fit_weight, fit_blocks):
    pair_count, pno_count, _ = pno_basis.shape
    group_total = lax.axis_size("blk")
    pieces = gather_pieces(fit_blocks, "dom")
    across = from_partner(pno_basis, "blk", 2)
    far = [([from_behind(fit_blocks, "blk", by)], by) for by in range(SET, group_total, SET)]
    sent = pack_pairs(send_list.reshape(-1), pno_basis, amplitudes)
    sent, *heads = lax.optimization_barrier((sent, *[group[0] for group, _ in far]))
    far = [([head], by) for head, (_, by) in zip(heads, far)]
    coupled = lax.all_to_all(sent, "blk", split_axis=0, concat_axis=0, tiled=True)
    across, pieces[1], pieces[-1] = lax.optimization_barrier((across, pieces[1], pieces[-1]))
    bases = [pno_basis, from_partner(pno_basis, "blk", 1), across, from_partner(across, "blk", 1)]
    coupled, *bases = lax.optimization_barrier((coupled, *bases))
    own, updated = dress(couple, couple_weight, fit_weight, pno_basis, amplitudes, coupled)
    last = len(pieces) // 2
    _, pieces[last] = lax.optimization_barrier((own, pieces[last]))
    groups = [pieces]
    for group, by in far:
        group += [from_behind(x, "blk", by) for x in pieces[1:]]
        if last > 1:
            source, pieces[-1] = lax.optimization_barrier((group[0], pieces[-1]))
            group[-1] = from_behind(source, "dom", len(pieces) - 1)
        groups.append(group)
    inner = [project(bases, group) for group in groups[:-1]]
    final = groups[-1]
    dressed = [own, *[from_partner(own, "blk", flip) for flip in range(1, SET)]]
    for members in ((2, 3), (0, 1)):
        partial = finish(
            members, inner, [bases[member] for member in members], final, [dressed[member] for member in members]
        )
        if members[0]:
            partial, *final = lax.optimization_barrier((partial, *final))
            for member, x in zip(members, partial):
                updated = updated + from_partner(x, "blk", member)
        else:
            mine, beside = partial
            updated, mine, beside = lax.optimization_barrier((updated, mine, from_partner(beside, "blk", 1)))
            updated = updated + mine + beside
    return updated.reshape(pair_count, pno_count * pno_count)


def dress_with(pair_amps, intersection, partner_amps, weights):
    half_product = jnp.einsum("pcab,pcbe->pcae", intersection, partner_amps, precision=HIGHEST)
    sandwich = jnp.einsum("pcae,pcfe->pcaf", half_product, intersection, precision=HIGHEST)
    return pair_amps + jnp.einsum("pc,pcaf->paf", weights, sandwich, precision=HIGHEST)


def fit_term(pair_basis, dressed, blocks, weights):
    pair_count, pno_count, orbital_count = pair_basis.shape
    flat_basis = pair_basis.reshape(pair_count * pno_count, orbital_count)
    stacked = blocks.reshape(2 * orbital_count, orbital_count)
    projected = jnp.dot(
        flat_basis, stacked.T, precision=HIGHEST, preferred_element_type=jnp.float32
    )
    projected = projected.reshape(pair_count, pno_count, 2, orbital_count)
    inner_blocks = jnp.einsum("par,pbmr->mpab", pair_basis, projected, precision=HIGHEST)
    left_product = jnp.einsum("pai,pij->paj", inner_blocks[0], dressed, precision=HIGHEST)
    fit_contrib = jnp.einsum("paj,pbj->pab", left_product, inner_blocks[1], precision=HIGHEST)
    return weights[:, None, None] * fit_contrib


def on_device_ring(pno_basis, amplitudes, send_list, couple, couple_weight, fit_weight, fit_blocks):
    pair_count, pno_count, _ = pno_basis.shape
    block_count = fit_blocks.shape[0]
    pair_amps = amplitudes.reshape(pair_count, pno_count, pno_count)
    send_order = send_list.reshape(-1)
    basis_in = lax.all_to_all(jnp.take(pno_basis, send_order, axis=0), "blk", split_axis=0, concat_axis=0, tiled=True)
    amps_in = lax.all_to_all(jnp.take(pair_amps, send_order, axis=0), "blk", split_axis=0, concat_axis=0, tiled=True)
    partner_basis = jnp.take(basis_in, couple, axis=0)
    intersection = jnp.einsum("par,pcbr->pcab", pno_basis, partner_basis, precision=HIGHEST)
    dressed = dress_with(pair_amps, intersection, jnp.take(amps_in, couple, axis=0), couple_weight)
    updated = dressed
    current = lax.all_gather(fit_blocks, "dom", axis=2, tiled=True)
    for stop in range(fit_weight.shape[1] // block_count):
        if stop > 0:
            current = from_behind(current, "blk", 1)
        for b in range(block_count):
            updated = updated + fit_term(pno_basis, dressed, current[b], fit_weight[:, stop * block_count + b])
    return updated.reshape(pair_count, pno_count * pno_count)


def solution(mesh):
    placed = (
        P(("blk", "dom"), None, None),
        P(("blk", "dom"), None),
        P("blk", "dom", None, None),
        P(("blk", "dom"), None),
        P(("blk", "dom"), None),
        P(("blk", "dom"), None),
        P("blk", None, "dom", None),
    )

    def on_device(*args):
        send_list, fit_weight, fit_blocks = args[2], args[5], args[6]
        group_total = mesh.shape["blk"]
        meets_all = fit_weight.shape[1] == group_total * fit_blocks.shape[0]
        if meets_all and group_total % SET == 0 and group_total > SET and group_total & (group_total - 1) == 0 and send_list.shape[3] == 1:
            return on_device_shared(*args)
        return on_device_ring(*args)

    return jax.shard_map(
        on_device, mesh=mesh, in_specs=placed, out_specs=P(("blk", "dom"), None), check_vma=False
    )
```

```python
import jax
import jax.numpy as jnp
from jax import lax
from jax.experimental import pallas as pl
from jax.experimental.pallas import tpu as pltpu
from jax.sharding import PartitionSpec as P

HIGHEST = lax.Precision.HIGHEST
SET = 4
NN = (((1,), (0,)), ((), ()))
NT = (((1,), (1,)), ((), ()))


def halves(x):
    high = x.astype(jnp.bfloat16)
    return high, (x - high.astype(jnp.float32)).astype(jnp.bfloat16)


def dot(a, b, dims):
    return lax.dot_general(a, b, dims, preferred_element_type=jnp.float32)


def dot3(a, b, dims):
    (a_high, a_low), (b_high, b_low) = a, b
    return dot(a_high, b_high, dims) + (dot(a_high, b_low, dims) + dot(a_low, b_high, dims))


def stack(parts, axis=0):
    return jnp.concatenate(parts, axis=axis)


def from_partner(x, axis, flip):
    return lax.ppermute(x, axis, [(i, i ^ flip) for i in range(lax.axis_size(axis))])


def from_behind(x, axis, by):
    count = lax.axis_size(axis)
    return lax.ppermute(x, axis, [(i, (i + by) % count) for i in range(count)])


def vmem(count):
    return [pl.BlockSpec(memory_space=pltpu.VMEM)] * count


def pack_kernel(send, basis, amps, out):
    peer_count, row_count, lane_count = out.shape
    pno_count = basis.shape[1]
    for peer in range(peer_count):
        pair = send[peer]
        out[peer, :pno_count] = basis[pair]
        for i in range(row_count - pno_count):
            at = pno_count + i
            out[peer, at:at + 1, :] = amps[pl.ds(pair, 1), i * lane_count:(i + 1) * lane_count]


def pack_pairs(send_order, basis, amps):
    _, pno_count, orbital_count = basis.shape
    rows = pno_count + amps.shape[1] // orbital_count
    return pl.pallas_call(
        pack_kernel,
        out_shape=jax.ShapeDtypeStruct((send_order.shape[0], rows, orbital_count), jnp.float32),
        in_specs=[pl.BlockSpec(memory_space=pltpu.SMEM), *vmem(2)],
        out_specs=vmem(1)[0],
        compiler_params=pltpu.CompilerParams(vmem_limit_bytes=62 * 2**20),
        cost_estimate=pl.CostEstimate(flops=0, bytes_accessed=4 * basis.size, transcendentals=0),
    )(send_order, basis, amps)


def dress_kernel(couple, couple_weight, fit_weight, basis, amps, coupled, dressed, result, turned, paired, partners):
    pair_count, pno_count, orbital_count = basis.shape
    half = pno_count // 2
    slot_count = coupled.shape[0]
    width = 2 * pno_count
    for i in range(half):
        paired[pl.ds(i, pair_count, stride=half), :] = amps[:, i * width:(i + 1) * width]
    for pair in range(pair_count):
        packed = paired[pair * half:(pair + 1) * half]
        for i in range(2):
            turned[pair, pl.ds(i, half, stride=2), :] = packed[:, i * pno_count:(i + 1) * pno_count]
    own = halves(basis[...].reshape(pair_count * pno_count, orbital_count))
    others = halves(coupled[:, :pno_count].reshape(slot_count * pno_count, orbital_count))
    overlap = halves(dot3(own, others, NT))
    step = orbital_count // pno_count
    left, slot_weight = [], []
    for both in range(slot_count // 2):
        named = []
        for j in range(2):
            packed = coupled[2 * both + j, pno_count:]
            for i in range(step):
                rows = pl.ds(j * pno_count + i, packed.shape[0], stride=step)
                block = packed[:, i * pno_count:(i + 1) * pno_count]
                none = jnp.zeros_like(block)
                partners[both, rows, :] = stack([none, block] if j else [block, none], 1)
            weight = jnp.where(couple[...] == 2 * both + j, couple_weight[...], 0.0)
            named.append(jnp.sum(weight, axis=1, keepdims=True))
        lane = lax.broadcasted_iota(jnp.int32, (pair_count, width), 1)
        slot_weight.append(jnp.where(lane < pno_count, *named))
        high, low = [x[:, both * width:(both + 1) * width] for x in overlap]
        diagonal = halves(partners[both])
        product = dot(high, stack(diagonal, 1), NN)
        left.append(product[:, :width] + (product[:, width:] + dot(low, diagonal[0], NN)))
    dressed[:, half:, :] = jnp.zeros((pair_count, dressed.shape[1] - half, 2 * pno_count), jnp.float32)
    for pair in range(pair_count):
        rows = slice(pair * pno_count, (pair + 1) * pno_count)
        high, low = halves(stack([x[rows] * w[pair:pair + 1] for x, w in zip(left, slot_weight)], 1))
        right = [x[rows] for x in overlap]
        product = dot(high, stack(right), NT)
        total = turned[pair] + product[:, :pno_count] + (product[:, pno_count:] + dot(low, right[0], NT))
        dressed[pair, :half] = stack([total[:half], total[half:]], 1)
        turned[pair] = total
        result[pair] = two_to_one(turned, pair, half)
        dressed[pair, half:half + 1, : fit_weight.shape[1]] = fit_weight[pair:pair + 1, :]


def two_to_one(ref, pair, half):
    return stack([ref[pair, pl.ds(i, half, stride=2), :] for i in range(2)], 1)


def dress(couple, couple_weight, fit_weight, basis, amps, coupled):
    pair_count, pno_count, _ = basis.shape
    return pl.pallas_call(
        dress_kernel,
        out_shape=tuple(
            jax.ShapeDtypeStruct((pair_count, pno_count // 2 + more, 2 * pno_count), jnp.float32) for more in (8, 0)
        ),
        in_specs=vmem(6),
        out_specs=tuple(vmem(2)),
        scratch_shapes=[
            pltpu.VMEM((pair_count, pno_count, pno_count), jnp.float32),
            pltpu.VMEM((pair_count * pno_count // 2, 2 * pno_count), jnp.float32),
            pltpu.VMEM((coupled.shape[0] // 2, 2 * pno_count, 2 * pno_count), jnp.float32),
        ],
        compiler_params=pltpu.CompilerParams(vmem_limit_bytes=10 * 2**20),
        cost_estimate=pl.CostEstimate(flops=4 * 10**9, bytes_accessed=8 * basis.size, transcendentals=0),
    )(couple, couple_weight, fit_weight, basis, amps, coupled)


def fold(x):
    return x + pltpu.roll(x, x.shape[1] // 2, 1)


def left_lanes(x):
    return lax.broadcasted_iota(jnp.int32, x.shape, 1) < x.shape[1] // 2


def split(x):
    high = x.astype(jnp.bfloat16)
    wide = high.astype(jnp.float32)
    return high, wide, x - wide


def high_low(x):
    _, high, low = split(x)
    return jnp.where(left_lanes(x), high, low).astype(jnp.bfloat16)


def split_blocks(pieces, block_cat):
    dom_count = len(pieces)
    block_count, part_count, row_count, orbital_count = pieces[0].shape
    place = lax.axis_index("dom")
    for shift, piece in enumerate(pieces):
        start = lax.rem(place + dom_count - shift, dom_count) * row_count
        for b in range(block_count):
            for m in range(part_count):
                high, low = halves(piece[b, m])
                for i, x in enumerate((high, high, low)):
                    at = pl.multiple_of(start + i * orbital_count, row_count)
                    block_cat[m, b, pl.ds(at, row_count), :] = x


def split_basis(basis, wide):
    orbital_count = basis.shape[2]
    high, low = halves(basis[...])
    for i, x in enumerate((high, low, high)):
        wide[:, :, i * orbital_count:(i + 1) * orbital_count] = x


def project_slice(wide, block, projected, at):
    pair_count, pno_count, lane_count = wide.shape
    orbital_count = block.shape[1]
    basis = wide[...].reshape(pair_count * pno_count, lane_count)
    product = halves(dot(basis, block[...], NN).reshape(pair_count, pno_count, orbital_count))
    for i in range(2):
        projected[:, at:at + pno_count, i * orbital_count:(i + 1) * orbital_count] = product[i]


def inner_pair(wide, projected, inner_left, inner_right, pair, here):
    _, pno_count, lane_count = wide.shape
    orbital_count = lane_count // 3
    size = inner_left.shape[1]
    both = stack([wide[pair, :, i * orbital_count:(i + 1) * orbital_count] for i in range(2)])
    product = [projected[pair, :, i * orbital_count:(i + 1) * orbital_count] for i in range(2)]
    inner = fold(dot(product[0], both, NT) + dot(product[1], both, NT))
    inner_left[here] = high_low(inner[:size])
    high, _, low = split(inner[size:])
    low = jnp.where(left_lanes(low), low, 0.0).astype(jnp.bfloat16)
    for b in range(size // pno_count):
        rows = slice(b * pno_count, (b + 1) * pno_count)
        lanes = slice(b * 2 * pno_count, (b + 1) * 2 * pno_count)
        inner_right[here, :pno_count, lanes] = high[rows]
        inner_right[here, pno_count:, lanes] = low[rows]


def project_all(bases, pieces, inner_left, inner_right, scratch):
    block_cat, wide, projected = scratch
    pair_count, pno_count, _ = bases[0].shape
    part_count, block_count = block_cat.shape[:2]
    split_blocks(pieces, block_cat)
    for member, basis in enumerate(bases):
        split_basis(basis, wide.at[pl.ds(member * pair_count, pair_count)])
    for m in range(part_count):
        for b in range(block_count):
            project_slice(wide, block_cat.at[m, b], projected, (m * block_count + b) * pno_count)
    for pair in range(len(bases) * pair_count):
        inner_pair(wide, projected, inner_left, inner_right, pair, pair)


def project_kernel(member_count, *refs):
    bases, refs = refs[:member_count], refs[member_count:]
    *pieces, inner_left, inner_right = refs[:-3]
    project_all(bases, pieces, inner_left, inner_right, refs[-3:])


def inner_shapes(pairs, pno_count, block_count):
    return (
        ((pairs, block_count * pno_count, 2 * pno_count), jnp.bfloat16),
        ((pairs, 2 * pno_count, block_count * 2 * pno_count), jnp.bfloat16),
    )


def project_scratch(bases, pieces):
    pair_count, pno_count, _ = bases[0].shape
    block_count, part_count, _, orbital_count = pieces[0].shape
    return [
        pltpu.VMEM((part_count, block_count, 3 * orbital_count, orbital_count), jnp.bfloat16),
        pltpu.VMEM((len(bases) * pair_count, pno_count, 3 * orbital_count), jnp.bfloat16),
        pltpu.VMEM((len(bases) * pair_count, part_count * block_count * pno_count, 2 * orbital_count), jnp.bfloat16),
    ]


def project_flops(bases, pieces):
    pair_count, pno_count, _ = bases[0].shape
    block_count, part_count, _, orbital_count = pieces[0].shape
    rows = len(bases) * pair_count * pno_count * block_count * part_count
    return 6 * rows * orbital_count * (orbital_count + pno_count)


def project(bases, pieces):
    pair_count, pno_count, _ = bases[0].shape
    shapes = inner_shapes(len(bases) * pair_count, pno_count, pieces[0].shape[0])
    return pl.pallas_call(
        lambda *refs: project_kernel(len(bases), *refs),
        out_shape=tuple(jax.ShapeDtypeStruct(*x) for x in shapes),
        in_specs=vmem(len(bases) + len(pieces)),
        out_specs=tuple(vmem(2)),
        scratch_shapes=project_scratch(bases, pieces),
        compiler_params=pltpu.CompilerParams(vmem_limit_bytes=28 * 2**20),
        cost_estimate=pl.CostEstimate(flops=project_flops(bases, pieces), bytes_accessed=2**20, transcendentals=0),
    )(*bases, *pieces)


def finish_kernel(members, group_count, dom_count, *refs):
    count = len(members)
    groups, refs = refs[:2 * group_count], refs[2 * group_count:]
    bases, pieces, refs = refs[:count], refs[count:count + dom_count], refs[count + dom_count:]
    dressed, after, scratch = refs[:count], refs[count:2 * count], refs[2 * count:]
    inner_left, inner_right, square, moved, total = scratch[:5]
    groups = [*groups, inner_left, inner_right]
    group_count += 1
    pair_count, _, lane_count = dressed[0].shape
    pno_count = lane_count // 2
    half = pno_count // 2
    block_count = inner_left.shape[1] // pno_count
    group_total = lax.axis_size("blk")
    me = lax.axis_index("blk")
    pairs = [(index, pair) for index in range(count) for pair in range(pair_count)]

    def row_of(group, at):
        full = group < group_count - 1
        return members[at // pair_count] * pair_count + at % pair_count if full else at

    weights = []
    for index, member in enumerate(members):
        row = dressed[index][:, half:half + 1, :]
        lane = lax.broadcasted_iota(jnp.int32, row.shape, 2)
        for group in range(group_count):
            stop = lax.rem((me ^ member) + 2 * group_total + group * SET - me, group_total)
            for b in range(block_count):
                kept = jnp.where(lane == stop * block_count + b, row, 0.0)
                weights.append(jnp.sum(kept, axis=2, keepdims=True))
    project_all(bases, pieces, inner_left, inner_right, scratch[5:])
    for at, (index, pair) in enumerate(pairs):
        packed = dressed[index][pair, :half]
        other = pltpu.roll(packed, pno_count, 1)
        keep = left_lanes(packed)
        _, high, low = split(stack([jnp.where(keep, packed, other), jnp.where(keep, other, packed)]))
        square[at, :pno_count] = jnp.where(left_lanes(low), high, low).astype(jnp.bfloat16)
        square[at, pno_count:] = jnp.where(left_lanes(low), high, 0.0).astype(jnp.bfloat16)
    for at, (index, pair) in enumerate(pairs):
        for group in range(group_count):
            product = fold(dot(groups[2 * group][row_of(group, at)], square[at], NN))
            for b in range(block_count):
                weight = weights[(index * group_count + group) * block_count + b][pair]
                lanes = slice(b * lane_count, (b + 1) * lane_count)
                moved[at, group, :, lanes] = high_low(product[b * pno_count:(b + 1) * pno_count] * weight)
    for at, (index, pair) in enumerate(pairs):
        terms = [dot(moved[at, group], groups[2 * group + 1][row_of(group, at)], NT) for group in range(group_count)]
        total[at] = fold(sum(terms[1:], terms[0]))
    for at, (index, pair) in enumerate(pairs):
        rows = [total[at, pl.ds(i, half, stride=2), :] for i in range(2)]
        after[index][pair] = jnp.where(left_lanes(rows[0]), *rows)


def finish(members, groups, bases, pieces, dressed):
    pair_count, _, lane_count = dressed[0].shape
    pno_count = lane_count // 2
    pairs = len(members) * pair_count
    group_count = len(groups)
    block_count = pieces[0].shape[0]
    operands = [x for group in groups for x in group] + bases + pieces + dressed
    products = pairs * pno_count**3 * 2 * (group_count + 1) * block_count
    shapes = inner_shapes(pairs, pno_count, block_count)
    return pl.pallas_call(
        lambda *refs: finish_kernel(members, group_count, len(pieces), *refs),
        out_shape=[jax.ShapeDtypeStruct((pair_count, pno_count // 2, lane_count), jnp.float32)] * len(members),
        in_specs=vmem(len(operands)),
        out_specs=vmem(len(members)),
        scratch_shapes=[
            *[pltpu.VMEM(*x) for x in shapes],
            pltpu.VMEM((pairs, lane_count, lane_count), jnp.bfloat16),
            pltpu.VMEM((pairs, group_count + 1, pno_count, block_count * lane_count), jnp.bfloat16),
            pltpu.VMEM((pairs, pno_count, lane_count), jnp.float32),
            *project_scratch(bases, pieces),
        ],
        compiler_params=pltpu.CompilerParams(vmem_limit_bytes=24 * 2**20),
        cost_estimate=pl.CostEstimate(
            flops=project_flops(bases, pieces) + 6 * products, bytes_accessed=2**20, transcendentals=0
        ),
    )(*operands)


def gather_pieces(mine, axis):
    count = lax.axis_size(axis)
    up, down = [mine], []
    for shift in range(1, count):
        if shift <= (count - 1) // 2:
            up.append(from_behind(up[-1], axis, 1))
        else:
            down.append(from_behind(down[-1] if down else mine, axis, count - 1))
    return up + down[::-1]


def on_device_shared(pno_basis, amplitudes, send_list, couple, couple_weight, fit_weight, fit_blocks):
    pair_count, pno_count, _ = pno_basis.shape
    group_total = lax.axis_size("blk")
    pieces = gather_pieces(fit_blocks, "dom")
    across = from_partner(pno_basis, "blk", 2)
    far = [([from_behind(fit_blocks, "blk", by)], by) for by in range(SET, group_total, SET)]
    sent = pack_pairs(send_list.reshape(-1), pno_basis, amplitudes)
    sent, *heads = lax.optimization_barrier((sent, *[group[0] for group, _ in far]))
    far = [([head], by) for head, (_, by) in zip(heads, far)]
    coupled = lax.all_to_all(sent, "blk", split_axis=0, concat_axis=0, tiled=True)
    across, pieces[1], pieces[-1] = lax.optimization_barrier((across, pieces[1], pieces[-1]))
    bases = [pno_basis, from_partner(pno_basis, "blk", 1), across, from_partner(across, "blk", 1)]
    coupled, *bases = lax.optimization_barrier((coupled, *bases))
    own, updated = dress(couple, couple_weight, fit_weight, pno_basis, amplitudes, coupled)
    last = len(pieces) // 2
    _, pieces[last] = lax.optimization_barrier((own, pieces[last]))
    groups = [pieces]
    for group, by in far:
        group += [from_behind(x, "blk", by) for x in pieces[1:]]
        if last > 1:
            source, pieces[-1] = lax.optimization_barrier((group[0], pieces[-1]))
            group[-1] = from_behind(source, "dom", len(pieces) - 1)
        groups.append(group)
    inner = [project(bases, group) for group in groups[:-1]]
    final = groups[-1]
    dressed = [own, *[from_partner(own, "blk", flip) for flip in range(1, SET)]]
    for members in ((3,), (2,), (0, 1)):
        partial = finish(
            members, inner, [bases[member] for member in members], final, [dressed[member] for member in members]
        )
        if members[0]:
            partial, *final = lax.optimization_barrier((partial, *final))
            for member, x in zip(members, partial):
                updated = updated + from_partner(x, "blk", member)
        else:
            mine, beside = partial
            updated, mine, beside = lax.optimization_barrier((updated, mine, from_partner(beside, "blk", 1)))
            updated = updated + mine + beside
    return updated.reshape(pair_count, pno_count * pno_count)


def dress_with(pair_amps, intersection, partner_amps, weights):
    half_product = jnp.einsum("pcab,pcbe->pcae", intersection, partner_amps, precision=HIGHEST)
    sandwich = jnp.einsum("pcae,pcfe->pcaf", half_product, intersection, precision=HIGHEST)
    return pair_amps + jnp.einsum("pc,pcaf->paf", weights, sandwich, precision=HIGHEST)


def fit_term(pair_basis, dressed, blocks, weights):
    pair_count, pno_count, orbital_count = pair_basis.shape
    flat_basis = pair_basis.reshape(pair_count * pno_count, orbital_count)
    stacked = blocks.reshape(2 * orbital_count, orbital_count)
    projected = jnp.dot(
        flat_basis, stacked.T, precision=HIGHEST, preferred_element_type=jnp.float32
    )
    projected = projected.reshape(pair_count, pno_count, 2, orbital_count)
    inner_blocks = jnp.einsum("par,pbmr->mpab", pair_basis, projected, precision=HIGHEST)
    left_product = jnp.einsum("pai,pij->paj", inner_blocks[0], dressed, precision=HIGHEST)
    fit_contrib = jnp.einsum("paj,pbj->pab", left_product, inner_blocks[1], precision=HIGHEST)
    return weights[:, None, None] * fit_contrib


def on_device_ring(pno_basis, amplitudes, send_list, couple, couple_weight, fit_weight, fit_blocks):
    pair_count, pno_count, _ = pno_basis.shape
    block_count = fit_blocks.shape[0]
    pair_amps = amplitudes.reshape(pair_count, pno_count, pno_count)
    send_order = send_list.reshape(-1)
    basis_in = lax.all_to_all(jnp.take(pno_basis, send_order, axis=0), "blk", split_axis=0, concat_axis=0, tiled=True)
    amps_in = lax.all_to_all(jnp.take(pair_amps, send_order, axis=0), "blk", split_axis=0, concat_axis=0, tiled=True)
    partner_basis = jnp.take(basis_in, couple, axis=0)
    intersection = jnp.einsum("par,pcbr->pcab", pno_basis, partner_basis, precision=HIGHEST)
    dressed = dress_with(pair_amps, intersection, jnp.take(amps_in, couple, axis=0), couple_weight)
    updated = dressed
    current = lax.all_gather(fit_blocks, "dom", axis=2, tiled=True)
    for stop in range(fit_weight.shape[1] // block_count):
        if stop > 0:
            current = from_behind(current, "blk", 1)
        for b in range(block_count):
            updated = updated + fit_term(pno_basis, dressed, current[b], fit_weight[:, stop * block_count + b])
    return updated.reshape(pair_count, pno_count * pno_count)


def solution(mesh):
    placed = (
        P(("blk", "dom"), None, None),
        P(("blk", "dom"), None),
        P("blk", "dom", None, None),
        P(("blk", "dom"), None),
        P(("blk", "dom"), None),
        P(("blk", "dom"), None),
        P("blk", None, "dom", None),
    )

    def on_device(*args):
        send_list, fit_weight, fit_blocks = args[2], args[5], args[6]
        group_total = mesh.shape["blk"]
        meets_all = fit_weight.shape[1] == group_total * fit_blocks.shape[0]
        if meets_all and group_total % SET == 0 and group_total > SET and group_total & (group_total - 1) == 0 and send_list.shape[3] == 1:
            return on_device_shared(*args)
        return on_device_ring(*args)

    return jax.shard_map(
        on_device, mesh=mesh, in_specs=placed, out_specs=P(("blk", "dom"), None), check_vma=False
    )
```

```python
import jax
import jax.numpy as jnp
from jax import lax
from jax.experimental import pallas as pl
from jax.experimental.pallas import tpu as pltpu
from jax.sharding import PartitionSpec as P

HIGHEST = lax.Precision.HIGHEST
SET = 4
NN = (((1,), (0,)), ((), ()))
NT = (((1,), (1,)), ((), ()))


def halves(x):
    high = x.astype(jnp.bfloat16)
    return high, (x - high.astype(jnp.float32)).astype(jnp.bfloat16)


def dot(a, b, dims):
    return lax.dot_general(a, b, dims, preferred_element_type=jnp.float32)


def dot3(a, b, dims):
    (a_high, a_low), (b_high, b_low) = a, b
    return dot(a_high, b_high, dims) + (dot(a_high, b_low, dims) + dot(a_low, b_high, dims))


def stack(parts, axis=0):
    return jnp.concatenate(parts, axis=axis)


def from_partner(x, axis, flip):
    return lax.ppermute(x, axis, [(i, i ^ flip) for i in range(lax.axis_size(axis))])


def from_behind(x, axis, by):
    count = lax.axis_size(axis)
    return lax.ppermute(x, axis, [(i, (i + by) % count) for i in range(count)])


def vmem(count):
    return [pl.BlockSpec(memory_space=pltpu.VMEM)] * count


def pack_kernel(send, basis, amps, out):
    peer_count, row_count, lane_count = out.shape
    pno_count = basis.shape[1]
    for peer in range(peer_count):
        pair = send[peer]
        out[peer, :pno_count] = basis[pair]
        for i in range(row_count - pno_count):
            at = pno_count + i
            out[peer, at:at + 1, :] = amps[pl.ds(pair, 1), i * lane_count:(i + 1) * lane_count]


def pack_pairs(send_order, basis, amps):
    _, pno_count, orbital_count = basis.shape
    rows = pno_count + amps.shape[1] // orbital_count
    return pl.pallas_call(
        pack_kernel,
        out_shape=jax.ShapeDtypeStruct((send_order.shape[0], rows, orbital_count), jnp.float32),
        in_specs=[pl.BlockSpec(memory_space=pltpu.SMEM), *vmem(2)],
        out_specs=vmem(1)[0],
        compiler_params=pltpu.CompilerParams(vmem_limit_bytes=62 * 2**20),
        cost_estimate=pl.CostEstimate(flops=0, bytes_accessed=4 * basis.size, transcendentals=0),
    )(send_order, basis, amps)


def dress_kernel(couple, couple_weight, fit_weight, basis, amps, coupled, dressed, result, turned, paired, partners):
    pair_count, pno_count, orbital_count = basis.shape
    half = pno_count // 2
    slot_count = coupled.shape[0]
    width = 2 * pno_count
    for i in range(half):
        paired[pl.ds(i, pair_count, stride=half), :] = amps[:, i * width:(i + 1) * width]
    for pair in range(pair_count):
        packed = paired[pair * half:(pair + 1) * half]
        for i in range(2):
            turned[pair, pl.ds(i, half, stride=2), :] = packed[:, i * pno_count:(i + 1) * pno_count]
    own = halves(basis[...].reshape(pair_count * pno_count, orbital_count))
    others = halves(coupled[:, :pno_count].reshape(slot_count * pno_count, orbital_count))
    overlap = halves(dot3(own, others, NT))
    step = orbital_count // pno_count
    left, slot_weight = [], []
    for both in range(slot_count // 2):
        named = []
        for j in range(2):
            packed = coupled[2 * both + j, pno_count:]
            for i in range(step):
                rows = pl.ds(j * pno_count + i, packed.shape[0], stride=step)
                block = packed[:, i * pno_count:(i + 1) * pno_count]
                none = jnp.zeros_like(block)
                partners[both, rows, :] = stack([none, block] if j else [block, none], 1)
            weight = jnp.where(couple[...] == 2 * both + j, couple_weight[...], 0.0)
            named.append(jnp.sum(weight, axis=1, keepdims=True))
        lane = lax.broadcasted_iota(jnp.int32, (pair_count, width), 1)
        slot_weight.append(jnp.where(lane < pno_count, *named))
        high, low = [x[:, both * width:(both + 1) * width] for x in overlap]
        diagonal = halves(partners[both])
        product = dot(high, stack(diagonal, 1), NN)
        left.append(product[:, :width] + (product[:, width:] + dot(low, diagonal[0], NN)))
    dressed[:, half:, :] = jnp.zeros((pair_count, dressed.shape[1] - half, 2 * pno_count), jnp.float32)
    for pair in range(pair_count):
        rows = slice(pair * pno_count, (pair + 1) * pno_count)
        high, low = halves(stack([x[rows] * w[pair:pair + 1] for x, w in zip(left, slot_weight)], 1))
        right = [x[rows] for x in overlap]
        product = dot(high, stack(right), NT)
        total = turned[pair] + product[:, :pno_count] + (product[:, pno_count:] + dot(low, right[0], NT))
        dressed[pair, :half] = stack([total[:half], total[half:]], 1)
        turned[pair] = total
        result[pair] = two_to_one(turned, pair, half)
        dressed[pair, half:half + 1, : fit_weight.shape[1]] = fit_weight[pair:pair + 1, :]


def two_to_one(ref, pair, half):
    return stack([ref[pair, pl.ds(i, half, stride=2), :] for i in range(2)], 1)


def dress(couple, couple_weight, fit_weight, basis, amps, coupled):
    pair_count, pno_count, _ = basis.shape
    return pl.pallas_call(
        dress_kernel,
        out_shape=tuple(
            jax.ShapeDtypeStruct((pair_count, pno_count // 2 + more, 2 * pno_count), jnp.float32) for more in (8, 0)
        ),
        in_specs=vmem(6),
        out_specs=tuple(vmem(2)),
        scratch_shapes=[
            pltpu.VMEM((pair_count, pno_count, pno_count), jnp.float32),
            pltpu.VMEM((pair_count * pno_count // 2, 2 * pno_count), jnp.float32),
            pltpu.VMEM((coupled.shape[0] // 2, 2 * pno_count, 2 * pno_count), jnp.float32),
        ],
        compiler_params=pltpu.CompilerParams(vmem_limit_bytes=10 * 2**20),
        cost_estimate=pl.CostEstimate(flops=4 * 10**9, bytes_accessed=8 * basis.size, transcendentals=0),
    )(couple, couple_weight, fit_weight, basis, amps, coupled)


def fold(x):
    return x + pltpu.roll(x, x.shape[1] // 2, 1)


def left_lanes(x):
    return lax.broadcasted_iota(jnp.int32, x.shape, 1) < x.shape[1] // 2


def split(x):
    high = x.astype(jnp.bfloat16)
    wide = high.astype(jnp.float32)
    return high, wide, x - wide


def high_low(x):
    _, high, low = split(x)
    return jnp.where(left_lanes(x), high, low).astype(jnp.bfloat16)


def split_blocks(pieces, block_cat):
    dom_count = len(pieces)
    block_count, part_count, row_count, orbital_count = pieces[0].shape
    place = lax.axis_index("dom")
    for shift, piece in enumerate(pieces):
        start = lax.rem(place + dom_count - shift, dom_count) * row_count
        for b in range(block_count):
            for m in range(part_count):
                high, low = halves(piece[b, m])
                for i, x in enumerate((high, high, low)):
                    at = pl.multiple_of(start + i * orbital_count, row_count)
                    block_cat[m, b, pl.ds(at, row_count), :] = x


def split_basis(basis, wide):
    orbital_count = basis.shape[2]
    high, low = halves(basis[...])
    for i, x in enumerate((high, low, high)):
        wide[:, :, i * orbital_count:(i + 1) * orbital_count] = x


def project_slice(wide, block, projected, at):
    pair_count, pno_count, lane_count = wide.shape
    orbital_count = block.shape[1]
    basis = wide[...].reshape(pair_count * pno_count, lane_count)
    product = halves(dot(basis, block[...], NN).reshape(pair_count, pno_count, orbital_count))
    for i in range(2):
        projected[:, at:at + pno_count, i * orbital_count:(i + 1) * orbital_count] = product[i]


def inner_pair(wide, projected, inner_left, inner_right, pair, here):
    _, pno_count, lane_count = wide.shape
    orbital_count = lane_count // 3
    size = inner_left.shape[1]
    both = stack([wide[pair, :, i * orbital_count:(i + 1) * orbital_count] for i in range(2)])
    product = [projected[pair, :, i * orbital_count:(i + 1) * orbital_count] for i in range(2)]
    inner = fold(dot(product[0], both, NT) + dot(product[1], both, NT))
    inner_left[here] = high_low(inner[:size])
    high, _, low = split(inner[size:])
    low = jnp.where(left_lanes(low), low, 0.0).astype(jnp.bfloat16)
    for b in range(size // pno_count):
        rows = slice(b * pno_count, (b + 1) * pno_count)
        lanes = slice(b * 2 * pno_count, (b + 1) * 2 * pno_count)
        inner_right[here, :pno_count, lanes] = high[rows]
        inner_right[here, pno_count:, lanes] = low[rows]


def project_all(bases, pieces, inner_left, inner_right, scratch):
    block_cat, wide, projected = scratch
    pair_count, pno_count, _ = bases[0].shape
    part_count, block_count = block_cat.shape[:2]
    split_blocks(pieces, block_cat)
    for member, basis in enumerate(bases):
        split_basis(basis, wide.at[pl.ds(member * pair_count, pair_count)])
    for m in range(part_count):
        for b in range(block_count):
            project_slice(wide, block_cat.at[m, b], projected, (m * block_count + b) * pno_count)
    for pair in range(len(bases) * pair_count):
        inner_pair(wide, projected, inner_left, inner_right, pair, pair)


def project_kernel(member_count, *refs):
    bases, refs = refs[:member_count], refs[member_count:]
    *pieces, inner_left, inner_right = refs[:-3]
    project_all(bases, pieces, inner_left, inner_right, refs[-3:])


def inner_shapes(pairs, pno_count, block_count):
    return (
        ((pairs, block_count * pno_count, 2 * pno_count), jnp.bfloat16),
        ((pairs, 2 * pno_count, block_count * 2 * pno_count), jnp.bfloat16),
    )


def project_scratch(bases, pieces):
    pair_count, pno_count, _ = bases[0].shape
    block_count, part_count, _, orbital_count = pieces[0].shape
    return [
        pltpu.VMEM((part_count, block_count, 3 * orbital_count, orbital_count), jnp.bfloat16),
        pltpu.VMEM((len(bases) * pair_count, pno_count, 3 * orbital_count), jnp.bfloat16),
        pltpu.VMEM((len(bases) * pair_count, part_count * block_count * pno_count, 2 * orbital_count), jnp.bfloat16),
    ]


def project_flops(bases, pieces):
    pair_count, pno_count, _ = bases[0].shape
    block_count, part_count, _, orbital_count = pieces[0].shape
    rows = len(bases) * pair_count * pno_count * block_count * part_count
    return 6 * rows * orbital_count * (orbital_count + pno_count)


def project(bases, pieces):
    pair_count, pno_count, _ = bases[0].shape
    shapes = inner_shapes(len(bases) * pair_count, pno_count, pieces[0].shape[0])
    return pl.pallas_call(
        lambda *refs: project_kernel(len(bases), *refs),
        out_shape=tuple(jax.ShapeDtypeStruct(*x) for x in shapes),
        in_specs=vmem(len(bases) + len(pieces)),
        out_specs=tuple(vmem(2)),
        scratch_shapes=project_scratch(bases, pieces),
        compiler_params=pltpu.CompilerParams(vmem_limit_bytes=28 * 2**20),
        cost_estimate=pl.CostEstimate(flops=project_flops(bases, pieces), bytes_accessed=2**20, transcendentals=0),
    )(*bases, *pieces)


def finish_kernel(members, group_count, dom_count, *refs):
    count = len(members)
    groups, refs = refs[:2 * group_count], refs[2 * group_count:]
    bases, pieces, refs = refs[:count], refs[count:count + dom_count], refs[count + dom_count:]
    dressed, after, scratch = refs[:count], refs[count:2 * count], refs[2 * count:]
    inner_left, inner_right, square, moved, total = scratch[:5]
    groups = [*groups, inner_left, inner_right]
    group_count += 1
    pair_count, _, lane_count = dressed[0].shape
    pno_count = lane_count // 2
    half = pno_count // 2
    block_count = inner_left.shape[1] // pno_count
    group_total = lax.axis_size("blk")
    me = lax.axis_index("blk")
    pairs = [(index, pair) for index in range(count) for pair in range(pair_count)]

    def row_of(group, at):
        full = group < group_count - 1
        return members[at // pair_count] * pair_count + at % pair_count if full else at

    weights = []
    for index, member in enumerate(members):
        row = dressed[index][:, half:half + 1, :]
        lane = lax.broadcasted_iota(jnp.int32, row.shape, 2)
        for group in range(group_count):
            stop = lax.rem((me ^ member) + 2 * group_total + group * SET - me, group_total)
            for b in range(block_count):
                kept = jnp.where(lane == stop * block_count + b, row, 0.0)
                weights.append(jnp.sum(kept, axis=2, keepdims=True))
    project_all(bases, pieces, inner_left, inner_right, scratch[5:])
    for at, (index, pair) in enumerate(pairs):
        packed = dressed[index][pair, :half]
        other = pltpu.roll(packed, pno_count, 1)
        keep = left_lanes(packed)
        _, high, low = split(stack([jnp.where(keep, packed, other), jnp.where(keep, other, packed)]))
        square[at, :pno_count] = jnp.where(left_lanes(low), high, low).astype(jnp.bfloat16)
        square[at, pno_count:] = jnp.where(left_lanes(low), high, 0.0).astype(jnp.bfloat16)
    for at, (index, pair) in enumerate(pairs):
        for group in range(group_count):
            product = fold(dot(groups[2 * group][row_of(group, at)], square[at], NN))
            for b in range(block_count):
                weight = weights[(index * group_count + group) * block_count + b][pair]
                lanes = slice(b * lane_count, (b + 1) * lane_count)
                moved[at, group, :, lanes] = high_low(product[b * pno_count:(b + 1) * pno_count] * weight)
    for at, (index, pair) in enumerate(pairs):
        terms = [dot(moved[at, group], groups[2 * group + 1][row_of(group, at)], NT) for group in range(group_count)]
        total[at] = fold(sum(terms[1:], terms[0]))
    for at, (index, pair) in enumerate(pairs):
        rows = [total[at, pl.ds(i, half, stride=2), :] for i in range(2)]
        after[index][pair] = jnp.where(left_lanes(rows[0]), *rows)


def finish(members, groups, bases, pieces, dressed):
    pair_count, _, lane_count = dressed[0].shape
    pno_count = lane_count // 2
    pairs = len(members) * pair_count
    group_count = len(groups)
    block_count = pieces[0].shape[0]
    operands = [x for group in groups for x in group] + bases + pieces + dressed
    products = pairs * pno_count**3 * 2 * (group_count + 1) * block_count
    shapes = inner_shapes(pairs, pno_count, block_count)
    return pl.pallas_call(
        lambda *refs: finish_kernel(members, group_count, len(pieces), *refs),
        out_shape=[jax.ShapeDtypeStruct((pair_count, pno_count // 2, lane_count), jnp.float32)] * len(members),
        in_specs=vmem(len(operands)),
        out_specs=vmem(len(members)),
        scratch_shapes=[
            *[pltpu.VMEM(*x) for x in shapes],
            pltpu.VMEM((pairs, lane_count, lane_count), jnp.bfloat16),
            pltpu.VMEM((pairs, group_count + 1, pno_count, block_count * lane_count), jnp.bfloat16),
            pltpu.VMEM((pairs, pno_count, lane_count), jnp.float32),
            *project_scratch(bases, pieces),
        ],
        compiler_params=pltpu.CompilerParams(vmem_limit_bytes=24 * 2**20),
        cost_estimate=pl.CostEstimate(
            flops=project_flops(bases, pieces) + 6 * products, bytes_accessed=2**20, transcendentals=0
        ),
    )(*operands)


def gather_pieces(mine, axis):
    count = lax.axis_size(axis)
    up, down = [mine], []
    for shift in range(1, count):
        if shift <= (count - 1) // 2:
            up.append(from_behind(up[-1], axis, 1))
        else:
            down.append(from_behind(down[-1] if down else mine, axis, count - 1))
    return up + down[::-1]


def on_device_shared(pno_basis, amplitudes, send_list, couple, couple_weight, fit_weight, fit_blocks):
    pair_count, pno_count, _ = pno_basis.shape
    group_total = lax.axis_size("blk")
    pieces = gather_pieces(fit_blocks, "dom")
    across = from_partner(pno_basis, "blk", 2)
    far = [([from_behind(fit_blocks, "blk", by)], by) for by in range(SET, group_total, SET)]
    sent = pack_pairs(send_list.reshape(-1), pno_basis, amplitudes)
    sent, *heads = lax.optimization_barrier((sent, *[group[0] for group, _ in far]))
    far = [([head], by) for head, (_, by) in zip(heads, far)]
    coupled = lax.all_to_all(sent, "blk", split_axis=0, concat_axis=0, tiled=True)
    across, pieces[1], pieces[-1] = lax.optimization_barrier((across, pieces[1], pieces[-1]))
    bases = [pno_basis, from_partner(pno_basis, "blk", 1), across, from_partner(across, "blk", 1)]
    coupled, *bases = lax.optimization_barrier((coupled, *bases))
    own, updated = dress(couple, couple_weight, fit_weight, pno_basis, amplitudes, coupled)
    last = len(pieces) // 2
    _, pieces[last] = lax.optimization_barrier((own, pieces[last]))
    groups = [pieces]
    for group, by in far:
        group += [from_behind(x, "blk", by) for x in pieces[1:]]
        if last > 1:
            source, pieces[-1] = lax.optimization_barrier((group[0], pieces[-1]))
            group[-1] = from_behind(source, "dom", len(pieces) - 1)
        groups.append(group)
    inner = [project(bases, group) for group in groups[:-1]]
    final = groups[-1]
    dressed = [own, *[from_partner(own, "blk", flip) for flip in range(1, SET)]]
    for member in (3, 2, 1, 0):
        partial = finish((member,), inner, [bases[member]], final, [dressed[member]])[0]
        if member:
            partial, *final = lax.optimization_barrier((partial, *final))
            partial = from_partner(partial, "blk", member)
        if member == 1:
            beside = partial
        else:
            updated = updated + partial
    updated, beside = lax.optimization_barrier((updated, beside))
    updated = updated + beside
    return updated.reshape(pair_count, pno_count * pno_count)


def dress_with(pair_amps, intersection, partner_amps, weights):
    half_product = jnp.einsum("pcab,pcbe->pcae", intersection, partner_amps, precision=HIGHEST)
    sandwich = jnp.einsum("pcae,pcfe->pcaf", half_product, intersection, precision=HIGHEST)
    return pair_amps + jnp.einsum("pc,pcaf->paf", weights, sandwich, precision=HIGHEST)


def fit_term(pair_basis, dressed, blocks, weights):
    pair_count, pno_count, orbital_count = pair_basis.shape
    flat_basis = pair_basis.reshape(pair_count * pno_count, orbital_count)
    stacked = blocks.reshape(2 * orbital_count, orbital_count)
    projected = jnp.dot(
        flat_basis, stacked.T, precision=HIGHEST, preferred_element_type=jnp.float32
    )
    projected = projected.reshape(pair_count, pno_count, 2, orbital_count)
    inner_blocks = jnp.einsum("par,pbmr->mpab", pair_basis, projected, precision=HIGHEST)
    left_product = jnp.einsum("pai,pij->paj", inner_blocks[0], dressed, precision=HIGHEST)
    fit_contrib = jnp.einsum("paj,pbj->pab", left_product, inner_blocks[1], precision=HIGHEST)
    return weights[:, None, None] * fit_contrib


def on_device_ring(pno_basis, amplitudes, send_list, couple, couple_weight, fit_weight, fit_blocks):
    pair_count, pno_count, _ = pno_basis.shape
    block_count = fit_blocks.shape[0]
    pair_amps = amplitudes.reshape(pair_count, pno_count, pno_count)
    send_order = send_list.reshape(-1)
    basis_in = lax.all_to_all(jnp.take(pno_basis, send_order, axis=0), "blk", split_axis=0, concat_axis=0, tiled=True)
    amps_in = lax.all_to_all(jnp.take(pair_amps, send_order, axis=0), "blk", split_axis=0, concat_axis=0, tiled=True)
    partner_basis = jnp.take(basis_in, couple, axis=0)
    intersection = jnp.einsum("par,pcbr->pcab", pno_basis, partner_basis, precision=HIGHEST)
    dressed = dress_with(pair_amps, intersection, jnp.take(amps_in, couple, axis=0), couple_weight)
    updated = dressed
    current = lax.all_gather(fit_blocks, "dom", axis=2, tiled=True)
    for stop in range(fit_weight.shape[1] // block_count):
        if stop > 0:
            current = from_behind(current, "blk", 1)
        for b in range(block_count):
            updated = updated + fit_term(pno_basis, dressed, current[b], fit_weight[:, stop * block_count + b])
    return updated.reshape(pair_count, pno_count * pno_count)


def solution(mesh):
    placed = (
        P(("blk", "dom"), None, None),
        P(("blk", "dom"), None),
        P("blk", "dom", None, None),
        P(("blk", "dom"), None),
        P(("blk", "dom"), None),
        P(("blk", "dom"), None),
        P("blk", None, "dom", None),
    )

    def on_device(*args):
        send_list, fit_weight, fit_blocks = args[2], args[5], args[6]
        group_total = mesh.shape["blk"]
        meets_all = fit_weight.shape[1] == group_total * fit_blocks.shape[0]
        if meets_all and group_total % SET == 0 and group_total > SET and group_total & (group_total - 1) == 0 and send_list.shape[3] == 1:
            return on_device_shared(*args)
        return on_device_ring(*args)

    return jax.shard_map(
        on_device, mesh=mesh, in_specs=placed, out_specs=P(("blk", "dom"), None), check_vma=False
    )
```

```python
import jax
import jax.numpy as jnp
from jax import lax
from jax.experimental import pallas as pl
from jax.experimental.pallas import tpu as pltpu
from jax.sharding import PartitionSpec as P

HIGHEST = lax.Precision.HIGHEST
SET = 4
NN = (((1,), (0,)), ((), ()))
NT = (((1,), (1,)), ((), ()))


def halves(x):
    high = x.astype(jnp.bfloat16)
    return high, (x - high.astype(jnp.float32)).astype(jnp.bfloat16)


def dot(a, b, dims):
    return lax.dot_general(a, b, dims, preferred_element_type=jnp.float32)


def dot3(a, b, dims):
    (a_high, a_low), (b_high, b_low) = a, b
    return dot(a_high, b_high, dims) + (dot(a_high, b_low, dims) + dot(a_low, b_high, dims))


def stack(parts, axis=0):
    return jnp.concatenate(parts, axis=axis)


def from_partner(x, axis, flip):
    return lax.ppermute(x, axis, [(i, i ^ flip) for i in range(lax.axis_size(axis))])


def from_behind(x, axis, by):
    count = lax.axis_size(axis)
    return lax.ppermute(x, axis, [(i, (i + by) % count) for i in range(count)])


def vmem(count):
    return [pl.BlockSpec(memory_space=pltpu.VMEM)] * count


def pack_kernel(send, basis, amps, out):
    peer_count, row_count, lane_count = out.shape
    pno_count = basis.shape[1]
    for peer in range(peer_count):
        pair = send[peer]
        out[peer, :pno_count] = basis[pair]
        for i in range(row_count - pno_count):
            at = pno_count + i
            out[peer, at:at + 1, :] = amps[pl.ds(pair, 1), i * lane_count:(i + 1) * lane_count]


def pack_pairs(send_order, basis, amps):
    _, pno_count, orbital_count = basis.shape
    rows = pno_count + amps.shape[1] // orbital_count
    return pl.pallas_call(
        pack_kernel,
        out_shape=jax.ShapeDtypeStruct((send_order.shape[0], rows, orbital_count), jnp.float32),
        in_specs=[pl.BlockSpec(memory_space=pltpu.SMEM), *vmem(2)],
        out_specs=vmem(1)[0],
        compiler_params=pltpu.CompilerParams(vmem_limit_bytes=62 * 2**20),
        cost_estimate=pl.CostEstimate(flops=0, bytes_accessed=4 * basis.size, transcendentals=0),
    )(send_order, basis, amps)


def dress_kernel(couple, couple_weight, fit_weight, basis, amps, coupled, dressed, result, turned, paired, partners):
    pair_count, pno_count, orbital_count = basis.shape
    half = pno_count // 2
    slot_count = coupled.shape[0]
    width = 2 * pno_count
    for i in range(half):
        paired[pl.ds(i, pair_count, stride=half), :] = amps[:, i * width:(i + 1) * width]
    for pair in range(pair_count):
        packed = paired[pair * half:(pair + 1) * half]
        for i in range(2):
            turned[pair, pl.ds(i, half, stride=2), :] = packed[:, i * pno_count:(i + 1) * pno_count]
    own = halves(basis[...].reshape(pair_count * pno_count, orbital_count))
    others = halves(coupled[:, :pno_count].reshape(slot_count * pno_count, orbital_count))
    overlap = halves(dot3(own, others, NT))
    step = orbital_count // pno_count
    left, slot_weight = [], []
    for both in range(slot_count // 2):
        named = []
        for j in range(2):
            packed = coupled[2 * both + j, pno_count:]
            for i in range(step):
                rows = pl.ds(j * pno_count + i, packed.shape[0], stride=step)
                block = packed[:, i * pno_count:(i + 1) * pno_count]
                none = jnp.zeros_like(block)
                partners[both, rows, :] = stack([none, block] if j else [block, none], 1)
            weight = jnp.where(couple[...] == 2 * both + j, couple_weight[...], 0.0)
            named.append(jnp.sum(weight, axis=1, keepdims=True))
        lane = lax.broadcasted_iota(jnp.int32, (pair_count, width), 1)
        slot_weight.append(jnp.where(lane < pno_count, *named))
        high, low = [x[:, both * width:(both + 1) * width] for x in overlap]
        diagonal = halves(partners[both])
        product = dot(high, stack(diagonal, 1), NN)
        left.append(product[:, :width] + (product[:, width:] + dot(low, diagonal[0], NN)))
    dressed[:, half:, :] = jnp.zeros((pair_count, dressed.shape[1] - half, 2 * pno_count), jnp.float32)
    for pair in range(pair_count):
        rows = slice(pair * pno_count, (pair + 1) * pno_count)
        high, low = halves(stack([x[rows] * w[pair:pair + 1] for x, w in zip(left, slot_weight)], 1))
        right = [x[rows] for x in overlap]
        product = dot(high, stack(right), NT)
        total = turned[pair] + product[:, :pno_count] + (product[:, pno_count:] + dot(low, right[0], NT))
        dressed[pair, :half] = stack([total[:half], total[half:]], 1)
        turned[pair] = total
        result[pair] = two_to_one(turned, pair, half)
        dressed[pair, half:half + 1, : fit_weight.shape[1]] = fit_weight[pair:pair + 1, :]


def two_to_one(ref, pair, half):
    return stack([ref[pair, pl.ds(i, half, stride=2), :] for i in range(2)], 1)


def dress(couple, couple_weight, fit_weight, basis, amps, coupled):
    pair_count, pno_count, _ = basis.shape
    return pl.pallas_call(
        dress_kernel,
        out_shape=tuple(
            jax.ShapeDtypeStruct((pair_count, pno_count // 2 + more, 2 * pno_count), jnp.float32) for more in (8, 0)
        ),
        in_specs=vmem(6),
        out_specs=tuple(vmem(2)),
        scratch_shapes=[
            pltpu.VMEM((pair_count, pno_count, pno_count), jnp.float32),
            pltpu.VMEM((pair_count * pno_count // 2, 2 * pno_count), jnp.float32),
            pltpu.VMEM((coupled.shape[0] // 2, 2 * pno_count, 2 * pno_count), jnp.float32),
        ],
        compiler_params=pltpu.CompilerParams(vmem_limit_bytes=10 * 2**20),
        cost_estimate=pl.CostEstimate(flops=4 * 10**9, bytes_accessed=8 * basis.size, transcendentals=0),
    )(couple, couple_weight, fit_weight, basis, amps, coupled)


def fold(x):
    return x + pltpu.roll(x, x.shape[1] // 2, 1)


def left_lanes(x):
    return lax.broadcasted_iota(jnp.int32, x.shape, 1) < x.shape[1] // 2


def split(x):
    high = x.astype(jnp.bfloat16)
    wide = high.astype(jnp.float32)
    return high, wide, x - wide


def high_low(x):
    _, high, low = split(x)
    return jnp.where(left_lanes(x), high, low).astype(jnp.bfloat16)


def split_blocks(pieces, block_cat):
    dom_count = len(pieces)
    block_count, part_count, row_count, orbital_count = pieces[0].shape
    place = lax.axis_index("dom")
    for shift, piece in enumerate(pieces):
        start = lax.rem(place + dom_count - shift, dom_count) * row_count
        for b in range(block_count):
            for m in range(part_count):
                high, low = halves(piece[b, m])
                for i, x in enumerate((high, high, low)):
                    at = pl.multiple_of(start + i * orbital_count, row_count)
                    block_cat[m, b, pl.ds(at, row_count), :] = x


def split_basis(basis, wide):
    orbital_count = basis.shape[2]
    high, low = halves(basis[...])
    for i, x in enumerate((high, low, high)):
        wide[:, :, i * orbital_count:(i + 1) * orbital_count] = x


def project_slice(wide, block, projected, at):
    pair_count, pno_count, lane_count = wide.shape
    orbital_count = block.shape[1]
    basis = wide[...].reshape(pair_count * pno_count, lane_count)
    product = halves(dot(basis, block[...], NN).reshape(pair_count, pno_count, orbital_count))
    for i in range(2):
        projected[:, at:at + pno_count, i * orbital_count:(i + 1) * orbital_count] = product[i]


def inner_pair(wide, projected, inner_left, inner_right, pair, here):
    _, pno_count, lane_count = wide.shape
    orbital_count = lane_count // 3
    size = inner_left.shape[1]
    both = stack([wide[pair, :, i * orbital_count:(i + 1) * orbital_count] for i in range(2)])
    product = [projected[pair, :, i * orbital_count:(i + 1) * orbital_count] for i in range(2)]
    inner = fold(dot(product[0], both, NT) + dot(product[1], both, NT))
    inner_left[here] = high_low(inner[:size])
    high, _, low = split(inner[size:])
    low = jnp.where(left_lanes(low), low, 0.0).astype(jnp.bfloat16)
    for b in range(size // pno_count):
        rows = slice(b * pno_count, (b + 1) * pno_count)
        lanes = slice(b * 2 * pno_count, (b + 1) * 2 * pno_count)
        inner_right[here, :pno_count, lanes] = high[rows]
        inner_right[here, pno_count:, lanes] = low[rows]


def project_all(bases, pieces, inner_left, inner_right, scratch):
    block_cat, wide, projected = scratch
    pair_count, pno_count, _ = bases[0].shape
    part_count, block_count = block_cat.shape[:2]
    split_blocks(pieces, block_cat)
    for member, basis in enumerate(bases):
        split_basis(basis, wide.at[pl.ds(member * pair_count, pair_count)])
    for m in range(part_count):
        for b in range(block_count):
            project_slice(wide, block_cat.at[m, b], projected, (m * block_count + b) * pno_count)
    for pair in range(len(bases) * pair_count):
        inner_pair(wide, projected, inner_left, inner_right, pair, pair)


def project_kernel(member_count, *refs):
    bases, refs = refs[:member_count], refs[member_count:]
    *pieces, inner_left, inner_right = refs[:-3]
    project_all(bases, pieces, inner_left, inner_right, refs[-3:])


def inner_shapes(pairs, pno_count, block_count):
    return (
        ((pairs, block_count * pno_count, 2 * pno_count), jnp.bfloat16),
        ((pairs, 2 * pno_count, block_count * 2 * pno_count), jnp.bfloat16),
    )


def project_scratch(bases, pieces):
    pair_count, pno_count, _ = bases[0].shape
    block_count, part_count, _, orbital_count = pieces[0].shape
    return [
        pltpu.VMEM((part_count, block_count, 3 * orbital_count, orbital_count), jnp.bfloat16),
        pltpu.VMEM((len(bases) * pair_count, pno_count, 3 * orbital_count), jnp.bfloat16),
        pltpu.VMEM((len(bases) * pair_count, part_count * block_count * pno_count, 2 * orbital_count), jnp.bfloat16),
    ]


def project_flops(bases, pieces):
    pair_count, pno_count, _ = bases[0].shape
    block_count, part_count, _, orbital_count = pieces[0].shape
    rows = len(bases) * pair_count * pno_count * block_count * part_count
    return 6 * rows * orbital_count * (orbital_count + pno_count)


def project(bases, pieces):
    pair_count, pno_count, _ = bases[0].shape
    shapes = inner_shapes(len(bases) * pair_count, pno_count, pieces[0].shape[0])
    return pl.pallas_call(
        lambda *refs: project_kernel(len(bases), *refs),
        out_shape=tuple(jax.ShapeDtypeStruct(*x) for x in shapes),
        in_specs=vmem(len(bases) + len(pieces)),
        out_specs=tuple(vmem(2)),
        scratch_shapes=project_scratch(bases, pieces),
        compiler_params=pltpu.CompilerParams(vmem_limit_bytes=24 * 2**20),
        cost_estimate=pl.CostEstimate(flops=project_flops(bases, pieces), bytes_accessed=2**20, transcendentals=0),
    )(*bases, *pieces)


def finish_kernel(members, group_count, dom_count, *refs):
    count = len(members)
    groups, refs = refs[:2 * group_count], refs[2 * group_count:]
    bases, pieces, refs = refs[:count], refs[count:count + dom_count], refs[count + dom_count:]
    dressed, after, scratch = refs[:count], refs[count:2 * count], refs[2 * count:]
    inner_left, inner_right, square, moved, total = scratch[:5]
    groups = [*groups, inner_left, inner_right]
    group_count += 1
    pair_count, _, lane_count = dressed[0].shape
    pno_count = lane_count // 2
    half = pno_count // 2
    block_count = inner_left.shape[1] // pno_count
    group_total = lax.axis_size("blk")
    me = lax.axis_index("blk")
    pairs = [(index, pair) for index in range(count) for pair in range(pair_count)]

    def row_of(group, at):
        full = group < group_count - 1
        return members[at // pair_count] * pair_count + at % pair_count if full else at

    weights = []
    for index, member in enumerate(members):
        row = dressed[index][:, half:half + 1, :]
        lane = lax.broadcasted_iota(jnp.int32, row.shape, 2)
        for group in range(group_count):
            stop = lax.rem((me ^ member) + 2 * group_total + group * SET - me, group_total)
            for b in range(block_count):
                kept = jnp.where(lane == stop * block_count + b, row, 0.0)
                weights.append(jnp.sum(kept, axis=2, keepdims=True))
    project_all(bases, pieces, inner_left, inner_right, scratch[5:])
    for at, (index, pair) in enumerate(pairs):
        packed = dressed[index][pair, :half]
        other = pltpu.roll(packed, pno_count, 1)
        keep = left_lanes(packed)
        _, high, low = split(stack([jnp.where(keep, packed, other), jnp.where(keep, other, packed)]))
        square[at, :pno_count] = jnp.where(left_lanes(low), high, low).astype(jnp.bfloat16)
        square[at, pno_count:] = jnp.where(left_lanes(low), high, 0.0).astype(jnp.bfloat16)
    for at, (index, pair) in enumerate(pairs):
        for group in range(group_count):
            product = fold(dot(groups[2 * group][row_of(group, at)], square[at], NN))
            for b in range(block_count):
                weight = weights[(index * group_count + group) * block_count + b][pair]
                lanes = slice(b * lane_count, (b + 1) * lane_count)
                moved[at, group, :, lanes] = high_low(product[b * pno_count:(b + 1) * pno_count] * weight)
    for at, (index, pair) in enumerate(pairs):
        terms = [dot(moved[at, group], groups[2 * group + 1][row_of(group, at)], NT) for group in range(group_count)]
        total[at] = fold(sum(terms[1:], terms[0]))
    for at, (index, pair) in enumerate(pairs):
        rows = [total[at, pl.ds(i, half, stride=2), :] for i in range(2)]
        after[index][pair] = jnp.where(left_lanes(rows[0]), *rows)


def finish(members, groups, bases, pieces, dressed):
    pair_count, _, lane_count = dressed[0].shape
    pno_count = lane_count // 2
    pairs = len(members) * pair_count
    group_count = len(groups)
    block_count = pieces[0].shape[0]
    operands = [x for group in groups for x in group] + bases + pieces + dressed
    products = pairs * pno_count**3 * 2 * (group_count + 1) * block_count
    shapes = inner_shapes(pairs, pno_count, block_count)
    return pl.pallas_call(
        lambda *refs: finish_kernel(members, group_count, len(pieces), *refs),
        out_shape=[jax.ShapeDtypeStruct((pair_count, pno_count // 2, lane_count), jnp.float32)] * len(members),
        in_specs=vmem(len(operands)),
        out_specs=vmem(len(members)),
        scratch_shapes=[
            *[pltpu.VMEM(*x) for x in shapes],
            pltpu.VMEM((pairs, lane_count, lane_count), jnp.bfloat16),
            pltpu.VMEM((pairs, group_count + 1, pno_count, block_count * lane_count), jnp.bfloat16),
            pltpu.VMEM((pairs, pno_count, lane_count), jnp.float32),
            *project_scratch(bases, pieces),
        ],
        compiler_params=pltpu.CompilerParams(vmem_limit_bytes=14 * 2**20),
        cost_estimate=pl.CostEstimate(
            flops=project_flops(bases, pieces) + 6 * products, bytes_accessed=2**20, transcendentals=0
        ),
    )(*operands)


def gather_pieces(mine, axis):
    count = lax.axis_size(axis)
    up, down = [mine], []
    for shift in range(1, count):
        if shift <= (count - 1) // 2:
            up.append(from_behind(up[-1], axis, 1))
        else:
            down.append(from_behind(down[-1] if down else mine, axis, count - 1))
    return up + down[::-1]


def on_device_shared(pno_basis, amplitudes, send_list, couple, couple_weight, fit_weight, fit_blocks):
    pair_count, pno_count, _ = pno_basis.shape
    group_total = lax.axis_size("blk")
    pieces = gather_pieces(fit_blocks, "dom")
    across = from_partner(pno_basis, "blk", 2)
    far = [([from_behind(fit_blocks, "blk", by)], by) for by in range(SET, group_total, SET)]
    sent = pack_pairs(send_list.reshape(-1), pno_basis, amplitudes)
    sent, *heads = lax.optimization_barrier((sent, *[group[0] for group, _ in far]))
    far = [([head], by) for head, (_, by) in zip(heads, far)]
    coupled = lax.all_to_all(sent, "blk", split_axis=0, concat_axis=0, tiled=True)
    across, pieces[1], pieces[-1] = lax.optimization_barrier((across, pieces[1], pieces[-1]))
    bases = [pno_basis, from_partner(pno_basis, "blk", 1), across, from_partner(across, "blk", 1)]
    coupled, *bases = lax.optimization_barrier((coupled, *bases))
    own, updated = dress(couple, couple_weight, fit_weight, pno_basis, amplitudes, coupled)
    last = len(pieces) // 2
    _, pieces[last] = lax.optimization_barrier((own, pieces[last]))
    groups = [pieces]
    for group, by in far:
        group += [from_behind(x, "blk", by) for x in pieces[1:]]
        if last > 1:
            source, pieces[-1] = lax.optimization_barrier((group[0], pieces[-1]))
            group[-1] = from_behind(source, "dom", len(pieces) - 1)
        groups.append(group)
    inner = [project(bases, group) for group in groups[:-1]]
    final = groups[-1]
    dressed = [own, *[from_partner(own, "blk", flip) for flip in range(1, SET)]]
    for member in (3, 2, 1, 0):
        partial = finish((member,), inner, [bases[member]], final, [dressed[member]])[0]
        if member:
            partial, *final = lax.optimization_barrier((partial, *final))
            partial = from_partner(partial, "blk", member)
        if member == 1:
            beside = partial
        else:
            updated = updated + partial
    updated, beside = lax.optimization_barrier((updated, beside))
    updated = updated + beside
    return updated.reshape(pair_count, pno_count * pno_count)


def dress_with(pair_amps, intersection, partner_amps, weights):
    half_product = jnp.einsum("pcab,pcbe->pcae", intersection, partner_amps, precision=HIGHEST)
    sandwich = jnp.einsum("pcae,pcfe->pcaf", half_product, intersection, precision=HIGHEST)
    return pair_amps + jnp.einsum("pc,pcaf->paf", weights, sandwich, precision=HIGHEST)


def fit_term(pair_basis, dressed, blocks, weights):
    pair_count, pno_count, orbital_count = pair_basis.shape
    flat_basis = pair_basis.reshape(pair_count * pno_count, orbital_count)
    stacked = blocks.reshape(2 * orbital_count, orbital_count)
    projected = jnp.dot(
        flat_basis, stacked.T, precision=HIGHEST, preferred_element_type=jnp.float32
    )
    projected = projected.reshape(pair_count, pno_count, 2, orbital_count)
    inner_blocks = jnp.einsum("par,pbmr->mpab", pair_basis, projected, precision=HIGHEST)
    left_product = jnp.einsum("pai,pij->paj", inner_blocks[0], dressed, precision=HIGHEST)
    fit_contrib = jnp.einsum("paj,pbj->pab", left_product, inner_blocks[1], precision=HIGHEST)
    return weights[:, None, None] * fit_contrib


def on_device_ring(pno_basis, amplitudes, send_list, couple, couple_weight, fit_weight, fit_blocks):
    pair_count, pno_count, _ = pno_basis.shape
    block_count = fit_blocks.shape[0]
    pair_amps = amplitudes.reshape(pair_count, pno_count, pno_count)
    send_order = send_list.reshape(-1)
    basis_in = lax.all_to_all(jnp.take(pno_basis, send_order, axis=0), "blk", split_axis=0, concat_axis=0, tiled=True)
    amps_in = lax.all_to_all(jnp.take(pair_amps, send_order, axis=0), "blk", split_axis=0, concat_axis=0, tiled=True)
    partner_basis = jnp.take(basis_in, couple, axis=0)
    intersection = jnp.einsum("par,pcbr->pcab", pno_basis, partner_basis, precision=HIGHEST)
    dressed = dress_with(pair_amps, intersection, jnp.take(amps_in, couple, axis=0), couple_weight)
    updated = dressed
    current = lax.all_gather(fit_blocks, "dom", axis=2, tiled=True)
    for stop in range(fit_weight.shape[1] // block_count):
        if stop > 0:
            current = from_behind(current, "blk", 1)
        for b in range(block_count):
            updated = updated + fit_term(pno_basis, dressed, current[b], fit_weight[:, stop * block_count + b])
    return updated.reshape(pair_count, pno_count * pno_count)


def solution(mesh):
    placed = (
        P(("blk", "dom"), None, None),
        P(("blk", "dom"), None),
        P("blk", "dom", None, None),
        P(("blk", "dom"), None),
        P(("blk", "dom"), None),
        P(("blk", "dom"), None),
        P("blk", None, "dom", None),
    )

    def on_device(*args):
        send_list, fit_weight, fit_blocks = args[2], args[5], args[6]
        group_total = mesh.shape["blk"]
        meets_all = fit_weight.shape[1] == group_total * fit_blocks.shape[0]
        if meets_all and group_total % SET == 0 and group_total > SET and group_total & (group_total - 1) == 0 and send_list.shape[3] == 1:
            return on_device_shared(*args)
        return on_device_ring(*args)

    return jax.shard_map(
        on_device, mesh=mesh, in_specs=placed, out_specs=P(("blk", "dom"), None), check_vma=False
    )
```
